32 devices in a mesh: dp: 2 (over x), ctx: 16 (over z, y, core).
Axes of the slice: x: 2, y: 2, z: 4, core: 2. Of those that a mesh axis runs over, the one named last changes fastest.
Arguments:
- tokens: bfloat16 [2, 2048, 1152], P('dp', 'ctx'), may hold values from -50 to 50
- cotangent: bfloat16 [2, 2048, 1152], P('dp', 'ctx'), may hold values from -45 to 45
- clip_frames: int32 [2, 8], P('dp'), may hold values from 1 to 8, as said below
- clip_offsets: int32 [2, 8], P('dp'), may hold values from 0 to 1920, as said below
- clip_heights: int32 [2, 8], P('dp'), may hold values from 8 to 16, as said below
- clip_widths: int32 [2, 8], P('dp'), may hold values from 4 to 8
- spatial_gain: float32 [1152], replicated, may hold values from 0.1 to 1.9
- spatial_qkv: bfloat16 [1728, 1152], P('ctx'), may hold values from -0.1875 to 0.1875
- spatial_out: bfloat16 [576, 1152], P('ctx'), may hold values from -0.25 to 0.25
- temporal_gain: float32 [1152], replicated, may hold values from 0.1 to 1.9
- temporal_qkv: bfloat16 [1728, 1152], P('ctx'), may hold values from -0.1875 to 0.1875
- temporal_out: bfloat16 [576, 1152], P('ctx'), may hold values from -0.25 to 0.25
Outputs:
- output: bfloat16 [2, 2048, 1152], P('dp', 'ctx')
- tokens_grad: bfloat16 [2, 2048, 1152], P('dp', 'ctx')
- gain_grads: float32 [2, 1152], replicated
The draws below stay inside these ranges and needn't reach their ends.
Inputs may be any that keep to these rules, and one draw needn't show every extreme that they name: `clip_frames`: clip 0 of every bin starts at offset 0 and has exactly 8 frame tiles; every later clip starts after the one before it ends, and the last ends by tile 16. `clip_offsets`: offsets are multiples of 128 and rise from clip to clip; the last clip of every bin starts at tile 16 - 1. `clip_heights`: clip 0 of every bin has 16 rows and 8 columns; heights times widths never exceed 128.
All inputs are finite; a program needn't handle non-finite values.
Results may differ from the reference program's by a relative error of at most 0.024.
Values may be sent and summed in bfloat16 or wider, within the bound.
No kernel may reach another device: no remote copies, remote signals or barrier semaphores. Data moves between devices by JAX's collectives and lax.ppermute only.
A program may use at most 64 MiB of HBM per device.

```python
import math
import jax
import jax.numpy as jnp
from jax import lax

D = 1152
HEADS = 8
FRAME = 128
NCLIP = 8
INNER = 576
NF = 16
TOKENS = 2048
BINS = 2


def frame_layout(key):

    def one_bin(bin_key):
        cut_key, size_key = jax.random.split(bin_key)
        half_frames = NF // 2
        shuffled = jax.random.permutation(cut_key, half_frames - 2) + 1
        chosen = jnp.concatenate([shuffled[:NCLIP - 3], jnp.full((1,), half_frames - 1, jnp.int32)])
        cut_points = jnp.sort(chosen).astype(jnp.int32)
        boundaries = jnp.concatenate([jnp.zeros((1,), jnp.int32), cut_points, jnp.full((1,), half_frames, jnp.int32)])
        span_sizes = boundaries[1:] - boundaries[:-1]
        later_counts = jax.random.randint(size_key, (NCLIP - 1,), 1, span_sizes + 1).astype(jnp.int32)
        counts = jnp.concatenate([jnp.full((1,), half_frames, jnp.int32), later_counts])
        starts = jnp.concatenate([jnp.zeros((1,), jnp.int32), half_frames + boundaries[:-1]])
        return (counts, starts * FRAME)
    return jax.vmap(one_bin)(jax.random.split(key, BINS))


def draw_clip_frames(key, part):
    counts, starts = frame_layout(key)
    return counts


def draw_clip_offsets(key, part):
    counts, starts = frame_layout(key)
    return starts


def draw_clip_heights(key, part):
    key = jax.random.fold_in(key, 3)
    heights = jax.random.randint(key, (BINS, NCLIP), max(1, FRAME // 16), FRAME // 8 + 1).astype(jnp.int32)
    return heights.at[:, 0].set(FRAME // 8)


def draw_clip_widths(key, part):
    key = jax.random.fold_in(key, 4)
    widths_drawn = jax.random.randint(key, (BINS, NCLIP), 4, 9).astype(jnp.int32)
    return widths_drawn.at[:, 0].set(8)


def draw_tokens(key, part):
    key = jax.random.fold_in(key, 5)
    column_key, row_key, base_key = jax.random.split(key, 3)
    column_scale = jnp.exp(jax.random.uniform(column_key, (D,)) * math.log(10.0))
    row_scale = jnp.exp(jax.random.uniform(row_key, (BINS, TOKENS, 1)) * math.log(10.0))
    base_draw = jnp.clip(jax.random.normal(base_key, (BINS, TOKENS, D)), -5.0, 5.0)
    return (base_draw * column_scale * row_scale * 0.1).astype(jnp.bfloat16)


def draw_cotangent(key, part):
    key = jax.random.fold_in(key, 6)
    position = jnp.arange(TOKENS).astype(jnp.float32) / (TOKENS - 1)
    rising = (3.0 ** position)[None, :, None]
    base_draw = jnp.clip(jax.random.normal(key, (BINS, TOKENS, D)), -5.0, 5.0)
    return (base_draw * rising).astype(jnp.bfloat16)


def steps_of(rng, shape, shards, smallest, top_value):
    def one(dim, blocks):
        steps = jax.random.uniform(jax.random.fold_in(jax.random.fold_in(rng, 6), dim), (blocks,), jnp.float32, smallest / len(shards), top_value / len(shards))
        return jnp.repeat(jnp.exp(steps), shape[dim] // blocks).reshape((-1,) + (1,) * (len(shape) - dim - 1))

    factor_of = one(*shards[0])
    for cut in shards[1:]:
        factor_of = factor_of * one(*cut)
    return factor_of


def noise(stream_key, dims, scale, limit, pieces=(), kind=jnp.bfloat16):
    values = jax.random.normal(stream_key, dims, jnp.float32) * scale
    if len(pieces) > 0:
        values = steps_of(stream_key, dims, pieces, -0.22, 0.18) * values
    return jnp.clip(values, min=-limit, max=limit).astype(kind)


def setup_inputs(seed: int = 0) -> dict:
    keys = jax.random.split(jax.random.key(seed), 13)
    return {
        "tokens": draw_tokens(jax.random.fold_in(keys[12], 71), 0),
        "cotangent": draw_cotangent(jax.random.fold_in(keys[12], 71), 0),
        "clip_frames": draw_clip_frames(jax.random.fold_in(keys[12], 71), 0),
        "clip_offsets": draw_clip_offsets(jax.random.fold_in(keys[12], 71), 0),
        "clip_heights": draw_clip_heights(jax.random.fold_in(keys[12], 71), 0),
        "clip_widths": draw_clip_widths(jax.random.fold_in(keys[12], 71), 0),
        "spatial_gain": jnp.clip(1.0 + 0.18 * jax.random.normal(keys[6], (D,), jnp.float32), 0.1, 1.9),
        "spatial_qkv": noise(keys[7], (3 * INNER, D), D ** -0.5, 0.1875, ((0, 16),)),
        "spatial_out": noise(keys[8], (INNER, D), INNER ** -0.5, 0.25, ((0, 16),)),
        "temporal_gain": jnp.clip(1.0 + 0.18 * jax.random.normal(keys[9], (D,), jnp.float32), 0.1, 1.9),
        "temporal_qkv": noise(keys[10], (3 * INNER, D), D ** -0.5, 0.1875, ((0, 16),)),
        "temporal_out": noise(keys[11], (INNER, D), INNER ** -0.5, 0.25, ((0, 16),)),
    }


EPSILON = 1e-06
ROPE_BASE = 10000.0

def normalize(values, norm_gain):
    widened = values.astype(jnp.float32)
    mean_square = lax.optimization_barrier(jnp.mean(widened * widened, axis=-1, keepdims=True))
    return (widened * lax.rsqrt(mean_square + EPSILON) * norm_gain).astype(jnp.bfloat16)

def contract(left, right):
    return lax.dot_general(left, right, (((1,), (1,)), ((), ())), preferred_element_type=jnp.float32)

def attend(queries, keys_in, values, allowed, live_rows):
    score_scale = queries.shape[-1] ** (-0.5)
    scores = jnp.einsum('gqhe,gkhe->ghqk', queries.astype(jnp.float32), keys_in.astype(jnp.float32)) * score_scale
    weights = jnp.exp(scores) * allowed[:, None, :, :]
    totals = lax.optimization_barrier(jnp.sum(weights, axis=-1, keepdims=True)) + (1.0 - live_rows)[:, None, :, None]
    shares = (weights / totals).astype(jnp.bfloat16)
    blended = jnp.einsum('ghqk,gkhe->gqhe', shares.astype(jnp.float32), values.astype(jnp.float32))
    return (blended * live_rows[:, :, None, None]).astype(jnp.bfloat16)

def rotate(vectors, frame_times):
    half_size = vectors.shape[-1] // 2
    pair_index = jnp.arange(half_size).astype(jnp.float32)
    frequency = ROPE_BASE ** (-pair_index / half_size)
    angles = frame_times[:, None] * frequency[None, :]
    cosine_table = jnp.cos(angles)[None, :, None, :]
    sine_table = jnp.sin(angles)[None, :, None, :]
    widened = vectors.astype(jnp.float32)
    first_half = widened[..., :half_size]
    second_half = widened[..., half_size:]
    turned = jnp.concatenate([first_half * cosine_table - second_half * sine_table, first_half * sine_table + second_half * cosine_table], axis=-1)
    return turned.astype(jnp.bfloat16)

def clip_tables(clip_frames, clip_offsets, clip_heights, clip_widths, total_frames):
    starts = clip_offsets // FRAME
    frame_ids = jnp.arange(total_frames, dtype=jnp.int32)[:, None]
    member = ((frame_ids >= starts[None, :]) & (frame_ids < (starts + clip_frames)[None, :])).astype(jnp.float32)
    frame_times = lax.optimization_barrier(jnp.sum(member * (frame_ids - starts[None, :]).astype(jnp.float32), axis=1))
    counts = lax.optimization_barrier(jnp.sum(member * (clip_heights * clip_widths).astype(jnp.float32)[None, :], axis=1))
    same_clip = jnp.dot(member, member.T, precision=lax.Precision.HIGHEST)
    return (frame_times, counts, same_clip)

def spatial_block(tokens_in, norm_gain, project, output, allowed, live_rows):
    local_frames, frame_size, feature_count = tokens_in.shape
    normed = normalize(tokens_in, norm_gain)
    projected = contract(normed.reshape(-1, feature_count), project).astype(jnp.bfloat16)
    divided = projected.reshape(local_frames, frame_size, 3, HEADS, -1)
    blended = attend(divided[:, :, 0], divided[:, :, 1], divided[:, :, 2], allowed, live_rows)
    update = jnp.dot(blended.reshape(local_frames * frame_size, -1), output, preferred_element_type=jnp.float32)
    return (tokens_in.astype(jnp.float32) + update.reshape(tokens_in.shape)).astype(jnp.bfloat16)

def temporal_front(hidden, norm_gain, project):
    normed = normalize(hidden, norm_gain)
    projected = contract(normed.reshape(-1, normed.shape[-1]), project).astype(jnp.bfloat16)
    return projected.reshape(hidden.shape[:-1] + (project.shape[0],))

def temporal_core(projected, frame_times, allowed, live_rows):
    total_frames, slot_count = (projected.shape[0], projected.shape[1])
    divided = projected.reshape(total_frames, slot_count, 3, HEADS, -1)
    arranged = jnp.transpose(divided, (2, 1, 0, 3, 4))
    queries = rotate(arranged[0], frame_times)
    keys_in = rotate(arranged[1], frame_times)
    blended = attend(queries, keys_in, arranged[2], allowed, live_rows)
    return jnp.transpose(blended, (1, 0, 2, 3)).reshape(total_frames, slot_count, -1)

def temporal_back(hidden, blended, output):
    update = jnp.dot(blended.reshape(-1, blended.shape[-1]), output, preferred_element_type=jnp.float32)
    return (hidden.astype(jnp.float32) + update.reshape(hidden.shape)).astype(jnp.bfloat16)

def reference(tokens, cotangent, clip_frames, clip_offsets, clip_heights, clip_widths, spatial_gain, spatial_qkv, spatial_out, temporal_gain, temporal_qkv, temporal_out):

    def one_bin(bundle):
        tokens_bin, cotangent_bin, frames_bin, offsets_bin, heights_bin, widths_bin = bundle
        frame_times, counts, same_clip = clip_tables(frames_bin, offsets_bin, heights_bin, widths_bin, NF)
        slot_ids = jnp.arange(FRAME).astype(jnp.float32)
        live_space = (slot_ids[None, :] < counts[:, None]).astype(jnp.float32)
        allowed_space = jnp.broadcast_to(live_space[:, None, :], (NF, FRAME, FRAME))
        live_time = live_space.T
        allowed_time = same_clip[None, :, :] * live_time[:, None, :]

        def forward(tokens_in, space_gain, time_gain):
            hidden = spatial_block(tokens_in, space_gain, spatial_qkv, spatial_out, allowed_space, live_space)
            projected = temporal_front(hidden, time_gain, temporal_qkv)
            blended = temporal_core(projected, frame_times, allowed_time, live_time)
            return temporal_back(hidden, blended, temporal_out)
        result, pullback = jax.vjp(forward, tokens_bin.reshape(NF, FRAME, D), spatial_gain, temporal_gain)
        grad_tokens, grad_space, grad_time = pullback(cotangent_bin.reshape(NF, FRAME, D))
        return (result.reshape(TOKENS, D), grad_tokens.reshape(TOKENS, D), grad_space, grad_time)
    output, tokens_grad, grad_space, grad_time = lax.map(one_bin, (tokens, cotangent, clip_frames, clip_offsets, clip_heights, clip_widths))
    gain_grads = jnp.stack([lax.optimization_barrier(jnp.sum(grad_space, axis=0)), lax.optimization_barrier(jnp.sum(grad_time, axis=0))]) / math.sqrt(BINS * TOKENS)
    return (output, tokens_grad, gain_grads)
```

```python
import functools
import math

import jax
import jax.numpy as jnp
from jax import lax
from jax.experimental import pallas as pl
from jax.experimental.pallas import tpu as pltpu
from jax.sharding import PartitionSpec as P

HEADS = 8
FRAME = 128
EPSILON = 1e-06
ROPE_BASE = 10000.0
F32 = jnp.float32
BF16 = jnp.bfloat16
VMEM_LIMIT = 40 * 1024 * 1024


def nn(a, b):
    return lax.dot_general(a, b, (((1,), (0,)), ((), ())), preferred_element_type=F32)


def nt(a, b):
    return lax.dot_general(a, b, (((1,), (1,)), ((), ())), preferred_element_type=F32)


def tn(a, b):
    return lax.dot_general(a, b, (((0,), (0,)), ((), ())), preferred_element_type=F32)


class Rows:
    def __init__(self, qkv_rows, out_rows, size):
        self.qkv, self.out, self.size = qkv_rows, out_rows, size
        self.shard = qkv_rows + out_rows
        self.total = self.shard * size
        self.inner = out_rows * size
        self.head = self.inner // HEADS

    def spans(self, first, count, per_shard, shift):
        found = []
        row = first
        while row < first + count:
            block, inside = divmod(row, per_shard)
            length = min(per_shard - inside, first + count - row)
            place = block * self.shard + shift + inside
            if found and found[-1][0] + found[-1][1] == place:
                found[-1] = (found[-1][0], found[-1][1] + length)
            else:
                found.append((place, length))
            row += length
        return found

    def qkv_spans(self, which, head):
        return self.spans(which * self.inner + head * self.head, self.head, self.qkv, 0)

    def out_spans(self, head):
        return self.spans(head * self.head, self.head, self.out, self.qkv)


def read_rows(ref, spans):
    parts = [ref[place : place + length, :] for place, length in spans]
    return parts[0] if len(parts) == 1 else jnp.concatenate(parts, axis=0)


def write_rows(ref, spans, value):
    done = 0
    for place, length in spans:
        ref[place : place + length, :] = value[done : done + length, :]
        done += length


def inverse_size(values):
    return lax.rsqrt(jnp.mean(values * values, axis=-1, keepdims=True) + EPSILON)


def norm_back(values, inverse, gain, grad):
    scaled = grad * gain
    middle = jnp.mean(scaled * values, axis=-1, keepdims=True)
    grad_values = inverse * scaled - values * (inverse * inverse * inverse * middle)
    grad_gain = jnp.sum(grad * (values * inverse), axis=0, keepdims=True)
    return grad_values, grad_gain


def shares_of(queries, keys, allowed, live, scale):
    scores = tn(keys, queries) * scale
    weights = jnp.where(allowed > 0.0, jnp.exp(jnp.where(allowed > 0.0, scores, 0.0)), 0.0)
    totals = jnp.sum(weights, axis=0, keepdims=True) + (1.0 - live)
    return weights * (1.0 / totals)


def attend_back(queries, keys, values, shares, shares_low, grad, scale):
    grad_shares = tn(values, grad)
    middle = jnp.sum(shares * grad_shares, axis=0, keepdims=True)
    grad_scores = (shares * (grad_shares - middle) * scale).astype(BF16)
    return nn(keys, grad_scores), nt(queries, grad_scores), nt(grad, shares_low)


def space_forward(rows, tokens, gain, weights, allowed, live, hidden, saved, shares_out, project, mixed):
    weight = weights[...].reshape(rows.total, -1)
    values = tokens[...].astype(F32)
    normed = (values * inverse_size(values) * gain[...]).astype(BF16)
    project[...] = nt(weight, normed)
    saved[...] = project[...].astype(BF16)
    mixed[...] = jnp.zeros_like(mixed)
    scale = rows.head ** (-0.5)
    for head in range(HEADS):
        query, key, value = (
            read_rows(project, rows.qkv_spans(which, head)).astype(BF16) for which in range(3)
        )
        shares = shares_of(query, key, allowed[...], live[...], scale).astype(BF16)
        shares_out[head] = shares
        write_rows(mixed, rows.out_spans(head), nn(value, shares) * live[...])
    update = tn(mixed[...].astype(BF16), weight)
    hidden[...] = (values + update).astype(BF16)


def time_front(rows, hidden, gain, cotangent, weights, is_out, sent):
    weight = weights[...].reshape(rows.total, -1)
    values = hidden[...].astype(F32)
    normed = (values * inverse_size(values) * gain[...]).astype(BF16)
    both = nt(jnp.concatenate([normed, cotangent[...]], axis=0), weight)
    count = values.shape[0]
    sent[...] = jnp.where(is_out[...] > 0.0, both[count:], both[:count]).astype(BF16)


def time_core(rows, arrived, allowed, live, cosine, sine, sent, project, result):
    count = arrived.shape[0]
    for first in range(0, rows.total, FRAME):
        project[first : first + FRAME, :] = arrived[:, first : first + FRAME].astype(F32).T
    scale = rows.head ** (-0.5)
    half = rows.head // 2

    def swapped(vectors):
        return jnp.concatenate([vectors[half:], vectors[:half]], axis=0)

    for head in range(HEADS):
        turned = []
        for which in range(2):
            vectors = read_rows(project, rows.qkv_spans(which, head))
            turned.append((vectors * cosine[...] + swapped(vectors) * sine[...]).astype(BF16))
        query, key = turned
        value = read_rows(project, rows.qkv_spans(2, head)).astype(BF16)
        grad = (read_rows(project, rows.out_spans(head)) * live[...]).astype(BF16)
        shares = shares_of(query, key, allowed[...], live[...], scale)
        shares_low = shares.astype(BF16)
        write_rows(result, rows.out_spans(head), nn(value, shares_low) * live[...])
        grads = attend_back(query, key, value, shares, shares_low, grad, scale)
        for which in range(2):
            turned_grad = grads[which].astype(BF16).astype(F32)
            write_rows(
                result,
                rows.qkv_spans(which, head),
                turned_grad * cosine[...] - swapped(turned_grad) * sine[...],
            )
        write_rows(result, rows.qkv_spans(2, head), grads[2])
    for first in range(0, rows.total, FRAME):
        sent[:, first : first + FRAME] = result[first : first + FRAME, :].T.astype(BF16)


def finish(
    rows,
    arrived,
    is_out,
    time_weights,
    hidden,
    time_gain,
    cotangent,
    space_weights,
    saved,
    shares_in,
    live,
    tokens,
    space_gain,
    output,
    grad_tokens,
    gains,
    project,
    grad_project,
):
    count = arrived.shape[0]
    time_weight = time_weights[...].reshape(rows.total, -1)
    space_weight = space_weights[...].reshape(rows.total, -1)
    received = arrived[...]
    zeros = jnp.zeros_like(received)
    mask = jnp.broadcast_to(is_out[...] > 0.0, received.shape)
    left = jnp.concatenate([jnp.where(mask, zeros, received), jnp.where(mask, received, zeros)], axis=0)
    both = nn(left, time_weight)
    values = hidden[...].astype(F32)
    output[...] = (values + both[count:]).astype(BF16)
    grad_normed = both[:count].astype(BF16).astype(F32)
    grad_front, grad_time_gain = norm_back(values, inverse_size(values), time_gain[...], grad_normed)
    grad_hidden = (cotangent[...].astype(F32) + grad_front).astype(BF16)

    project[...] = nt(space_weight, grad_hidden)
    grad_project[...] = jnp.zeros_like(grad_project)
    scale = rows.head ** (-0.5)
    for head in range(HEADS):
        query, key, value = (
            read_rows(saved, rows.qkv_spans(which, head)).astype(BF16) for which in range(3)
        )
        grad = (read_rows(project, rows.out_spans(head)) * live[...]).astype(BF16)
        shares_low = shares_in[head]
        grads = attend_back(query, key, value, shares_low.astype(F32), shares_low, grad, scale)
        for which in range(3):
            write_rows(grad_project, rows.qkv_spans(which, head), grads[which])
    grad_normed = tn(grad_project[...].astype(BF16), space_weight).astype(BF16).astype(F32)
    values = tokens[...].astype(F32)
    grad_values, grad_space_gain = norm_back(values, inverse_size(values), space_gain[...], grad_normed)
    grad_tokens[...] = (grad_hidden.astype(F32) + grad_values).astype(BF16)
    both_gains = jnp.concatenate([grad_space_gain, grad_time_gain], axis=0)
    gains[...] = jnp.broadcast_to(both_gains[None], gains.shape)


def whole(shape, place=None):
    place = (0,) * len(shape) if place is None else place
    return pl.BlockSpec(shape, lambda step: place)


def call(body, out_shapes, scratch, operands, specs=None, cost=None):
    specs = [None] * len(operands) if specs is None else specs
    return pl.pallas_call(
        body,
        out_shape=out_shapes,
        grid=(1,),
        in_specs=[whole(x.shape) if spec is None else spec for x, spec in zip(operands, specs)],
        out_specs=jax.tree.map(lambda x: whole(x.shape), out_shapes),
        scratch_shapes=scratch,
        compiler_params=pltpu.CompilerParams(vmem_limit_bytes=VMEM_LIMIT),
        cost_estimate=cost,
    )(*operands)


def clip_tables(clip_frames, clip_offsets, clip_heights, clip_widths, total_frames):
    starts = clip_offsets // FRAME
    frame_ids = jnp.arange(total_frames, dtype=jnp.int32)[:, None]
    member = (frame_ids >= starts[None, :]) & (frame_ids < (starts + clip_frames)[None, :])
    frame_times = jnp.sum(jnp.where(member, frame_ids - starts[None, :], 0), axis=1).astype(F32)
    counts = jnp.sum(jnp.where(member, (clip_heights * clip_widths)[None, :], 0), axis=1)
    same_clip = jnp.any(member[:, None, :] & member[None, :, :], axis=-1)
    return frame_times, counts, same_clip


def shards(
    tokens,
    cotangent,
    clip_frames,
    clip_offsets,
    clip_heights,
    clip_widths,
    spatial_gain,
    spatial_qkv,
    spatial_out,
    temporal_gain,
    temporal_qkv,
    temporal_out,
):
    size = lax.axis_size("ctx")
    rank = lax.axis_index("ctx")
    everyone = lax.axis_size("dp") * size
    count, features = tokens.shape[1], tokens.shape[2]
    assert count == FRAME and FRAME % size == 0
    slots = FRAME // size
    rows = Rows(spatial_qkv.shape[0], spatial_out.shape[0], size)
    half = rows.head // 2

    packed = jnp.concatenate([spatial_qkv, spatial_out, temporal_qkv, temporal_out], axis=0)
    gathered = lax.all_gather(packed, "ctx", axis=0)
    if rows.shard % 16 == 0:
        space_weights = time_weights = gathered
        space_spec = whole((size, rows.shard, features), (0, 0, 0))
        time_spec = whole((size, rows.shard, features), (0, 1, 0))
    else:
        space_weights = gathered[:, : rows.shard].reshape(rows.total, features)
        time_weights = gathered[:, rows.shard :].reshape(rows.total, features)
        space_spec = time_spec = None

    frame_times, counts, same_clip = clip_tables(
        clip_frames[0], clip_offsets[0], clip_heights[0], clip_widths[0], size
    )
    space_live = jnp.arange(FRAME, dtype=jnp.int32) < counts[rank]
    space_allowed = jnp.broadcast_to(space_live[:, None], (FRAME, FRAME)).astype(F32)
    space_live = space_live[None, :].astype(F32)
    slot_ids = rank * slots + jnp.arange(slots, dtype=jnp.int32)
    time_live = (slot_ids[None, :] < counts[:, None]).reshape(FRAME)
    same_slot = jnp.eye(slots, dtype=bool)
    time_allowed = (same_clip[:, None, :, None] & same_slot[None, :, None, :]).reshape(FRAME, FRAME)
    time_allowed = (time_allowed & time_live[:, None]).astype(F32)
    time_live = time_live[None, :].astype(F32)
    frequency = ROPE_BASE ** (-jnp.arange(half).astype(F32) / half)
    angles = frequency[:, None] * jnp.repeat(frame_times, slots)[None, :]
    cosine = jnp.cos(angles)
    sine = jnp.sin(angles)
    cosine = jnp.concatenate([cosine, cosine], axis=0)
    sine = jnp.concatenate([-sine, sine], axis=0)
    is_out = (jnp.arange(rows.total, dtype=jnp.int32) % rows.shard >= rows.qkv).astype(F32)[None, :]

    tokens_local = tokens[0]
    cotangent_local = cotangent[0]
    space_gain = spatial_gain[None, :]
    time_gain = temporal_gain[None, :]
    wide = pltpu.VMEM((rows.total, FRAME), F32)

    hidden, saved, shares = call(
        functools.partial(space_forward, rows),
        (
            jax.ShapeDtypeStruct((FRAME, features), BF16),
            jax.ShapeDtypeStruct((rows.total, FRAME), BF16),
            jax.ShapeDtypeStruct((HEADS, FRAME, FRAME), BF16),
        ),
        [wide, wide],
        (tokens_local, space_gain, space_weights, space_allowed, space_live),
        [None, None, space_spec, None, None],
    )
    sent = call(
        functools.partial(time_front, rows),
        jax.ShapeDtypeStruct((FRAME, rows.total), BF16),
        [],
        (hidden, time_gain, cotangent_local, time_weights, is_out),
        [None, None, None, time_spec, None],
    )
    arrived = lax.all_to_all(
        sent.reshape(size, slots, rows.total), "ctx", split_axis=0, concat_axis=0, tiled=True
    )
    sent = call(
        functools.partial(time_core, rows),
        jax.ShapeDtypeStruct((FRAME, rows.total), BF16),
        [wide, wide],
        (arrived.reshape(FRAME, rows.total), time_allowed, time_live, cosine, sine),
    )
    arrived = lax.all_to_all(
        sent.reshape(size, slots, rows.total), "ctx", split_axis=0, concat_axis=0, tiled=True
    )
    result, grad_tokens, gains = call(
        functools.partial(finish, rows),
        (
            jax.ShapeDtypeStruct((FRAME, features), BF16),
            jax.ShapeDtypeStruct((FRAME, features), BF16),
            jax.ShapeDtypeStruct((everyone, 2, features), F32),
        ),
        [wide, wide],
        (
            arrived.reshape(FRAME, rows.total),
            is_out,
            time_weights,
            hidden,
            time_gain,
            cotangent_local,
            space_weights,
            saved,
            shares,
            space_live,
            tokens_local,
            space_gain,
        ),
        [None, None, time_spec, None, None, None, space_spec, None, None, None, None, None],
    )
    gains = lax.all_to_all(gains, ("dp", "ctx"), split_axis=0, concat_axis=0, tiled=True)
    gain_grads = jnp.sum(gains, axis=0) * (1.0 / math.sqrt(everyone * FRAME))
    return result[None], grad_tokens[None], gain_grads


def solution(mesh):
    return jax.shard_map(
        shards,
        mesh=mesh,
        in_specs=(
            P("dp", "ctx", None),
            P("dp", "ctx", None),
            P("dp", None),
            P("dp", None),
            P("dp", None),
            P("dp", None),
            P(),
            P("ctx", None),
            P("ctx", None),
            P(),
            P("ctx", None),
            P("ctx", None),
        ),
        out_specs=(P("dp", "ctx", None), P("dp", "ctx", None), P()),
        check_vma=False,
    )
```

```python
import functools
import math

import jax
import jax.numpy as jnp
from jax import lax
from jax.experimental import pallas as pl
from jax.experimental.pallas import tpu as pltpu
from jax.sharding import PartitionSpec as P

HEADS = 8
FRAME = 128
EPSILON = 1e-06
ROPE_BASE = 10000.0
F32 = jnp.float32
BF16 = jnp.bfloat16
VMEM_LIMIT = 40 * 1024 * 1024


def nn(a, b):
    return lax.dot_general(a, b, (((1,), (0,)), ((), ())), preferred_element_type=F32)


def nt(a, b):
    return lax.dot_general(a, b, (((1,), (1,)), ((), ())), preferred_element_type=F32)


def tn(a, b):
    return lax.dot_general(a, b, (((0,), (0,)), ((), ())), preferred_element_type=F32)


class Rows:
    def __init__(self, qkv_rows, out_rows, size):
        self.qkv, self.out, self.size = qkv_rows, out_rows, size
        self.shard = qkv_rows + out_rows
        self.total = self.shard * size
        self.inner = out_rows * size
        self.head = self.inner // HEADS

    def spans(self, first, count, per_shard, shift):
        found = []
        row = first
        while row < first + count:
            block, inside = divmod(row, per_shard)
            length = min(per_shard - inside, first + count - row)
            place = block * self.shard + shift + inside
            if found and found[-1][0] + found[-1][1] == place:
                found[-1] = (found[-1][0], found[-1][1] + length)
            else:
                found.append((place, length))
            row += length
        return found

    def qkv_spans(self, which, head):
        return self.spans(which * self.inner + head * self.head, self.head, self.qkv, 0)

    def out_spans(self, head):
        return self.spans(head * self.head, self.head, self.out, self.qkv)


def read_rows(ref, spans):
    parts = [ref[place : place + length, :] for place, length in spans]
    return parts[0] if len(parts) == 1 else jnp.concatenate(parts, axis=0)


def write_rows(ref, spans, value):
    done = 0
    for place, length in spans:
        ref[place : place + length, :] = value[done : done + length, :]
        done += length


def inverse_size(values):
    return lax.rsqrt(jnp.mean(values * values, axis=-1, keepdims=True) + EPSILON)


def norm_back(values, inverse, gain, grad):
    scaled = grad * gain
    middle = jnp.mean(scaled * values, axis=-1, keepdims=True)
    grad_values = inverse * scaled - values * (inverse * inverse * inverse * middle)
    grad_gain = jnp.sum(grad * (values * inverse), axis=0, keepdims=True)
    return grad_values, grad_gain


def shares_of(queries, keys, allowed, live, scale):
    scores = tn(keys, queries) * scale
    weights = jnp.where(allowed > 0.0, jnp.exp(jnp.where(allowed > 0.0, scores, 0.0)), 0.0)
    totals = jnp.sum(weights, axis=0, keepdims=True) + (1.0 - live)
    return weights * (1.0 / totals)


def attend_back(queries, keys, values, shares, shares_low, grad, scale):
    grad_shares = tn(values, grad)
    middle = jnp.sum(shares * grad_shares, axis=0, keepdims=True)
    grad_scores = (shares * (grad_shares - middle) * scale).astype(BF16)
    return nn(keys, grad_scores), nt(queries, grad_scores), nt(grad, shares_low)


def start_weights(count, order, mine, other, space, time, sems):
    def start(first, second):
        for index in range(count):
            pltpu.make_async_copy(first[index], space.at[order[index]], sems.at[0, index]).start()
        for index in range(count):
            pltpu.make_async_copy(second[index], time.at[order[index]], sems.at[1, index]).start()

    @pl.when(order[count] == 0)
    def _():
        start(mine, other)

    @pl.when(order[count] != 0)
    def _():
        start(other, mine)


def wait_weights(count, order, pieces, target, sems, which):
    for index in range(count):
        pltpu.make_async_copy(pieces[index], target.at[order[index]], sems.at[which, index]).wait()


def front(rows, pieces, order, tokens, space_gain, allowed, live, time_gain, cotangent, is_out, *refs):
    mine, other, refs = refs[:pieces], refs[pieces : 2 * pieces], refs[2 * pieces :]
    hidden, saved, shares_out, sent, space, time, project, mixed, sems = refs
    start_weights(pieces, order, mine, other, space, time, sems)
    values = tokens[...].astype(F32)
    normed = (values * inverse_size(values) * space_gain[...]).astype(BF16)
    mixed[...] = jnp.zeros_like(mixed)
    wait_weights(pieces, order, mine, space, sems, 0)
    weight = space[...].reshape(rows.total, -1)
    project[...] = nt(weight, normed)
    saved[...] = project[...].astype(BF16)
    scale = rows.head ** (-0.5)
    for head in range(HEADS):
        query, key, value = (
            read_rows(project, rows.qkv_spans(which, head)).astype(BF16) for which in range(3)
        )
        shares = shares_of(query, key, allowed[...], live[...], scale).astype(BF16)
        shares_out[head] = shares
        write_rows(mixed, rows.out_spans(head), nn(value, shares) * live[...])
    update = tn(mixed[...].astype(BF16), weight)
    low = (values + update).astype(BF16)
    hidden[...] = low
    values = low.astype(F32)
    normed = (values * inverse_size(values) * time_gain[...]).astype(BF16)
    wait_weights(pieces, order, mine, time, sems, 1)
    weight = time[...].reshape(rows.total, -1)
    both = nt(jnp.concatenate([normed, cotangent[...]], axis=0), weight)
    count = values.shape[0]
    sent[...] = jnp.where(is_out[...] > 0.0, both[count:], both[:count]).astype(BF16)


def time_core(rows, arrived, allowed, live, cosine, sine, sent, project, result):
    count = arrived.shape[0]
    for first in range(0, rows.total, FRAME):
        project[first : first + FRAME, :] = arrived[:, first : first + FRAME].astype(F32).T
    scale = rows.head ** (-0.5)
    half = rows.head // 2

    def swapped(vectors):
        return jnp.concatenate([vectors[half:], vectors[:half]], axis=0)

    for head in range(HEADS):
        turned = []
        for which in range(2):
            vectors = read_rows(project, rows.qkv_spans(which, head))
            turned.append((vectors * cosine[...] + swapped(vectors) * sine[...]).astype(BF16))
        query, key = turned
        value = read_rows(project, rows.qkv_spans(2, head)).astype(BF16)
        grad = (read_rows(project, rows.out_spans(head)) * live[...]).astype(BF16)
        shares = shares_of(query, key, allowed[...], live[...], scale)
        shares_low = shares.astype(BF16)
        write_rows(result, rows.out_spans(head), nn(value, shares_low) * live[...])
        grads = attend_back(query, key, value, shares, shares_low, grad, scale)
        for which in range(2):
            turned_grad = grads[which].astype(BF16).astype(F32)
            write_rows(
                result,
                rows.qkv_spans(which, head),
                turned_grad * cosine[...] - swapped(turned_grad) * sine[...],
            )
        write_rows(result, rows.qkv_spans(2, head), grads[2])
    for first in range(0, rows.total, FRAME):
        sent[:, first : first + FRAME] = result[first : first + FRAME, :].T.astype(BF16)


def finish(
    rows,
    pieces,
    order,
    arrived,
    is_out,
    hidden,
    time_gain,
    cotangent,
    saved,
    shares_in,
    live,
    tokens,
    space_gain,
    *refs,
):
    mine, other, refs = refs[:pieces], refs[pieces : 2 * pieces], refs[2 * pieces :]
    output, grad_tokens, gains, space, time, project, grad_project, sems = refs
    start_weights(pieces, order, mine, other, space, time, sems)
    count = arrived.shape[0]
    wait_weights(pieces, order, mine, time, sems, 1)
    time_weight = time[...].reshape(rows.total, -1)
    received = arrived[...]
    zeros = jnp.zeros_like(received)
    mask = jnp.broadcast_to(is_out[...] > 0.0, received.shape)
    left = jnp.concatenate([jnp.where(mask, zeros, received), jnp.where(mask, received, zeros)], axis=0)
    both = nn(left, time_weight)
    values = hidden[...].astype(F32)
    output[...] = (values + both[count:]).astype(BF16)
    grad_normed = both[:count].astype(BF16).astype(F32)
    grad_front, grad_time_gain = norm_back(values, inverse_size(values), time_gain[...], grad_normed)
    grad_hidden = (cotangent[...].astype(F32) + grad_front).astype(BF16)

    wait_weights(pieces, order, mine, space, sems, 0)
    space_weight = space[...].reshape(rows.total, -1)
    project[...] = nt(space_weight, grad_hidden)
    grad_project[...] = jnp.zeros_like(grad_project)
    scale = rows.head ** (-0.5)
    for head in range(HEADS):
        query, key, value = (
            read_rows(saved, rows.qkv_spans(which, head)).astype(BF16) for which in range(3)
        )
        grad = (read_rows(project, rows.out_spans(head)) * live[...]).astype(BF16)
        shares_low = shares_in[head]
        grads = attend_back(query, key, value, shares_low.astype(F32), shares_low, grad, scale)
        for which in range(3):
            write_rows(grad_project, rows.qkv_spans(which, head), grads[which])
    grad_normed = tn(grad_project[...].astype(BF16), space_weight).astype(BF16).astype(F32)
    values = tokens[...].astype(F32)
    grad_values, grad_space_gain = norm_back(values, inverse_size(values), space_gain[...], grad_normed)
    grad_tokens[...] = (grad_hidden.astype(F32) + grad_values).astype(BF16)
    both_gains = jnp.concatenate([grad_space_gain, grad_time_gain], axis=0)
    gains[...] = jnp.broadcast_to(both_gains[None], gains.shape)


def call(body, out_shapes, scratch, operands, in_order=None, pieces=()):
    whole = pl.BlockSpec(memory_space=pltpu.VMEM)
    scalars = pl.BlockSpec(memory_space=pltpu.SMEM)
    anywhere = pl.BlockSpec(memory_space=pl.ANY)
    first = () if in_order is None else (in_order,)
    return pl.pallas_call(
        body,
        out_shape=out_shapes,
        in_specs=[scalars] * len(first) + [whole] * len(operands) + [anywhere] * len(pieces),
        out_specs=jax.tree.map(lambda _: whole, out_shapes),
        scratch_shapes=scratch,
        compiler_params=pltpu.CompilerParams(vmem_limit_bytes=VMEM_LIMIT),
    )(*first, *operands, *pieces)


def gather_ring(space_rows, time_rows, size, rank):
    chips = size // 2
    chain = chips // 2

    def chip_at(place):
        place = place % chips
        return 2 * place if place < chain else 2 * (chips - 1 - place) + 1

    def chip_at_traced(place):
        place = lax.rem(place + chips, chips)
        return jnp.where(place < chain, 2 * place, 2 * (chips - 1 - place) + 1)

    forth = [
        (2 * chip_at(place) + core, 2 * chip_at(place + 1) + core)
        for place in range(chips)
        for core in range(2)
    ]
    back = [(target, source) for source, target in forth]
    planes = lax.axis_size("dp")
    plane = lax.rem(lax.axis_index("dp"), 2)

    def onward(rows):
        return lax.ppermute(rows, "ctx", forth)

    def backward(rows):
        return lax.ppermute(rows, "ctx", back)

    def across(rows):
        return lax.ppermute(rows, "dp", [(index, index ^ 1) for index in range(planes)])

    def twin(rows):
        return lax.ppermute(rows, "ctx", [(index, index ^ 1) for index in range(size)])

    own = jnp.where(plane == 0, space_rows, time_rows)
    own_other = jnp.where(plane == 0, time_rows, space_rows)
    far = chips // 2
    up, down = [own], [own]
    for step in range(1, far + 1):
        up.append(onward(up[-1]))
        if step < far:
            down.append(backward(down[-1]))
    down_other = [own_other]
    for step in range(1, far - 1):
        down_other.append(backward(down_other[-1]))
    up_other = [own_other, onward(own_other)]
    for step in range(2, far + 1):
        up_other.append(across(up[step]))
    for step in range(far - 1, far):
        down_other.append(across(down[step]))
    mine = up + down[1:]
    other = up_other + down_other[1:]
    steps = list(range(0, -far - 1, -1)) + list(range(1, far))
    mine += [twin(rows) for rows in mine]
    other += [twin(rows) for rows in other]
    chip, core = rank // 2, lax.rem(rank, 2)
    column, level = lax.rem(chip, 2), chip // 2
    place = jnp.where(column == 0, level, chips - 1 - level)
    found = [chip_at_traced(place + step) for step in steps]
    order = [2 * at + core for at in found] + [2 * at + 1 - core for at in found]
    return mine, other, jnp.stack(order + [plane]).astype(jnp.int32)


def gather_weights(space_rows, time_rows, size, rank):
    if size == 16 and lax.axis_size("dp") % 2 == 0:
        return gather_ring(space_rows, time_rows, size, rank)
    shard, features = space_rows.shape
    gathered = lax.all_gather(jnp.concatenate([space_rows, time_rows], axis=0), "ctx", axis=0)
    gathered = gathered.reshape(size, 2, shard, features)
    mine = gathered[:, 0].reshape(size * shard, features)
    other = gathered[:, 1].reshape(size * shard, features)
    return [mine], [other], jnp.zeros((2,), jnp.int32)


def clip_tables(clip_frames, clip_offsets, clip_heights, clip_widths, total_frames):
    starts = clip_offsets // FRAME
    frame_ids = jnp.arange(total_frames, dtype=jnp.int32)[:, None]
    member = (frame_ids >= starts[None, :]) & (frame_ids < (starts + clip_frames)[None, :])
    frame_times = jnp.sum(jnp.where(member, frame_ids - starts[None, :], 0), axis=1).astype(F32)
    counts = jnp.sum(jnp.where(member, (clip_heights * clip_widths)[None, :], 0), axis=1)
    same_clip = jnp.any(member[:, None, :] & member[None, :, :], axis=-1)
    return frame_times, counts, same_clip


def shards(
    tokens,
    cotangent,
    clip_frames,
    clip_offsets,
    clip_heights,
    clip_widths,
    spatial_gain,
    spatial_qkv,
    spatial_out,
    temporal_gain,
    temporal_qkv,
    temporal_out,
):
    size = lax.axis_size("ctx")
    rank = lax.axis_index("ctx")
    everyone = lax.axis_size("dp") * size
    count, features = tokens.shape[1], tokens.shape[2]
    assert count == FRAME and FRAME % size == 0
    near = size // 2
    slots = FRAME // near
    rows = Rows(spatial_qkv.shape[0], spatial_out.shape[0], size)
    half = rows.head // 2

    mine, other, order = gather_weights(
        jnp.concatenate([spatial_qkv, spatial_out], axis=0),
        jnp.concatenate([temporal_qkv, temporal_out], axis=0),
        size,
        rank,
    )
    pieces = len(mine)
    weight_scratch = pltpu.VMEM((pieces, rows.total // pieces, features), BF16)

    frame_times, counts, same_clip = clip_tables(
        clip_frames[0], clip_offsets[0], clip_heights[0], clip_widths[0], size
    )
    space_live = jnp.arange(FRAME, dtype=jnp.int32) < counts[rank]
    space_allowed = jnp.broadcast_to(space_live[:, None], (FRAME, FRAME)).astype(F32)
    space_live = space_live[None, :].astype(F32)
    first_frame = (rank // near) * near
    near_times = lax.dynamic_slice_in_dim(frame_times, first_frame, near)
    near_counts = lax.dynamic_slice_in_dim(counts, first_frame, near)
    near_clip = lax.dynamic_slice(same_clip, (first_frame, first_frame), (near, near))
    slot_ids = lax.rem(rank, near) * slots + jnp.arange(slots, dtype=jnp.int32)
    time_live = (slot_ids[None, :] < near_counts[:, None]).reshape(FRAME)
    same_slot = jnp.eye(slots, dtype=bool)
    time_allowed = (near_clip[:, None, :, None] & same_slot[None, :, None, :]).reshape(FRAME, FRAME)
    time_allowed = (time_allowed & time_live[:, None]).astype(F32)
    time_live = time_live[None, :].astype(F32)
    frequency = ROPE_BASE ** (-jnp.arange(half).astype(F32) / half)
    angles = frequency[:, None] * jnp.repeat(near_times, slots)[None, :]
    cosine = jnp.cos(angles)
    sine = jnp.sin(angles)
    cosine = jnp.concatenate([cosine, cosine], axis=0)
    sine = jnp.concatenate([-sine, sine], axis=0)
    is_out = (jnp.arange(rows.total, dtype=jnp.int32) % rows.shard >= rows.qkv).astype(F32)[None, :]

    tokens_local = tokens[0]
    cotangent_local = cotangent[0]
    space_gain = spatial_gain[None, :]
    time_gain = temporal_gain[None, :]
    wide = pltpu.VMEM((rows.total, FRAME), F32)

    sems = pltpu.SemaphoreType.DMA((2, pieces))
    groups = [list(range(first, first + near)) for first in range(0, size, near)]

    def exchange(sent):
        arrived = lax.all_to_all(
            sent.reshape(near, slots, rows.total),
            "ctx",
            split_axis=0,
            concat_axis=0,
            axis_index_groups=groups,
            tiled=True,
        )
        return arrived.reshape(FRAME, rows.total)

    hidden, saved, shares, sent = call(
        functools.partial(front, rows, pieces),
        (
            jax.ShapeDtypeStruct((FRAME, features), BF16),
            jax.ShapeDtypeStruct((rows.total, FRAME), BF16),
            jax.ShapeDtypeStruct((HEADS, FRAME, FRAME), BF16),
            jax.ShapeDtypeStruct((FRAME, rows.total), BF16),
        ),
        [weight_scratch, weight_scratch, wide, wide, sems],
        (tokens_local, space_gain, space_allowed, space_live, time_gain, cotangent_local, is_out),
        order,
        mine + other,
    )
    arrived = exchange(sent)
    sent = call(
        functools.partial(time_core, rows),
        jax.ShapeDtypeStruct((FRAME, rows.total), BF16),
        [wide, wide],
        (arrived, time_allowed, time_live, cosine, sine),
    )
    arrived = exchange(sent)
    result, grad_tokens, gains = call(
        functools.partial(finish, rows, pieces),
        (
            jax.ShapeDtypeStruct((FRAME, features), BF16),
            jax.ShapeDtypeStruct((FRAME, features), BF16),
            jax.ShapeDtypeStruct((everyone, 2, features), F32),
        ),
        [weight_scratch, weight_scratch, wide, wide, sems],
        (
            arrived,
            is_out,
            hidden,
            time_gain,
            cotangent_local,
            saved,
            shares,
            space_live,
            tokens_local,
            space_gain,
        ),
        order,
        mine + other,
    )
    gains = lax.all_to_all(gains, ("dp", "ctx"), split_axis=0, concat_axis=0, tiled=True)
    gain_grads = jnp.sum(gains, axis=0) * (1.0 / math.sqrt(everyone * FRAME))
    return result[None], grad_tokens[None], gain_grads


def solution(mesh):
    return jax.shard_map(
        shards,
        mesh=mesh,
        in_specs=(
            P("dp", "ctx", None),
            P("dp", "ctx", None),
            P("dp", None),
            P("dp", None),
            P("dp", None),
            P("dp", None),
            P(),
            P("ctx", None),
            P("ctx", None),
            P(),
            P("ctx", None),
            P("ctx", None),
        ),
        out_specs=(P("dp", "ctx", None), P("dp", "ctx", None), P()),
        check_vma=False,
    )
```

```python
import functools
import math

import jax
import jax.numpy as jnp
from jax import lax
from jax.experimental import pallas as pl
from jax.experimental.pallas import tpu as pltpu
from jax.sharding import PartitionSpec as P

HEADS = 8
FRAME = 128
EPSILON = 1e-06
ROPE_BASE = 10000.0
F32 = jnp.float32
BF16 = jnp.bfloat16
VMEM_LIMIT = 20 * 1024 * 1024


def nn(a, b):
    return lax.dot_general(a, b, (((1,), (0,)), ((), ())), preferred_element_type=F32)


def nt(a, b):
    return lax.dot_general(a, b, (((1,), (1,)), ((), ())), preferred_element_type=F32)


def tn(a, b):
    return lax.dot_general(a, b, (((0,), (0,)), ((), ())), preferred_element_type=F32)


class Rows:
    def __init__(self, qkv_rows, out_rows, size):
        self.qkv, self.out, self.size = qkv_rows, out_rows, size
        self.shard = qkv_rows + out_rows
        self.total = self.shard * size
        self.inner = out_rows * size
        self.head = self.inner // HEADS

    def spans(self, first, count, per_shard, shift):
        found = []
        row = first
        while row < first + count:
            block, inside = divmod(row, per_shard)
            length = min(per_shard - inside, first + count - row)
            place = block * self.shard + shift + inside
            if found and found[-1][0] + found[-1][1] == place:
                found[-1] = (found[-1][0], found[-1][1] + length)
            else:
                found.append((place, length))
            row += length
        return found

    def qkv_spans(self, which, head):
        return self.spans(which * self.inner + head * self.head, self.head, self.qkv, 0)

    def out_spans(self, head):
        return self.spans(head * self.head, self.head, self.out, self.qkv)


def read_rows(ref, spans):
    parts = [ref[place : place + length, :] for place, length in spans]
    return parts[0] if len(parts) == 1 else jnp.concatenate(parts, axis=0)


def write_rows(ref, spans, value):
    done = 0
    for place, length in spans:
        ref[place : place + length, :] = value[done : done + length, :]
        done += length


def inverse_size(values):
    return lax.rsqrt(jnp.mean(values * values, axis=-1, keepdims=True) + EPSILON)


def norm_back(values, inverse, gain, grad):
    scaled = grad * gain
    middle = jnp.mean(scaled * values, axis=-1, keepdims=True)
    grad_values = inverse * scaled - values * (inverse * inverse * inverse * middle)
    grad_gain = jnp.sum(grad * (values * inverse), axis=0, keepdims=True)
    return grad_values, grad_gain


def shares_of(queries, keys, allowed, live, scale):
    scores = tn(keys, queries) * scale
    weights = jnp.where(allowed > 0.0, jnp.exp(jnp.where(allowed > 0.0, scores, 0.0)), 0.0)
    totals = jnp.sum(weights, axis=0, keepdims=True) + (1.0 - live)
    return weights * (1.0 / totals)


def attend_back(queries, keys, values, shares, shares_low, grad, scale):
    grad_shares = tn(values, grad)
    middle = jnp.sum(shares * grad_shares, axis=0, keepdims=True)
    grad_scores = (shares * (grad_shares - middle) * scale).astype(BF16)
    return nn(keys, grad_scores), nt(queries, grad_scores), nt(grad, shares_low)


def start_weights(parts, order, mine, other, space, time, sems):
    def start(pieces, target, which):
        for index, (piece, first, count) in enumerate(parts):
            source = pieces[piece].at[pl.ds(first, count)]
            pltpu.make_async_copy(source, target.at[order[index]], sems.at[which, index]).start()

    @pl.when(order[len(parts)] == 0)
    def _():
        start(mine, space, 0)
        start(other, time, 1)

    @pl.when(order[len(parts)] != 0)
    def _():
        start(other, space, 0)
        start(mine, time, 1)


def wait_weights(parts, order, pieces, target, sems, which):
    for index, (piece, first, count) in enumerate(parts):
        source = pieces[piece].at[pl.ds(first, count)]
        pltpu.make_async_copy(source, target.at[order[index]], sems.at[which, index]).wait()


def front(rows, parts, order, tokens, space_gain, allowed, live, time_gain, cotangent, is_out, *refs):
    pieces = parts[-1][0] + 1
    mine, other, refs = refs[:pieces], refs[pieces : 2 * pieces], refs[2 * pieces :]
    hidden, saved, shares_out, sent, space, time, project, mixed, sems = refs
    start_weights(parts, order, mine, other, space, time, sems)
    values = tokens[...].astype(F32)
    normed = (values * inverse_size(values) * space_gain[...]).astype(BF16)
    mixed[...] = jnp.zeros_like(mixed)
    wait_weights(parts, order, mine, space, sems, 0)
    weight = space[...].reshape(rows.total, -1)
    project[...] = nt(weight, normed)
    saved[...] = project[...].astype(BF16)
    scale = rows.head ** (-0.5)
    for head in range(HEADS):
        query, key, value = (
            read_rows(project, rows.qkv_spans(which, head)).astype(BF16) for which in range(3)
        )
        shares = shares_of(query, key, allowed[...], live[...], scale).astype(BF16)
        shares_out[head] = shares
        write_rows(mixed, rows.out_spans(head), nn(value, shares) * live[...])
    update = tn(mixed[...].astype(BF16), weight)
    low = (values + update).astype(BF16)
    hidden[...] = low
    values = low.astype(F32)
    normed = (values * inverse_size(values) * time_gain[...]).astype(BF16)
    wait_weights(parts, order, mine, time, sems, 1)
    weight = time[...].reshape(rows.total, -1)
    both = nt(jnp.concatenate([normed, cotangent[...]], axis=0), weight)
    count = values.shape[0]
    sent[...] = jnp.where(is_out[...] > 0.0, both[count:], both[:count]).astype(BF16)


def time_core(rows, arrived, allowed, live, cosine, sine, sent, project, result):
    count = arrived.shape[0]
    for first in range(0, rows.total, FRAME):
        project[first : first + FRAME, :] = arrived[:, first : first + FRAME].astype(F32).T
    scale = rows.head ** (-0.5)
    half = rows.head // 2

    def swapped(vectors):
        return jnp.concatenate([vectors[half:], vectors[:half]], axis=0)

    for head in range(HEADS):
        turned = []
        for which in range(2):
            vectors = read_rows(project, rows.qkv_spans(which, head))
            turned.append((vectors * cosine[...] + swapped(vectors) * sine[...]).astype(BF16))
        query, key = turned
        value = read_rows(project, rows.qkv_spans(2, head)).astype(BF16)
        grad = (read_rows(project, rows.out_spans(head)) * live[...]).astype(BF16)
        shares = shares_of(query, key, allowed[...], live[...], scale)
        shares_low = shares.astype(BF16)
        write_rows(result, rows.out_spans(head), nn(value, shares_low) * live[...])
        grads = attend_back(query, key, value, shares, shares_low, grad, scale)
        for which in range(2):
            turned_grad = grads[which].astype(BF16).astype(F32)
            write_rows(
                result,
                rows.qkv_spans(which, head),
                turned_grad * cosine[...] - swapped(turned_grad) * sine[...],
            )
        write_rows(result, rows.qkv_spans(2, head), grads[2])
    for first in range(0, rows.total, FRAME):
        sent[:, first : first + FRAME] = result[first : first + FRAME, :].T.astype(BF16)


def finish(
    rows,
    arrived,
    is_out,
    time,
    hidden,
    time_gain,
    cotangent,
    space,
    saved,
    shares_in,
    live,
    tokens,
    space_gain,
    output,
    grad_tokens,
    gains,
    project,
    grad_project,
):
    count = arrived.shape[0]
    time_weight = time[...].reshape(rows.total, -1)
    space_weight = space[...].reshape(rows.total, -1)
    received = arrived[...]
    zeros = jnp.zeros_like(received)
    mask = jnp.broadcast_to(is_out[...] > 0.0, received.shape)
    left = jnp.concatenate([jnp.where(mask, zeros, received), jnp.where(mask, received, zeros)], axis=0)
    both = nn(left, time_weight)
    values = hidden[...].astype(F32)
    output[...] = (values + both[count:]).astype(BF16)
    grad_normed = both[:count].astype(BF16).astype(F32)
    grad_front, grad_time_gain = norm_back(values, inverse_size(values), time_gain[...], grad_normed)
    grad_hidden = (cotangent[...].astype(F32) + grad_front).astype(BF16)

    project[...] = nt(space_weight, grad_hidden)
    grad_project[...] = jnp.zeros_like(grad_project)
    scale = rows.head ** (-0.5)
    for head in range(HEADS):
        query, key, value = (
            read_rows(saved, rows.qkv_spans(which, head)).astype(BF16) for which in range(3)
        )
        grad = (read_rows(project, rows.out_spans(head)) * live[...]).astype(BF16)
        shares_low = shares_in[head]
        grads = attend_back(query, key, value, shares_low.astype(F32), shares_low, grad, scale)
        for which in range(3):
            write_rows(grad_project, rows.qkv_spans(which, head), grads[which])
    grad_normed = tn(grad_project[...].astype(BF16), space_weight).astype(BF16).astype(F32)
    values = tokens[...].astype(F32)
    grad_values, grad_space_gain = norm_back(values, inverse_size(values), space_gain[...], grad_normed)
    grad_tokens[...] = (grad_hidden.astype(F32) + grad_values).astype(BF16)
    both_gains = jnp.concatenate([grad_space_gain, grad_time_gain], axis=0)
    gains[...] = jnp.broadcast_to(both_gains[None], gains.shape)


def call(body, out_shapes, scratch, operands, in_order=None, pieces=()):
    whole = pl.BlockSpec(memory_space=pltpu.VMEM)
    scalars = pl.BlockSpec(memory_space=pltpu.SMEM)
    anywhere = pl.BlockSpec(memory_space=pl.ANY)
    first = () if in_order is None else (in_order,)
    return pl.pallas_call(
        body,
        out_shape=out_shapes,
        in_specs=[scalars] * len(first) + [whole] * len(operands) + [anywhere] * len(pieces),
        out_specs=jax.tree.map(lambda _: whole, out_shapes),
        scratch_shapes=scratch,
        compiler_params=pltpu.CompilerParams(vmem_limit_bytes=VMEM_LIMIT),
    )(*first, *operands, *pieces)


def gather_ring(space_rows, time_rows, size, rank):
    chips = size // 2
    chain = chips // 2
    shard = space_rows.shape[0]

    def chip_at(place):
        place = place % chips
        return 2 * place if place < chain else 2 * (chips - 1 - place) + 1

    ring_pairs = []
    for place in range(chips):
        ring_pairs.append((2 * chip_at(place), 2 * chip_at(place + 1)))
        ring_pairs.append((2 * chip_at(place) + 1, 2 * chip_at(place - 1) + 1))
    planes = lax.axis_size("dp")
    plane = lax.rem(lax.axis_index("dp"), 2)

    def ring(rows):
        return lax.ppermute(rows, "ctx", ring_pairs)

    def across(rows):
        return lax.ppermute(rows, "dp", [(index, index ^ 1) for index in range(planes)])

    def twin(rows):
        return lax.ppermute(rows, "ctx", [(index, index ^ 1) for index in range(size)])

    def after(rows, event):
        return lax.optimization_barrier((rows, event))[0]

    own = jnp.where(plane == 0, space_rows, time_rows)
    own_other = jnp.where(plane == 0, time_rows, space_rows)
    held = [jnp.concatenate([own, twin(own)], axis=0)]
    for step in range(3):
        held.append(ring(held[-1]))
    held.append(ring(held[3][:shard]))
    swapped = [jnp.concatenate([own_other, twin(own_other)], axis=0)]
    swapped.append(after(across(held[1]), held[3]))
    swapped.append(ring(swapped[1]))
    swapped.append(across(held[3]))
    swapped.append(ring(swapped[3][:shard]))
    mine = held + [twin(rows) for rows in held[1:]]
    other = swapped + [twin(rows) for rows in swapped[1:]]

    chip, core = rank // 2, lax.rem(rank, 2)
    column, level = lax.rem(chip, 2), chip // 2
    place = jnp.where(column == 0, level, chips - 1 - level)

    def rank_at(steps, at_core):
        at = lax.rem(place + steps + chips, chips)
        return 2 * jnp.where(at < chain, 2 * at, 2 * (chips - 1 - at) + 1) + at_core

    parts, order = [], []
    for index in range(9):
        steps, far_core = (index, core) if index < 5 else (index - 4, 1 - core)
        towards = steps * (2 * far_core - 1)
        for half in range(1 if steps == 4 else 2):
            parts.append((index, half * shard, shard))
            order.append(rank_at(towards, far_core if half == 0 else 1 - far_core))
    return mine, other, parts, jnp.stack(order + [plane]).astype(jnp.int32)


def gather_weights(space_rows, time_rows, size, rank):
    if size == 16 and lax.axis_size("dp") % 2 == 0:
        return gather_ring(space_rows, time_rows, size, rank)
    shard, features = space_rows.shape
    gathered = lax.all_gather(jnp.concatenate([space_rows, time_rows], axis=0), "ctx", axis=0)
    gathered = gathered.reshape(size, 2, shard, features)
    mine = gathered[:, 0].reshape(size * shard, features)
    other = gathered[:, 1].reshape(size * shard, features)
    return [mine], [other], [(0, 0, size * shard)], jnp.zeros((2,), jnp.int32)


def clip_tables(clip_frames, clip_offsets, clip_heights, clip_widths, total_frames):
    starts = clip_offsets // FRAME
    frame_ids = jnp.arange(total_frames, dtype=jnp.int32)[:, None]
    member = (frame_ids >= starts[None, :]) & (frame_ids < (starts + clip_frames)[None, :])
    frame_times = jnp.sum(jnp.where(member, frame_ids - starts[None, :], 0), axis=1).astype(F32)
    counts = jnp.sum(jnp.where(member, (clip_heights * clip_widths)[None, :], 0), axis=1)
    same_clip = jnp.any(member[:, None, :] & member[None, :, :], axis=-1)
    return frame_times, counts, same_clip


def shards(
    tokens,
    cotangent,
    clip_frames,
    clip_offsets,
    clip_heights,
    clip_widths,
    spatial_gain,
    spatial_qkv,
    spatial_out,
    temporal_gain,
    temporal_qkv,
    temporal_out,
):
    size = lax.axis_size("ctx")
    rank = lax.axis_index("ctx")
    everyone = lax.axis_size("dp") * size
    count, features = tokens.shape[1], tokens.shape[2]
    assert count == FRAME and FRAME % size == 0
    near = size // 2
    slots = FRAME // near
    rows = Rows(spatial_qkv.shape[0], spatial_out.shape[0], size)
    half = rows.head // 2

    mine, other, parts, order = gather_weights(
        jnp.concatenate([spatial_qkv, spatial_out], axis=0),
        jnp.concatenate([temporal_qkv, temporal_out], axis=0),
        size,
        rank,
    )
    frame_times, counts, same_clip = clip_tables(
        clip_frames[0], clip_offsets[0], clip_heights[0], clip_widths[0], size
    )
    space_live = jnp.arange(FRAME, dtype=jnp.int32) < counts[rank]
    space_allowed = jnp.broadcast_to(space_live[:, None], (FRAME, FRAME)).astype(F32)
    space_live = space_live[None, :].astype(F32)
    first_frame = (rank // near) * near
    near_times = lax.dynamic_slice_in_dim(frame_times, first_frame, near)
    near_counts = lax.dynamic_slice_in_dim(counts, first_frame, near)
    near_clip = lax.dynamic_slice(same_clip, (first_frame, first_frame), (near, near))
    slot_ids = lax.rem(rank, near) * slots + jnp.arange(slots, dtype=jnp.int32)
    time_live = (slot_ids[None, :] < near_counts[:, None]).reshape(FRAME)
    same_slot = jnp.eye(slots, dtype=bool)
    time_allowed = (near_clip[:, None, :, None] & same_slot[None, :, None, :]).reshape(FRAME, FRAME)
    time_allowed = (time_allowed & time_live[:, None]).astype(F32)
    time_live = time_live[None, :].astype(F32)
    frequency = ROPE_BASE ** (-jnp.arange(half).astype(F32) / half)
    angles = frequency[:, None] * jnp.repeat(near_times, slots)[None, :]
    cosine = jnp.cos(angles)
    sine = jnp.sin(angles)
    cosine = jnp.concatenate([cosine, cosine], axis=0)
    sine = jnp.concatenate([-sine, sine], axis=0)
    is_out = (jnp.arange(rows.total, dtype=jnp.int32) % rows.shard >= rows.qkv).astype(F32)[None, :]

    tokens_local = tokens[0]
    cotangent_local = cotangent[0]
    space_gain = spatial_gain[None, :]
    time_gain = temporal_gain[None, :]
    wide = pltpu.VMEM((rows.total, FRAME), F32)

    order, time_allowed, time_live, cosine, sine, is_out = lax.optimization_barrier(
        (order, time_allowed, time_live, cosine, sine, is_out)
    )
    sems = pltpu.SemaphoreType.DMA((2, len(parts)))
    weight_shape = jax.ShapeDtypeStruct((len(parts), rows.total // len(parts), features), BF16)
    groups = [list(range(first, first + near)) for first in range(0, size, near)]

    def exchange(sent):
        arrived = lax.all_to_all(
            sent.reshape(near, slots, rows.total),
            "ctx",
            split_axis=0,
            concat_axis=0,
            axis_index_groups=groups,
            tiled=True,
        )
        return arrived.reshape(FRAME, rows.total)

    hidden, saved, shares, sent, space_weights, time_weights = call(
        functools.partial(front, rows, parts),
        (
            jax.ShapeDtypeStruct((FRAME, features), BF16),
            jax.ShapeDtypeStruct((rows.total, FRAME), BF16),
            jax.ShapeDtypeStruct((HEADS, FRAME, FRAME), BF16),
            jax.ShapeDtypeStruct((FRAME, rows.total), BF16),
            weight_shape,
            weight_shape,
        ),
        [wide, wide, sems],
        (tokens_local, space_gain, space_allowed, space_live, time_gain, cotangent_local, is_out),
        order,
        mine + other,
    )
    arrived = exchange(sent)
    sent = call(
        functools.partial(time_core, rows),
        jax.ShapeDtypeStruct((FRAME, rows.total), BF16),
        [wide, wide],
        (arrived, time_allowed, time_live, cosine, sine),
    )
    arrived = exchange(sent)
    result, grad_tokens, gains = call(
        functools.partial(finish, rows),
        (
            jax.ShapeDtypeStruct((FRAME, features), BF16),
            jax.ShapeDtypeStruct((FRAME, features), BF16),
            jax.ShapeDtypeStruct((everyone, 2, features), F32),
        ),
        [wide, wide],
        (
            arrived,
            is_out,
            time_weights,
            hidden,
            time_gain,
            cotangent_local,
            space_weights,
            saved,
            shares,
            space_live,
            tokens_local,
            space_gain,
        ),
    )
    gains = lax.all_to_all(gains, ("dp", "ctx"), split_axis=0, concat_axis=0, tiled=True)
    gain_grads = jnp.sum(gains, axis=0) * (1.0 / math.sqrt(everyone * FRAME))
    return result[None], grad_tokens[None], gain_grads


def solution(mesh):
    return jax.shard_map(
        shards,
        mesh=mesh,
        in_specs=(
            P("dp", "ctx", None),
            P("dp", "ctx", None),
            P("dp", None),
            P("dp", None),
            P("dp", None),
            P("dp", None),
            P(),
            P("ctx", None),
            P("ctx", None),
            P(),
            P("ctx", None),
            P("ctx", None),
        ),
        out_specs=(P("dp", "ctx", None), P("dp", "ctx", None), P()),
        check_vma=False,
    )
```

```python
import functools
import math

import jax
import jax.numpy as jnp
from jax import lax
from jax.experimental import pallas as pl
from jax.experimental.pallas import tpu as pltpu
from jax.sharding import PartitionSpec as P

HEADS = 8
FRAME = 128
EPSILON = 1e-06
ROPE_BASE = 10000.0
F32 = jnp.float32
BF16 = jnp.bfloat16
VMEM_LIMIT = 20 * 1024 * 1024


def nn(a, b):
    return lax.dot_general(a, b, (((1,), (0,)), ((), ())), preferred_element_type=F32)


def nt(a, b):
    return lax.dot_general(a, b, (((1,), (1,)), ((), ())), preferred_element_type=F32)


def tn(a, b):
    return lax.dot_general(a, b, (((0,), (0,)), ((), ())), preferred_element_type=F32)


class Rows:
    def __init__(self, qkv_rows, out_rows, size):
        self.qkv, self.out, self.size = qkv_rows, out_rows, size
        self.shard = qkv_rows + out_rows
        self.total = self.shard * size
        self.inner = out_rows * size
        self.head = self.inner // HEADS

    def spans(self, first, count, per_shard, shift):
        found = []
        row = first
        while row < first + count:
            block, inside = divmod(row, per_shard)
            length = min(per_shard - inside, first + count - row)
            place = block * self.shard + shift + inside
            if found and found[-1][0] + found[-1][1] == place:
                found[-1] = (found[-1][0], found[-1][1] + length)
            else:
                found.append((place, length))
            row += length
        return found

    def qkv_spans(self, which, head):
        return self.spans(which * self.inner + head * self.head, self.head, self.qkv, 0)

    def out_spans(self, head):
        return self.spans(head * self.head, self.head, self.out, self.qkv)


def read_rows(ref, spans):
    parts = [ref[place : place + length, :] for place, length in spans]
    return parts[0] if len(parts) == 1 else jnp.concatenate(parts, axis=0)


def write_rows(ref, spans, value):
    done = 0
    for place, length in spans:
        ref[place : place + length, :] = value[done : done + length, :]
        done += length


def inverse_size(values):
    return lax.rsqrt(jnp.mean(values * values, axis=-1, keepdims=True) + EPSILON)


def norm_back(values, inverse, gain, grad):
    scaled = grad * gain
    middle = jnp.mean(scaled * values, axis=-1, keepdims=True)
    grad_values = inverse * scaled - values * (inverse * inverse * inverse * middle)
    grad_gain = jnp.sum(grad * (values * inverse), axis=0, keepdims=True)
    return grad_values, grad_gain


def shares_of(queries, keys, allowed, live, scale):
    scores = tn(keys, queries) * scale
    weights = jnp.where(allowed > 0.0, jnp.exp(jnp.where(allowed > 0.0, scores, 0.0)), 0.0)
    totals = jnp.sum(weights, axis=0, keepdims=True) + (1.0 - live)
    return weights * (1.0 / totals)


def attend_back(queries, keys, values, shares, shares_low, grad, scale):
    grad_shares = tn(values, grad)
    middle = jnp.sum(shares * grad_shares, axis=0, keepdims=True)
    grad_scores = (shares * (grad_shares - middle) * scale).astype(BF16)
    return nn(keys, grad_scores), nt(queries, grad_scores), nt(grad, shares_low)


def start_weights(parts, order, mine, other, space, time, sems):
    def start(pieces, target, which):
        for index, (piece, first, count) in enumerate(parts):
            source = pieces[piece].at[pl.ds(first, count)]
            pltpu.make_async_copy(source, target.at[order[index]], sems.at[which, index]).start()

    @pl.when(order[len(parts)] == 0)
    def _():
        start(mine, space, 0)
        start(other, time, 1)

    @pl.when(order[len(parts)] != 0)
    def _():
        start(other, space, 0)
        start(mine, time, 1)


def wait_weights(parts, order, pieces, target, sems, which):
    for index, (piece, first, count) in enumerate(parts):
        source = pieces[piece].at[pl.ds(first, count)]
        pltpu.make_async_copy(source, target.at[order[index]], sems.at[which, index]).wait()


def front(rows, parts, order, tokens, space_gain, allowed, live, time_gain, cotangent, is_out, *refs):
    pieces = parts[-1][0] + 1
    mine, other, refs = refs[:pieces], refs[pieces : 2 * pieces], refs[2 * pieces :]
    hidden, saved, shares_out, sent, space, time, project, mixed, sems = refs
    start_weights(parts, order, mine, other, space, time, sems)
    values = tokens[...].astype(F32)
    normed = (values * inverse_size(values) * space_gain[...]).astype(BF16)
    mixed[...] = jnp.zeros_like(mixed)
    wait_weights(parts, order, mine, space, sems, 0)
    weight = space[...].reshape(rows.total, -1)
    project[...] = nt(weight, normed)
    saved[...] = project[...].astype(BF16)
    scale = rows.head ** (-0.5)
    for head in range(HEADS):
        query, key, value = (
            read_rows(project, rows.qkv_spans(which, head)).astype(BF16) for which in range(3)
        )
        shares = shares_of(query, key, allowed[...], live[...], scale).astype(BF16)
        shares_out[head] = shares
        write_rows(mixed, rows.out_spans(head), nn(value, shares) * live[...])
    update = tn(mixed[...].astype(BF16), weight)
    low = (values + update).astype(BF16)
    hidden[...] = low
    values = low.astype(F32)
    normed = (values * inverse_size(values) * time_gain[...]).astype(BF16)
    wait_weights(parts, order, mine, time, sems, 1)
    weight = time[...].reshape(rows.total, -1)
    both = nt(jnp.concatenate([normed, cotangent[...]], axis=0), weight)
    count = values.shape[0]
    sent[...] = jnp.where(is_out[...] > 0.0, both[count:], both[:count]).astype(BF16)


def time_core(rows, arrived, allowed, live, cosine, sine, sent, project, result):
    count = arrived.shape[0]
    for first in range(0, rows.total, FRAME):
        project[first : first + FRAME, :] = arrived[:, first : first + FRAME].astype(F32).T
    scale = rows.head ** (-0.5)
    half = rows.head // 2

    def swapped(vectors):
        return jnp.concatenate([vectors[half:], vectors[:half]], axis=0)

    for head in range(HEADS):
        turned = []
        for which in range(2):
            vectors = read_rows(project, rows.qkv_spans(which, head))
            turned.append((vectors * cosine[...] + swapped(vectors) * sine[...]).astype(BF16))
        query, key = turned
        value = read_rows(project, rows.qkv_spans(2, head)).astype(BF16)
        grad = (read_rows(project, rows.out_spans(head)) * live[...]).astype(BF16)
        shares = shares_of(query, key, allowed[...], live[...], scale)
        shares_low = shares.astype(BF16)
        write_rows(result, rows.out_spans(head), nn(value, shares_low) * live[...])
        grads = attend_back(query, key, value, shares, shares_low, grad, scale)
        for which in range(2):
            turned_grad = grads[which].astype(BF16).astype(F32)
            write_rows(
                result,
                rows.qkv_spans(which, head),
                turned_grad * cosine[...] - swapped(turned_grad) * sine[...],
            )
        write_rows(result, rows.qkv_spans(2, head), grads[2])
    for first in range(0, rows.total, FRAME):
        sent[:, first : first + FRAME] = result[first : first + FRAME, :].T.astype(BF16)


def finish(
    rows,
    arrived,
    is_out,
    time,
    hidden,
    time_gain,
    cotangent,
    space,
    saved,
    shares_in,
    live,
    tokens,
    space_gain,
    output,
    grad_tokens,
    gains,
    project,
    grad_project,
):
    count = arrived.shape[0]
    time_weight = time[...].reshape(rows.total, -1)
    space_weight = space[...].reshape(rows.total, -1)
    received = arrived[...]
    zeros = jnp.zeros_like(received)
    mask = jnp.broadcast_to(is_out[...] > 0.0, received.shape)
    left = jnp.concatenate([jnp.where(mask, zeros, received), jnp.where(mask, received, zeros)], axis=0)
    both = nn(left, time_weight)
    values = hidden[...].astype(F32)
    output[...] = (values + both[count:]).astype(BF16)
    grad_normed = both[:count].astype(BF16).astype(F32)
    grad_front, grad_time_gain = norm_back(values, inverse_size(values), time_gain[...], grad_normed)
    grad_hidden = (cotangent[...].astype(F32) + grad_front).astype(BF16)

    project[...] = nt(space_weight, grad_hidden)
    grad_project[...] = jnp.zeros_like(grad_project)
    scale = rows.head ** (-0.5)
    for head in range(HEADS):
        query, key, value = (
            read_rows(saved, rows.qkv_spans(which, head)).astype(BF16) for which in range(3)
        )
        grad = (read_rows(project, rows.out_spans(head)) * live[...]).astype(BF16)
        shares_low = shares_in[head]
        grads = attend_back(query, key, value, shares_low.astype(F32), shares_low, grad, scale)
        for which in range(3):
            write_rows(grad_project, rows.qkv_spans(which, head), grads[which])
    grad_normed = tn(grad_project[...].astype(BF16), space_weight).astype(BF16).astype(F32)
    values = tokens[...].astype(F32)
    grad_values, grad_space_gain = norm_back(values, inverse_size(values), space_gain[...], grad_normed)
    grad_tokens[...] = (grad_hidden.astype(F32) + grad_values).astype(BF16)
    both_gains = jnp.concatenate([grad_space_gain, grad_time_gain], axis=0)
    gains[...] = jnp.broadcast_to(both_gains[None], gains.shape)


def call(body, out_shapes, scratch, operands, in_order=None, pieces=()):
    whole = pl.BlockSpec(memory_space=pltpu.VMEM)
    scalars = pl.BlockSpec(memory_space=pltpu.SMEM)
    anywhere = pl.BlockSpec(memory_space=pl.ANY)
    first = () if in_order is None else (in_order,)
    return pl.pallas_call(
        body,
        out_shape=out_shapes,
        in_specs=[scalars] * len(first) + [whole] * len(operands) + [anywhere] * len(pieces),
        out_specs=jax.tree.map(lambda _: whole, out_shapes),
        scratch_shapes=scratch,
        compiler_params=pltpu.CompilerParams(vmem_limit_bytes=VMEM_LIMIT),
    )(*first, *operands, *pieces)


def gather_ring(space_rows, time_rows, size, rank):
    chips = size // 2
    chain = chips // 2
    shard = space_rows.shape[0]

    def chip_at(place):
        place = place % chips
        return 2 * place if place < chain else 2 * (chips - 1 - place) + 1

    ring_pairs = []
    for place in range(chips):
        ring_pairs.append((2 * chip_at(place), 2 * chip_at(place + 1)))
        ring_pairs.append((2 * chip_at(place) + 1, 2 * chip_at(place - 1) + 1))
    planes = lax.axis_size("dp")
    plane = lax.rem(lax.axis_index("dp"), 2)

    def ring(rows):
        return lax.ppermute(rows, "ctx", ring_pairs)

    def across(rows):
        return lax.ppermute(rows, "dp", [(index, index ^ 1) for index in range(planes)])

    def twin(rows):
        return lax.ppermute(rows, "ctx", [(index, index ^ 1) for index in range(size)])

    def rounds_end(*rows):
        return lax.optimization_barrier(rows)

    own = jnp.where(plane == 0, space_rows, time_rows)
    own_other = jnp.where(plane == 0, time_rows, space_rows)
    o1, t0, twin_other = rounds_end(ring(own), twin(own), twin(own_other))
    o2, t1, x_o1, o1_twin = rounds_end(ring(o1), ring(t0), across(o1), twin(o1))
    o3, t2, x_t1, o2_twin, t1_twin, x_o1_twin = rounds_end(
        ring(o2), ring(t1), across(t1), twin(o2), twin(t1), twin(x_o1)
    )
    o4, t3, x_o3, o3_twin, t2_twin, x_t1_twin = rounds_end(
        ring(o3), ring(t2), across(o3), twin(o3), twin(t2), twin(x_t1)
    )
    x_o2, x_t2, x_t3, o4_twin, t3_twin, x_o3_twin = rounds_end(
        ring(x_o1), ring(x_t1), across(t3), twin(o4), twin(t3), twin(x_o3)
    )
    x_o4, x_o2_twin, x_t2_twin, x_t3_twin = rounds_end(
        ring(x_o3), twin(x_o2), twin(x_t2), twin(x_t3)
    )
    x_o4_twin = twin(x_o4)
    mine = [own, o1, o2, o3, o4, t1, t2, t3]
    mine += [t0, o1_twin, o2_twin, o3_twin, o4_twin, t1_twin, t2_twin, t3_twin]
    other = [own_other, x_o1, x_o2, x_o3, x_o4, x_t1, x_t2, x_t3]
    other += [twin_other, x_o1_twin, x_o2_twin, x_o3_twin, x_o4_twin]
    other += [x_t1_twin, x_t2_twin, x_t3_twin]

    chip, core = rank // 2, lax.rem(rank, 2)
    column, level = lax.rem(chip, 2), chip // 2
    place = jnp.where(column == 0, level, chips - 1 - level)
    order = []
    for carrier in (core, 1 - core):
        for steps, shard_core in [(n, carrier) for n in range(5)] + [(n, 1 - carrier) for n in range(1, 4)]:
            at = lax.rem(place + steps * (2 * carrier - 1) + chips, chips)
            order.append(2 * jnp.where(at < chain, 2 * at, 2 * (chips - 1 - at) + 1) + shard_core)
    parts = [(index, 0, shard) for index in range(size)]
    return mine, other, parts, jnp.stack(order + [plane]).astype(jnp.int32)


def gather_weights(space_rows, time_rows, size, rank):
    if size == 16 and lax.axis_size("dp") % 2 == 0:
        return gather_ring(space_rows, time_rows, size, rank)
    shard, features = space_rows.shape
    gathered = lax.all_gather(jnp.concatenate([space_rows, time_rows], axis=0), "ctx", axis=0)
    gathered = gathered.reshape(size, 2, shard, features)
    mine = gathered[:, 0].reshape(size * shard, features)
    other = gathered[:, 1].reshape(size * shard, features)
    return [mine], [other], [(0, 0, size * shard)], jnp.zeros((2,), jnp.int32)


def clip_tables(clip_frames, clip_offsets, clip_heights, clip_widths, total_frames):
    starts = clip_offsets // FRAME
    frame_ids = jnp.arange(total_frames, dtype=jnp.int32)[:, None]
    member = (frame_ids >= starts[None, :]) & (frame_ids < (starts + clip_frames)[None, :])
    frame_times = jnp.sum(jnp.where(member, frame_ids - starts[None, :], 0), axis=1).astype(F32)
    counts = jnp.sum(jnp.where(member, (clip_heights * clip_widths)[None, :], 0), axis=1)
    same_clip = jnp.any(member[:, None, :] & member[None, :, :], axis=-1)
    return frame_times, counts, same_clip


def shards(
    tokens,
    cotangent,
    clip_frames,
    clip_offsets,
    clip_heights,
    clip_widths,
    spatial_gain,
    spatial_qkv,
    spatial_out,
    temporal_gain,
    temporal_qkv,
    temporal_out,
):
    size = lax.axis_size("ctx")
    rank = lax.axis_index("ctx")
    everyone = lax.axis_size("dp") * size
    count, features = tokens.shape[1], tokens.shape[2]
    assert count == FRAME and FRAME % size == 0
    near = size // 2
    slots = FRAME // near
    rows = Rows(spatial_qkv.shape[0], spatial_out.shape[0], size)
    half = rows.head // 2

    mine, other, parts, order = gather_weights(
        jnp.concatenate([spatial_qkv, spatial_out], axis=0),
        jnp.concatenate([temporal_qkv, temporal_out], axis=0),
        size,
        rank,
    )
    frame_times, counts, same_clip = clip_tables(
        clip_frames[0], clip_offsets[0], clip_heights[0], clip_widths[0], size
    )
    space_live = jnp.arange(FRAME, dtype=jnp.int32) < counts[rank]
    space_allowed = jnp.broadcast_to(space_live[:, None], (FRAME, FRAME)).astype(F32)
    space_live = space_live[None, :].astype(F32)
    first_frame = (rank // near) * near
    near_times = lax.dynamic_slice_in_dim(frame_times, first_frame, near)
    near_counts = lax.dynamic_slice_in_dim(counts, first_frame, near)
    near_clip = lax.dynamic_slice(same_clip, (first_frame, first_frame), (near, near))
    slot_ids = lax.rem(rank, near) * slots + jnp.arange(slots, dtype=jnp.int32)
    time_live = (slot_ids[None, :] < near_counts[:, None]).reshape(FRAME)
    same_slot = jnp.eye(slots, dtype=bool)
    time_allowed = (near_clip[:, None, :, None] & same_slot[None, :, None, :]).reshape(FRAME, FRAME)
    time_allowed = (time_allowed & time_live[:, None]).astype(F32)
    time_live = time_live[None, :].astype(F32)
    frequency = ROPE_BASE ** (-jnp.arange(half).astype(F32) / half)
    angles = frequency[:, None] * jnp.repeat(near_times, slots)[None, :]
    cosine = jnp.cos(angles)
    sine = jnp.sin(angles)
    cosine = jnp.concatenate([cosine, cosine], axis=0)
    sine = jnp.concatenate([-sine, sine], axis=0)
    is_out = (jnp.arange(rows.total, dtype=jnp.int32) % rows.shard >= rows.qkv).astype(F32)[None, :]

    tokens_local = tokens[0]
    cotangent_local = cotangent[0]
    space_gain = spatial_gain[None, :]
    time_gain = temporal_gain[None, :]
    wide = pltpu.VMEM((rows.total, FRAME), F32)

    order, time_allowed, time_live, cosine, sine, is_out = lax.optimization_barrier(
        (order, time_allowed, time_live, cosine, sine, is_out)
    )
    sems = pltpu.SemaphoreType.DMA((2, len(parts)))
    weight_shape = jax.ShapeDtypeStruct((len(parts), rows.total // len(parts), features), BF16)
    groups = [list(range(first, first + near)) for first in range(0, size, near)]

    def exchange(sent):
        arrived = lax.all_to_all(
            sent.reshape(near, slots, rows.total),
            "ctx",
            split_axis=0,
            concat_axis=0,
            axis_index_groups=groups,
            tiled=True,
        )
        return arrived.reshape(FRAME, rows.total)

    hidden, saved, shares, sent, space_weights, time_weights = call(
        functools.partial(front, rows, parts),
        (
            jax.ShapeDtypeStruct((FRAME, features), BF16),
            jax.ShapeDtypeStruct((rows.total, FRAME), BF16),
            jax.ShapeDtypeStruct((HEADS, FRAME, FRAME), BF16),
            jax.ShapeDtypeStruct((FRAME, rows.total), BF16),
            weight_shape,
            weight_shape,
        ),
        [wide, wide, sems],
        (tokens_local, space_gain, space_allowed, space_live, time_gain, cotangent_local, is_out),
        order,
        mine + other,
    )
    arrived = exchange(sent)
    sent = call(
        functools.partial(time_core, rows),
        jax.ShapeDtypeStruct((FRAME, rows.total), BF16),
        [wide, wide],
        (arrived, time_allowed, time_live, cosine, sine),
    )
    arrived = exchange(sent)
    result, grad_tokens, gains = call(
        functools.partial(finish, rows),
        (
            jax.ShapeDtypeStruct((FRAME, features), BF16),
            jax.ShapeDtypeStruct((FRAME, features), BF16),
            jax.ShapeDtypeStruct((everyone, 2, features), F32),
        ),
        [wide, wide],
        (
            arrived,
            is_out,
            time_weights,
            hidden,
            time_gain,
            cotangent_local,
            space_weights,
            saved,
            shares,
            space_live,
            tokens_local,
            space_gain,
        ),
    )
    gains = lax.all_to_all(gains, ("dp", "ctx"), split_axis=0, concat_axis=0, tiled=True)
    gain_grads = jnp.sum(gains, axis=0) * (1.0 / math.sqrt(everyone * FRAME))
    return result[None], grad_tokens[None], gain_grads


def solution(mesh):
    return jax.shard_map(
        shards,
        mesh=mesh,
        in_specs=(
            P("dp", "ctx", None),
            P("dp", "ctx", None),
            P("dp", None),
            P("dp", None),
            P("dp", None),
            P("dp", None),
            P(),
            P("ctx", None),
            P("ctx", None),
            P(),
            P("ctx", None),
            P("ctx", None),
        ),
        out_specs=(P("dp", "ctx", None), P("dp", "ctx", None), P()),
        check_vma=False,
    )
```

```python
import functools
import math

import jax
import jax.numpy as jnp
from jax import lax
from jax.experimental import pallas as pl
from jax.experimental.pallas import tpu as pltpu
from jax.sharding import PartitionSpec as P

HEADS = 8
FRAME = 128
EPSILON = 1e-06
ROPE_BASE = 10000.0
F32 = jnp.float32
BF16 = jnp.bfloat16
VMEM_LIMIT = 20 * 1024 * 1024


def nn(a, b):
    return lax.dot_general(a, b, (((1,), (0,)), ((), ())), preferred_element_type=F32)


def nt(a, b):
    return lax.dot_general(a, b, (((1,), (1,)), ((), ())), preferred_element_type=F32)


def tn(a, b):
    return lax.dot_general(a, b, (((0,), (0,)), ((), ())), preferred_element_type=F32)


class Rows:
    def __init__(self, qkv_rows, out_rows, size):
        self.qkv, self.out, self.size = qkv_rows, out_rows, size
        self.shard = qkv_rows + out_rows
        self.total = self.shard * size
        self.inner = out_rows * size
        self.head = self.inner // HEADS

    def spans(self, first, count, per_shard, shift):
        found = []
        row = first
        while row < first + count:
            block, inside = divmod(row, per_shard)
            length = min(per_shard - inside, first + count - row)
            place = block * self.shard + shift + inside
            if found and found[-1][0] + found[-1][1] == place:
                found[-1] = (found[-1][0], found[-1][1] + length)
            else:
                found.append((place, length))
            row += length
        return found

    def qkv_spans(self, which, head):
        return self.spans(which * self.inner + head * self.head, self.head, self.qkv, 0)

    def out_spans(self, head):
        return self.spans(head * self.head, self.head, self.out, self.qkv)


def read_rows(ref, spans):
    parts = [ref[place : place + length, :] for place, length in spans]
    return parts[0] if len(parts) == 1 else jnp.concatenate(parts, axis=0)


def write_rows(ref, spans, value):
    done = 0
    for place, length in spans:
        ref[place : place + length, :] = value[done : done + length, :]
        done += length


def inverse_size(values):
    return lax.rsqrt(jnp.mean(values * values, axis=-1, keepdims=True) + EPSILON)


def norm_back(values, inverse, gain, grad):
    scaled = grad * gain
    middle = jnp.mean(scaled * values, axis=-1, keepdims=True)
    grad_values = inverse * scaled - values * (inverse * inverse * inverse * middle)
    grad_gain = jnp.sum(grad * (values * inverse), axis=0, keepdims=True)
    return grad_values, grad_gain


def shares_of(queries, keys, allowed, live, scale):
    scores = tn(keys, queries) * scale
    weights = jnp.where(allowed > 0.0, jnp.exp(jnp.where(allowed > 0.0, scores, 0.0)), 0.0)
    totals = jnp.sum(weights, axis=0, keepdims=True) + (1.0 - live)
    return weights * (1.0 / totals)


def attend_back(queries, keys, values, shares, shares_low, grad, scale):
    grad_shares = tn(values, grad)
    middle = jnp.sum(shares * grad_shares, axis=0, keepdims=True)
    grad_scores = (shares * (grad_shares - middle) * scale).astype(BF16)
    return nn(keys, grad_scores), nt(queries, grad_scores), nt(grad, shares_low)


def start_weights(parts, order, mine, other, space, time, sems):
    def start(pieces, target, which):
        for index, (piece, first, count) in enumerate(parts):
            source = pieces[piece].at[pl.ds(first, count)]
            pltpu.make_async_copy(source, target.at[order[index]], sems.at[which, index]).start()

    @pl.when(order[len(parts)] == 0)
    def _():
        start(mine, space, 0)
        start(other, time, 1)

    @pl.when(order[len(parts)] != 0)
    def _():
        start(other, space, 0)
        start(mine, time, 1)


def wait_weights(parts, order, pieces, target, sems, which):
    for index, (piece, first, count) in enumerate(parts):
        source = pieces[piece].at[pl.ds(first, count)]
        pltpu.make_async_copy(source, target.at[order[index]], sems.at[which, index]).wait()


def front(rows, parts, order, tokens, space_gain, allowed, live, time_gain, cotangent, is_out, *refs):
    pieces = parts[-1][0] + 1
    mine, other, refs = refs[:pieces], refs[pieces : 2 * pieces], refs[2 * pieces :]
    hidden, saved, shares_out, sent, space, time, project, mixed, sems = refs
    start_weights(parts, order, mine, other, space, time, sems)
    values = tokens[...].astype(F32)
    normed = (values * inverse_size(values) * space_gain[...]).astype(BF16)
    mixed[...] = jnp.zeros_like(mixed)
    wait_weights(parts, order, mine, space, sems, 0)
    weight = space[...].reshape(rows.total, -1)
    project[...] = nt(weight, normed)
    saved[...] = project[...].astype(BF16)
    scale = rows.head ** (-0.5)
    for head in range(HEADS):
        query, key, value = (
            read_rows(project, rows.qkv_spans(which, head)).astype(BF16) for which in range(3)
        )
        shares = shares_of(query, key, allowed[...], live[...], scale).astype(BF16)
        shares_out[head] = shares
        write_rows(mixed, rows.out_spans(head), nn(value, shares) * live[...])
    update = tn(mixed[...].astype(BF16), weight)
    low = (values + update).astype(BF16)
    hidden[...] = low
    values = low.astype(F32)
    normed = (values * inverse_size(values) * time_gain[...]).astype(BF16)
    wait_weights(parts, order, mine, time, sems, 1)
    weight = time[...].reshape(rows.total, -1)
    both = nt(jnp.concatenate([normed, cotangent[...]], axis=0), weight)
    count = values.shape[0]
    sent[...] = jnp.where(is_out[...] > 0.0, both[count:], both[:count]).astype(BF16)


def time_core(rows, arrived, allowed, live, cosine, sine, sent, project, result):
    count = arrived.shape[0]
    for first in range(0, rows.total, FRAME):
        project[first : first + FRAME, :] = arrived[:, first : first + FRAME].astype(F32).T
    scale = rows.head ** (-0.5)
    half = rows.head // 2

    def swapped(vectors):
        return jnp.concatenate([vectors[half:], vectors[:half]], axis=0)

    for head in range(HEADS):
        turned = []
        for which in range(2):
            vectors = read_rows(project, rows.qkv_spans(which, head))
            turned.append((vectors * cosine[...] + swapped(vectors) * sine[...]).astype(BF16))
        query, key = turned
        value = read_rows(project, rows.qkv_spans(2, head)).astype(BF16)
        grad = (read_rows(project, rows.out_spans(head)) * live[...]).astype(BF16)
        shares = shares_of(query, key, allowed[...], live[...], scale)
        shares_low = shares.astype(BF16)
        write_rows(result, rows.out_spans(head), nn(value, shares_low) * live[...])
        grads = attend_back(query, key, value, shares, shares_low, grad, scale)
        for which in range(2):
            turned_grad = grads[which].astype(BF16).astype(F32)
            write_rows(
                result,
                rows.qkv_spans(which, head),
                turned_grad * cosine[...] - swapped(turned_grad) * sine[...],
            )
        write_rows(result, rows.qkv_spans(2, head), grads[2])
    for first in range(0, rows.total, FRAME):
        sent[:, first : first + FRAME] = result[first : first + FRAME, :].T.astype(BF16)


def finish(
    rows,
    arrived,
    is_out,
    time,
    hidden,
    time_gain,
    cotangent,
    space,
    saved,
    shares_in,
    live,
    tokens,
    space_gain,
    output,
    grad_tokens,
    gains,
    project,
    grad_project,
):
    count = arrived.shape[0]
    time_weight = time[...].reshape(rows.total, -1)
    space_weight = space[...].reshape(rows.total, -1)
    received = arrived[...]
    zeros = jnp.zeros_like(received)
    mask = jnp.broadcast_to(is_out[...] > 0.0, received.shape)
    left = jnp.concatenate([jnp.where(mask, zeros, received), jnp.where(mask, received, zeros)], axis=0)
    both = nn(left, time_weight)
    values = hidden[...].astype(F32)
    output[...] = (values + both[count:]).astype(BF16)
    grad_normed = both[:count].astype(BF16).astype(F32)
    grad_front, grad_time_gain = norm_back(values, inverse_size(values), time_gain[...], grad_normed)
    grad_hidden = (cotangent[...].astype(F32) + grad_front).astype(BF16)

    project[...] = nt(space_weight, grad_hidden)
    grad_project[...] = jnp.zeros_like(grad_project)
    scale = rows.head ** (-0.5)
    for head in range(HEADS):
        query, key, value = (
            read_rows(saved, rows.qkv_spans(which, head)).astype(BF16) for which in range(3)
        )
        grad = (read_rows(project, rows.out_spans(head)) * live[...]).astype(BF16)
        shares_low = shares_in[head]
        grads = attend_back(query, key, value, shares_low.astype(F32), shares_low, grad, scale)
        for which in range(3):
            write_rows(grad_project, rows.qkv_spans(which, head), grads[which])
    grad_normed = tn(grad_project[...].astype(BF16), space_weight).astype(BF16).astype(F32)
    values = tokens[...].astype(F32)
    grad_values, grad_space_gain = norm_back(values, inverse_size(values), space_gain[...], grad_normed)
    grad_tokens[...] = (grad_hidden.astype(F32) + grad_values).astype(BF16)
    both_gains = jnp.concatenate([grad_space_gain, grad_time_gain], axis=0).astype(gains.dtype)
    gains[...] = jnp.broadcast_to(both_gains[None], gains.shape)


def call(body, out_shapes, scratch, operands, in_order=None, pieces=()):
    whole = pl.BlockSpec(memory_space=pltpu.VMEM)
    scalars = pl.BlockSpec(memory_space=pltpu.SMEM)
    anywhere = pl.BlockSpec(memory_space=pl.ANY)
    first = () if in_order is None else (in_order,)
    return pl.pallas_call(
        body,
        out_shape=out_shapes,
        in_specs=[scalars] * len(first) + [whole] * len(operands) + [anywhere] * len(pieces),
        out_specs=jax.tree.map(lambda _: whole, out_shapes),
        scratch_shapes=scratch,
        compiler_params=pltpu.CompilerParams(vmem_limit_bytes=VMEM_LIMIT),
    )(*first, *operands, *pieces)


def gather_ring(space_rows, time_rows, size, rank):
    chips = size // 2
    chain = chips // 2
    shard = space_rows.shape[0]

    def chip_at(place):
        place = place % chips
        return 2 * place if place < chain else 2 * (chips - 1 - place) + 1

    ring_pairs = []
    for place in range(chips):
        ring_pairs.append((2 * chip_at(place), 2 * chip_at(place + 1)))
        ring_pairs.append((2 * chip_at(place) + 1, 2 * chip_at(place - 1) + 1))
    planes = lax.axis_size("dp")
    plane = lax.rem(lax.axis_index("dp"), 2)

    def ring(rows):
        return lax.ppermute(rows, "ctx", ring_pairs)

    def across(rows):
        return lax.ppermute(rows, "dp", [(index, index ^ 1) for index in range(planes)])

    def twin(rows):
        return lax.ppermute(rows, "ctx", [(index, index ^ 1) for index in range(size)])

    def after(rows, *events):
        return lax.optimization_barrier((rows, *events))[0]

    own = jnp.where(plane == 0, space_rows, time_rows)
    own_other = jnp.where(plane == 0, time_rows, space_rows)
    o1 = ring(own)
    t0 = twin(own)
    t1 = ring(t0)
    o2 = ring(o1)
    x_o1 = across(o1)
    o1_twin = twin(o1)
    t2 = ring(t1)
    t1_twin = twin(t1)
    o3 = ring(after(o2, o1_twin))
    x_t1 = across(after(t1, x_o1))
    o2_twin = twin(o2)
    t3 = ring(after(t2, t1_twin))
    x_o1_twin = twin(x_o1)
    o4 = ring(after(o3, o2_twin))
    x_o3 = across(after(o3, x_t1, x_o1_twin))
    t2_twin = twin(t2)
    o3_twin = twin(o3)
    x_t1_twin = twin(x_t1)
    x_t2 = ring(after(x_t1, t3, t2_twin))
    x_o2 = ring(after(x_o1, o4, o3_twin))
    x_t3 = across(after(t3, x_o3, x_t1_twin))
    t3_twin = twin(t3)
    o4_twin = twin(o4)
    x_o4 = ring(after(x_o3, x_o2, t3_twin, o4_twin))
    x_o3_twin = twin(x_o3)
    x_o2_twin = twin(x_o2)
    x_t2_twin = twin(x_t2)
    twin_other = twin(own_other)
    x_t3_twin = twin(x_t3)
    x_o4_twin = twin(x_o4)
    mine = [own, o1, o2, o3, o4, t1, t2, t3]
    mine += [t0, o1_twin, o2_twin, o3_twin, o4_twin, t1_twin, t2_twin, t3_twin]
    other = [own_other, x_o1, x_o2, x_o3, x_o4, x_t1, x_t2, x_t3]
    other += [twin_other, x_o1_twin, x_o2_twin, x_o3_twin, x_o4_twin]
    other += [x_t1_twin, x_t2_twin, x_t3_twin]

    chip, core = rank // 2, lax.rem(rank, 2)
    column, level = lax.rem(chip, 2), chip // 2
    place = jnp.where(column == 0, level, chips - 1 - level)
    order = []
    for carrier in (core, 1 - core):
        for steps, shard_core in [(n, carrier) for n in range(5)] + [(n, 1 - carrier) for n in range(1, 4)]:
            at = lax.rem(place + steps * (2 * carrier - 1) + chips, chips)
            order.append(2 * jnp.where(at < chain, 2 * at, 2 * (chips - 1 - at) + 1) + shard_core)
    parts = [(index, 0, shard) for index in range(size)]
    return mine, other, parts, jnp.stack(order + [plane]).astype(jnp.int32)


def gather_weights(space_rows, time_rows, size, rank):
    if size == 16 and lax.axis_size("dp") % 2 == 0:
        return gather_ring(space_rows, time_rows, size, rank)
    shard, features = space_rows.shape
    gathered = lax.all_gather(jnp.concatenate([space_rows, time_rows], axis=0), "ctx", axis=0)
    gathered = gathered.reshape(size, 2, shard, features)
    mine = gathered[:, 0].reshape(size * shard, features)
    other = gathered[:, 1].reshape(size * shard, features)
    return [mine], [other], [(0, 0, size * shard)], jnp.zeros((2,), jnp.int32)


def clip_tables(clip_frames, clip_offsets, clip_heights, clip_widths, total_frames):
    starts = clip_offsets // FRAME
    frame_ids = jnp.arange(total_frames, dtype=jnp.int32)[:, None]
    member = (frame_ids >= starts[None, :]) & (frame_ids < (starts + clip_frames)[None, :])
    frame_times = jnp.sum(jnp.where(member, frame_ids - starts[None, :], 0), axis=1).astype(F32)
    counts = jnp.sum(jnp.where(member, (clip_heights * clip_widths)[None, :], 0), axis=1)
    same_clip = jnp.any(member[:, None, :] & member[None, :, :], axis=-1)
    return frame_times, counts, same_clip


def shards(
    tokens,
    cotangent,
    clip_frames,
    clip_offsets,
    clip_heights,
    clip_widths,
    spatial_gain,
    spatial_qkv,
    spatial_out,
    temporal_gain,
    temporal_qkv,
    temporal_out,
):
    size = lax.axis_size("ctx")
    rank = lax.axis_index("ctx")
    everyone = lax.axis_size("dp") * size
    count, features = tokens.shape[1], tokens.shape[2]
    assert count == FRAME and FRAME % size == 0
    near = size // 2
    slots = FRAME // near
    rows = Rows(spatial_qkv.shape[0], spatial_out.shape[0], size)
    half = rows.head // 2

    mine, other, parts, order = gather_weights(
        jnp.concatenate([spatial_qkv, spatial_out], axis=0),
        jnp.concatenate([temporal_qkv, temporal_out], axis=0),
        size,
        rank,
    )
    frame_times, counts, same_clip = clip_tables(
        clip_frames[0], clip_offsets[0], clip_heights[0], clip_widths[0], size
    )
    space_live = jnp.arange(FRAME, dtype=jnp.int32) < counts[rank]
    space_allowed = jnp.broadcast_to(space_live[:, None], (FRAME, FRAME)).astype(F32)
    space_live = space_live[None, :].astype(F32)
    first_frame = (rank // near) * near
    near_times = lax.dynamic_slice_in_dim(frame_times, first_frame, near)
    near_counts = lax.dynamic_slice_in_dim(counts, first_frame, near)
    near_clip = lax.dynamic_slice(same_clip, (first_frame, first_frame), (near, near))
    slot_ids = lax.rem(rank, near) * slots + jnp.arange(slots, dtype=jnp.int32)
    time_live = (slot_ids[None, :] < near_counts[:, None]).reshape(FRAME)
    same_slot = jnp.eye(slots, dtype=bool)
    time_allowed = (near_clip[:, None, :, None] & same_slot[None, :, None, :]).reshape(FRAME, FRAME)
    time_allowed = (time_allowed & time_live[:, None]).astype(F32)
    time_live = time_live[None, :].astype(F32)
    frequency = ROPE_BASE ** (-jnp.arange(half).astype(F32) / half)
    angles = frequency[:, None] * jnp.repeat(near_times, slots)[None, :]
    cosine = jnp.cos(angles)
    sine = jnp.sin(angles)
    cosine = jnp.concatenate([cosine, cosine], axis=0)
    sine = jnp.concatenate([-sine, sine], axis=0)
    is_out = (jnp.arange(rows.total, dtype=jnp.int32) % rows.shard >= rows.qkv).astype(F32)[None, :]

    tokens_local = tokens[0]
    cotangent_local = cotangent[0]
    space_gain = spatial_gain[None, :]
    time_gain = temporal_gain[None, :]
    wide = pltpu.VMEM((rows.total, FRAME), F32)

    order, time_allowed, time_live, cosine, sine, is_out = lax.optimization_barrier(
        (order, time_allowed, time_live, cosine, sine, is_out)
    )
    sems = pltpu.SemaphoreType.DMA((2, len(parts)))
    weight_shape = jax.ShapeDtypeStruct((len(parts), rows.total // len(parts), features), BF16)
    groups = [list(range(first, first + near)) for first in range(0, size, near)]

    def exchange(sent):
        arrived = lax.all_to_all(
            sent.reshape(near, slots, rows.total),
            "ctx",
            split_axis=0,
            concat_axis=0,
            axis_index_groups=groups,
            tiled=True,
        )
        return arrived.reshape(FRAME, rows.total)

    hidden, saved, shares, sent, space_weights, time_weights = call(
        functools.partial(front, rows, parts),
        (
            jax.ShapeDtypeStruct((FRAME, features), BF16),
            jax.ShapeDtypeStruct((rows.total, FRAME), BF16),
            jax.ShapeDtypeStruct((HEADS, FRAME, FRAME), BF16),
            jax.ShapeDtypeStruct((FRAME, rows.total), BF16),
            weight_shape,
            weight_shape,
        ),
        [wide, wide, sems],
        (tokens_local, space_gain, space_allowed, space_live, time_gain, cotangent_local, is_out),
        order,
        mine + other,
    )
    arrived = exchange(sent)
    sent = call(
        functools.partial(time_core, rows),
        jax.ShapeDtypeStruct((FRAME, rows.total), BF16),
        [wide, wide],
        (arrived, time_allowed, time_live, cosine, sine),
    )
    arrived = exchange(sent)
    result, grad_tokens, gains = call(
        functools.partial(finish, rows),
        (
            jax.ShapeDtypeStruct((FRAME, features), BF16),
            jax.ShapeDtypeStruct((FRAME, features), BF16),
            jax.ShapeDtypeStruct((everyone, 2, features), BF16),
        ),
        [wide, wide],
        (
            arrived,
            is_out,
            time_weights,
            hidden,
            time_gain,
            cotangent_local,
            space_weights,
            saved,
            shares,
            space_live,
            tokens_local,
            space_gain,
        ),
    )
    gains = lax.all_to_all(gains, ("dp", "ctx"), split_axis=0, concat_axis=0, tiled=True)
    gain_grads = jnp.sum(gains.astype(F32), axis=0) * (1.0 / math.sqrt(everyone * FRAME))
    return result[None], grad_tokens[None], gain_grads


def solution(mesh):
    return jax.shard_map(
        shards,
        mesh=mesh,
        in_specs=(
            P("dp", "ctx", None),
            P("dp", "ctx", None),
            P("dp", None),
            P("dp", None),
            P("dp", None),
            P("dp", None),
            P(),
            P("ctx", None),
            P("ctx", None),
            P(),
            P("ctx", None),
            P("ctx", None),
        ),
        out_specs=(P("dp", "ctx", None), P("dp", "ctx", None), P()),
        check_vma=False,
    )
```

```python
import functools
import math

import jax
import jax.numpy as jnp
from jax import lax
from jax.experimental import pallas as pl
from jax.experimental.pallas import tpu as pltpu
from jax.sharding import PartitionSpec as P

HEADS = 8
FRAME = 128
EPSILON = 1e-06
ROPE_BASE = 10000.0
F32 = jnp.float32
BF16 = jnp.bfloat16
VMEM_LIMIT = 20 * 1024 * 1024


def nn(a, b):
    return lax.dot_general(a, b, (((1,), (0,)), ((), ())), preferred_element_type=F32)


def nt(a, b):
    return lax.dot_general(a, b, (((1,), (1,)), ((), ())), preferred_element_type=F32)


def tn(a, b):
    return lax.dot_general(a, b, (((0,), (0,)), ((), ())), preferred_element_type=F32)


class Rows:
    def __init__(self, qkv_rows, out_rows, size):
        self.qkv, self.out, self.size = qkv_rows, out_rows, size
        self.shard = qkv_rows + out_rows
        self.total = self.shard * size
        self.inner = out_rows * size
        self.head = self.inner // HEADS

    def spans(self, first, count, per_shard, shift):
        found = []
        row = first
        while row < first + count:
            block, inside = divmod(row, per_shard)
            length = min(per_shard - inside, first + count - row)
            place = block * self.shard + shift + inside
            if found and found[-1][0] + found[-1][1] == place:
                found[-1] = (found[-1][0], found[-1][1] + length)
            else:
                found.append((place, length))
            row += length
        return found

    def qkv_spans(self, which, head):
        return self.spans(which * self.inner + head * self.head, self.head, self.qkv, 0)

    def out_spans(self, head):
        return self.spans(head * self.head, self.head, self.out, self.qkv)


def read_rows(ref, spans):
    parts = [ref[place : place + length, :] for place, length in spans]
    return parts[0] if len(parts) == 1 else jnp.concatenate(parts, axis=0)


def write_rows(ref, spans, value):
    done = 0
    for place, length in spans:
        ref[place : place + length, :] = value[done : done + length, :]
        done += length


def inverse_size(values):
    return lax.rsqrt(jnp.mean(values * values, axis=-1, keepdims=True) + EPSILON)


def norm_back(values, inverse, gain, grad):
    scaled = grad * gain
    middle = jnp.mean(scaled * values, axis=-1, keepdims=True)
    grad_values = inverse * scaled - values * (inverse * inverse * inverse * middle)
    grad_gain = jnp.sum(grad * (values * inverse), axis=0, keepdims=True)
    return grad_values, grad_gain


def shares_of(queries, keys, allowed, live, scale):
    scores = tn(keys, queries) * scale
    weights = jnp.where(allowed > 0.0, jnp.exp(jnp.where(allowed > 0.0, scores, 0.0)), 0.0)
    totals = jnp.sum(weights, axis=0, keepdims=True) + (1.0 - live)
    return weights * (1.0 / totals)


def attend_back(queries, keys, values, shares, shares_low, grad, scale):
    grad_shares = tn(values, grad)
    middle = jnp.sum(shares * grad_shares, axis=0, keepdims=True)
    grad_scores = (shares * (grad_shares - middle) * scale).astype(BF16)
    return nn(keys, grad_scores), nt(queries, grad_scores), nt(grad, shares_low)


def weight_copies(layout, order, pieces, target, sems, which):
    count = target.shape[1]
    return [
        pltpu.make_async_copy(
            pieces[piece].at[pl.ds(first, count)], target.at[order[index]], sems.at[which, index]
        )
        for index, (piece, first) in enumerate(layout)
    ]


def start_weights(layouts, order, pieces, space, time, sems):
    def start(first, second):
        for copy in weight_copies(first, order, pieces, space, sems, 0):
            copy.start()
        for copy in weight_copies(second, order, pieces, time, sems, 1):
            copy.start()

    plane = order[len(layouts[0])]

    @pl.when(plane == 0)
    def _():
        start(layouts[0], layouts[1])

    @pl.when(plane != 0)
    def _():
        start(layouts[1], layouts[0])


def wait_weights(layouts, order, pieces, target, sems, which):
    for copy in weight_copies(layouts[0], order, pieces, target, sems, which):
        copy.wait()


def front(rows, layouts, order, space_gain, allowed, live, time_gain, is_out, *refs):
    pieces, refs = refs[:-14], refs[-14:]
    tokens_in, cotangent_in, hidden, saved, shares_out, sent, space, time = refs[:8]
    project, mixed, tokens, cotangent, sems, token_sems = refs[8:]
    token_copy = pltpu.make_async_copy(tokens_in, tokens, token_sems.at[0])
    token_copy.start()
    cotangent_copy = pltpu.make_async_copy(cotangent_in, cotangent, token_sems.at[1])
    cotangent_copy.start()
    start_weights(layouts, order, pieces, space, time, sems)
    token_copy.wait()
    values = tokens[...].astype(F32)
    normed = (values * inverse_size(values) * space_gain[...]).astype(BF16)
    mixed[...] = jnp.zeros_like(mixed)
    wait_weights(layouts, order, pieces, space, sems, 0)
    weight = space[...].reshape(rows.total, -1)
    project[...] = nt(weight, normed)
    saved[...] = project[...].astype(BF16)
    scale = rows.head ** (-0.5)
    for head in range(HEADS):
        query, key, value = (
            read_rows(project, rows.qkv_spans(which, head)).astype(BF16) for which in range(3)
        )
        shares = shares_of(query, key, allowed[...], live[...], scale).astype(BF16)
        shares_out[head] = shares
        write_rows(mixed, rows.out_spans(head), nn(value, shares) * live[...])
    update = tn(mixed[...].astype(BF16), weight)
    low = (values + update).astype(BF16)
    hidden[...] = low
    values = low.astype(F32)
    normed = (values * inverse_size(values) * time_gain[...]).astype(BF16)
    wait_weights(layouts, order, pieces, time, sems, 1)
    cotangent_copy.wait()
    weight = time[...].reshape(rows.total, -1)
    both = nt(jnp.concatenate([normed, cotangent[...]], axis=0), weight)
    count = values.shape[0]
    sent[...] = jnp.where(is_out[...] > 0.0, both[count:], both[:count]).astype(BF16)


def time_core(rows, arrived, allowed, live, cosine, sine, sent, project, result):
    count = arrived.shape[0]
    for first in range(0, rows.total, FRAME):
        project[first : first + FRAME, :] = arrived[:, first : first + FRAME].astype(F32).T
    scale = rows.head ** (-0.5)
    half = rows.head // 2

    def swapped(vectors):
        return jnp.concatenate([vectors[half:], vectors[:half]], axis=0)

    for head in range(HEADS):
        turned = []
        for which in range(2):
            vectors = read_rows(project, rows.qkv_spans(which, head))
            turned.append((vectors * cosine[...] + swapped(vectors) * sine[...]).astype(BF16))
        query, key = turned
        value = read_rows(project, rows.qkv_spans(2, head)).astype(BF16)
        grad = (read_rows(project, rows.out_spans(head)) * live[...]).astype(BF16)
        shares = shares_of(query, key, allowed[...], live[...], scale)
        shares_low = shares.astype(BF16)
        write_rows(result, rows.out_spans(head), nn(value, shares_low) * live[...])
        grads = attend_back(query, key, value, shares, shares_low, grad, scale)
        for which in range(2):
            turned_grad = grads[which].astype(BF16).astype(F32)
            write_rows(
                result,
                rows.qkv_spans(which, head),
                turned_grad * cosine[...] - swapped(turned_grad) * sine[...],
            )
        write_rows(result, rows.qkv_spans(2, head), grads[2])
    for first in range(0, rows.total, FRAME):
        sent[:, first : first + FRAME] = result[first : first + FRAME, :].T.astype(BF16)


def finish(
    rows,
    arrived,
    is_out,
    time,
    hidden,
    time_gain,
    cotangent,
    space,
    saved,
    shares_in,
    live,
    tokens,
    space_gain,
    output,
    grad_tokens,
    gains,
    project,
    grad_project,
):
    count = arrived.shape[0]
    time_weight = time[...].reshape(rows.total, -1)
    space_weight = space[...].reshape(rows.total, -1)
    received = arrived[...]
    zeros = jnp.zeros_like(received)
    mask = jnp.broadcast_to(is_out[...] > 0.0, received.shape)
    left = jnp.concatenate([jnp.where(mask, zeros, received), jnp.where(mask, received, zeros)], axis=0)
    both = nn(left, time_weight)
    values = hidden[...].astype(F32)
    output[...] = (values + both[count:]).astype(BF16)
    grad_normed = both[:count].astype(BF16).astype(F32)
    grad_front, grad_time_gain = norm_back(values, inverse_size(values), time_gain[...], grad_normed)
    grad_hidden = (cotangent[...].astype(F32) + grad_front).astype(BF16)

    project[...] = nt(space_weight, grad_hidden)
    grad_project[...] = jnp.zeros_like(grad_project)
    scale = rows.head ** (-0.5)
    for head in range(HEADS):
        query, key, value = (
            read_rows(saved, rows.qkv_spans(which, head)).astype(BF16) for which in range(3)
        )
        grad = (read_rows(project, rows.out_spans(head)) * live[...]).astype(BF16)
        shares_low = shares_in[head]
        grads = attend_back(query, key, value, shares_low.astype(F32), shares_low, grad, scale)
        for which in range(3):
            write_rows(grad_project, rows.qkv_spans(which, head), grads[which])
    grad_normed = tn(grad_project[...].astype(BF16), space_weight).astype(BF16).astype(F32)
    values = tokens[...].astype(F32)
    grad_values, grad_space_gain = norm_back(values, inverse_size(values), space_gain[...], grad_normed)
    grad_tokens[...] = (grad_hidden.astype(F32) + grad_values).astype(BF16)
    both_gains = jnp.concatenate([grad_space_gain, grad_time_gain], axis=0).astype(gains.dtype)
    gains[...] = jnp.broadcast_to(both_gains[None], gains.shape)


def call(body, out_shapes, scratch, operands, in_order=None, pieces=()):
    whole = pl.BlockSpec(memory_space=pltpu.VMEM)
    scalars = pl.BlockSpec(memory_space=pltpu.SMEM)
    anywhere = pl.BlockSpec(memory_space=pltpu.HBM)
    first = () if in_order is None else (in_order,)
    return pl.pallas_call(
        body,
        out_shape=out_shapes,
        in_specs=[scalars] * len(first) + [whole] * len(operands) + [anywhere] * len(pieces),
        out_specs=jax.tree.map(lambda _: whole, out_shapes),
        scratch_shapes=scratch,
        compiler_params=pltpu.CompilerParams(vmem_limit_bytes=VMEM_LIMIT),
    )(*first, *operands, *pieces)


def gather_ring(space_rows, time_rows, size, rank):
    chips = size // 2
    chain = chips // 2
    shard = space_rows.shape[0]

    def chip_at(place):
        place = place % chips
        return 2 * place if place < chain else 2 * (chips - 1 - place) + 1

    ring_pairs = []
    for place in range(chips):
        ring_pairs.append((2 * chip_at(place), 2 * chip_at(place + 1)))
        ring_pairs.append((2 * chip_at(place) + 1, 2 * chip_at(place - 1) + 1))
    planes = lax.axis_size("dp")
    plane = lax.rem(lax.axis_index("dp"), 2)

    def ring(rows):
        return lax.ppermute(rows, "ctx", ring_pairs)

    def across(rows):
        return lax.ppermute(rows, "dp", [(index, index ^ 1) for index in range(planes)])

    def twin(rows):
        return lax.ppermute(rows, "ctx", [(index, index ^ 1) for index in range(size)])

    def after(rows, *events):
        return lax.optimization_barrier((rows, *events))[0]

    own = jnp.where(plane == 0, space_rows, time_rows)
    own_other = jnp.where(plane == 0, time_rows, space_rows)
    t0 = twin(own)
    o1 = ring(after(own, t0))
    t1 = ring(t0)
    o2 = ring(o1)
    t2 = ring(t1)
    x_o1 = across(o1)
    x_t1 = across(after(t1, o2, x_o1))
    x_t2 = ring(x_t1)
    o1_twin = twin(o1)
    o2_twin = twin(o2)
    t1_twin = twin(t1)
    t2_twin = twin(t2)
    x_o1_twin = twin(x_o1)
    x_t1_twin = twin(x_t1)
    x_t2_twin = twin(x_t2)
    t0_other = twin(own_other)
    o3 = ring(after(o2, x_o1))
    o4 = ring(o3)
    t3 = ring(after(t2, o3))
    x_o3 = across(o3)
    x_t3 = ring(after(x_t2, t3))
    x_o4 = across(after(o4, x_t2))
    o3_twin = twin(o3)
    o4_twin = twin(o4)
    t3_twin = twin(t3)
    x_o3_twin = twin(x_o3)
    x_o4_twin = twin(x_o4)
    x_t3_twin = twin(x_t3)
    x_o2 = ring(after(x_o1, o4, t2, x_o3))
    x_o2_twin = twin(x_o2)
    mine = {"o0": (own, 0), "t0": (t0, 0)}
    other = {"o0": (own_other, 0), "t0": (t0_other, 0)}
    mine |= {"o1": (o1, 0), "o1_twin": (o1_twin, 0)}
    other |= {"o1": (x_o1, 0), "o1_twin": (x_o1_twin, 0)}
    mine |= {"o2": (o2, 0), "o2_twin": (o2_twin, 0)}
    other |= {"o2": (x_o2, 0), "o2_twin": (x_o2_twin, 0)}
    mine |= {"o3": (o3, 0), "o3_twin": (o3_twin, 0)}
    other |= {"o3": (x_o3, 0), "o3_twin": (x_o3_twin, 0)}
    mine |= {"o4": (o4, 0), "o4_twin": (o4_twin, 0)}
    other |= {"o4": (x_o4, 0), "o4_twin": (x_o4_twin, 0)}
    mine |= {"t1": (t1, 0), "t1_twin": (t1_twin, 0)}
    other |= {"t1": (x_t1, 0), "t1_twin": (x_t1_twin, 0)}
    mine |= {"t2": (t2, 0), "t2_twin": (t2_twin, 0)}
    other |= {"t2": (x_t2, 0), "t2_twin": (x_t2_twin, 0)}
    mine |= {"t3": (t3, 0), "t3_twin": (t3_twin, 0)}
    other |= {"t3": (x_t3, 0), "t3_twin": (x_t3_twin, 0)}
    chip, core = rank // 2, lax.rem(rank, 2)
    column, level = lax.rem(chip, 2), chip // 2
    place = jnp.where(column == 0, level, chips - 1 - level)

    def came(carrier, name):
        steps, shard_core = int(name[1]), carrier if name[0] == "o" else 1 - carrier
        at = lax.rem(place + steps * (2 * carrier - 1) + chips, chips)
        return 2 * jnp.where(at < chain, 2 * at, 2 * (chips - 1 - at) + 1) + shard_core

    names = ["o0", "t0", "o1", "o2", "o3", "o4", "t1", "t2", "t3"]
    twins = names[2:]
    order = [came(core, name) for name in names] + [came(1 - core, name) for name in twins]
    pieces, layouts = [], ([], [])
    for half, found in enumerate((mine, other)):
        for name in names + [name + "_twin" for name in twins]:
            array, first = found[name]
            place_in = [index for index, piece in enumerate(pieces) if piece is array]
            if not place_in:
                place_in = [len(pieces)]
                pieces.append(array)
            layouts[half].append((place_in[0], first * shard))
    return pieces, layouts, jnp.stack(order + [plane]).astype(jnp.int32)


def gather_weights(space_rows, time_rows, size, rank):
    if size == 16 and lax.axis_size("dp") % 2 == 0:
        return gather_ring(space_rows, time_rows, size, rank)
    shard, features = space_rows.shape
    gathered = lax.all_gather(jnp.concatenate([space_rows, time_rows], axis=0), "ctx", axis=0)
    gathered = gathered.reshape(size, 2, shard, features)
    halves = [gathered[:, half].reshape(size * shard, features) for half in range(2)]
    return halves, ([(0, 0)], [(1, 0)]), jnp.zeros((2,), jnp.int32)


def clip_tables(clip_frames, clip_offsets, clip_heights, clip_widths, total_frames):
    starts = clip_offsets // FRAME
    frame_ids = jnp.arange(total_frames, dtype=jnp.int32)[:, None]
    member = (frame_ids >= starts[None, :]) & (frame_ids < (starts + clip_frames)[None, :])
    frame_times = jnp.sum(jnp.where(member, frame_ids - starts[None, :], 0), axis=1).astype(F32)
    counts = jnp.sum(jnp.where(member, (clip_heights * clip_widths)[None, :], 0), axis=1)
    same_clip = jnp.any(member[:, None, :] & member[None, :, :], axis=-1)
    return frame_times, counts, same_clip


def shards(
    tokens,
    cotangent,
    clip_frames,
    clip_offsets,
    clip_heights,
    clip_widths,
    spatial_gain,
    spatial_qkv,
    spatial_out,
    temporal_gain,
    temporal_qkv,
    temporal_out,
):
    size = lax.axis_size("ctx")
    rank = lax.axis_index("ctx")
    everyone = lax.axis_size("dp") * size
    count, features = tokens.shape[1], tokens.shape[2]
    assert count == FRAME and FRAME % size == 0
    near = size // 2
    slots = FRAME // near
    rows = Rows(spatial_qkv.shape[0], spatial_out.shape[0], size)
    half = rows.head // 2

    pieces, layouts, order = gather_weights(
        jnp.concatenate([spatial_qkv, spatial_out], axis=0),
        jnp.concatenate([temporal_qkv, temporal_out], axis=0),
        size,
        rank,
    )
    frame_times, counts, same_clip = clip_tables(
        clip_frames[0], clip_offsets[0], clip_heights[0], clip_widths[0], size
    )
    space_live = jnp.arange(FRAME, dtype=jnp.int32) < counts[rank]
    space_allowed = jnp.broadcast_to(space_live[:, None], (FRAME, FRAME)).astype(F32)
    space_live = space_live[None, :].astype(F32)
    first_frame = (rank // near) * near
    near_times = lax.dynamic_slice_in_dim(frame_times, first_frame, near)
    near_counts = lax.dynamic_slice_in_dim(counts, first_frame, near)
    near_clip = lax.dynamic_slice(same_clip, (first_frame, first_frame), (near, near))
    slot_ids = lax.rem(rank, near) * slots + jnp.arange(slots, dtype=jnp.int32)
    time_live = (slot_ids[None, :] < near_counts[:, None]).reshape(FRAME)
    same_slot = jnp.eye(slots, dtype=bool)
    time_allowed = (near_clip[:, None, :, None] & same_slot[None, :, None, :]).reshape(FRAME, FRAME)
    time_allowed = (time_allowed & time_live[:, None]).astype(F32)
    time_live = time_live[None, :].astype(F32)
    frequency = ROPE_BASE ** (-jnp.arange(half).astype(F32) / half)
    angles = frequency[:, None] * jnp.repeat(near_times, slots)[None, :]
    cosine = jnp.cos(angles)
    sine = jnp.sin(angles)
    cosine = jnp.concatenate([cosine, cosine], axis=0)
    sine = jnp.concatenate([-sine, sine], axis=0)
    is_out = (jnp.arange(rows.total, dtype=jnp.int32) % rows.shard >= rows.qkv).astype(F32)[None, :]

    tokens_local = tokens[0]
    cotangent_local = cotangent[0]
    space_gain = spatial_gain[None, :]
    time_gain = temporal_gain[None, :]
    wide = pltpu.VMEM((rows.total, FRAME), F32)

    order, time_allowed, time_live, cosine, sine, is_out = lax.optimization_barrier(
        (order, time_allowed, time_live, cosine, sine, is_out)
    )
    blocks = len(layouts[0])
    sems = pltpu.SemaphoreType.DMA((2, blocks))
    weight_shape = jax.ShapeDtypeStruct((blocks, rows.total // blocks, features), BF16)
    groups = [list(range(first, first + near)) for first in range(0, size, near)]

    def exchange(sent):
        arrived = lax.all_to_all(
            sent.reshape(near, slots, rows.total),
            "ctx",
            split_axis=0,
            concat_axis=0,
            axis_index_groups=groups,
            tiled=True,
        )
        return arrived.reshape(FRAME, rows.total)

    token_scratch = pltpu.VMEM((FRAME, features), BF16)
    hidden, saved, shares, sent, space_weights, time_weights = call(
        functools.partial(front, rows, layouts),
        (
            jax.ShapeDtypeStruct((FRAME, features), BF16),
            jax.ShapeDtypeStruct((rows.total, FRAME), BF16),
            jax.ShapeDtypeStruct((HEADS, FRAME, FRAME), BF16),
            jax.ShapeDtypeStruct((FRAME, rows.total), BF16),
            weight_shape,
            weight_shape,
        ),
        [wide, wide, token_scratch, token_scratch, sems, pltpu.SemaphoreType.DMA((2,))],
        (space_gain, space_allowed, space_live, time_gain, is_out),
        order,
        (*pieces, tokens_local, cotangent_local),
    )
    arrived = exchange(sent)
    sent = call(
        functools.partial(time_core, rows),
        jax.ShapeDtypeStruct((FRAME, rows.total), BF16),
        [wide, wide],
        (arrived, time_allowed, time_live, cosine, sine),
    )
    arrived = exchange(sent)
    result, grad_tokens, gains = call(
        functools.partial(finish, rows),
        (
            jax.ShapeDtypeStruct((FRAME, features), BF16),
            jax.ShapeDtypeStruct((FRAME, features), BF16),
            jax.ShapeDtypeStruct((everyone, 2, features), BF16),
        ),
        [wide, wide],
        (
            arrived,
            is_out,
            time_weights,
            hidden,
            time_gain,
            cotangent_local,
            space_weights,
            saved,
            shares,
            space_live,
            tokens_local,
            space_gain,
        ),
    )
    gains = lax.all_to_all(gains, ("dp", "ctx"), split_axis=0, concat_axis=0, tiled=True)
    gain_grads = jnp.sum(gains.astype(F32), axis=0) * (1.0 / math.sqrt(everyone * FRAME))
    return result[None], grad_tokens[None], gain_grads


def solution(mesh):
    return jax.shard_map(
        shards,
        mesh=mesh,
        in_specs=(
            P("dp", "ctx", None),
            P("dp", "ctx", None),
            P("dp", None),
            P("dp", None),
            P("dp", None),
            P("dp", None),
            P(),
            P("ctx", None),
            P("ctx", None),
            P(),
            P("ctx", None),
            P("ctx", None),
        ),
        out_specs=(P("dp", "ctx", None), P("dp", "ctx", None), P()),
        check_vma=False,
    )
```

```python
import functools
import math

import jax
import jax.numpy as jnp
from jax import lax
from jax.experimental import pallas as pl
from jax.experimental.pallas import tpu as pltpu
from jax.sharding import PartitionSpec as P

HEADS = 8
FRAME = 128
EPSILON = 1e-06
ROPE_BASE = 10000.0
F32 = jnp.float32
BF16 = jnp.bfloat16
VMEM_LIMIT = 12 * 1024 * 1024


def nn(a, b):
    return lax.dot_general(a, b, (((1,), (0,)), ((), ())), preferred_element_type=F32)


def nt(a, b):
    return lax.dot_general(a, b, (((1,), (1,)), ((), ())), preferred_element_type=F32)


def tn(a, b):
    return lax.dot_general(a, b, (((0,), (0,)), ((), ())), preferred_element_type=F32)


class Rows:
    def __init__(self, qkv_rows, out_rows, size):
        self.qkv, self.out, self.size = qkv_rows, out_rows, size
        self.shard = qkv_rows + out_rows
        self.total = self.shard * size
        self.inner = out_rows * size
        self.head = self.inner // HEADS

    def spans(self, first, count, per_shard, shift):
        found = []
        row = first
        while row < first + count:
            block, inside = divmod(row, per_shard)
            length = min(per_shard - inside, first + count - row)
            place = block * self.shard + shift + inside
            if found and found[-1][0] + found[-1][1] == place:
                found[-1] = (found[-1][0], found[-1][1] + length)
            else:
                found.append((place, length))
            row += length
        return found

    def qkv_spans(self, which, head):
        return self.spans(which * self.inner + head * self.head, self.head, self.qkv, 0)

    def out_spans(self, head):
        return self.spans(head * self.head, self.head, self.out, self.qkv)


def read_rows(ref, spans):
    parts = [ref[place : place + length, :] for place, length in spans]
    return parts[0] if len(parts) == 1 else jnp.concatenate(parts, axis=0)


def write_rows(ref, spans, value):
    done = 0
    for place, length in spans:
        ref[place : place + length, :] = value[done : done + length, :]
        done += length


def inverse_size(values):
    return lax.rsqrt(jnp.mean(values * values, axis=-1, keepdims=True) + EPSILON)


def norm_back(values, inverse, gain, grad):
    scaled = grad * gain
    middle = jnp.mean(scaled * values, axis=-1, keepdims=True)
    grad_values = inverse * scaled - values * (inverse * inverse * inverse * middle)
    grad_gain = jnp.sum(grad * (values * inverse), axis=0, keepdims=True)
    return grad_values, grad_gain


def shares_of(queries, keys, allowed, live, scale):
    scores = tn(keys, queries) * scale
    weights = jnp.where(allowed > 0.0, jnp.exp(jnp.where(allowed > 0.0, scores, 0.0)), 0.0)
    totals = jnp.sum(weights, axis=0, keepdims=True) + (1.0 - live)
    return weights * (1.0 / totals)


def attend_back(queries, keys, values, shares, shares_low, grad, scale):
    grad_shares = tn(values, grad)
    middle = jnp.sum(shares * grad_shares, axis=0, keepdims=True)
    grad_scores = (shares * (grad_shares - middle) * scale).astype(BF16)
    return nn(keys, grad_scores), nt(queries, grad_scores), nt(grad, shares_low)


def weight_copies(layout, order, pieces, target, sems, which):
    count = target.shape[1]
    return [
        pltpu.make_async_copy(
            pieces[piece].at[pl.ds(first, count)], target.at[order[index]], sems.at[which, index]
        )
        for index, (piece, first) in enumerate(layout)
    ]


def start_weights(layouts, order, pieces, space, time, sems):
    def start(first, second):
        for copy in weight_copies(first, order, pieces, space, sems, 0):
            copy.start()
        for copy in weight_copies(second, order, pieces, time, sems, 1):
            copy.start()

    plane = order[len(layouts[0])]

    @pl.when(plane == 0)
    def _():
        start(layouts[0], layouts[1])

    @pl.when(plane != 0)
    def _():
        start(layouts[1], layouts[0])


def wait_weights(layouts, order, pieces, target, sems, which):
    for copy in weight_copies(layouts[0], order, pieces, target, sems, which):
        copy.wait()


def front(rows, layouts, order, space_gain, allowed, live, time_gain, is_out, *refs):
    pieces, refs = refs[:-14], refs[-14:]
    tokens_in, cotangent_in, hidden, saved, shares_out, sent, space, time = refs[:8]
    project, mixed, tokens, cotangent, sems, token_sems = refs[8:]
    token_copy = pltpu.make_async_copy(tokens_in, tokens, token_sems.at[0])
    token_copy.start()
    cotangent_copy = pltpu.make_async_copy(cotangent_in, cotangent, token_sems.at[1])
    cotangent_copy.start()
    start_weights(layouts, order, pieces, space, time, sems)
    token_copy.wait()
    values = tokens[...].astype(F32)
    normed = (values * inverse_size(values) * space_gain[...]).astype(BF16)
    mixed[...] = jnp.zeros_like(mixed)
    wait_weights(layouts, order, pieces, space, sems, 0)
    weight = space[...].reshape(rows.total, -1)
    project[...] = nt(weight, normed)
    saved[...] = project[...].astype(BF16)
    scale = rows.head ** (-0.5)
    for head in range(HEADS):
        query, key, value = (
            read_rows(project, rows.qkv_spans(which, head)).astype(BF16) for which in range(3)
        )
        shares = shares_of(query, key, allowed[...], live[...], scale).astype(BF16)
        shares_out[head] = shares
        write_rows(mixed, rows.out_spans(head), nn(value, shares) * live[...])
    update = tn(mixed[...].astype(BF16), weight)
    low = (values + update).astype(BF16)
    hidden[...] = low
    values = low.astype(F32)
    normed = (values * inverse_size(values) * time_gain[...]).astype(BF16)
    wait_weights(layouts, order, pieces, time, sems, 1)
    cotangent_copy.wait()
    weight = time[...].reshape(rows.total, -1)
    both = nt(jnp.concatenate([normed, cotangent[...]], axis=0), weight)
    count = values.shape[0]
    sent[...] = jnp.where(is_out[...] > 0.0, both[count:], both[:count]).astype(BF16)


def time_core(rows, arrived, allowed, live, cosine, sine, sent, project, result):
    count = arrived.shape[0]
    for first in range(0, rows.total, FRAME):
        project[first : first + FRAME, :] = arrived[:, first : first + FRAME].astype(F32).T
    scale = rows.head ** (-0.5)
    half = rows.head // 2

    def swapped(vectors):
        return jnp.concatenate([vectors[half:], vectors[:half]], axis=0)

    for head in range(HEADS):
        turned = []
        for which in range(2):
            vectors = read_rows(project, rows.qkv_spans(which, head))
            turned.append((vectors * cosine[...] + swapped(vectors) * sine[...]).astype(BF16))
        query, key = turned
        value = read_rows(project, rows.qkv_spans(2, head)).astype(BF16)
        grad = (read_rows(project, rows.out_spans(head)) * live[...]).astype(BF16)
        shares = shares_of(query, key, allowed[...], live[...], scale)
        shares_low = shares.astype(BF16)
        write_rows(result, rows.out_spans(head), nn(value, shares_low) * live[...])
        grads = attend_back(query, key, value, shares, shares_low, grad, scale)
        for which in range(2):
            turned_grad = grads[which].astype(BF16).astype(F32)
            write_rows(
                result,
                rows.qkv_spans(which, head),
                turned_grad * cosine[...] - swapped(turned_grad) * sine[...],
            )
        write_rows(result, rows.qkv_spans(2, head), grads[2])
    for first in range(0, rows.total, FRAME):
        sent[:, first : first + FRAME] = result[first : first + FRAME, :].T.astype(BF16)


def finish(
    rows,
    arrived,
    is_out,
    time,
    hidden,
    time_gain,
    cotangent,
    space,
    saved,
    shares_in,
    live,
    tokens,
    space_gain,
    output,
    grad_tokens,
    gains,
    project,
    grad_project,
):
    count = arrived.shape[0]
    time_weight = time[...].reshape(rows.total, -1)
    space_weight = space[...].reshape(rows.total, -1)
    received = arrived[...]
    zeros = jnp.zeros_like(received)
    mask = jnp.broadcast_to(is_out[...] > 0.0, received.shape)
    left = jnp.concatenate([jnp.where(mask, zeros, received), jnp.where(mask, received, zeros)], axis=0)
    both = nn(left, time_weight)
    values = hidden[...].astype(F32)
    output[...] = (values + both[count:]).astype(BF16)
    grad_normed = both[:count].astype(BF16).astype(F32)
    grad_front, grad_time_gain = norm_back(values, inverse_size(values), time_gain[...], grad_normed)
    grad_hidden = (cotangent[...].astype(F32) + grad_front).astype(BF16)

    project[...] = nt(space_weight, grad_hidden)
    grad_project[...] = jnp.zeros_like(grad_project)
    scale = rows.head ** (-0.5)
    for head in range(HEADS):
        query, key, value = (
            read_rows(saved, rows.qkv_spans(which, head)).astype(BF16) for which in range(3)
        )
        grad = (read_rows(project, rows.out_spans(head)) * live[...]).astype(BF16)
        shares_low = shares_in[head]
        grads = attend_back(query, key, value, shares_low.astype(F32), shares_low, grad, scale)
        for which in range(3):
            write_rows(grad_project, rows.qkv_spans(which, head), grads[which])
    grad_normed = tn(grad_project[...].astype(BF16), space_weight).astype(BF16).astype(F32)
    values = tokens[...].astype(F32)
    grad_values, grad_space_gain = norm_back(values, inverse_size(values), space_gain[...], grad_normed)
    grad_tokens[...] = (grad_hidden.astype(F32) + grad_values).astype(BF16)
    both_gains = jnp.concatenate([grad_space_gain, grad_time_gain], axis=0).astype(gains.dtype)
    gains[...] = jnp.broadcast_to(both_gains[None], gains.shape)


def call(body, out_shapes, scratch, operands, in_order=None, pieces=()):
    whole = pl.BlockSpec(memory_space=pltpu.VMEM)
    scalars = pl.BlockSpec(memory_space=pltpu.SMEM)
    anywhere = pl.BlockSpec(memory_space=pl.ANY)
    first = () if in_order is None else (in_order,)
    return pl.pallas_call(
        body,
        out_shape=out_shapes,
        in_specs=[scalars] * len(first) + [whole] * len(operands) + [anywhere] * len(pieces),
        out_specs=jax.tree.map(lambda _: whole, out_shapes),
        scratch_shapes=scratch,
        compiler_params=pltpu.CompilerParams(vmem_limit_bytes=VMEM_LIMIT),
    )(*first, *operands, *pieces)


def gather_ring(space_rows, time_rows, size, rank):
    chips = size // 2
    chain = chips // 2
    shard = space_rows.shape[0]

    def chip_at(place):
        place = place % chips
        return 2 * place if place < chain else 2 * (chips - 1 - place) + 1

    ring_pairs = []
    for place in range(chips):
        ring_pairs.append((2 * chip_at(place), 2 * chip_at(place + 1)))
        ring_pairs.append((2 * chip_at(place) + 1, 2 * chip_at(place - 1) + 1))
    planes = lax.axis_size("dp")
    plane = lax.rem(lax.axis_index("dp"), 2)

    def ring(rows):
        return lax.ppermute(rows, "ctx", ring_pairs)

    def across(rows):
        return lax.ppermute(rows, "dp", [(index, index ^ 1) for index in range(planes)])

    def twin(rows):
        return lax.ppermute(rows, "ctx", [(index, index ^ 1) for index in range(size)])

    def after(rows, *events):
        return lax.optimization_barrier((rows, *events))[0]

    own = jnp.where(plane == 0, space_rows, time_rows)
    own_other = jnp.where(plane == 0, time_rows, space_rows)
    t0 = twin(own)
    o1 = ring(after(own, t0))
    t1 = ring(t0)
    o2 = ring(o1)
    t2 = ring(t1)
    x_o1 = across(o1)
    x_t1 = across(after(t1, o2, x_o1))
    x_t2 = ring(x_t1)
    o1_twin = twin(o1)
    o2_twin = twin(o2)
    t1_twin = twin(t1)
    t2_twin = twin(t2)
    x_o1_twin = twin(x_o1)
    x_t1_twin = twin(x_t1)
    x_t2_twin = twin(x_t2)
    t0_other = twin(after(own_other, o2))
    o3 = ring(after(o2, x_o1))
    o4 = ring(after(o3, x_o1))
    t3 = ring(after(t2, o1_twin, x_o1))
    x_o3 = across(o3)
    x_t3 = ring(after(x_t2, t3))
    x_o4 = across(after(o4, x_t2))
    o3_twin = twin(o3)
    o4_twin = twin(o4)
    t3_twin = twin(t3)
    x_o3_twin = twin(x_o3)
    x_o4_twin = twin(x_o4)
    x_t3_twin = twin(x_t3)
    x_o2 = ring(after(x_o1, o4, t2, x_o3))
    x_o2_twin = twin(x_o2)
    mine = {"o0": (own, 0), "t0": (t0, 0)}
    other = {"o0": (own_other, 0), "t0": (t0_other, 0)}
    mine |= {"o1": (o1, 0), "o1_twin": (o1_twin, 0)}
    other |= {"o1": (x_o1, 0), "o1_twin": (x_o1_twin, 0)}
    mine |= {"o2": (o2, 0), "o2_twin": (o2_twin, 0)}
    other |= {"o2": (x_o2, 0), "o2_twin": (x_o2_twin, 0)}
    mine |= {"o3": (o3, 0), "o3_twin": (o3_twin, 0)}
    other |= {"o3": (x_o3, 0), "o3_twin": (x_o3_twin, 0)}
    mine |= {"o4": (o4, 0), "o4_twin": (o4_twin, 0)}
    other |= {"o4": (x_o4, 0), "o4_twin": (x_o4_twin, 0)}
    mine |= {"t1": (t1, 0), "t1_twin": (t1_twin, 0)}
    other |= {"t1": (x_t1, 0), "t1_twin": (x_t1_twin, 0)}
    mine |= {"t2": (t2, 0), "t2_twin": (t2_twin, 0)}
    other |= {"t2": (x_t2, 0), "t2_twin": (x_t2_twin, 0)}
    mine |= {"t3": (t3, 0), "t3_twin": (t3_twin, 0)}
    other |= {"t3": (x_t3, 0), "t3_twin": (x_t3_twin, 0)}
    chip, core = rank // 2, lax.rem(rank, 2)
    column, level = lax.rem(chip, 2), chip // 2
    place = jnp.where(column == 0, level, chips - 1 - level)

    def came(carrier, name):
        steps, shard_core = int(name[1]), carrier if name[0] == "o" else 1 - carrier
        at = lax.rem(place + steps * (2 * carrier - 1) + chips, chips)
        return 2 * jnp.where(at < chain, 2 * at, 2 * (chips - 1 - at) + 1) + shard_core

    names = ["o0", "t0", "o1", "o2", "o3", "o4", "t1", "t2", "t3"]
    twins = names[2:]
    order = [came(core, name) for name in names] + [came(1 - core, name) for name in twins]
    pieces, layouts = [], ([], [])
    for half, found in enumerate((mine, other)):
        for name in names + [name + "_twin" for name in twins]:
            array, first = found[name]
            place_in = [index for index, piece in enumerate(pieces) if piece is array]
            if not place_in:
                place_in = [len(pieces)]
                pieces.append(array)
            layouts[half].append((place_in[0], first * shard))
    return pieces, layouts, jnp.stack(order + [plane]).astype(jnp.int32)


def gather_weights(space_rows, time_rows, size, rank):
    if size == 16 and lax.axis_size("dp") % 2 == 0:
        return gather_ring(space_rows, time_rows, size, rank)
    shard, features = space_rows.shape
    gathered = lax.all_gather(jnp.concatenate([space_rows, time_rows], axis=0), "ctx", axis=0)
    gathered = gathered.reshape(size, 2, shard, features)
    halves = [gathered[:, half].reshape(size * shard, features) for half in range(2)]
    return halves, ([(0, 0)], [(1, 0)]), jnp.zeros((2,), jnp.int32)


def clip_tables(clip_frames, clip_offsets, clip_heights, clip_widths, total_frames):
    starts = clip_offsets // FRAME
    frame_ids = jnp.arange(total_frames, dtype=jnp.int32)[:, None]
    member = (frame_ids >= starts[None, :]) & (frame_ids < (starts + clip_frames)[None, :])
    frame_times = jnp.sum(jnp.where(member, frame_ids - starts[None, :], 0), axis=1).astype(F32)
    counts = jnp.sum(jnp.where(member, (clip_heights * clip_widths)[None, :], 0), axis=1)
    same_clip = jnp.any(member[:, None, :] & member[None, :, :], axis=-1)
    return frame_times, counts, same_clip


def shards(
    tokens,
    cotangent,
    clip_frames,
    clip_offsets,
    clip_heights,
    clip_widths,
    spatial_gain,
    spatial_qkv,
    spatial_out,
    temporal_gain,
    temporal_qkv,
    temporal_out,
):
    size = lax.axis_size("ctx")
    rank = lax.axis_index("ctx")
    everyone = lax.axis_size("dp") * size
    count, features = tokens.shape[1], tokens.shape[2]
    assert count == FRAME and FRAME % size == 0
    near = size // 2
    slots = FRAME // near
    rows = Rows(spatial_qkv.shape[0], spatial_out.shape[0], size)
    half = rows.head // 2

    pieces, layouts, order = gather_weights(
        jnp.concatenate([spatial_qkv, spatial_out], axis=0),
        jnp.concatenate([temporal_qkv, temporal_out], axis=0),
        size,
        rank,
    )
    frame_times, counts, same_clip = clip_tables(
        clip_frames[0], clip_offsets[0], clip_heights[0], clip_widths[0], size
    )
    space_live = jnp.arange(FRAME, dtype=jnp.int32) < counts[rank]
    space_allowed = jnp.broadcast_to(space_live[:, None], (FRAME, FRAME)).astype(F32)
    space_live = space_live[None, :].astype(F32)
    first_frame = (rank // near) * near
    near_times = lax.dynamic_slice_in_dim(frame_times, first_frame, near)
    near_counts = lax.dynamic_slice_in_dim(counts, first_frame, near)
    near_clip = lax.dynamic_slice(same_clip, (first_frame, first_frame), (near, near))
    slot_ids = lax.rem(rank, near) * slots + jnp.arange(slots, dtype=jnp.int32)
    time_live = (slot_ids[None, :] < near_counts[:, None]).reshape(FRAME)
    same_slot = jnp.eye(slots, dtype=bool)
    time_allowed = (near_clip[:, None, :, None] & same_slot[None, :, None, :]).reshape(FRAME, FRAME)
    time_allowed = (time_allowed & time_live[:, None]).astype(F32)
    time_live = time_live[None, :].astype(F32)
    frequency = ROPE_BASE ** (-jnp.arange(half).astype(F32) / half)
    angles = frequency[:, None] * jnp.repeat(near_times, slots)[None, :]
    cosine = jnp.cos(angles)
    sine = jnp.sin(angles)
    cosine = jnp.concatenate([cosine, cosine], axis=0)
    sine = jnp.concatenate([-sine, sine], axis=0)
    is_out = (jnp.arange(rows.total, dtype=jnp.int32) % rows.shard >= rows.qkv).astype(F32)[None, :]

    tokens_local = tokens[0]
    cotangent_local = cotangent[0]
    space_gain = spatial_gain[None, :]
    time_gain = temporal_gain[None, :]
    wide = pltpu.VMEM((rows.total, FRAME), F32)

    order, time_allowed, time_live, cosine, sine, is_out = lax.optimization_barrier(
        (order, time_allowed, time_live, cosine, sine, is_out)
    )
    blocks = len(layouts[0])
    sems = pltpu.SemaphoreType.DMA((2, blocks))
    weight_shape = jax.ShapeDtypeStruct((blocks, rows.total // blocks, features), BF16)
    groups = [list(range(first, first + near)) for first in range(0, size, near)]

    def exchange(sent):
        arrived = lax.all_to_all(
            sent.reshape(near, slots, rows.total),
            "ctx",
            split_axis=0,
            concat_axis=0,
            axis_index_groups=groups,
            tiled=True,
        )
        return arrived.reshape(FRAME, rows.total)

    token_scratch = pltpu.VMEM((FRAME, features), BF16)
    hidden, saved, shares, sent, space_weights, time_weights = call(
        functools.partial(front, rows, layouts),
        (
            jax.ShapeDtypeStruct((FRAME, features), BF16),
            jax.ShapeDtypeStruct((rows.total, FRAME), BF16),
            jax.ShapeDtypeStruct((HEADS, FRAME, FRAME), BF16),
            jax.ShapeDtypeStruct((FRAME, rows.total), BF16),
            weight_shape,
            weight_shape,
        ),
        [wide, wide, token_scratch, token_scratch, sems, pltpu.SemaphoreType.DMA((2,))],
        (space_gain, space_allowed, space_live, time_gain, is_out),
        order,
        (*pieces, tokens_local, cotangent_local),
    )
    arrived = exchange(sent)
    sent = call(
        functools.partial(time_core, rows),
        jax.ShapeDtypeStruct((FRAME, rows.total), BF16),
        [wide, wide],
        (arrived, time_allowed, time_live, cosine, sine),
    )
    arrived = exchange(sent)
    result, grad_tokens, gains = call(
        functools.partial(finish, rows),
        (
            jax.ShapeDtypeStruct((FRAME, features), BF16),
            jax.ShapeDtypeStruct((FRAME, features), BF16),
            jax.ShapeDtypeStruct((everyone, 2, features), BF16),
        ),
        [wide, wide],
        (
            arrived,
            is_out,
            time_weights,
            hidden,
            time_gain,
            cotangent_local,
            space_weights,
            saved,
            shares,
            space_live,
            tokens_local,
            space_gain,
        ),
    )
    gains = lax.all_to_all(gains, ("dp", "ctx"), split_axis=0, concat_axis=0, tiled=True)
    gain_grads = jnp.sum(gains.astype(F32), axis=0) * (1.0 / math.sqrt(everyone * FRAME))
    return result[None], grad_tokens[None], gain_grads


def solution(mesh):
    return jax.shard_map(
        shards,
        mesh=mesh,
        in_specs=(
            P("dp", "ctx", None),
            P("dp", "ctx", None),
            P("dp", None),
            P("dp", None),
            P("dp", None),
            P("dp", None),
            P(),
            P("ctx", None),
            P("ctx", None),
            P(),
            P("ctx", None),
            P("ctx", None),
        ),
        out_specs=(P("dp", "ctx", None), P("dp", "ctx", None), P()),
        check_vma=False,
    )
```

```python
import functools
import math

import jax
import jax.numpy as jnp
from jax import lax
from jax.experimental import pallas as pl
from jax.experimental.pallas import tpu as pltpu
from jax.sharding import PartitionSpec as P

HEADS = 8
FRAME = 128
EPSILON = 1e-06
ROPE_BASE = 10000.0
F32 = jnp.float32
BF16 = jnp.bfloat16
VMEM_LIMIT = 12 * 1024 * 1024


def nn(a, b):
    return lax.dot_general(a, b, (((1,), (0,)), ((), ())), preferred_element_type=F32)


def nt(a, b):
    return lax.dot_general(a, b, (((1,), (1,)), ((), ())), preferred_element_type=F32)


def tn(a, b):
    return lax.dot_general(a, b, (((0,), (0,)), ((), ())), preferred_element_type=F32)


class Rows:
    def __init__(self, qkv_rows, out_rows, size):
        self.qkv, self.out, self.size = qkv_rows, out_rows, size
        self.shard = qkv_rows + out_rows
        self.total = self.shard * size
        self.inner = out_rows * size
        self.head = self.inner // HEADS

    def spans(self, first, count, per_shard, shift):
        found = []
        row = first
        while row < first + count:
            block, inside = divmod(row, per_shard)
            length = min(per_shard - inside, first + count - row)
            place = block * self.shard + shift + inside
            if found and found[-1][0] + found[-1][1] == place:
                found[-1] = (found[-1][0], found[-1][1] + length)
            else:
                found.append((place, length))
            row += length
        return found

    def qkv_spans(self, which, head):
        return self.spans(which * self.inner + head * self.head, self.head, self.qkv, 0)

    def out_spans(self, head):
        return self.spans(head * self.head, self.head, self.out, self.qkv)


def read_rows(ref, spans):
    parts = [ref[place : place + length, :] for place, length in spans]
    return parts[0] if len(parts) == 1 else jnp.concatenate(parts, axis=0)


def write_rows(ref, spans, value):
    done = 0
    for place, length in spans:
        ref[place : place + length, :] = value[done : done + length, :]
        done += length


def inverse_size(values):
    return lax.rsqrt(jnp.mean(values * values, axis=-1, keepdims=True) + EPSILON)


def norm_back(values, inverse, gain, grad):
    scaled = grad * gain
    middle = jnp.mean(scaled * values, axis=-1, keepdims=True)
    grad_values = inverse * scaled - values * (inverse * inverse * inverse * middle)
    grad_gain = jnp.sum(grad * (values * inverse), axis=0, keepdims=True)
    return grad_values, grad_gain


def shares_of(queries, keys, allowed, live, scale):
    scores = tn(keys, queries) * scale
    weights = jnp.where(allowed, jnp.exp(jnp.where(allowed, scores, 0.0)), 0.0)
    totals = jnp.sum(weights, axis=0, keepdims=True) + (1.0 - live)
    return weights * (1.0 / totals)


def attend_back(queries, keys, values, shares, shares_low, grad, scale):
    grad_shares = tn(values, grad)
    middle = jnp.sum(shares * grad_shares, axis=0, keepdims=True)
    grad_scores = (shares * (grad_shares - middle) * scale).astype(BF16)
    return nn(keys, grad_scores), nt(queries, grad_scores), nt(grad, shares_low)


def clips_at(clips, frames):
    counts, times, numbers = (jnp.zeros(frames.shape, jnp.int32) for _ in range(3))
    length, offset, height, width = clips
    for clip in range(length.shape[1]):
        start = offset[0, clip] // FRAME
        member = (frames >= start) & (frames < start + length[0, clip])
        counts = jnp.where(member, height[0, clip] * width[0, clip], counts)
        times = jnp.where(member, frames - start, times)
        numbers = jnp.where(member, clip + 1, numbers)
    return counts, times, numbers


def ids(shape, dim):
    return lax.broadcasted_iota(jnp.int32, shape, dim)


def space_masks(clips):
    rank = lax.axis_index("ctx")
    counts = clips_at(clips, jnp.full((FRAME, FRAME), rank, jnp.int32))[0]
    allowed = ids((FRAME, FRAME), 0) < counts
    live = (ids((1, FRAME), 1) < counts[:1]).astype(F32)
    return allowed, live


def time_masks(clips, near, slots):
    rank = lax.axis_index("ctx")
    first = (rank // near) * near

    def at(dim):
        token = ids((FRAME, FRAME), dim)
        slot = lax.rem(token, slots)
        counts, times, numbers = clips_at(clips, first + token // slots)
        alive = lax.rem(rank, near) * slots + slot < counts
        return slot, times, numbers, alive

    slot, _, numbers, alive = at(0)
    query_slot, query_times, query_numbers, query_alive = at(1)
    allowed = alive & (slot == query_slot) & (numbers == query_numbers)
    return allowed, query_alive[:1].astype(F32), query_times[:1].astype(F32)


def turn_tables(times, half):
    pair = ids((2 * half, FRAME), 0)
    lower = pair < half
    frequency = jnp.exp(jnp.where(lower, pair, pair - half).astype(F32) * (-math.log(ROPE_BASE) / half))
    angles = frequency * times
    sine = jnp.sin(angles)
    return jnp.cos(angles), jnp.where(lower, -sine, sine)


def out_columns(rows):
    return lax.rem(ids((1, rows.total), 1), rows.shard) >= rows.qkv


def weight_copies(layout, order, pieces, target, sems, which):
    count = target.shape[1]
    return [
        pltpu.make_async_copy(
            pieces[piece].at[pl.ds(first, count)], target.at[order[index]], sems.at[which, index]
        )
        for index, (piece, first) in enumerate(layout)
    ]


def start_weights(layouts, order, pieces, space, time, sems):
    def start(first, second):
        for copy in weight_copies(first, order, pieces, space, sems, 0):
            copy.start()
        for copy in weight_copies(second, order, pieces, time, sems, 1):
            copy.start()

    plane = order[len(layouts[0])]

    @pl.when(plane == 0)
    def _():
        start(layouts[0], layouts[1])

    @pl.when(plane != 0)
    def _():
        start(layouts[1], layouts[0])


def wait_weights(layouts, order, pieces, target, sems, which):
    for copy in weight_copies(layouts[0], order, pieces, target, sems, which):
        copy.wait()


def front(rows, layouts, order_of, clip0, clip1, clip2, clip3, space_gain, time_gain, *refs):
    pieces, refs = refs[:-14], refs[-14:]
    tokens_in, cotangent_in, hidden, saved, shares_out, sent, space, time = refs[:8]
    project, mixed, tokens, cotangent, sems, token_sems = refs[8:]
    token_copy = pltpu.make_async_copy(tokens_in, tokens, token_sems.at[0])
    token_copy.start()
    cotangent_copy = pltpu.make_async_copy(cotangent_in, cotangent, token_sems.at[1])
    cotangent_copy.start()
    order = order_of()
    start_weights(layouts, order, pieces, space, time, sems)
    allowed, live = space_masks((clip0, clip1, clip2, clip3))
    token_copy.wait()
    values = tokens[...].astype(F32)
    normed = (values * inverse_size(values) * space_gain[...].reshape(1, -1)).astype(BF16)
    mixed[...] = jnp.zeros_like(mixed)
    wait_weights(layouts, order, pieces, space, sems, 0)
    weight = space[...].reshape(rows.total, -1)
    project[...] = nt(weight, normed)
    saved[...] = project[...].astype(BF16)
    scale = rows.head ** (-0.5)
    for head in range(HEADS):
        query, key, value = (
            read_rows(project, rows.qkv_spans(which, head)).astype(BF16) for which in range(3)
        )
        shares = shares_of(query, key, allowed, live, scale).astype(BF16)
        shares_out[head] = shares
        write_rows(mixed, rows.out_spans(head), nn(value, shares) * live)
    update = tn(mixed[...].astype(BF16), weight)
    low = (values + update).astype(BF16)
    hidden[...] = low
    values = low.astype(F32)
    normed = (values * inverse_size(values) * time_gain[...].reshape(1, -1)).astype(BF16)
    wait_weights(layouts, order, pieces, time, sems, 1)
    cotangent_copy.wait()
    weight = time[...].reshape(rows.total, -1)
    both = nt(jnp.concatenate([normed, cotangent[...]], axis=0), weight)
    count = values.shape[0]
    sent[...] = jnp.where(out_columns(rows), both[count:], both[:count]).astype(BF16)


def time_core(rows, near, slots, clip0, clip1, clip2, clip3, arrived, sent, project, result):
    allowed, live, times = time_masks((clip0, clip1, clip2, clip3), near, slots)
    for first in range(0, rows.total, FRAME):
        project[first : first + FRAME, :] = arrived[:, first : first + FRAME].astype(F32).T
    scale = rows.head ** (-0.5)
    half = rows.head // 2
    cosine, sine = turn_tables(times, half)

    def swapped(vectors):
        return jnp.concatenate([vectors[half:], vectors[:half]], axis=0)

    for head in range(HEADS):
        turned = []
        for which in range(2):
            vectors = read_rows(project, rows.qkv_spans(which, head))
            turned.append((vectors * cosine + swapped(vectors) * sine).astype(BF16))
        query, key = turned
        value = read_rows(project, rows.qkv_spans(2, head)).astype(BF16)
        grad = (read_rows(project, rows.out_spans(head)) * live).astype(BF16)
        shares = shares_of(query, key, allowed, live, scale)
        shares_low = shares.astype(BF16)
        write_rows(result, rows.out_spans(head), nn(value, shares_low) * live)
        grads = attend_back(query, key, value, shares, shares_low, grad, scale)
        for which in range(2):
            turned_grad = grads[which].astype(BF16).astype(F32)
            write_rows(
                result,
                rows.qkv_spans(which, head),
                turned_grad * cosine - swapped(turned_grad) * sine,
            )
        write_rows(result, rows.qkv_spans(2, head), grads[2])
    for first in range(0, rows.total, FRAME):
        sent[:, first : first + FRAME] = result[first : first + FRAME, :].T.astype(BF16)


def finish(
    rows,
    clip0,
    clip1,
    clip2,
    clip3,
    arrived,
    time,
    hidden,
    time_gain,
    cotangent,
    space,
    saved,
    shares_in,
    tokens,
    space_gain,
    output,
    grad_tokens,
    gains,
    project,
    grad_project,
):
    count = arrived.shape[0]
    live = space_masks((clip0, clip1, clip2, clip3))[1]
    time_weight = time[...].reshape(rows.total, -1)
    space_weight = space[...].reshape(rows.total, -1)
    received = arrived[...]
    zeros = jnp.zeros_like(received)
    mask = jnp.broadcast_to(out_columns(rows), received.shape)
    left = jnp.concatenate([jnp.where(mask, zeros, received), jnp.where(mask, received, zeros)], axis=0)
    both = nn(left, time_weight)
    values = hidden[...].astype(F32)
    output[...] = (values + both[count:]).astype(BF16)
    grad_normed = both[:count].astype(BF16).astype(F32)
    grad_front, grad_time_gain = norm_back(values, inverse_size(values), time_gain[...].reshape(1, -1), grad_normed)
    grad_hidden = (cotangent[...].astype(F32) + grad_front).astype(BF16)

    project[...] = nt(space_weight, grad_hidden)
    grad_project[...] = jnp.zeros_like(grad_project)
    scale = rows.head ** (-0.5)
    for head in range(HEADS):
        query, key, value = (
            read_rows(saved, rows.qkv_spans(which, head)).astype(BF16) for which in range(3)
        )
        grad = (read_rows(project, rows.out_spans(head)) * live).astype(BF16)
        shares_low = shares_in[head]
        grads = attend_back(query, key, value, shares_low.astype(F32), shares_low, grad, scale)
        for which in range(3):
            write_rows(grad_project, rows.qkv_spans(which, head), grads[which])
    grad_normed = tn(grad_project[...].astype(BF16), space_weight).astype(BF16).astype(F32)
    values = tokens[...].astype(F32)
    grad_values, grad_space_gain = norm_back(values, inverse_size(values), space_gain[...].reshape(1, -1), grad_normed)
    grad_tokens[...] = (grad_hidden.astype(F32) + grad_values).astype(BF16)
    both_gains = jnp.concatenate([grad_space_gain, grad_time_gain], axis=0).astype(gains.dtype)
    gains[...] = jnp.broadcast_to(both_gains[None], gains.shape)


def call(body, out_shapes, scratch, clips, operands, pieces=()):
    whole = pl.BlockSpec(memory_space=pltpu.VMEM)
    scalars = pl.BlockSpec(memory_space=pltpu.SMEM)
    anywhere = pl.BlockSpec(memory_space=pl.ANY)
    return pl.pallas_call(
        body,
        out_shape=out_shapes,
        in_specs=[scalars] * len(clips) + [whole] * len(operands) + [anywhere] * len(pieces),
        out_specs=jax.tree.map(lambda _: whole, out_shapes),
        scratch_shapes=scratch,
        compiler_params=pltpu.CompilerParams(vmem_limit_bytes=VMEM_LIMIT),
    )(*clips, *operands, *pieces)


def gather_ring(space_rows, time_rows, size):
    chips = size // 2
    chain = chips // 2
    shard = space_rows.shape[0]

    def chip_at(place):
        place = place % chips
        return 2 * place if place < chain else 2 * (chips - 1 - place) + 1

    ring_pairs = []
    for place in range(chips):
        ring_pairs.append((2 * chip_at(place), 2 * chip_at(place + 1)))
        ring_pairs.append((2 * chip_at(place) + 1, 2 * chip_at(place - 1) + 1))
    planes = lax.axis_size("dp")
    plane = lax.rem(lax.axis_index("dp"), 2)

    def ring(rows):
        return lax.ppermute(rows, "ctx", ring_pairs)

    def across(rows):
        return lax.ppermute(rows, "dp", [(index, index ^ 1) for index in range(planes)])

    def twin(rows):
        return lax.ppermute(rows, "ctx", [(index, index ^ 1) for index in range(size)])

    def after(rows, *events):
        return lax.optimization_barrier((rows, *events))[0]

    own = jnp.where(plane == 0, space_rows, time_rows)
    own_other = jnp.where(plane == 0, time_rows, space_rows)
    t0 = twin(own)
    o1 = ring(after(own, t0))
    t1 = ring(t0)
    o2 = ring(o1)
    t2 = ring(t1)
    x_o1 = across(o1)
    x_t1 = across(after(t1, o2, x_o1))
    x_t2 = ring(x_t1)
    o1_twin = twin(o1)
    o2_twin = twin(o2)
    t1_twin = twin(t1)
    t2_twin = twin(t2)
    x_o1_twin = twin(x_o1)
    x_t1_twin = twin(x_t1)
    x_t2_twin = twin(x_t2)
    t0_other = twin(after(own_other, o2))
    o3 = ring(after(o2, x_o1))
    o4 = ring(after(o3, x_o1))
    t3 = ring(after(t2, o1_twin, x_o1))
    x_o3 = across(o3)
    x_t3 = ring(after(x_t2, t3))
    x_o4 = across(after(o4, x_t2))
    o3_twin = twin(o3)
    o4_twin = twin(o4)
    t3_twin = twin(t3)
    x_o3_twin = twin(x_o3)
    x_o4_twin = twin(x_o4)
    x_t3_twin = twin(x_t3)
    x_o2 = ring(after(x_o1, o4, t2, x_o3))
    x_o2_twin = twin(x_o2)
    mine = {"o0": (own, 0), "t0": (t0, 0)}
    other = {"o0": (own_other, 0), "t0": (t0_other, 0)}
    mine |= {"o1": (o1, 0), "o1_twin": (o1_twin, 0)}
    other |= {"o1": (x_o1, 0), "o1_twin": (x_o1_twin, 0)}
    mine |= {"o2": (o2, 0), "o2_twin": (o2_twin, 0)}
    other |= {"o2": (x_o2, 0), "o2_twin": (x_o2_twin, 0)}
    mine |= {"o3": (o3, 0), "o3_twin": (o3_twin, 0)}
    other |= {"o3": (x_o3, 0), "o3_twin": (x_o3_twin, 0)}
    mine |= {"o4": (o4, 0), "o4_twin": (o4_twin, 0)}
    other |= {"o4": (x_o4, 0), "o4_twin": (x_o4_twin, 0)}
    mine |= {"t1": (t1, 0), "t1_twin": (t1_twin, 0)}
    other |= {"t1": (x_t1, 0), "t1_twin": (x_t1_twin, 0)}
    mine |= {"t2": (t2, 0), "t2_twin": (t2_twin, 0)}
    other |= {"t2": (x_t2, 0), "t2_twin": (x_t2_twin, 0)}
    mine |= {"t3": (t3, 0), "t3_twin": (t3_twin, 0)}
    other |= {"t3": (x_t3, 0), "t3_twin": (x_t3_twin, 0)}
    names = ["o0", "t0", "o1", "o2", "o3", "o4", "t1", "t2", "t3"]
    twins = names[2:]

    def order_of():
        rank = lax.axis_index("ctx")
        chip, core = rank // 2, lax.rem(rank, 2)
        column, level = lax.rem(chip, 2), chip // 2
        place = jnp.where(column == 0, level, chips - 1 - level)

        def came(carrier, name):
            steps, shard_core = int(name[1]), carrier if name[0] == "o" else 1 - carrier
            at = lax.rem(place + steps * (2 * carrier - 1) + chips, chips)
            return 2 * jnp.where(at < chain, 2 * at, 2 * (chips - 1 - at) + 1) + shard_core

        order = [came(core, name) for name in names] + [came(1 - core, name) for name in twins]
        return order + [lax.rem(lax.axis_index("dp"), 2)]

    pieces, layouts = [], ([], [])
    for half, found in enumerate((mine, other)):
        for name in names + [name + "_twin" for name in twins]:
            array, first = found[name]
            place_in = [index for index, piece in enumerate(pieces) if piece is array]
            if not place_in:
                place_in = [len(pieces)]
                pieces.append(array)
            layouts[half].append((place_in[0], first * shard))
    return pieces, layouts, order_of


def gather_weights(space_rows, time_rows, size):
    if size == 16 and lax.axis_size("dp") % 2 == 0:
        return gather_ring(space_rows, time_rows, size)
    shard, features = space_rows.shape
    gathered = lax.all_gather(jnp.concatenate([space_rows, time_rows], axis=0), "ctx", axis=0)
    gathered = gathered.reshape(size, 2, shard, features)
    halves = [gathered[:, half].reshape(size * shard, features) for half in range(2)]
    return halves, ([(0, 0)], [(1, 0)]), lambda: [0, 0]


def shards(
    tokens,
    cotangent,
    clip_frames,
    clip_offsets,
    clip_heights,
    clip_widths,
    spatial_gain,
    spatial_qkv,
    spatial_out,
    temporal_gain,
    temporal_qkv,
    temporal_out,
):
    size = lax.axis_size("ctx")
    everyone = lax.axis_size("dp") * size
    count, features = tokens.shape[1], tokens.shape[2]
    assert count == FRAME and FRAME % size == 0
    near = size // 2
    slots = FRAME // near
    rows = Rows(spatial_qkv.shape[0], spatial_out.shape[0], size)
    pieces, layouts, order_of = gather_weights(
        jnp.concatenate([spatial_qkv, spatial_out], axis=0),
        jnp.concatenate([temporal_qkv, temporal_out], axis=0),
        size,
    )
    tokens_local = tokens[0]
    cotangent_local = cotangent[0]
    clips = (clip_frames, clip_offsets, clip_heights, clip_widths)
    wide = pltpu.VMEM((rows.total, FRAME), F32)

    blocks = len(layouts[0])
    sems = pltpu.SemaphoreType.DMA((2, blocks))
    weight_shape = jax.ShapeDtypeStruct((blocks, rows.total // blocks, features), BF16)
    groups = [list(range(first, first + near)) for first in range(0, size, near)]

    def exchange(sent):
        arrived = lax.all_to_all(
            sent.reshape(near, slots, rows.total),
            "ctx",
            split_axis=0,
            concat_axis=0,
            axis_index_groups=groups,
            tiled=True,
        )
        return arrived.reshape(FRAME, rows.total)

    token_scratch = pltpu.VMEM((FRAME, features), BF16)
    hidden, saved, shares, sent, space_weights, time_weights = call(
        functools.partial(front, rows, layouts, order_of),
        (
            jax.ShapeDtypeStruct((FRAME, features), BF16),
            jax.ShapeDtypeStruct((rows.total, FRAME), BF16),
            jax.ShapeDtypeStruct((HEADS, FRAME, FRAME), BF16),
            jax.ShapeDtypeStruct((FRAME, rows.total), BF16),
            weight_shape,
            weight_shape,
        ),
        [wide, wide, token_scratch, token_scratch, sems, pltpu.SemaphoreType.DMA((2,))],
        clips,
        (spatial_gain, temporal_gain),
        (*pieces, tokens_local, cotangent_local),
    )
    arrived = exchange(sent)
    sent = call(
        functools.partial(time_core, rows, near, slots),
        jax.ShapeDtypeStruct((FRAME, rows.total), BF16),
        [wide, wide],
        clips,
        (arrived,),
    )
    arrived = exchange(sent)
    result, grad_tokens, gains = call(
        functools.partial(finish, rows),
        (
            jax.ShapeDtypeStruct((FRAME, features), BF16),
            jax.ShapeDtypeStruct((FRAME, features), BF16),
            jax.ShapeDtypeStruct((everyone, 2, features), BF16),
        ),
        [wide, wide],
        clips,
        (
            arrived,
            time_weights,
            hidden,
            temporal_gain,
            cotangent_local,
            space_weights,
            saved,
            shares,
            tokens_local,
            spatial_gain,
        ),
    )
    gains = lax.all_to_all(gains, ("dp", "ctx"), split_axis=0, concat_axis=0, tiled=True)
    gain_grads = jnp.sum(gains.astype(F32), axis=0) * (1.0 / math.sqrt(everyone * FRAME))
    return result[None], grad_tokens[None], gain_grads


def solution(mesh):
    return jax.shard_map(
        shards,
        mesh=mesh,
        in_specs=(
            P("dp", "ctx", None),
            P("dp", "ctx", None),
            P("dp", None),
            P("dp", None),
            P("dp", None),
            P("dp", None),
            P(),
            P("ctx", None),
            P("ctx", None),
            P(),
            P("ctx", None),
            P("ctx", None),
        ),
        out_specs=(P("dp", "ctx", None), P("dp", "ctx", None), P()),
        check_vma=False,
    )
```

```python
import functools
import math

import jax
import jax.numpy as jnp
from jax import lax
from jax.experimental import pallas as pl
from jax.experimental.pallas import tpu as pltpu
from jax.sharding import PartitionSpec as P

HEADS = 8
FRAME = 128
EPSILON = 1e-06
ROPE_BASE = 10000.0
F32 = jnp.float32
BF16 = jnp.bfloat16
VMEM_LIMIT = 12 * 1024 * 1024


def nn(a, b):
    return lax.dot_general(a, b, (((1,), (0,)), ((), ())), preferred_element_type=F32)


def nt(a, b):
    return lax.dot_general(a, b, (((1,), (1,)), ((), ())), preferred_element_type=F32)


def tn(a, b):
    return lax.dot_general(a, b, (((0,), (0,)), ((), ())), preferred_element_type=F32)


class Rows:
    def __init__(self, qkv_rows, out_rows, size):
        self.qkv, self.out = qkv_rows, out_rows
        self.shard = qkv_rows + out_rows
        self.total = self.shard * size
        self.inner = out_rows * size
        self.head = self.inner // HEADS
        cut = self.shard % 16 == 0
        self.qkv_cut = -(-qkv_rows // 16) * 16 if cut else self.shard
        self.out_cut = qkv_rows // 16 * 16 if cut else 0
        self.qkv_total = self.qkv_cut * size
        self.out_total = (self.shard - self.out_cut) * size

    def spans(self, first, count, per_shard, stride, shift):
        found = []
        row = first
        while row < first + count:
            block, inside = divmod(row, per_shard)
            length = min(per_shard - inside, first + count - row)
            place = block * stride + shift + inside
            if found and found[-1][0] + found[-1][1] == place:
                found[-1] = (found[-1][0], found[-1][1] + length)
            else:
                found.append((place, length))
            row += length
        return found

    def qkv_spans(self, which, head, stride):
        return self.spans(which * self.inner + head * self.head, self.head, self.qkv, stride, 0)

    def out_spans(self, head, cut):
        stride = self.shard - cut
        return self.spans(head * self.head, self.head, self.out, stride, self.qkv - cut)

    def qkv_weight(self, ref):
        if self.qkv_cut == self.shard:
            return ref[...].reshape(self.total, -1)
        return ref[:, : self.qkv_cut, :].reshape(self.qkv_total, -1)

    def out_weight(self, ref):
        if self.out_cut == 0:
            return ref[...].reshape(self.total, -1)
        return ref[:, self.out_cut :, :].reshape(self.out_total, -1)


def read_rows(ref, spans):
    parts = [ref[place : place + length, :] for place, length in spans]
    return parts[0] if len(parts) == 1 else jnp.concatenate(parts, axis=0)


def write_rows(ref, spans, value):
    done = 0
    for place, length in spans:
        ref[place : place + length, :] = value[done : done + length, :]
        done += length


def inverse_size(values):
    return lax.rsqrt(jnp.mean(values * values, axis=-1, keepdims=True) + EPSILON)


def norm_back(values, inverse, gain, grad):
    scaled = grad * gain
    middle = jnp.mean(scaled * values, axis=-1, keepdims=True)
    grad_values = inverse * scaled - values * (inverse * inverse * inverse * middle)
    grad_gain = jnp.sum(grad * (values * inverse), axis=0, keepdims=True)
    return grad_values, grad_gain


def shares_of(queries, keys, allowed, live, scale):
    scores = tn(keys, queries) * scale
    weights = jnp.where(allowed, jnp.exp(jnp.where(allowed, scores, 0.0)), 0.0)
    totals = jnp.sum(weights, axis=0, keepdims=True) + (1.0 - live)
    return weights * (1.0 / totals)


def attend_back(queries, keys, values, shares, shares_low, grad, scale):
    grad_shares = tn(values, grad)
    middle = jnp.sum(shares * grad_shares, axis=0, keepdims=True)
    grad_scores = (shares * (grad_shares - middle) * scale).astype(BF16)
    return nn(keys, grad_scores), nt(queries, grad_scores), nt(grad, shares_low)


def clips_at(clips, frames):
    counts, times, numbers = (jnp.zeros_like(frames) for _ in range(3))
    for clip in range(clips.shape[1]):
        start = clips[1, clip] // FRAME
        member = (frames >= start) & (frames < start + clips[0, clip])
        counts = jnp.where(member, clips[2, clip] * clips[3, clip], counts)
        times = jnp.where(member, frames - start, times)
        numbers = jnp.where(member, clip + 1, numbers)
    return counts, times, numbers


def ids(shape, dim):
    return lax.broadcasted_iota(jnp.int32, shape, dim)


def space_masks(clips):
    count = clips_at(clips, lax.axis_index("ctx").astype(jnp.int32))[0]
    return ids((FRAME, FRAME), 0) < count, (ids((1, FRAME), 1) < count).astype(F32)


def time_masks(clips, near, slots):
    rank = lax.axis_index("ctx")
    token = ids((1, FRAME), 1)
    slot = lax.rem(token, slots)
    counts, times, numbers = clips_at(clips, (rank // near) * near + token // slots)
    alive = lax.rem(rank, near) * slots + slot < counts
    group = (numbers * FRAME + slot).astype(F32)
    keys = jnp.where(alive, group, -1.0)
    allowed = jnp.broadcast_to(keys, (FRAME, FRAME)).T == group
    return allowed, alive.astype(F32), times.astype(F32)


def turn_tables(times, half):
    pair = ids((2 * half, FRAME), 0)
    lower = pair < half
    frequency = jnp.exp(jnp.where(lower, pair, pair - half).astype(F32) * (-math.log(ROPE_BASE) / half))
    angles = frequency * times
    sine = jnp.sin(angles)
    return jnp.cos(angles), jnp.where(lower, -sine, sine)


def out_columns(rows):
    return lax.rem(ids((1, rows.total), 1), rows.shard) >= rows.qkv


def weight_copies(layout, order, pieces, target, sems, which):
    count = target.shape[1]
    return [
        pltpu.make_async_copy(
            pieces[piece].at[pl.ds(first, count)], target.at[order[index]], sems.at[which, index]
        )
        for index, (piece, first) in enumerate(layout)
    ]


def start_weights(layouts, order, pieces, space, time, sems):
    def start(first, second):
        for copy in weight_copies(first, order, pieces, space, sems, 0):
            copy.start()
        for copy in weight_copies(second, order, pieces, time, sems, 1):
            copy.start()

    plane = order[len(layouts[0])]

    @pl.when(plane == 0)
    def _():
        start(layouts[0], layouts[1])

    @pl.when(plane != 0)
    def _():
        start(layouts[1], layouts[0])


def wait_weights(layouts, order, pieces, target, sems, which):
    for copy in weight_copies(layouts[0], order, pieces, target, sems, which):
        copy.wait()


def front(rows, layouts, order_of, clips, tokens, gains, *refs):
    pieces, refs = refs[:-9], refs[-9:]
    hidden, saved, shares_out, sent, space, time, project, mixed, sems = refs
    order = order_of()
    start_weights(layouts, order, pieces, space, time, sems)
    allowed, live = space_masks(clips)
    values = tokens[0].astype(F32)
    normed = (values * inverse_size(values) * gains[:1]).astype(BF16)
    mixed[...] = jnp.zeros_like(mixed)
    stride = rows.qkv_cut
    length = stride if len(layouts[0]) > 1 else rows.total

    def project_from(layout):
        for index, (piece, first) in enumerate(layout):
            target = pl.ds(pl.multiple_of(order[index] * length, 16), length)
            project[target, :] = nt(pieces[piece][first : first + length, :], normed)

    pl.when(order[-1] == 0)(lambda: project_from(layouts[0]))
    pl.when(order[-1] != 0)(lambda: project_from(layouts[1]))
    saved[...] = project[...].astype(BF16)
    scale = rows.head ** (-0.5)
    for head in range(HEADS):
        query, key, value = (
            read_rows(project, rows.qkv_spans(which, head, stride)).astype(BF16) for which in range(3)
        )
        shares = shares_of(query, key, allowed, live, scale).astype(BF16)
        shares_out[head] = shares
        write_rows(mixed, rows.out_spans(head, rows.out_cut), nn(value, shares) * live)
    wait_weights(layouts, order, pieces, space, sems, 0)
    update = tn(mixed[...].astype(BF16), rows.out_weight(space))
    low = (values + update).astype(BF16)
    hidden[...] = low
    values = low.astype(F32)
    normed = (values * inverse_size(values) * gains[1:]).astype(BF16)
    wait_weights(layouts, order, pieces, time, sems, 1)
    both = nt(jnp.concatenate([normed, tokens[1]], axis=0), time[...].reshape(rows.total, -1))
    count = values.shape[0]
    sent[...] = jnp.where(out_columns(rows), both[count:], both[:count]).astype(BF16)


def time_core(rows, near, slots, clips, arrived, sent, project, result):
    allowed, live, times = time_masks(clips, near, slots)
    for first in range(0, rows.total, FRAME):
        project[first : first + FRAME, :] = arrived[:, first : first + FRAME].astype(F32).T
    scale = rows.head ** (-0.5)
    half = rows.head // 2
    cosine, sine = turn_tables(times, half)

    def swapped(vectors):
        return jnp.concatenate([vectors[half:], vectors[:half]], axis=0)

    for head in range(HEADS):
        turned = []
        for which in range(2):
            vectors = read_rows(project, rows.qkv_spans(which, head, rows.shard))
            turned.append((vectors * cosine + swapped(vectors) * sine).astype(BF16))
        query, key = turned
        value = read_rows(project, rows.qkv_spans(2, head, rows.shard)).astype(BF16)
        grad = (read_rows(project, rows.out_spans(head, 0)) * live).astype(BF16)
        shares = shares_of(query, key, allowed, live, scale)
        shares_low = shares.astype(BF16)
        write_rows(result, rows.out_spans(head, 0), nn(value, shares_low) * live)
        grads = attend_back(query, key, value, shares, shares_low, grad, scale)
        for which in range(2):
            turned_grad = grads[which].astype(BF16).astype(F32)
            write_rows(
                result,
                rows.qkv_spans(which, head, rows.shard),
                turned_grad * cosine - swapped(turned_grad) * sine,
            )
        write_rows(result, rows.qkv_spans(2, head, rows.shard), grads[2])
    for first in range(0, rows.total, FRAME):
        sent[:, first : first + FRAME] = result[first : first + FRAME, :].T.astype(BF16)


def finish(
    rows,
    clips,
    arrived,
    tokens,
    gains,
    time,
    space,
    hidden,
    saved,
    shares_in,
    output,
    grad_tokens,
    gain_parts,
    project,
    grad_project,
):
    count = arrived.shape[0]
    live = space_masks(clips)[1]
    received = arrived[...]
    zeros = jnp.zeros_like(received)
    mask = jnp.broadcast_to(out_columns(rows), received.shape)
    left = jnp.concatenate([jnp.where(mask, zeros, received), jnp.where(mask, received, zeros)], axis=0)
    both = nn(left, time[...].reshape(rows.total, -1))
    values = hidden[...].astype(F32)
    output[...] = (values + both[count:]).astype(BF16)
    grad_normed = both[:count].astype(BF16).astype(F32)
    grad_front, grad_time_gain = norm_back(values, inverse_size(values), gains[1:], grad_normed)
    grad_hidden = (tokens[1].astype(F32) + grad_front).astype(BF16)

    project[...] = nt(rows.out_weight(space), grad_hidden)
    grad_project[...] = jnp.zeros_like(grad_project)
    scale = rows.head ** (-0.5)
    for head in range(HEADS):
        spans = [rows.qkv_spans(which, head, rows.qkv_cut) for which in range(3)]
        query, key, value = (read_rows(saved, where).astype(BF16) for where in spans)
        grad = (read_rows(project, rows.out_spans(head, rows.out_cut)) * live).astype(BF16)
        shares_low = shares_in[head]
        grads = attend_back(query, key, value, shares_low.astype(F32), shares_low, grad, scale)
        for where, part in zip(spans, grads):
            write_rows(grad_project, where, part)
    grad_normed = tn(grad_project[...].astype(BF16), rows.qkv_weight(space)).astype(BF16).astype(F32)
    values = tokens[0].astype(F32)
    grad_values, grad_space_gain = norm_back(values, inverse_size(values), gains[:1], grad_normed)
    grad_tokens[...] = (grad_hidden.astype(F32) + grad_values).astype(BF16)
    both_gains = jnp.concatenate([grad_space_gain, grad_time_gain], axis=0).astype(gain_parts.dtype)
    gain_parts[...] = jnp.broadcast_to(both_gains[None], gain_parts.shape)


def call(body, out_shapes, scratch, clips, operands):
    whole = pl.BlockSpec(memory_space=pltpu.VMEM)
    scalars = pl.BlockSpec(memory_space=pltpu.SMEM)
    return pl.pallas_call(
        body,
        out_shape=out_shapes,
        in_specs=[scalars] + [whole] * len(operands),
        out_specs=jax.tree.map(lambda _: whole, out_shapes),
        scratch_shapes=scratch,
        compiler_params=pltpu.CompilerParams(vmem_limit_bytes=VMEM_LIMIT),
    )(clips, *operands)


def gather_ring(space_rows, time_rows, size):
    chips = size // 2
    chain = chips // 2
    shard = space_rows.shape[0]

    def chip_at(place):
        place = place % chips
        return 2 * place if place < chain else 2 * (chips - 1 - place) + 1

    ring_pairs = []
    for place in range(chips):
        ring_pairs.append((2 * chip_at(place), 2 * chip_at(place + 1)))
        ring_pairs.append((2 * chip_at(place) + 1, 2 * chip_at(place - 1) + 1))
    planes = lax.axis_size("dp")
    plane = lax.rem(lax.axis_index("dp"), 2)

    def ring(rows):
        return lax.ppermute(rows, "ctx", ring_pairs)

    def across(rows):
        return lax.ppermute(rows, "dp", [(index, index ^ 1) for index in range(planes)])

    def twin(rows):
        return lax.ppermute(rows, "ctx", [(index, index ^ 1) for index in range(size)])

    def after(rows, *events):
        return lax.optimization_barrier((rows, *events))[0]

    own = jnp.where(plane == 0, space_rows, time_rows)
    own_other = jnp.where(plane == 0, time_rows, space_rows)
    t0 = twin(own)
    o1 = ring(after(own, t0))
    t1 = ring(t0)
    o2 = ring(o1)
    t2 = ring(t1)
    x_o1 = across(o1)
    x_t1 = across(after(t1, o2, x_o1))
    x_t2 = ring(x_t1)
    o1_twin = twin(o1)
    o2_twin = twin(o2)
    t1_twin = twin(t1)
    t2_twin = twin(t2)
    x_o1_twin = twin(x_o1)
    x_t1_twin = twin(x_t1)
    x_t2_twin = twin(x_t2)
    t0_other = twin(after(own_other, o2))
    o3 = ring(after(o2, x_o1))
    o4 = ring(after(o3, x_o1))
    t3 = ring(after(t2, o1_twin, x_o1))
    x_o3 = across(o3)
    x_t3 = ring(after(x_t2, t3))
    x_o4 = across(after(o4, x_t2))
    o3_twin = twin(o3)
    o4_twin = twin(o4)
    t3_twin = twin(t3)
    x_o3_twin = twin(x_o3)
    x_o4_twin = twin(x_o4)
    x_t3_twin = twin(x_t3)
    x_o2 = ring(after(x_o1, o4, t2, x_o3))
    x_o2_twin = twin(x_o2)
    mine = {"o0": (own, 0), "t0": (t0, 0)}
    other = {"o0": (own_other, 0), "t0": (t0_other, 0)}
    mine |= {"o1": (o1, 0), "o1_twin": (o1_twin, 0)}
    other |= {"o1": (x_o1, 0), "o1_twin": (x_o1_twin, 0)}
    mine |= {"o2": (o2, 0), "o2_twin": (o2_twin, 0)}
    other |= {"o2": (x_o2, 0), "o2_twin": (x_o2_twin, 0)}
    mine |= {"o3": (o3, 0), "o3_twin": (o3_twin, 0)}
    other |= {"o3": (x_o3, 0), "o3_twin": (x_o3_twin, 0)}
    mine |= {"o4": (o4, 0), "o4_twin": (o4_twin, 0)}
    other |= {"o4": (x_o4, 0), "o4_twin": (x_o4_twin, 0)}
    mine |= {"t1": (t1, 0), "t1_twin": (t1_twin, 0)}
    other |= {"t1": (x_t1, 0), "t1_twin": (x_t1_twin, 0)}
    mine |= {"t2": (t2, 0), "t2_twin": (t2_twin, 0)}
    other |= {"t2": (x_t2, 0), "t2_twin": (x_t2_twin, 0)}
    mine |= {"t3": (t3, 0), "t3_twin": (t3_twin, 0)}
    other |= {"t3": (x_t3, 0), "t3_twin": (x_t3_twin, 0)}
    names = ["o0", "t0", "o1", "o2", "o3", "o4", "t1", "t2", "t3"]
    twins = names[2:]

    def order_of():
        rank = lax.axis_index("ctx")
        chip, core = rank // 2, lax.rem(rank, 2)
        column, level = lax.rem(chip, 2), chip // 2
        place = jnp.where(column == 0, level, chips - 1 - level)

        def came(carrier, name):
            steps, shard_core = int(name[1]), carrier if name[0] == "o" else 1 - carrier
            at = lax.rem(place + steps * (2 * carrier - 1) + chips, chips)
            return 2 * jnp.where(at < chain, 2 * at, 2 * (chips - 1 - at) + 1) + shard_core

        order = [came(core, name) for name in names] + [came(1 - core, name) for name in twins]
        return order + [lax.rem(lax.axis_index("dp"), 2)]

    pieces, layouts = [], ([], [])
    for half, found in enumerate((mine, other)):
        for name in names + [name + "_twin" for name in twins]:
            array, first = found[name]
            place_in = [index for index, piece in enumerate(pieces) if piece is array]
            if not place_in:
                place_in = [len(pieces)]
                pieces.append(array)
            layouts[half].append((place_in[0], first * shard))
    return pieces, layouts, order_of


def gather_weights(space_rows, time_rows, size):
    if size == 16 and lax.axis_size("dp") % 2 == 0:
        return gather_ring(space_rows, time_rows, size)
    shard, features = space_rows.shape
    gathered = lax.all_gather(jnp.concatenate([space_rows, time_rows], axis=0), "ctx", axis=0)
    gathered = gathered.reshape(size, 2, shard, features)
    halves = [gathered[:, half].reshape(size * shard, features) for half in range(2)]
    return halves, ([(0, 0)], [(1, 0)]), lambda: [0, 0]


def shards(
    tokens,
    cotangent,
    clip_frames,
    clip_offsets,
    clip_heights,
    clip_widths,
    spatial_gain,
    spatial_qkv,
    spatial_out,
    temporal_gain,
    temporal_qkv,
    temporal_out,
):
    size = lax.axis_size("ctx")
    everyone = lax.axis_size("dp") * size
    count, features = tokens.shape[1], tokens.shape[2]
    assert count == FRAME and FRAME % size == 0
    near = size // 2
    slots = FRAME // near
    rows = Rows(spatial_qkv.shape[0], spatial_out.shape[0], size)
    pieces, layouts, order_of = gather_weights(
        jnp.concatenate([spatial_qkv, spatial_out], axis=0),
        jnp.concatenate([temporal_qkv, temporal_out], axis=0),
        size,
    )
    both_tokens = jnp.concatenate([tokens, cotangent], axis=0)
    both_gains = jnp.stack([spatial_gain, temporal_gain])
    clips = jnp.concatenate([clip_frames, clip_offsets, clip_heights, clip_widths], axis=0)
    wide = pltpu.VMEM((rows.total, FRAME), F32)
    qkv_wide = pltpu.VMEM((rows.qkv_total, FRAME), F32)
    out_wide = pltpu.VMEM((rows.out_total, FRAME), F32)
    blocks = len(layouts[0])
    sems = pltpu.SemaphoreType.DMA((2, blocks))
    weight_shape = jax.ShapeDtypeStruct((blocks, rows.total // blocks, features), BF16)
    groups = [list(range(first, first + near)) for first in range(0, size, near)]

    def exchange(sent):
        arrived = lax.all_to_all(
            sent.reshape(near, slots, rows.total),
            "ctx",
            split_axis=0,
            concat_axis=0,
            axis_index_groups=groups,
            tiled=True,
        )
        return arrived.reshape(FRAME, rows.total)

    hidden, saved, shares, sent, space_weights, time_weights = call(
        functools.partial(front, rows, layouts, order_of),
        (
            jax.ShapeDtypeStruct((FRAME, features), BF16),
            jax.ShapeDtypeStruct((rows.qkv_total, FRAME), BF16),
            jax.ShapeDtypeStruct((HEADS, FRAME, FRAME), BF16),
            jax.ShapeDtypeStruct((FRAME, rows.total), BF16),
            weight_shape,
            weight_shape,
        ),
        [qkv_wide, out_wide, sems],
        clips,
        (both_tokens, both_gains, *pieces),
    )
    arrived = exchange(sent)
    sent = call(
        functools.partial(time_core, rows, near, slots),
        jax.ShapeDtypeStruct((FRAME, rows.total), BF16),
        [wide, wide],
        clips,
        (arrived,),
    )
    arrived = exchange(sent)
    result, grad_tokens, gains = call(
        functools.partial(finish, rows),
        (
            jax.ShapeDtypeStruct((FRAME, features), BF16),
            jax.ShapeDtypeStruct((FRAME, features), BF16),
            jax.ShapeDtypeStruct((everyone, 2, features), BF16),
        ),
        [out_wide, qkv_wide],
        clips,
        (arrived, both_tokens, both_gains, time_weights, space_weights, hidden, saved, shares),
    )
    gains = lax.all_to_all(gains, ("dp", "ctx"), split_axis=0, concat_axis=0, tiled=True)
    gain_grads = jnp.sum(gains.astype(F32), axis=0) * (1.0 / math.sqrt(everyone * FRAME))
    return result[None], grad_tokens[None], gain_grads


def solution(mesh):
    return jax.shard_map(
        shards,
        mesh=mesh,
        in_specs=(
            P("dp", "ctx", None),
            P("dp", "ctx", None),
            P("dp", None),
            P("dp", None),
            P("dp", None),
            P("dp", None),
            P(),
            P("ctx", None),
            P("ctx", None),
            P(),
            P("ctx", None),
            P("ctx", None),
        ),
        out_specs=(P("dp", "ctx", None), P("dp", "ctx", None), P()),
        check_vma=False,
    )
```

```python
import functools
import math

import jax
import jax.numpy as jnp
from jax import lax
from jax.experimental import pallas as pl
from jax.experimental.pallas import tpu as pltpu
from jax.sharding import PartitionSpec as P

HEADS = 8
FRAME = 128
EPSILON = 1e-06
ROPE_BASE = 10000.0
F32 = jnp.float32
BF16 = jnp.bfloat16
VMEM_LIMIT = 12 * 1024 * 1024


def nn(a, b):
    return lax.dot_general(a, b, (((1,), (0,)), ((), ())), preferred_element_type=F32)


def nt(a, b):
    return lax.dot_general(a, b, (((1,), (1,)), ((), ())), preferred_element_type=F32)


def tn(a, b):
    return lax.dot_general(a, b, (((0,), (0,)), ((), ())), preferred_element_type=F32)


class Rows:
    def __init__(self, qkv_rows, out_rows, size):
        self.qkv, self.out = qkv_rows, out_rows
        self.shard = qkv_rows + out_rows
        self.total = self.shard * size
        self.inner = out_rows * size
        self.head = self.inner // HEADS
        cut = self.shard % 16 == 0
        self.qkv_cut = -(-qkv_rows // 16) * 16 if cut else self.shard
        self.out_cut = qkv_rows // 16 * 16 if cut else 0
        self.qkv_total = self.qkv_cut * size
        self.out_total = (self.shard - self.out_cut) * size

    def spans(self, first, count, per_shard, stride, shift):
        found = []
        row = first
        while row < first + count:
            block, inside = divmod(row, per_shard)
            length = min(per_shard - inside, first + count - row)
            place = block * stride + shift + inside
            if found and found[-1][0] + found[-1][1] == place:
                found[-1] = (found[-1][0], found[-1][1] + length)
            else:
                found.append((place, length))
            row += length
        return found

    def qkv_spans(self, which, head, stride):
        return self.spans(which * self.inner + head * self.head, self.head, self.qkv, stride, 0)

    def out_spans(self, head, cut):
        stride = self.shard - cut
        return self.spans(head * self.head, self.head, self.out, stride, self.qkv - cut)

    def qkv_weight(self, ref):
        if self.qkv_cut == self.shard:
            return ref[...].reshape(self.total, -1)
        return ref[:, : self.qkv_cut, :].reshape(self.qkv_total, -1)

    def out_weight(self, ref):
        if self.out_cut == 0:
            return ref[...].reshape(self.total, -1)
        return ref[:, self.out_cut :, :].reshape(self.out_total, -1)


def read_rows(ref, spans):
    parts = [ref[place : place + length, :] for place, length in spans]
    return parts[0] if len(parts) == 1 else jnp.concatenate(parts, axis=0)


def write_rows(ref, spans, value):
    done = 0
    for place, length in spans:
        ref[place : place + length, :] = value[done : done + length, :]
        done += length


def inverse_size(values):
    return lax.rsqrt(jnp.mean(values * values, axis=-1, keepdims=True) + EPSILON)


def norm_back(values, inverse, gain, grad):
    scaled = grad * gain
    middle = jnp.mean(scaled * values, axis=-1, keepdims=True)
    grad_values = inverse * scaled - values * (inverse * inverse * inverse * middle)
    grad_gain = jnp.sum(grad * (values * inverse), axis=0, keepdims=True)
    return grad_values, grad_gain


def shares_of(queries, keys, allowed, live, scale):
    scores = tn(keys, queries) * scale
    weights = jnp.where(allowed, jnp.exp(jnp.where(allowed, scores, 0.0)), 0.0)
    totals = jnp.sum(weights, axis=0, keepdims=True) + (1.0 - live)
    return weights * (1.0 / totals)


def attend_back(queries, keys, values, shares, shares_low, grad, scale):
    grad_shares = tn(values, grad)
    middle = jnp.sum(shares * grad_shares, axis=0, keepdims=True)
    grad_scores = (shares * (grad_shares - middle) * scale).astype(BF16)
    return nn(keys, grad_scores), nt(queries, grad_scores), nt(grad, shares_low)


def clips_at(clips, frames):
    counts, times, numbers = (jnp.zeros_like(frames) for _ in range(3))
    for clip in range(clips.shape[1]):
        start = clips[1, clip] // FRAME
        member = (frames >= start) & (frames < start + clips[0, clip])
        counts = jnp.where(member, clips[2, clip] * clips[3, clip], counts)
        times = jnp.where(member, frames - start, times)
        numbers = jnp.where(member, clip + 1, numbers)
    return counts, times, numbers


def ids(shape, dim):
    return lax.broadcasted_iota(jnp.int32, shape, dim)


def space_masks(clips):
    count = clips_at(clips, lax.axis_index("ctx").astype(jnp.int32))[0]
    return ids((FRAME, FRAME), 0) < count, (ids((1, FRAME), 1) < count).astype(F32)


def time_masks(clips, near, slots):
    rank = lax.axis_index("ctx")
    token = ids((1, FRAME), 1)
    slot = lax.rem(token, slots)
    counts, times, numbers = clips_at(clips, (rank // near) * near + token // slots)
    alive = lax.rem(rank, near) * slots + slot < counts
    group = (numbers * FRAME + slot).astype(F32)
    keys = jnp.where(alive, group, -1.0)
    allowed = jnp.broadcast_to(keys, (FRAME, FRAME)).T == group
    return allowed, alive.astype(F32), times.astype(F32)


def turn_tables(times, half):
    pair = ids((2 * half, FRAME), 0)
    lower = pair < half
    frequency = jnp.exp(jnp.where(lower, pair, pair - half).astype(F32) * (-math.log(ROPE_BASE) / half))
    angles = frequency * times
    sine = jnp.sin(angles)
    return jnp.cos(angles), jnp.where(lower, -sine, sine)


def out_columns(rows):
    return lax.rem(ids((1, rows.total), 1), rows.shard) >= rows.qkv


def weight_copies(layout, order, pieces, target, sems, which):
    count = target.shape[1]
    return [
        pltpu.make_async_copy(
            pieces[piece].at[pl.ds(first, count)], target.at[order[index]], sems.at[which, index]
        )
        for index, (piece, first) in enumerate(layout)
    ]


def gate(*arrays):
    anywhere = pl.BlockSpec(memory_space=pl.ANY)
    count = len(arrays)
    return pl.pallas_call(
        lambda *refs: None,
        out_shape=tuple(jax.ShapeDtypeStruct(array.shape, array.dtype) for array in arrays),
        in_specs=[anywhere] * count,
        out_specs=(anywhere,) * count,
        input_output_aliases={index: index for index in range(count)},
    )(*arrays)


def start_weights(layouts, order, pieces, space, time, sems):
    def start(first, second):
        for copy in weight_copies(first, order, pieces, space, sems, 0):
            copy.start()
        for copy in weight_copies(second, order, pieces, time, sems, 1):
            copy.start()

    plane = order[len(layouts[0])]

    @pl.when(plane == 0)
    def _():
        start(layouts[0], layouts[1])

    @pl.when(plane != 0)
    def _():
        start(layouts[1], layouts[0])


def wait_weights(layouts, order, pieces, target, sems, which):
    for copy in weight_copies(layouts[0], order, pieces, target, sems, which):
        copy.wait()


def front(rows, layouts, order_of, clips, tokens, gains, *refs):
    pieces, refs = refs[:-9], refs[-9:]
    hidden, saved, shares_out, sent, space, time, project, mixed, sems = refs
    order = order_of()
    start_weights(layouts, order, pieces, space, time, sems)
    allowed, live = space_masks(clips)
    values = tokens[0].astype(F32)
    normed = (values * inverse_size(values) * gains[:1]).astype(BF16)
    mixed[...] = jnp.zeros_like(mixed)
    stride = rows.qkv_cut
    length = stride if len(layouts[0]) > 1 else rows.total

    def project_from(layout):
        for index, (piece, first) in enumerate(layout):
            target = pl.ds(pl.multiple_of(order[index] * length, 16), length)
            project[target, :] = nt(pieces[piece][first : first + length, :], normed)

    pl.when(order[-1] == 0)(lambda: project_from(layouts[0]))
    pl.when(order[-1] != 0)(lambda: project_from(layouts[1]))
    saved[...] = project[...].astype(BF16)
    scale = rows.head ** (-0.5)
    for head in range(HEADS):
        query, key, value = (
            read_rows(project, rows.qkv_spans(which, head, stride)).astype(BF16) for which in range(3)
        )
        shares = shares_of(query, key, allowed, live, scale).astype(BF16)
        shares_out[head] = shares
        write_rows(mixed, rows.out_spans(head, rows.out_cut), nn(value, shares) * live)
    wait_weights(layouts, order, pieces, space, sems, 0)
    update = tn(mixed[...].astype(BF16), rows.out_weight(space))
    low = (values + update).astype(BF16)
    hidden[...] = low
    values = low.astype(F32)
    normed = (values * inverse_size(values) * gains[1:]).astype(BF16)
    wait_weights(layouts, order, pieces, time, sems, 1)
    both = nt(jnp.concatenate([normed, tokens[1]], axis=0), time[...].reshape(rows.total, -1))
    count = values.shape[0]
    sent[...] = jnp.where(out_columns(rows), both[count:], both[:count]).astype(BF16)


def time_core(rows, near, slots, clips, arrived, sent, project, result):
    allowed, live, times = time_masks(clips, near, slots)
    for first in range(0, rows.total, FRAME):
        project[first : first + FRAME, :] = arrived[:, first : first + FRAME].astype(F32).T
    scale = rows.head ** (-0.5)
    half = rows.head // 2
    cosine, sine = turn_tables(times, half)

    def swapped(vectors):
        return jnp.concatenate([vectors[half:], vectors[:half]], axis=0)

    for head in range(HEADS):
        turned = []
        for which in range(2):
            vectors = read_rows(project, rows.qkv_spans(which, head, rows.shard))
            turned.append((vectors * cosine + swapped(vectors) * sine).astype(BF16))
        query, key = turned
        value = read_rows(project, rows.qkv_spans(2, head, rows.shard)).astype(BF16)
        grad = (read_rows(project, rows.out_spans(head, 0)) * live).astype(BF16)
        shares = shares_of(query, key, allowed, live, scale)
        shares_low = shares.astype(BF16)
        write_rows(result, rows.out_spans(head, 0), nn(value, shares_low) * live)
        grads = attend_back(query, key, value, shares, shares_low, grad, scale)
        for which in range(2):
            turned_grad = grads[which].astype(BF16).astype(F32)
            write_rows(
                result,
                rows.qkv_spans(which, head, rows.shard),
                turned_grad * cosine - swapped(turned_grad) * sine,
            )
        write_rows(result, rows.qkv_spans(2, head, rows.shard), grads[2])
    for first in range(0, rows.total, FRAME):
        sent[:, first : first + FRAME] = result[first : first + FRAME, :].T.astype(BF16)


def finish(
    rows,
    clips,
    arrived,
    tokens,
    gains,
    time,
    space,
    hidden,
    saved,
    shares_in,
    output,
    grad_tokens,
    gain_parts,
    project,
    grad_project,
):
    count = arrived.shape[0]
    live = space_masks(clips)[1]
    received = arrived[...]
    zeros = jnp.zeros_like(received)
    mask = jnp.broadcast_to(out_columns(rows), received.shape)
    left = jnp.concatenate([jnp.where(mask, zeros, received), jnp.where(mask, received, zeros)], axis=0)
    both = nn(left, time[...].reshape(rows.total, -1))
    values = hidden[...].astype(F32)
    output[...] = (values + both[count:]).astype(BF16)
    grad_normed = both[:count].astype(BF16).astype(F32)
    grad_front, grad_time_gain = norm_back(values, inverse_size(values), gains[1:], grad_normed)
    grad_hidden = (tokens[1].astype(F32) + grad_front).astype(BF16)

    project[...] = nt(rows.out_weight(space), grad_hidden)
    grad_project[...] = jnp.zeros_like(grad_project)
    scale = rows.head ** (-0.5)
    for head in range(HEADS):
        spans = [rows.qkv_spans(which, head, rows.qkv_cut) for which in range(3)]
        query, key, value = (read_rows(saved, where).astype(BF16) for where in spans)
        grad = (read_rows(project, rows.out_spans(head, rows.out_cut)) * live).astype(BF16)
        shares_low = shares_in[head]
        grads = attend_back(query, key, value, shares_low.astype(F32), shares_low, grad, scale)
        for where, part in zip(spans, grads):
            write_rows(grad_project, where, part)
    grad_normed = tn(grad_project[...].astype(BF16), rows.qkv_weight(space)).astype(BF16).astype(F32)
    values = tokens[0].astype(F32)
    grad_values, grad_space_gain = norm_back(values, inverse_size(values), gains[:1], grad_normed)
    grad_tokens[...] = (grad_hidden.astype(F32) + grad_values).astype(BF16)
    both_gains = jnp.concatenate([grad_space_gain, grad_time_gain], axis=0).astype(gain_parts.dtype)
    gain_parts[...] = jnp.broadcast_to(both_gains[None], gain_parts.shape)


def call(body, out_shapes, scratch, clips, operands):
    whole = pl.BlockSpec(memory_space=pltpu.VMEM)
    scalars = pl.BlockSpec(memory_space=pltpu.SMEM)
    return pl.pallas_call(
        body,
        out_shape=out_shapes,
        in_specs=[scalars] + [whole] * len(operands),
        out_specs=jax.tree.map(lambda _: whole, out_shapes),
        scratch_shapes=scratch,
        compiler_params=pltpu.CompilerParams(vmem_limit_bytes=VMEM_LIMIT),
    )(clips, *operands)


def gather_ring(space_rows, time_rows, size, others):
    chips = size // 2
    chain = chips // 2
    shard = space_rows.shape[0]

    def chip_at(place):
        place = place % chips
        return 2 * place if place < chain else 2 * (chips - 1 - place) + 1

    ring_pairs = []
    for place in range(chips):
        ring_pairs.append((2 * chip_at(place), 2 * chip_at(place + 1)))
        ring_pairs.append((2 * chip_at(place) + 1, 2 * chip_at(place - 1) + 1))
    planes = lax.axis_size("dp")
    plane = lax.rem(lax.axis_index("dp"), 2)

    def ring(rows):
        return lax.ppermute(rows, "ctx", ring_pairs)

    def across(rows):
        return lax.ppermute(rows, "dp", [(index, index ^ 1) for index in range(planes)])

    def twin(rows):
        return lax.ppermute(rows, "ctx", [(index, index ^ 1) for index in range(size)])

    own = jnp.where(plane == 0, space_rows, time_rows)
    own_other = jnp.where(plane == 0, time_rows, space_rows)
    t0 = twin(own)
    t1 = ring(t0)
    o1 = ring(own)
    o2 = ring(o1)
    t0_other = twin(own_other)
    x_o1 = across(o1)
    t2 = ring(t1)
    o3 = ring(o2)
    o1_twin = twin(o1)
    t1_twin = twin(t1)
    t2, t1_twin, t0_other, o1_twin, *others = gate(t2, t1_twin, t0_other, o1_twin, *others)
    x_t1 = across(t1)
    o2_twin = twin(o2)
    t3 = ring(t2)
    t2_twin = twin(t2)
    x_o1_twin = twin(x_o1)
    o3_twin = twin(o3)
    x_o3 = across(o3)
    x_t1_twin = twin(x_t1)
    x_o2 = ring(x_o1)
    o4 = ring(o3)
    t3_twin = twin(t3)
    x_o4 = across(o4)
    x_t2 = ring(x_t1)
    o4_twin = twin(o4)
    x_t3 = ring(x_t2)
    x_o2_twin = twin(x_o2)
    x_o3_twin = twin(x_o3)
    x_t2_twin = twin(x_t2)
    x_o4_twin = twin(x_o4)
    x_t3_twin = twin(x_t3)
    mine = {"o0": (own, 0), "t0": (t0, 0)}
    other = {"o0": (own_other, 0), "t0": (t0_other, 0)}
    mine |= {"o1": (o1, 0), "o1_twin": (o1_twin, 0)}
    other |= {"o1": (x_o1, 0), "o1_twin": (x_o1_twin, 0)}
    mine |= {"t1": (t1, 0), "t1_twin": (t1_twin, 0)}
    other |= {"t1": (x_t1, 0), "t1_twin": (x_t1_twin, 0)}
    mine |= {"o2": (o2, 0), "o2_twin": (o2_twin, 0)}
    other |= {"o2": (x_o2, 0), "o2_twin": (x_o2_twin, 0)}
    mine |= {"t2": (t2, 0), "t2_twin": (t2_twin, 0)}
    other |= {"t2": (x_t2, 0), "t2_twin": (x_t2_twin, 0)}
    mine |= {"o3": (o3, 0), "o3_twin": (o3_twin, 0)}
    other |= {"o3": (x_o3, 0), "o3_twin": (x_o3_twin, 0)}
    mine |= {"t3": (t3, 0), "t3_twin": (t3_twin, 0)}
    other |= {"t3": (x_t3, 0), "t3_twin": (x_t3_twin, 0)}
    mine |= {"o4": (o4, 0), "o4_twin": (o4_twin, 0)}
    other |= {"o4": (x_o4, 0), "o4_twin": (x_o4_twin, 0)}
    names = ["o0", "t0", "o1", "o2", "o3", "o4", "t1", "t2", "t3"]
    twins = names[2:]

    def order_of():
        rank = lax.axis_index("ctx")
        chip, core = rank // 2, lax.rem(rank, 2)
        column, level = lax.rem(chip, 2), chip // 2
        place = jnp.where(column == 0, level, chips - 1 - level)

        def came(carrier, name):
            steps, shard_core = int(name[1]), carrier if name[0] == "o" else 1 - carrier
            at = lax.rem(place + steps * (2 * carrier - 1) + chips, chips)
            return 2 * jnp.where(at < chain, 2 * at, 2 * (chips - 1 - at) + 1) + shard_core

        order = [came(core, name) for name in names] + [came(1 - core, name) for name in twins]
        return order + [lax.rem(lax.axis_index("dp"), 2)]

    pieces, layouts = [], ([], [])
    for half, found in enumerate((mine, other)):
        for name in names + [name + "_twin" for name in twins]:
            array, first = found[name]
            place_in = [index for index, piece in enumerate(pieces) if piece is array]
            if not place_in:
                place_in = [len(pieces)]
                pieces.append(array)
            layouts[half].append((place_in[0], first * shard))
    return pieces, layouts, order_of, others


def gather_weights(space_rows, time_rows, size, others):
    if size == 16 and lax.axis_size("dp") % 2 == 0:
        return gather_ring(space_rows, time_rows, size, others)
    shard, features = space_rows.shape
    gathered = lax.all_gather(jnp.concatenate([space_rows, time_rows], axis=0), "ctx", axis=0)
    gathered = gathered.reshape(size, 2, shard, features)
    halves = [gathered[:, half].reshape(size * shard, features) for half in range(2)]
    return halves, ([(0, 0)], [(1, 0)]), lambda: [0, 0], others


def shards(
    tokens,
    cotangent,
    clip_frames,
    clip_offsets,
    clip_heights,
    clip_widths,
    spatial_gain,
    spatial_qkv,
    spatial_out,
    temporal_gain,
    temporal_qkv,
    temporal_out,
):
    size = lax.axis_size("ctx")
    everyone = lax.axis_size("dp") * size
    count, features = tokens.shape[1], tokens.shape[2]
    assert count == FRAME and FRAME % size == 0
    near = size // 2
    slots = FRAME // near
    rows = Rows(spatial_qkv.shape[0], spatial_out.shape[0], size)
    both_tokens = jnp.concatenate([tokens, cotangent], axis=0)
    both_gains = jnp.stack([spatial_gain, temporal_gain])
    clips = jnp.concatenate([clip_frames, clip_offsets, clip_heights, clip_widths], axis=0)
    pieces, layouts, order_of, others = gather_weights(
        jnp.concatenate([spatial_qkv, spatial_out], axis=0),
        jnp.concatenate([temporal_qkv, temporal_out], axis=0),
        size,
        (both_tokens, both_gains, clips),
    )
    both_tokens, both_gains, clips = others
    wide = pltpu.VMEM((rows.total, FRAME), F32)
    qkv_wide = pltpu.VMEM((rows.qkv_total, FRAME), F32)
    out_wide = pltpu.VMEM((rows.out_total, FRAME), F32)
    blocks = len(layouts[0])
    sems = pltpu.SemaphoreType.DMA((2, blocks))
    weight_shape = jax.ShapeDtypeStruct((blocks, rows.total // blocks, features), BF16)
    groups = [list(range(first, first + near)) for first in range(0, size, near)]

    def exchange(sent):
        arrived = lax.all_to_all(
            sent.reshape(near, slots, rows.total),
            "ctx",
            split_axis=0,
            concat_axis=0,
            axis_index_groups=groups,
            tiled=True,
        )
        return arrived.reshape(FRAME, rows.total)

    hidden, saved, shares, sent, space_weights, time_weights = call(
        functools.partial(front, rows, layouts, order_of),
        (
            jax.ShapeDtypeStruct((FRAME, features), BF16),
            jax.ShapeDtypeStruct((rows.qkv_total, FRAME), BF16),
            jax.ShapeDtypeStruct((HEADS, FRAME, FRAME), BF16),
            jax.ShapeDtypeStruct((FRAME, rows.total), BF16),
            weight_shape,
            weight_shape,
        ),
        [qkv_wide, out_wide, sems],
        clips,
        (both_tokens, both_gains, *pieces),
    )
    arrived = exchange(sent)
    sent = call(
        functools.partial(time_core, rows, near, slots),
        jax.ShapeDtypeStruct((FRAME, rows.total), BF16),
        [wide, wide],
        clips,
        (arrived,),
    )
    arrived = exchange(sent)
    result, grad_tokens, gains = call(
        functools.partial(finish, rows),
        (
            jax.ShapeDtypeStruct((FRAME, features), BF16),
            jax.ShapeDtypeStruct((FRAME, features), BF16),
            jax.ShapeDtypeStruct((everyone, 2, features), BF16),
        ),
        [out_wide, qkv_wide],
        clips,
        (arrived, both_tokens, both_gains, time_weights, space_weights, hidden, saved, shares),
    )
    gains = lax.all_to_all(gains, ("dp", "ctx"), split_axis=0, concat_axis=0, tiled=True)
    gain_grads = jnp.sum(gains.astype(F32), axis=0) * (1.0 / math.sqrt(everyone * FRAME))
    return result[None], grad_tokens[None], gain_grads


def solution(mesh):
    return jax.shard_map(
        shards,
        mesh=mesh,
        in_specs=(
            P("dp", "ctx", None),
            P("dp", "ctx", None),
            P("dp", None),
            P("dp", None),
            P("dp", None),
            P("dp", None),
            P(),
            P("ctx", None),
            P("ctx", None),
            P(),
            P("ctx", None),
            P("ctx", None),
        ),
        out_specs=(P("dp", "ctx", None), P("dp", "ctx", None), P()),
        check_vma=False,
    )
```

```python
import functools
import math

import jax
import jax.numpy as jnp
from jax import lax
from jax.experimental import pallas as pl
from jax.experimental.pallas import tpu as pltpu
from jax.sharding import PartitionSpec as P

HEADS = 8
FRAME = 128
EPSILON = 1e-06
ROPE_BASE = 10000.0
F32 = jnp.float32
BF16 = jnp.bfloat16
VMEM_LIMIT = 12 * 1024 * 1024


def nn(a, b):
    return lax.dot_general(a, b, (((1,), (0,)), ((), ())), preferred_element_type=F32)


def nt(a, b):
    return lax.dot_general(a, b, (((1,), (1,)), ((), ())), preferred_element_type=F32)


def tn(a, b):
    return lax.dot_general(a, b, (((0,), (0,)), ((), ())), preferred_element_type=F32)


class Rows:
    def __init__(self, qkv_rows, out_rows, size):
        self.qkv, self.out = qkv_rows, out_rows
        self.shard = qkv_rows + out_rows
        self.total = self.shard * size
        self.inner = out_rows * size
        self.head = self.inner // HEADS
        cut = self.shard % 16 == 0
        self.qkv_cut = -(-qkv_rows // 16) * 16 if cut else self.shard
        self.out_cut = qkv_rows // 16 * 16 if cut else 0
        self.qkv_total = self.qkv_cut * size
        self.out_total = (self.shard - self.out_cut) * size

    def spans(self, first, count, per_shard, stride, shift):
        found = []
        row = first
        while row < first + count:
            block, inside = divmod(row, per_shard)
            length = min(per_shard - inside, first + count - row)
            place = block * stride + shift + inside
            if found and found[-1][0] + found[-1][1] == place:
                found[-1] = (found[-1][0], found[-1][1] + length)
            else:
                found.append((place, length))
            row += length
        return found

    def qkv_spans(self, which, head, stride):
        return self.spans(which * self.inner + head * self.head, self.head, self.qkv, stride, 0)

    def out_spans(self, head, cut):
        stride = self.shard - cut
        return self.spans(head * self.head, self.head, self.out, stride, self.qkv - cut)

    def qkv_weight(self, ref):
        if self.qkv_cut == self.shard:
            return ref[...].reshape(self.total, -1)
        return ref[:, : self.qkv_cut, :].reshape(self.qkv_total, -1)

    def out_weight(self, ref):
        if self.out_cut == 0:
            return ref[...].reshape(self.total, -1)
        return ref[:, self.out_cut :, :].reshape(self.out_total, -1)


def read_rows(ref, spans):
    parts = [ref[place : place + length, :] for place, length in spans]
    return parts[0] if len(parts) == 1 else jnp.concatenate(parts, axis=0)


def write_rows(ref, spans, value):
    done = 0
    for place, length in spans:
        ref[place : place + length, :] = value[done : done + length, :]
        done += length


def inverse_size(values):
    return lax.rsqrt(jnp.mean(values * values, axis=-1, keepdims=True) + EPSILON)


def norm_back(values, inverse, gain, grad):
    scaled = grad * gain
    middle = jnp.mean(scaled * values, axis=-1, keepdims=True)
    grad_values = inverse * scaled - values * (inverse * inverse * inverse * middle)
    grad_gain = jnp.sum(grad * (values * inverse), axis=0, keepdims=True)
    return grad_values, grad_gain


def shares_of(queries, keys, allowed, live, scale):
    scores = tn(keys, queries) * scale
    weights = jnp.where(allowed, jnp.exp(jnp.where(allowed, scores, 0.0)), 0.0)
    totals = jnp.sum(weights, axis=0, keepdims=True) + (1.0 - live)
    return weights * (1.0 / totals)


def attend_back(queries, keys, values, shares, shares_low, grad, scale):
    grad_shares = tn(values, grad)
    middle = jnp.sum(shares * grad_shares, axis=0, keepdims=True)
    grad_scores = (shares * (grad_shares - middle) * scale).astype(BF16)
    return nn(keys, grad_scores), nt(queries, grad_scores), nt(grad, shares_low)


def clips_at(clips, frames):
    counts, times, numbers = (jnp.zeros_like(frames) for _ in range(3))
    for clip in range(clips.shape[1]):
        start = clips[1, clip] // FRAME
        member = (frames >= start) & (frames < start + clips[0, clip])
        counts = jnp.where(member, clips[2, clip] * clips[3, clip], counts)
        times = jnp.where(member, frames - start, times)
        numbers = jnp.where(member, clip + 1, numbers)
    return counts, times, numbers


def ids(shape, dim):
    return lax.broadcasted_iota(jnp.int32, shape, dim)


def space_masks(clips):
    count = clips_at(clips, lax.axis_index("ctx").astype(jnp.int32))[0]
    return ids((FRAME, FRAME), 0) < count, (ids((1, FRAME), 1) < count).astype(F32)


def time_masks(clips, near, slots):
    rank = lax.axis_index("ctx")
    token = ids((1, FRAME), 1)
    slot = lax.rem(token, slots)
    counts, times, numbers = clips_at(clips, (rank // near) * near + token // slots)
    alive = lax.rem(rank, near) * slots + slot < counts
    group = (numbers * FRAME + slot).astype(F32)
    keys = jnp.where(alive, group, -1.0)
    allowed = jnp.broadcast_to(keys, (FRAME, FRAME)).T == group
    return allowed, alive.astype(F32), times.astype(F32)


def turn_tables(times, half):
    pair = ids((2 * half, FRAME), 0)
    lower = pair < half
    frequency = jnp.exp(jnp.where(lower, pair, pair - half).astype(F32) * (-math.log(ROPE_BASE) / half))
    angles = frequency * times
    sine = jnp.sin(angles)
    return jnp.cos(angles), jnp.where(lower, -sine, sine)


def out_columns(rows):
    return lax.rem(ids((1, rows.total), 1), rows.shard) >= rows.qkv


def weight_copies(layout, order, pieces, target, sems, which):
    count = target.shape[1]
    return [
        pltpu.make_async_copy(
            pieces[piece].at[pl.ds(first, count)], target.at[order[index]], sems.at[which, index]
        )
        for index, (piece, first) in enumerate(layout)
    ]


def gate(*arrays):
    anywhere = pl.BlockSpec(memory_space=pl.ANY)
    count = len(arrays)
    return pl.pallas_call(
        lambda *refs: None,
        out_shape=tuple(jax.ShapeDtypeStruct(array.shape, array.dtype) for array in arrays),
        in_specs=[anywhere] * count,
        out_specs=(anywhere,) * count,
        input_output_aliases={index: index for index in range(count)},
        compiler_params=pltpu.CompilerParams(vmem_limit_bytes=1024 * 1024),
    )(*arrays)


def start_weights(layouts, order, pieces, space, time, sems):
    def start(first, second):
        for copy in weight_copies(first, order, pieces, space, sems, 0):
            copy.start()
        for copy in weight_copies(second, order, pieces, time, sems, 1):
            copy.start()

    plane = order[len(layouts[0])]

    @pl.when(plane == 0)
    def _():
        start(layouts[0], layouts[1])

    @pl.when(plane != 0)
    def _():
        start(layouts[1], layouts[0])


def wait_weights(layouts, order, pieces, target, sems, which):
    for copy in weight_copies(layouts[0], order, pieces, target, sems, which):
        copy.wait()


def front(rows, layouts, order_of, clips, tokens, gains, *refs):
    pieces, refs = refs[:-9], refs[-9:]
    hidden, saved, shares_out, sent, space, time, project, mixed, sems = refs
    order = order_of()
    start_weights(layouts, order, pieces, space, time, sems)
    allowed, live = space_masks(clips)
    values = tokens[0].astype(F32)
    normed = (values * inverse_size(values) * gains[:1]).astype(BF16)
    mixed[...] = jnp.zeros_like(mixed)
    stride = rows.qkv_cut
    length = stride if len(layouts[0]) > 1 else rows.total

    def project_from(layout):
        for index, (piece, first) in enumerate(layout):
            target = pl.ds(pl.multiple_of(order[index] * length, 16), length)
            project[target, :] = nt(pieces[piece][first : first + length, :], normed)

    pl.when(order[-1] == 0)(lambda: project_from(layouts[0]))
    pl.when(order[-1] != 0)(lambda: project_from(layouts[1]))
    saved[...] = project[...].astype(BF16)
    scale = rows.head ** (-0.5)
    for head in range(HEADS):
        query, key, value = (
            read_rows(project, rows.qkv_spans(which, head, stride)).astype(BF16) for which in range(3)
        )
        shares = shares_of(query, key, allowed, live, scale).astype(BF16)
        shares_out[head] = shares
        write_rows(mixed, rows.out_spans(head, rows.out_cut), nn(value, shares) * live)
    wait_weights(layouts, order, pieces, space, sems, 0)
    update = tn(mixed[...].astype(BF16), rows.out_weight(space))
    low = (values + update).astype(BF16)
    hidden[...] = low
    values = low.astype(F32)
    normed = (values * inverse_size(values) * gains[1:]).astype(BF16)
    wait_weights(layouts, order, pieces, time, sems, 1)
    both = nt(jnp.concatenate([normed, tokens[1]], axis=0), time[...].reshape(rows.total, -1))
    count = values.shape[0]
    sent[...] = jnp.where(out_columns(rows), both[count:], both[:count]).astype(BF16)


def time_core(rows, near, slots, clips, arrived, sent, project, result):
    allowed, live, times = time_masks(clips, near, slots)
    for first in range(0, rows.total, FRAME):
        project[first : first + FRAME, :] = arrived[:, first : first + FRAME].astype(F32).T
    scale = rows.head ** (-0.5)
    half = rows.head // 2
    cosine, sine = turn_tables(times, half)

    def swapped(vectors):
        return jnp.concatenate([vectors[half:], vectors[:half]], axis=0)

    for head in range(HEADS):
        turned = []
        for which in range(2):
            vectors = read_rows(project, rows.qkv_spans(which, head, rows.shard))
            turned.append((vectors * cosine + swapped(vectors) * sine).astype(BF16))
        query, key = turned
        value = read_rows(project, rows.qkv_spans(2, head, rows.shard)).astype(BF16)
        grad = (read_rows(project, rows.out_spans(head, 0)) * live).astype(BF16)
        shares = shares_of(query, key, allowed, live, scale)
        shares_low = shares.astype(BF16)
        write_rows(result, rows.out_spans(head, 0), nn(value, shares_low) * live)
        grads = attend_back(query, key, value, shares, shares_low, grad, scale)
        for which in range(2):
            turned_grad = grads[which].astype(BF16).astype(F32)
            write_rows(
                result,
                rows.qkv_spans(which, head, rows.shard),
                turned_grad * cosine - swapped(turned_grad) * sine,
            )
        write_rows(result, rows.qkv_spans(2, head, rows.shard), grads[2])
    for first in range(0, rows.total, FRAME):
        sent[:, first : first + FRAME] = result[first : first + FRAME, :].T.astype(BF16)


def finish(
    rows,
    clips,
    arrived,
    tokens,
    gains,
    time,
    space,
    hidden,
    saved,
    shares_in,
    output,
    grad_tokens,
    gain_parts,
    project,
    grad_project,
):
    count = arrived.shape[0]
    live = space_masks(clips)[1]
    received = arrived[...]
    zeros = jnp.zeros_like(received)
    mask = jnp.broadcast_to(out_columns(rows), received.shape)
    left = jnp.concatenate([jnp.where(mask, zeros, received), jnp.where(mask, received, zeros)], axis=0)
    both = nn(left, time[...].reshape(rows.total, -1))
    values = hidden[...].astype(F32)
    output[...] = (values + both[count:]).astype(BF16)
    grad_normed = both[:count].astype(BF16).astype(F32)
    grad_front, grad_time_gain = norm_back(values, inverse_size(values), gains[1:], grad_normed)
    grad_hidden = (tokens[1].astype(F32) + grad_front).astype(BF16)

    project[...] = nt(rows.out_weight(space), grad_hidden)
    grad_project[...] = jnp.zeros_like(grad_project)
    scale = rows.head ** (-0.5)
    for head in range(HEADS):
        spans = [rows.qkv_spans(which, head, rows.qkv_cut) for which in range(3)]
        query, key, value = (read_rows(saved, where).astype(BF16) for where in spans)
        grad = (read_rows(project, rows.out_spans(head, rows.out_cut)) * live).astype(BF16)
        shares_low = shares_in[head]
        grads = attend_back(query, key, value, shares_low.astype(F32), shares_low, grad, scale)
        for where, part in zip(spans, grads):
            write_rows(grad_project, where, part)
    grad_normed = tn(grad_project[...].astype(BF16), rows.qkv_weight(space)).astype(BF16).astype(F32)
    values = tokens[0].astype(F32)
    grad_values, grad_space_gain = norm_back(values, inverse_size(values), gains[:1], grad_normed)
    grad_tokens[...] = (grad_hidden.astype(F32) + grad_values).astype(BF16)
    both_gains = jnp.concatenate([grad_space_gain, grad_time_gain], axis=0).astype(gain_parts.dtype)
    gain_parts[...] = jnp.broadcast_to(both_gains[None], gain_parts.shape)


def call(body, out_shapes, scratch, clips, operands):
    whole = pl.BlockSpec(memory_space=pltpu.VMEM)
    scalars = pl.BlockSpec(memory_space=pltpu.SMEM)
    return pl.pallas_call(
        body,
        out_shape=out_shapes,
        in_specs=[scalars] + [whole] * len(operands),
        out_specs=jax.tree.map(lambda _: whole, out_shapes),
        scratch_shapes=scratch,
        compiler_params=pltpu.CompilerParams(vmem_limit_bytes=VMEM_LIMIT),
    )(clips, *operands)


def gather_ring(space_rows, time_rows, size, others):
    chips = size // 2
    chain = chips // 2
    shard = space_rows.shape[0]

    def chip_at(place):
        place = place % chips
        return 2 * place if place < chain else 2 * (chips - 1 - place) + 1

    ring_pairs = []
    for place in range(chips):
        ring_pairs.append((2 * chip_at(place), 2 * chip_at(place + 1)))
        ring_pairs.append((2 * chip_at(place) + 1, 2 * chip_at(place - 1) + 1))
    planes = lax.axis_size("dp")
    plane = lax.rem(lax.axis_index("dp"), 2)

    def ring(rows):
        return lax.ppermute(rows, "ctx", ring_pairs)

    def across(rows):
        return lax.ppermute(rows, "dp", [(index, index ^ 1) for index in range(planes)])

    def twin(rows):
        return lax.ppermute(rows, "ctx", [(index, index ^ 1) for index in range(size)])

    own = jnp.where(plane == 0, space_rows, time_rows)
    own_other = jnp.where(plane == 0, time_rows, space_rows)
    t0 = twin(own)
    t1 = ring(t0)
    o1 = ring(own)
    o2 = ring(o1)
    t0_other = twin(own_other)
    x_o1 = across(o1)
    t2 = ring(t1)
    o3 = ring(o2)
    o1_twin = twin(o1)
    t1_twin = twin(t1)
    t2, t1_twin, t0_other, o1_twin, *others = gate(t2, t1_twin, t0_other, o1_twin, *others)
    x_t1 = across(t1)
    o2_twin = twin(o2)
    t3 = ring(t2)
    t2_twin = twin(t2)
    x_o1_twin = twin(x_o1)
    o3_twin = twin(o3)
    x_o3 = across(o3)
    x_t1_twin = twin(x_t1)
    x_o2 = ring(x_o1)
    o4 = ring(o3)
    t3_twin = twin(t3)
    x_o4 = across(o4)
    x_t2 = ring(x_t1)
    o4_twin = twin(o4)
    x_t3 = ring(x_t2)
    x_o2_twin = twin(x_o2)
    x_o3_twin = twin(x_o3)
    x_t2_twin = twin(x_t2)
    x_o4_twin = twin(x_o4)
    x_t3_twin = twin(x_t3)
    mine = {"o0": (own, 0), "t0": (t0, 0)}
    other = {"o0": (own_other, 0), "t0": (t0_other, 0)}
    mine |= {"o1": (o1, 0), "o1_twin": (o1_twin, 0)}
    other |= {"o1": (x_o1, 0), "o1_twin": (x_o1_twin, 0)}
    mine |= {"t1": (t1, 0), "t1_twin": (t1_twin, 0)}
    other |= {"t1": (x_t1, 0), "t1_twin": (x_t1_twin, 0)}
    mine |= {"o2": (o2, 0), "o2_twin": (o2_twin, 0)}
    other |= {"o2": (x_o2, 0), "o2_twin": (x_o2_twin, 0)}
    mine |= {"t2": (t2, 0), "t2_twin": (t2_twin, 0)}
    other |= {"t2": (x_t2, 0), "t2_twin": (x_t2_twin, 0)}
    mine |= {"o3": (o3, 0), "o3_twin": (o3_twin, 0)}
    other |= {"o3": (x_o3, 0), "o3_twin": (x_o3_twin, 0)}
    mine |= {"t3": (t3, 0), "t3_twin": (t3_twin, 0)}
    other |= {"t3": (x_t3, 0), "t3_twin": (x_t3_twin, 0)}
    mine |= {"o4": (o4, 0), "o4_twin": (o4_twin, 0)}
    other |= {"o4": (x_o4, 0), "o4_twin": (x_o4_twin, 0)}
    names = ["o0", "t0", "o1", "o2", "o3", "o4", "t1", "t2", "t3"]
    twins = names[2:]

    def order_of():
        rank = lax.axis_index("ctx")
        chip, core = rank // 2, lax.rem(rank, 2)
        column, level = lax.rem(chip, 2), chip // 2
        place = jnp.where(column == 0, level, chips - 1 - level)

        def came(carrier, name):
            steps, shard_core = int(name[1]), carrier if name[0] == "o" else 1 - carrier
            at = lax.rem(place + steps * (2 * carrier - 1) + chips, chips)
            return 2 * jnp.where(at < chain, 2 * at, 2 * (chips - 1 - at) + 1) + shard_core

        order = [came(core, name) for name in names] + [came(1 - core, name) for name in twins]
        return order + [lax.rem(lax.axis_index("dp"), 2)]

    pieces, layouts = [], ([], [])
    for half, found in enumerate((mine, other)):
        for name in names + [name + "_twin" for name in twins]:
            array, first = found[name]
            place_in = [index for index, piece in enumerate(pieces) if piece is array]
            if not place_in:
                place_in = [len(pieces)]
                pieces.append(array)
            layouts[half].append((place_in[0], first * shard))
    return pieces, layouts, order_of, others


def gather_weights(space_rows, time_rows, size, others):
    if size == 16 and lax.axis_size("dp") % 2 == 0:
        return gather_ring(space_rows, time_rows, size, others)
    shard, features = space_rows.shape
    gathered = lax.all_gather(jnp.concatenate([space_rows, time_rows], axis=0), "ctx", axis=0)
    gathered = gathered.reshape(size, 2, shard, features)
    halves = [gathered[:, half].reshape(size * shard, features) for half in range(2)]
    return halves, ([(0, 0)], [(1, 0)]), lambda: [0, 0], others


def shards(
    tokens,
    cotangent,
    clip_frames,
    clip_offsets,
    clip_heights,
    clip_widths,
    spatial_gain,
    spatial_qkv,
    spatial_out,
    temporal_gain,
    temporal_qkv,
    temporal_out,
):
    size = lax.axis_size("ctx")
    everyone = lax.axis_size("dp") * size
    count, features = tokens.shape[1], tokens.shape[2]
    assert count == FRAME and FRAME % size == 0
    near = size // 2
    slots = FRAME // near
    rows = Rows(spatial_qkv.shape[0], spatial_out.shape[0], size)
    both_tokens = jnp.concatenate([tokens, cotangent], axis=0)
    both_gains = jnp.stack([spatial_gain, temporal_gain])
    clips = jnp.concatenate([clip_frames, clip_offsets, clip_heights, clip_widths], axis=0)
    pieces, layouts, order_of, others = gather_weights(
        jnp.concatenate([spatial_qkv, spatial_out], axis=0),
        jnp.concatenate([temporal_qkv, temporal_out], axis=0),
        size,
        (both_tokens, both_gains, clips),
    )
    both_tokens, both_gains, clips = others
    wide = pltpu.VMEM((rows.total, FRAME), F32)
    qkv_wide = pltpu.VMEM((rows.qkv_total, FRAME), F32)
    out_wide = pltpu.VMEM((rows.out_total, FRAME), F32)
    blocks = len(layouts[0])
    sems = pltpu.SemaphoreType.DMA((2, blocks))
    weight_shape = jax.ShapeDtypeStruct((blocks, rows.total // blocks, features), BF16)
    groups = [list(range(first, first + near)) for first in range(0, size, near)]

    def exchange(sent):
        arrived = lax.all_to_all(
            sent.reshape(near, slots, rows.total),
            "ctx",
            split_axis=0,
            concat_axis=0,
            axis_index_groups=groups,
            tiled=True,
        )
        return arrived.reshape(FRAME, rows.total)

    hidden, saved, shares, sent, space_weights, time_weights = call(
        functools.partial(front, rows, layouts, order_of),
        (
            jax.ShapeDtypeStruct((FRAME, features), BF16),
            jax.ShapeDtypeStruct((rows.qkv_total, FRAME), BF16),
            jax.ShapeDtypeStruct((HEADS, FRAME, FRAME), BF16),
            jax.ShapeDtypeStruct((FRAME, rows.total), BF16),
            weight_shape,
            weight_shape,
        ),
        [qkv_wide, out_wide, sems],
        clips,
        (both_tokens, both_gains, *pieces),
    )
    arrived = exchange(sent)
    sent = call(
        functools.partial(time_core, rows, near, slots),
        jax.ShapeDtypeStruct((FRAME, rows.total), BF16),
        [wide, wide],
        clips,
        (arrived,),
    )
    arrived = exchange(sent)
    result, grad_tokens, gains = call(
        functools.partial(finish, rows),
        (
            jax.ShapeDtypeStruct((FRAME, features), BF16),
            jax.ShapeDtypeStruct((FRAME, features), BF16),
            jax.ShapeDtypeStruct((everyone, 2, features), BF16),
        ),
        [out_wide, qkv_wide],
        clips,
        (arrived, both_tokens, both_gains, time_weights, space_weights, hidden, saved, shares),
    )
    gains = lax.all_to_all(gains, ("dp", "ctx"), split_axis=0, concat_axis=0, tiled=True)
    gain_grads = jnp.sum(gains.astype(F32), axis=0) * (1.0 / math.sqrt(everyone * FRAME))
    return result[None], grad_tokens[None], gain_grads


def solution(mesh):
    return jax.shard_map(
        shards,
        mesh=mesh,
        in_specs=(
            P("dp", "ctx", None),
            P("dp", "ctx", None),
            P("dp", None),
            P("dp", None),
            P("dp", None),
            P("dp", None),
            P(),
            P("ctx", None),
            P("ctx", None),
            P(),
            P("ctx", None),
            P("ctx", None),
        ),
        out_specs=(P("dp", "ctx", None), P("dp", "ctx", None), P()),
        check_vma=False,
    )
```

```python
import functools
import math

import jax
import jax.numpy as jnp
from jax import lax
from jax.experimental import pallas as pl
from jax.experimental.pallas import tpu as pltpu
from jax.sharding import PartitionSpec as P

HEADS = 8
FRAME = 128
EPSILON = 1e-06
ROPE_BASE = 10000.0
MASKED = -1e30
F32 = jnp.float32
BF16 = jnp.bfloat16
VMEM_LIMIT = 12 * 1024 * 1024


def nn(a, b):
    return lax.dot_general(a, b, (((1,), (0,)), ((), ())), preferred_element_type=F32)


def nt(a, b):
    return lax.dot_general(a, b, (((1,), (1,)), ((), ())), preferred_element_type=F32)


def tn(a, b):
    return lax.dot_general(a, b, (((0,), (0,)), ((), ())), preferred_element_type=F32)


class Rows:
    def __init__(self, qkv_rows, out_rows, size):
        self.qkv, self.out = qkv_rows, out_rows
        self.shard = qkv_rows + out_rows
        self.total = self.shard * size
        self.inner = out_rows * size
        self.head = self.inner // HEADS
        cut = self.shard % 16 == 0
        self.qkv_cut = -(-qkv_rows // 16) * 16 if cut else self.shard
        self.out_cut = qkv_rows // 16 * 16 if cut else 0
        self.qkv_total = self.qkv_cut * size
        self.out_total = (self.shard - self.out_cut) * size

    def spans(self, first, count, per_shard, stride, shift):
        found = []
        row = first
        while row < first + count:
            block, inside = divmod(row, per_shard)
            length = min(per_shard - inside, first + count - row)
            place = block * stride + shift + inside
            if found and found[-1][0] + found[-1][1] == place:
                found[-1] = (found[-1][0], found[-1][1] + length)
            else:
                found.append((place, length))
            row += length
        return found

    def qkv_spans(self, which, head, stride):
        return self.spans(which * self.inner + head * self.head, self.head, self.qkv, stride, 0)

    def out_spans(self, head, cut):
        stride = self.shard - cut
        return self.spans(head * self.head, self.head, self.out, stride, self.qkv - cut)

    def qkv_weight(self, ref):
        if self.qkv_cut == self.shard:
            return ref[...].reshape(self.total, -1)
        return ref[:, : self.qkv_cut, :].reshape(self.qkv_total, -1)

    def out_weight(self, ref):
        if self.out_cut == 0:
            return ref[...].reshape(self.total, -1)
        return ref[:, self.out_cut :, :].reshape(self.out_total, -1)


def read_rows(ref, spans):
    parts = [ref[place : place + length, :] for place, length in spans]
    return parts[0] if len(parts) == 1 else jnp.concatenate(parts, axis=0)


def write_rows(ref, spans, value):
    done = 0
    for place, length in spans:
        ref[place : place + length, :] = value[done : done + length, :]
        done += length


def inverse_size(values):
    return lax.rsqrt(jnp.mean(values * values, axis=-1, keepdims=True) + EPSILON)


def norm_back(values, inverse, gain, grad):
    scaled = grad * gain
    middle = jnp.mean(scaled * values, axis=-1, keepdims=True)
    grad_values = inverse * scaled - values * (inverse * inverse * inverse * middle)
    grad_gain = jnp.sum(grad * (values * inverse), axis=0, keepdims=True)
    return grad_values, grad_gain


def shares_of(queries, keys, allowed, live, scale):
    scores = [tn(key, query) for key, query in zip(keys, queries)]
    weights = [jnp.exp(jnp.where(allowed, score * scale, MASKED)) for score in scores]
    totals = [jnp.sum(weight, axis=0, keepdims=True) + (1.0 - live) for weight in weights]
    return [weight * (1.0 / total) for weight, total in zip(weights, totals)]


def attend_back(queries, keys, values, shares, shares_low, grads, scale):
    grad_shares = [tn(value, grad) for value, grad in zip(values, grads)]
    middles = [jnp.sum(a * b, axis=0, keepdims=True) for a, b in zip(shares, grad_shares)]
    grad_scores = [
        (share * (grad_share - middle) * scale).astype(BF16)
        for share, grad_share, middle in zip(shares, grad_shares, middles)
    ]
    return (
        [nn(key, grad_score) for key, grad_score in zip(keys, grad_scores)],
        [nt(query, grad_score) for query, grad_score in zip(queries, grad_scores)],
        [nt(grad, share) for grad, share in zip(grads, shares_low)],
    )


def clips_at(clips, frames):
    counts, times, numbers = (jnp.zeros_like(frames) for _ in range(3))
    for clip in range(clips.shape[1]):
        start = clips[1, clip] // FRAME
        member = (frames >= start) & (frames < start + clips[0, clip])
        counts = jnp.where(member, clips[2, clip] * clips[3, clip], counts)
        times = jnp.where(member, frames - start, times)
        numbers = jnp.where(member, clip + 1, numbers)
    return counts, times, numbers


def ids(shape, dim):
    return lax.broadcasted_iota(jnp.int32, shape, dim)


def space_masks(clips):
    count = clips_at(clips, lax.axis_index("ctx").astype(jnp.int32))[0]
    return ids((FRAME, FRAME), 0) < count, (ids((1, FRAME), 1) < count).astype(F32)


def time_masks(clips, near, slots):
    rank = lax.axis_index("ctx")
    token = ids((1, FRAME), 1)
    slot = lax.rem(token, slots)
    counts, times, numbers = clips_at(clips, (rank // near) * near + token // slots)
    alive = lax.rem(rank, near) * slots + slot < counts
    group = (numbers * FRAME + slot).astype(F32)
    keys = jnp.where(alive, group, -1.0)
    allowed = jnp.broadcast_to(keys, (FRAME, FRAME)).T == group
    return allowed, alive.astype(F32), times.astype(F32)


def turn_tables(times, half):
    frequency = jnp.exp(ids((half, FRAME), 0).astype(F32) * (-math.log(ROPE_BASE) / half))
    angles = frequency * times
    cosine, sine = jnp.cos(angles), jnp.sin(angles)
    return jnp.concatenate([cosine, cosine], axis=0), jnp.concatenate([-sine, sine], axis=0)


def out_columns(rows):
    return lax.rem(ids((1, rows.total), 1), rows.shard) >= rows.qkv


def weight_copies(layout, order, pieces, target, sems, which):
    count = target.shape[1]
    return [
        pltpu.make_async_copy(
            pieces[piece].at[pl.ds(first, count)], target.at[order[index]], sems.at[which, index]
        )
        for index, (piece, first) in enumerate(layout)
    ]


def gate(*arrays):
    anywhere = pl.BlockSpec(memory_space=pl.ANY)
    count = len(arrays)
    return pl.pallas_call(
        lambda *refs: None,
        out_shape=tuple(jax.ShapeDtypeStruct(array.shape, array.dtype) for array in arrays),
        in_specs=[anywhere] * count,
        out_specs=(anywhere,) * count,
        input_output_aliases={index: index for index in range(count)},
        compiler_params=pltpu.CompilerParams(vmem_limit_bytes=1024 * 1024),
    )(*arrays)


def start_weights(layouts, order, pieces, space, time, sems):
    def start(first, second):
        for copy in weight_copies(first, order, pieces, space, sems, 0):
            copy.start()
        for copy in weight_copies(second, order, pieces, time, sems, 1):
            copy.start()

    plane = order[len(layouts[0])]

    @pl.when(plane == 0)
    def _():
        start(layouts[0], layouts[1])

    @pl.when(plane != 0)
    def _():
        start(layouts[1], layouts[0])


def wait_weights(layouts, order, pieces, target, sems, which):
    for copy in weight_copies(layouts[0], order, pieces, target, sems, which):
        copy.wait()


def front(rows, layouts, order_of, clips, tokens, gains, *refs):
    pieces, refs = refs[:-9], refs[-9:]
    hidden, saved, shares_out, sent, space, time, project, mixed, sems = refs
    order = order_of()
    start_weights(layouts, order, pieces, space, time, sems)
    allowed, live = space_masks(clips)
    values = tokens[0].astype(F32)
    normed = (values * inverse_size(values) * gains[:1]).astype(BF16)
    mixed[...] = jnp.zeros_like(mixed)
    stride = rows.qkv_cut
    length = stride if len(layouts[0]) > 1 else rows.total

    def project_from(layout):
        for index, (piece, first) in enumerate(layout):
            target = pl.ds(pl.multiple_of(order[index] * length, 16), length)
            project[target, :] = nt(pieces[piece][first : first + length, :], normed)

    pl.when(order[-1] == 0)(lambda: project_from(layouts[0]))
    pl.when(order[-1] != 0)(lambda: project_from(layouts[1]))
    saved[...] = project[...].astype(BF16)
    scale = rows.head ** (-0.5)
    queries, keys, values_in = (
        [read_rows(project, rows.qkv_spans(which, head, stride)).astype(BF16) for head in range(HEADS)]
        for which in range(3)
    )
    shares = [share.astype(BF16) for share in shares_of(queries, keys, allowed, live, scale)]
    blended = [nn(value, share) * live for value, share in zip(values_in, shares)]
    for head in range(HEADS):
        shares_out[head] = shares[head]
        write_rows(mixed, rows.out_spans(head, rows.out_cut), blended[head])
    wait_weights(layouts, order, pieces, space, sems, 0)
    update = tn(mixed[...].astype(BF16), rows.out_weight(space))
    low = (values + update).astype(BF16)
    hidden[...] = low
    values = low.astype(F32)
    normed = (values * inverse_size(values) * gains[1:]).astype(BF16)
    wait_weights(layouts, order, pieces, time, sems, 1)
    both = nt(jnp.concatenate([normed, tokens[1]], axis=0), time[...].reshape(rows.total, -1))
    count = values.shape[0]
    sent[...] = jnp.where(out_columns(rows), both[count:], both[:count]).astype(BF16)


def time_core(rows, near, slots, clips, arrived, sent, project, result):
    allowed, live, times = time_masks(clips, near, slots)
    for first in range(0, rows.total, FRAME):
        project[first : first + FRAME, :] = arrived[:, first : first + FRAME].astype(F32).T
    scale = rows.head ** (-0.5)
    half = rows.head // 2
    cosine, sine = turn_tables(times, half)

    def swapped(vectors):
        return jnp.concatenate([vectors[half:], vectors[:half]], axis=0)

    heads = range(HEADS)
    turned = []
    for which in range(2):
        vectors = [read_rows(project, rows.qkv_spans(which, head, rows.shard)) for head in heads]
        turned.append([(part * cosine + swapped(part) * sine).astype(BF16) for part in vectors])
    queries, keys = turned
    values = [read_rows(project, rows.qkv_spans(2, head, rows.shard)).astype(BF16) for head in heads]
    grads = [(read_rows(project, rows.out_spans(head, 0)) * live).astype(BF16) for head in heads]
    shares = shares_of(queries, keys, allowed, live, scale)
    shares_low = [share.astype(BF16) for share in shares]
    blended = [nn(value, share) * live for value, share in zip(values, shares_low)]
    parts = attend_back(queries, keys, values, shares, shares_low, grads, scale)
    for head in heads:
        write_rows(result, rows.out_spans(head, 0), blended[head])
        for which in range(2):
            turned_grad = parts[which][head].astype(BF16).astype(F32)
            write_rows(
                result,
                rows.qkv_spans(which, head, rows.shard),
                turned_grad * cosine - swapped(turned_grad) * sine,
            )
        write_rows(result, rows.qkv_spans(2, head, rows.shard), parts[2][head])
    for first in range(0, rows.total, FRAME):
        sent[:, first : first + FRAME] = result[first : first + FRAME, :].T.astype(BF16)


def finish(
    rows,
    clips,
    arrived,
    tokens,
    gains,
    time,
    space,
    hidden,
    saved,
    shares_in,
    output,
    grad_tokens,
    gain_parts,
    project,
    grad_project,
):
    count = arrived.shape[0]
    live = space_masks(clips)[1]
    received = arrived[...]
    zeros = jnp.zeros_like(received)
    mask = jnp.broadcast_to(out_columns(rows), received.shape)
    left = jnp.concatenate([jnp.where(mask, zeros, received), jnp.where(mask, received, zeros)], axis=0)
    both = nn(left, time[...].reshape(rows.total, -1))
    values = hidden[...].astype(F32)
    output[...] = (values + both[count:]).astype(BF16)
    grad_normed = both[:count].astype(BF16).astype(F32)
    grad_front, grad_time_gain = norm_back(values, inverse_size(values), gains[1:], grad_normed)
    grad_hidden = (tokens[1].astype(F32) + grad_front).astype(BF16)

    project[...] = nt(rows.out_weight(space), grad_hidden)
    grad_project[...] = jnp.zeros_like(grad_project)
    scale = rows.head ** (-0.5)
    heads = range(HEADS)
    spans = [[rows.qkv_spans(which, head, rows.qkv_cut) for head in heads] for which in range(3)]
    queries, keys, values_in = (
        [read_rows(saved, where).astype(BF16) for where in places] for places in spans
    )
    grads = [
        (read_rows(project, rows.out_spans(head, rows.out_cut)) * live).astype(BF16) for head in heads
    ]
    shares_low = [shares_in[head] for head in heads]
    shares = [share.astype(F32) for share in shares_low]
    parts = attend_back(queries, keys, values_in, shares, shares_low, grads, scale)
    for places, found in zip(spans, parts):
        for where, part in zip(places, found):
            write_rows(grad_project, where, part)
    grad_normed = tn(grad_project[...].astype(BF16), rows.qkv_weight(space)).astype(BF16).astype(F32)
    values = tokens[0].astype(F32)
    grad_values, grad_space_gain = norm_back(values, inverse_size(values), gains[:1], grad_normed)
    grad_tokens[...] = (grad_hidden.astype(F32) + grad_values).astype(BF16)
    both_gains = jnp.concatenate([grad_space_gain, grad_time_gain], axis=0).astype(gain_parts.dtype)
    gain_parts[...] = jnp.broadcast_to(both_gains[None], gain_parts.shape)


def call(body, out_shapes, scratch, clips, operands):
    whole = pl.BlockSpec(memory_space=pltpu.VMEM)
    scalars = pl.BlockSpec(memory_space=pltpu.SMEM)
    return pl.pallas_call(
        body,
        out_shape=out_shapes,
        in_specs=[scalars] + [whole] * len(operands),
        out_specs=jax.tree.map(lambda _: whole, out_shapes),
        scratch_shapes=scratch,
        compiler_params=pltpu.CompilerParams(vmem_limit_bytes=VMEM_LIMIT),
    )(clips, *operands)


def gather_ring(space_rows, time_rows, size, others):
    chips = size // 2
    chain = chips // 2
    shard = space_rows.shape[0]

    def chip_at(place):
        place = place % chips
        return 2 * place if place < chain else 2 * (chips - 1 - place) + 1

    ring_pairs = []
    for place in range(chips):
        ring_pairs.append((2 * chip_at(place), 2 * chip_at(place + 1)))
        ring_pairs.append((2 * chip_at(place) + 1, 2 * chip_at(place - 1) + 1))
    planes = lax.axis_size("dp")
    plane = lax.rem(lax.axis_index("dp"), 2)

    def ring(rows):
        return lax.ppermute(rows, "ctx", ring_pairs)

    def across(rows):
        return lax.ppermute(rows, "dp", [(index, index ^ 1) for index in range(planes)])

    def twin(rows):
        return lax.ppermute(rows, "ctx", [(index, index ^ 1) for index in range(size)])

    own = jnp.where(plane == 0, space_rows, time_rows)
    own_other = jnp.where(plane == 0, time_rows, space_rows)
    t0 = twin(own)
    t1 = ring(t0)
    o1 = ring(own)
    o2 = ring(o1)
    t0_other = twin(own_other)
    x_o1 = across(o1)
    t2 = ring(t1)
    o3 = ring(o2)
    o1_twin = twin(o1)
    t1_twin = twin(t1)
    t2, t1_twin, t0_other, o1_twin, *others = gate(t2, t1_twin, t0_other, o1_twin, *others)
    x_t1 = across(t1)
    o2_twin = twin(o2)
    t3 = ring(t2)
    t2_twin = twin(t2)
    x_o1_twin = twin(x_o1)
    o3_twin = twin(o3)
    x_o3 = across(o3)
    x_t1_twin = twin(x_t1)
    x_o2 = ring(x_o1)
    o4 = ring(o3)
    t3_twin = twin(t3)
    x_o4 = across(o4)
    x_t2 = ring(x_t1)
    o4_twin = twin(o4)
    x_t3 = ring(x_t2)
    x_o2_twin = twin(x_o2)
    x_o3_twin = twin(x_o3)
    x_t2_twin = twin(x_t2)
    x_o4_twin = twin(x_o4)
    x_t3_twin = twin(x_t3)
    mine = {"o0": (own, 0), "t0": (t0, 0)}
    other = {"o0": (own_other, 0), "t0": (t0_other, 0)}
    mine |= {"o1": (o1, 0), "o1_twin": (o1_twin, 0)}
    other |= {"o1": (x_o1, 0), "o1_twin": (x_o1_twin, 0)}
    mine |= {"t1": (t1, 0), "t1_twin": (t1_twin, 0)}
    other |= {"t1": (x_t1, 0), "t1_twin": (x_t1_twin, 0)}
    mine |= {"o2": (o2, 0), "o2_twin": (o2_twin, 0)}
    other |= {"o2": (x_o2, 0), "o2_twin": (x_o2_twin, 0)}
    mine |= {"t2": (t2, 0), "t2_twin": (t2_twin, 0)}
    other |= {"t2": (x_t2, 0), "t2_twin": (x_t2_twin, 0)}
    mine |= {"o3": (o3, 0), "o3_twin": (o3_twin, 0)}
    other |= {"o3": (x_o3, 0), "o3_twin": (x_o3_twin, 0)}
    mine |= {"t3": (t3, 0), "t3_twin": (t3_twin, 0)}
    other |= {"t3": (x_t3, 0), "t3_twin": (x_t3_twin, 0)}
    mine |= {"o4": (o4, 0), "o4_twin": (o4_twin, 0)}
    other |= {"o4": (x_o4, 0), "o4_twin": (x_o4_twin, 0)}
    names = ["o0", "t0", "o1", "o2", "o3", "o4", "t1", "t2", "t3"]
    twins = names[2:]

    def order_of():
        rank = lax.axis_index("ctx")
        chip, core = rank // 2, lax.rem(rank, 2)
        column, level = lax.rem(chip, 2), chip // 2
        place = jnp.where(column == 0, level, chips - 1 - level)

        def came(carrier, name):
            steps, shard_core = int(name[1]), carrier if name[0] == "o" else 1 - carrier
            at = lax.rem(place + steps * (2 * carrier - 1) + chips, chips)
            return 2 * jnp.where(at < chain, 2 * at, 2 * (chips - 1 - at) + 1) + shard_core

        order = [came(core, name) for name in names] + [came(1 - core, name) for name in twins]
        return order + [lax.rem(lax.axis_index("dp"), 2)]

    pieces, layouts = [], ([], [])
    for half, found in enumerate((mine, other)):
        for name in names + [name + "_twin" for name in twins]:
            array, first = found[name]
            place_in = [index for index, piece in enumerate(pieces) if piece is array]
            if not place_in:
                place_in = [len(pieces)]
                pieces.append(array)
            layouts[half].append((place_in[0], first * shard))
    return pieces, layouts, order_of, others


def gather_weights(space_rows, time_rows, size, others):
    if size == 16 and lax.axis_size("dp") % 2 == 0:
        return gather_ring(space_rows, time_rows, size, others)
    shard, features = space_rows.shape
    gathered = lax.all_gather(jnp.concatenate([space_rows, time_rows], axis=0), "ctx", axis=0)
    gathered = gathered.reshape(size, 2, shard, features)
    halves = [gathered[:, half].reshape(size * shard, features) for half in range(2)]
    return halves, ([(0, 0)], [(1, 0)]), lambda: [0, 0], others


def shards(
    tokens,
    cotangent,
    clip_frames,
    clip_offsets,
    clip_heights,
    clip_widths,
    spatial_gain,
    spatial_qkv,
    spatial_out,
    temporal_gain,
    temporal_qkv,
    temporal_out,
):
    size = lax.axis_size("ctx")
    everyone = lax.axis_size("dp") * size
    count, features = tokens.shape[1], tokens.shape[2]
    assert count == FRAME and FRAME % size == 0
    near = size // 2
    slots = FRAME // near
    rows = Rows(spatial_qkv.shape[0], spatial_out.shape[0], size)
    both_tokens = jnp.concatenate([tokens, cotangent], axis=0)
    both_gains = jnp.stack([spatial_gain, temporal_gain])
    clips = jnp.concatenate([clip_frames, clip_offsets, clip_heights, clip_widths], axis=0)
    pieces, layouts, order_of, others = gather_weights(
        jnp.concatenate([spatial_qkv, spatial_out], axis=0),
        jnp.concatenate([temporal_qkv, temporal_out], axis=0),
        size,
        (both_tokens, both_gains, clips),
    )
    both_tokens, both_gains, clips = others
    wide = pltpu.VMEM((rows.total, FRAME), F32)
    qkv_wide = pltpu.VMEM((rows.qkv_total, FRAME), F32)
    out_wide = pltpu.VMEM((rows.out_total, FRAME), F32)
    blocks = len(layouts[0])
    sems = pltpu.SemaphoreType.DMA((2, blocks))
    weight_shape = jax.ShapeDtypeStruct((blocks, rows.total // blocks, features), BF16)
    groups = [list(range(first, first + near)) for first in range(0, size, near)]

    def exchange(sent):
        arrived = lax.all_to_all(
            sent.reshape(near, slots, rows.total),
            "ctx",
            split_axis=0,
            concat_axis=0,
            axis_index_groups=groups,
            tiled=True,
        )
        return arrived.reshape(FRAME, rows.total)

    hidden, saved, shares, sent, space_weights, time_weights = call(
        functools.partial(front, rows, layouts, order_of),
        (
            jax.ShapeDtypeStruct((FRAME, features), BF16),
            jax.ShapeDtypeStruct((rows.qkv_total, FRAME), BF16),
            jax.ShapeDtypeStruct((HEADS, FRAME, FRAME), BF16),
            jax.ShapeDtypeStruct((FRAME, rows.total), BF16),
            weight_shape,
            weight_shape,
        ),
        [qkv_wide, out_wide, sems],
        clips,
        (both_tokens, both_gains, *pieces),
    )
    arrived = exchange(sent)
    sent = call(
        functools.partial(time_core, rows, near, slots),
        jax.ShapeDtypeStruct((FRAME, rows.total), BF16),
        [wide, wide],
        clips,
        (arrived,),
    )
    arrived = exchange(sent)
    result, grad_tokens, gains = call(
        functools.partial(finish, rows),
        (
            jax.ShapeDtypeStruct((FRAME, features), BF16),
            jax.ShapeDtypeStruct((FRAME, features), BF16),
            jax.ShapeDtypeStruct((everyone, 2, features), BF16),
        ),
        [out_wide, qkv_wide],
        clips,
        (arrived, both_tokens, both_gains, time_weights, space_weights, hidden, saved, shares),
    )
    gains = lax.all_to_all(gains, ("dp", "ctx"), split_axis=0, concat_axis=0, tiled=True)
    gain_grads = jnp.sum(gains.astype(F32), axis=0) * (1.0 / math.sqrt(everyone * FRAME))
    return result[None], grad_tokens[None], gain_grads


def solution(mesh):
    return jax.shard_map(
        shards,
        mesh=mesh,
        in_specs=(
            P("dp", "ctx", None),
            P("dp", "ctx", None),
            P("dp", None),
            P("dp", None),
            P("dp", None),
            P("dp", None),
            P(),
            P("ctx", None),
            P("ctx", None),
            P(),
            P("ctx", None),
            P("ctx", None),
        ),
        out_specs=(P("dp", "ctx", None), P("dp", "ctx", None), P()),
        check_vma=False,
    )
```

```python
import functools
import math

import jax
import jax.numpy as jnp
from jax import lax
from jax.experimental import pallas as pl
from jax.experimental.pallas import tpu as pltpu
from jax.sharding import PartitionSpec as P

HEADS = 8
FRAME = 128
EPSILON = 1e-06
ROPE_BASE = 10000.0
MASKED = -1e30
F32 = jnp.float32
BF16 = jnp.bfloat16
VMEM_LIMIT = 12 * 1024 * 1024


def nn(a, b):
    return lax.dot_general(a, b, (((1,), (0,)), ((), ())), preferred_element_type=F32)


def nt(a, b):
    return lax.dot_general(a, b, (((1,), (1,)), ((), ())), preferred_element_type=F32)


def tn(a, b):
    return lax.dot_general(a, b, (((0,), (0,)), ((), ())), preferred_element_type=F32)


class Rows:
    def __init__(self, qkv_rows, out_rows, size):
        self.qkv, self.out = qkv_rows, out_rows
        self.shard = qkv_rows + out_rows
        self.total = self.shard * size
        self.inner = out_rows * size
        self.head = self.inner // HEADS
        cut = self.shard % 16 == 0
        self.qkv_cut = -(-qkv_rows // 16) * 16 if cut else self.shard
        self.out_cut = qkv_rows // 16 * 16 if cut else 0
        self.qkv_total = self.qkv_cut * size
        self.out_total = (self.shard - self.out_cut) * size

    def spans(self, first, count, per_shard, stride, shift):
        found = []
        row = first
        while row < first + count:
            block, inside = divmod(row, per_shard)
            length = min(per_shard - inside, first + count - row)
            place = block * stride + shift + inside
            if found and found[-1][0] + found[-1][1] == place:
                found[-1] = (found[-1][0], found[-1][1] + length)
            else:
                found.append((place, length))
            row += length
        return found

    def qkv_spans(self, which, head, stride):
        return self.spans(which * self.inner + head * self.head, self.head, self.qkv, stride, 0)

    def out_spans(self, head, cut):
        stride = self.shard - cut
        return self.spans(head * self.head, self.head, self.out, stride, self.qkv - cut)

    def qkv_weight(self, ref):
        if self.qkv_cut == self.shard:
            return ref[...].reshape(self.total, -1)
        return ref[:, : self.qkv_cut, :].reshape(self.qkv_total, -1)

    def out_weight(self, ref):
        if self.out_cut == 0:
            return ref[...].reshape(self.total, -1)
        return ref[:, self.out_cut :, :].reshape(self.out_total, -1)


def read_rows(ref, spans):
    parts = [ref[place : place + length, :] for place, length in spans]
    return parts[0] if len(parts) == 1 else jnp.concatenate(parts, axis=0)


def write_rows(ref, spans, value):
    done = 0
    for place, length in spans:
        ref[place : place + length, :] = value[done : done + length, :]
        done += length


def inverse_size(values):
    return lax.rsqrt(jnp.mean(values * values, axis=-1, keepdims=True) + EPSILON)


def norm_back(values, inverse, gain, grad):
    scaled = grad * gain
    middle = jnp.mean(scaled * values, axis=-1, keepdims=True)
    grad_values = inverse * scaled - values * (inverse * inverse * inverse * middle)
    grad_gain = jnp.sum(grad * (values * inverse), axis=0, keepdims=True)
    return grad_values, grad_gain


def shares_of(queries, keys, allowed, live, scale):
    scores = [tn(key, query) for key, query in zip(keys, queries)]
    weights = [jnp.exp(jnp.where(allowed, score * scale, MASKED)) for score in scores]
    totals = [jnp.sum(weight, axis=0, keepdims=True) + (1.0 - live) for weight in weights]
    return [weight * (1.0 / total) for weight, total in zip(weights, totals)]


def attend_back(queries, keys, values, shares, shares_low, grads, scale):
    grad_shares = [tn(value, grad) for value, grad in zip(values, grads)]
    middles = [jnp.sum(a * b, axis=0, keepdims=True) for a, b in zip(shares, grad_shares)]
    grad_scores = [
        (share * (grad_share - middle) * scale).astype(BF16)
        for share, grad_share, middle in zip(shares, grad_shares, middles)
    ]
    return (
        [nn(key, grad_score) for key, grad_score in zip(keys, grad_scores)],
        [nt(query, grad_score) for query, grad_score in zip(queries, grad_scores)],
        [nt(grad, share) for grad, share in zip(grads, shares_low)],
    )


def clips_at(clips, frames):
    counts, times, numbers = (jnp.zeros_like(frames) for _ in range(3))
    for clip in range(clips.shape[1]):
        start = clips[1, clip] // FRAME
        member = (frames >= start) & (frames < start + clips[0, clip])
        counts = jnp.where(member, clips[2, clip] * clips[3, clip], counts)
        times = jnp.where(member, frames - start, times)
        numbers = jnp.where(member, clip + 1, numbers)
    return counts, times, numbers


def ids(shape, dim):
    return lax.broadcasted_iota(jnp.int32, shape, dim)


def space_masks(clips):
    count = clips_at(clips, lax.axis_index("ctx").astype(jnp.int32))[0]
    return ids((FRAME, FRAME), 0) < count, (ids((1, FRAME), 1) < count).astype(F32)


def time_masks(clips, near, slots):
    rank = lax.axis_index("ctx")
    token = ids((1, FRAME), 1)
    slot = lax.rem(token, slots)
    counts, times, numbers = clips_at(clips, (rank // near) * near + token // slots)
    alive = lax.rem(rank, near) * slots + slot < counts
    group = (numbers * FRAME + slot).astype(F32)
    keys = jnp.where(alive, group, -1.0)
    allowed = jnp.broadcast_to(keys, (FRAME, FRAME)).T == group
    return allowed, alive.astype(F32), times.astype(F32)


def turn_tables(times, half):
    frequency = jnp.exp(ids((half, FRAME), 0).astype(F32) * (-math.log(ROPE_BASE) / half))
    angles = frequency * times
    cosine, sine = jnp.cos(angles), jnp.sin(angles)
    return jnp.concatenate([cosine, cosine], axis=0), jnp.concatenate([-sine, sine], axis=0)


def out_columns(rows):
    return lax.rem(ids((1, rows.total), 1), rows.shard) >= rows.qkv


def weight_copies(layout, order, pieces, target, sems, which):
    count = target.shape[1]
    return [
        pltpu.make_async_copy(
            pieces[piece].at[pl.ds(first, count)], target.at[order[index]], sems.at[which, index]
        )
        for index, (piece, first) in enumerate(layout)
    ]


def gate(rows, *events, others=()):
    anywhere = pl.BlockSpec(memory_space=pl.ANY)
    arrays = (rows, *others)
    count = len(arrays)
    results = pl.pallas_call(
        lambda *refs: None,
        out_shape=tuple(jax.ShapeDtypeStruct(array.shape, array.dtype) for array in arrays),
        in_specs=[anywhere] * (count + len(events)),
        out_specs=(anywhere,) * count,
        input_output_aliases={index: index for index in range(count)},
        compiler_params=pltpu.CompilerParams(vmem_limit_bytes=1024 * 1024),
    )(*arrays, *events)
    return results if others else results[0]


def start_weights(layouts, order, pieces, space, time, sems):
    def start(first, second):
        for copy in weight_copies(first, order, pieces, space, sems, 0):
            copy.start()
        for copy in weight_copies(second, order, pieces, time, sems, 1):
            copy.start()

    plane = order[len(layouts[0])]

    @pl.when(plane == 0)
    def _():
        start(layouts[0], layouts[1])

    @pl.when(plane != 0)
    def _():
        start(layouts[1], layouts[0])


def wait_weights(layouts, order, pieces, target, sems, which):
    for copy in weight_copies(layouts[0], order, pieces, target, sems, which):
        copy.wait()


def give(direct, stage, outs):
    if not direct:
        outs[0][...] = stage[...]
        return
    core = lax.rem(lax.axis_index("ctx"), 2)
    length = FRAME // (2 * direct)
    for chip in range(direct):
        for out, to in zip(outs, (core, 1 - core)):
            source = pl.ds(pl.multiple_of((2 * chip + to) * length, 16), length)
            out[chip * length : (chip + 1) * length, :] = stage[source, :]


def join(direct, own, from_twin, *outs):
    rank = lax.axis_index("ctx")
    core, chip = lax.rem(rank, 2), lax.rem(rank // 2, direct)
    length = own.shape[0] // direct
    for distance, out in enumerate(outs):
        source = pl.ds(pl.multiple_of((chip ^ distance) * length, 16), length)
        out[pl.ds(pl.multiple_of(core * length, 16), length), :] = own[source, :]
        out[pl.ds(pl.multiple_of((1 - core) * length, 16), length), :] = from_twin[source, :]


def collect(direct, arrived, stage):
    if not direct:
        return arrived[0]
    chip = lax.rem(lax.axis_index("ctx") // 2, direct)
    length = arrived[0].shape[0]
    for distance, part in enumerate(arrived):
        target = pl.ds(pl.multiple_of((chip ^ distance) * length, 16), length)
        stage[target, :] = part[...]
    return stage


def front(rows, layouts, order_of, direct, clips, tokens, gains, *refs):
    sends = 2 if direct else 1
    pieces, refs = refs[: -9 - sends], refs[-9 - sends :]
    hidden, saved, shares_out, space, time = refs[:5]
    project, mixed, stage, sems = refs[-4:]
    order = order_of()
    start_weights(layouts, order, pieces, space, time, sems)
    allowed, live = space_masks(clips)
    values = tokens[0].astype(F32)
    normed = (values * inverse_size(values) * gains[:1]).astype(BF16)
    mixed[...] = jnp.zeros_like(mixed)
    stride = rows.qkv_cut
    length = stride if len(layouts[0]) > 1 else rows.total

    def project_from(layout):
        for index, (piece, first) in enumerate(layout):
            target = pl.ds(pl.multiple_of(order[index] * length, 16), length)
            project[target, :] = nt(pieces[piece][first : first + length, :], normed)

    pl.when(order[-1] == 0)(lambda: project_from(layouts[0]))
    pl.when(order[-1] != 0)(lambda: project_from(layouts[1]))
    saved[...] = project[...].astype(BF16)
    scale = rows.head ** (-0.5)
    queries, keys, values_in = (
        [read_rows(project, rows.qkv_spans(which, head, stride)).astype(BF16) for head in range(HEADS)]
        for which in range(3)
    )
    shares = [share.astype(BF16) for share in shares_of(queries, keys, allowed, live, scale)]
    blended = [nn(value, share) * live for value, share in zip(values_in, shares)]
    for head in range(HEADS):
        shares_out[head] = shares[head]
        write_rows(mixed, rows.out_spans(head, rows.out_cut), blended[head])
    wait_weights(layouts, order, pieces, space, sems, 0)
    update = tn(mixed[...].astype(BF16), rows.out_weight(space))
    low = (values + update).astype(BF16)
    hidden[...] = low
    values = low.astype(F32)
    normed = (values * inverse_size(values) * gains[1:]).astype(BF16)
    wait_weights(layouts, order, pieces, time, sems, 1)
    both = nt(jnp.concatenate([normed, tokens[1]], axis=0), time[...].reshape(rows.total, -1))
    count = values.shape[0]
    stage[...] = jnp.where(out_columns(rows), both[count:], both[:count]).astype(BF16)
    give(direct, stage, refs[5:-4])


def time_core(rows, near, slots, direct, clips, *refs):
    project, result, stage = refs[-3:]
    arrived = collect(direct, refs[: direct or 1], stage)
    allowed, live, times = time_masks(clips, near, slots)
    for first in range(0, rows.total, FRAME):
        project[first : first + FRAME, :] = arrived[:, first : first + FRAME].astype(F32).T
    scale = rows.head ** (-0.5)
    half = rows.head // 2
    cosine, sine = turn_tables(times, half)

    def swapped(vectors):
        return jnp.concatenate([vectors[half:], vectors[:half]], axis=0)

    heads = range(HEADS)
    turned = []
    for which in range(2):
        vectors = [read_rows(project, rows.qkv_spans(which, head, rows.shard)) for head in heads]
        turned.append([(part * cosine + swapped(part) * sine).astype(BF16) for part in vectors])
    queries, keys = turned
    values = [read_rows(project, rows.qkv_spans(2, head, rows.shard)).astype(BF16) for head in heads]
    grads = [(read_rows(project, rows.out_spans(head, 0)) * live).astype(BF16) for head in heads]
    shares = shares_of(queries, keys, allowed, live, scale)
    shares_low = [share.astype(BF16) for share in shares]
    blended = [nn(value, share) * live for value, share in zip(values, shares_low)]
    parts = attend_back(queries, keys, values, shares, shares_low, grads, scale)
    for head in heads:
        write_rows(result, rows.out_spans(head, 0), blended[head])
        for which in range(2):
            turned_grad = parts[which][head].astype(BF16).astype(F32)
            write_rows(
                result,
                rows.qkv_spans(which, head, rows.shard),
                turned_grad * cosine - swapped(turned_grad) * sine,
            )
        write_rows(result, rows.qkv_spans(2, head, rows.shard), parts[2][head])
    for first in range(0, rows.total, FRAME):
        stage[:, first : first + FRAME] = result[first : first + FRAME, :].T.astype(BF16)
    give(direct, stage, refs[direct or 1 : -3])


def finish(rows, direct, clips, *refs):
    arrived, refs = refs[: direct or 1], refs[direct or 1 :]
    tokens, gains, time, space, hidden, saved, shares_in = refs[:7]
    output, grad_tokens, gain_parts, project, grad_project, stage = refs[7:]
    arrived = collect(direct, arrived, stage)
    count = arrived.shape[0]
    live = space_masks(clips)[1]
    received = arrived[...]
    zeros = jnp.zeros_like(received)
    mask = jnp.broadcast_to(out_columns(rows), received.shape)
    left = jnp.concatenate([jnp.where(mask, zeros, received), jnp.where(mask, received, zeros)], axis=0)
    both = nn(left, time[...].reshape(rows.total, -1))
    values = hidden[...].astype(F32)
    output[...] = (values + both[count:]).astype(BF16)
    grad_normed = both[:count].astype(BF16).astype(F32)
    grad_front, grad_time_gain = norm_back(values, inverse_size(values), gains[1:], grad_normed)
    grad_hidden = (tokens[1].astype(F32) + grad_front).astype(BF16)

    project[...] = nt(rows.out_weight(space), grad_hidden)
    grad_project[...] = jnp.zeros_like(grad_project)
    scale = rows.head ** (-0.5)
    heads = range(HEADS)
    spans = [[rows.qkv_spans(which, head, rows.qkv_cut) for head in heads] for which in range(3)]
    queries, keys, values_in = (
        [read_rows(saved, where).astype(BF16) for where in places] for places in spans
    )
    grads = [
        (read_rows(project, rows.out_spans(head, rows.out_cut)) * live).astype(BF16) for head in heads
    ]
    shares_low = [shares_in[head] for head in heads]
    shares = [share.astype(F32) for share in shares_low]
    parts = attend_back(queries, keys, values_in, shares, shares_low, grads, scale)
    for places, found in zip(spans, parts):
        for where, part in zip(places, found):
            write_rows(grad_project, where, part)
    grad_normed = tn(grad_project[...].astype(BF16), rows.qkv_weight(space)).astype(BF16).astype(F32)
    values = tokens[0].astype(F32)
    grad_values, grad_space_gain = norm_back(values, inverse_size(values), gains[:1], grad_normed)
    grad_tokens[...] = (grad_hidden.astype(F32) + grad_values).astype(BF16)
    both_gains = jnp.concatenate([grad_space_gain, grad_time_gain], axis=0).astype(gain_parts.dtype)
    gain_parts[...] = jnp.broadcast_to(both_gains[None], gain_parts.shape)


def call(body, out_shapes, scratch, clips, operands):
    clips = () if clips is None else (clips,)
    whole = pl.BlockSpec(memory_space=pltpu.VMEM)
    scalars = pl.BlockSpec(memory_space=pltpu.SMEM)
    return pl.pallas_call(
        body,
        out_shape=out_shapes,
        in_specs=[scalars] * len(clips) + [whole] * len(operands),
        out_specs=jax.tree.map(lambda _: whole, out_shapes),
        scratch_shapes=scratch,
        compiler_params=pltpu.CompilerParams(vmem_limit_bytes=VMEM_LIMIT),
    )(*clips, *operands)


def gather_ring(space_rows, time_rows, size, others):
    chips = size // 2
    chain = chips // 2
    shard = space_rows.shape[0]

    def chip_at(place):
        place = place % chips
        return 2 * place if place < chain else 2 * (chips - 1 - place) + 1

    ring_pairs = []
    for place in range(chips):
        ring_pairs.append((2 * chip_at(place), 2 * chip_at(place + 1)))
        ring_pairs.append((2 * chip_at(place) + 1, 2 * chip_at(place - 1) + 1))
    planes = lax.axis_size("dp")
    plane = lax.rem(lax.axis_index("dp"), 2)

    def ring(rows):
        return lax.ppermute(rows, "ctx", ring_pairs)

    def across(rows):
        return lax.ppermute(rows, "dp", [(index, index ^ 1) for index in range(planes)])

    def twin(rows):
        return lax.ppermute(rows, "ctx", [(index, index ^ 1) for index in range(size)])

    own = jnp.where(plane == 0, space_rows, time_rows)
    own_other = jnp.where(plane == 0, time_rows, space_rows)
    t0 = twin(own)
    t1 = ring(t0)
    o1 = ring(own)
    o2 = ring(o1)
    t0_other = twin(own_other)
    x_o1 = across(o1)
    t2 = ring(t1)
    o3 = ring(o2)
    o1_twin = twin(o1)
    t1_twin = twin(t1)
    t2, *others = gate(t2, t1_twin, t0_other, o1_twin, others=others)
    x_t1 = across(t1)
    o2_twin = twin(o2)
    t3 = ring(t2)
    t2_twin = twin(t2)
    x_o1_twin = twin(x_o1)
    o3_twin = twin(o3)
    x_o3 = across(o3)
    x_t1_twin = twin(x_t1)
    x_o2 = ring(x_o1)
    o4 = ring(o3)
    t3_twin = twin(t3)
    x_o4 = across(o4)
    x_t2 = ring(x_t1)
    o4_twin = twin(o4)
    x_t3 = ring(x_t2)
    x_o2_twin = twin(x_o2)
    x_o3_twin = twin(x_o3)
    x_t2_twin = twin(x_t2)
    x_o4_twin = twin(x_o4)
    x_t3_twin = twin(x_t3)
    mine = {"o0": (own, 0), "t0": (t0, 0)}
    other = {"o0": (own_other, 0), "t0": (t0_other, 0)}
    mine |= {"o1": (o1, 0), "o1_twin": (o1_twin, 0)}
    other |= {"o1": (x_o1, 0), "o1_twin": (x_o1_twin, 0)}
    mine |= {"t1": (t1, 0), "t1_twin": (t1_twin, 0)}
    other |= {"t1": (x_t1, 0), "t1_twin": (x_t1_twin, 0)}
    mine |= {"o2": (o2, 0), "o2_twin": (o2_twin, 0)}
    other |= {"o2": (x_o2, 0), "o2_twin": (x_o2_twin, 0)}
    mine |= {"t2": (t2, 0), "t2_twin": (t2_twin, 0)}
    other |= {"t2": (x_t2, 0), "t2_twin": (x_t2_twin, 0)}
    mine |= {"o3": (o3, 0), "o3_twin": (o3_twin, 0)}
    other |= {"o3": (x_o3, 0), "o3_twin": (x_o3_twin, 0)}
    mine |= {"t3": (t3, 0), "t3_twin": (t3_twin, 0)}
    other |= {"t3": (x_t3, 0), "t3_twin": (x_t3_twin, 0)}
    mine |= {"o4": (o4, 0), "o4_twin": (o4_twin, 0)}
    other |= {"o4": (x_o4, 0), "o4_twin": (x_o4_twin, 0)}
    names = ["o0", "t0", "o1", "o2", "o3", "o4", "t1", "t2", "t3"]
    twins = names[2:]

    def order_of():
        rank = lax.axis_index("ctx")
        chip, core = rank // 2, lax.rem(rank, 2)
        column, level = lax.rem(chip, 2), chip // 2
        place = jnp.where(column == 0, level, chips - 1 - level)

        def came(carrier, name):
            steps, shard_core = int(name[1]), carrier if name[0] == "o" else 1 - carrier
            at = lax.rem(place + steps * (2 * carrier - 1) + chips, chips)
            return 2 * jnp.where(at < chain, 2 * at, 2 * (chips - 1 - at) + 1) + shard_core

        order = [came(core, name) for name in names] + [came(1 - core, name) for name in twins]
        return order + [lax.rem(lax.axis_index("dp"), 2)]

    pieces, layouts = [], ([], [])
    for half, found in enumerate((mine, other)):
        for name in names + [name + "_twin" for name in twins]:
            array, first = found[name]
            place_in = [index for index, piece in enumerate(pieces) if piece is array]
            if not place_in:
                place_in = [len(pieces)]
                pieces.append(array)
            layouts[half].append((place_in[0], first * shard))
    return pieces, layouts, order_of, others


def gather_weights(space_rows, time_rows, size, others):
    if size == 16 and lax.axis_size("dp") % 2 == 0:
        return gather_ring(space_rows, time_rows, size, others)
    shard, features = space_rows.shape
    gathered = lax.all_gather(jnp.concatenate([space_rows, time_rows], axis=0), "ctx", axis=0)
    gathered = gathered.reshape(size, 2, shard, features)
    halves = [gathered[:, half].reshape(size * shard, features) for half in range(2)]
    return halves, ([(0, 0)], [(1, 0)]), lambda: [0, 0], others


def shards(
    tokens,
    cotangent,
    clip_frames,
    clip_offsets,
    clip_heights,
    clip_widths,
    spatial_gain,
    spatial_qkv,
    spatial_out,
    temporal_gain,
    temporal_qkv,
    temporal_out,
):
    size = lax.axis_size("ctx")
    everyone = lax.axis_size("dp") * size
    count, features = tokens.shape[1], tokens.shape[2]
    assert count == FRAME and FRAME % size == 0
    near = size // 2
    slots = FRAME // near
    rows = Rows(spatial_qkv.shape[0], spatial_out.shape[0], size)
    both_tokens = jnp.concatenate([tokens, cotangent], axis=0)
    both_gains = jnp.stack([spatial_gain, temporal_gain])
    clips = jnp.concatenate([clip_frames, clip_offsets, clip_heights, clip_widths], axis=0)
    pieces, layouts, order_of, others = gather_weights(
        jnp.concatenate([spatial_qkv, spatial_out], axis=0),
        jnp.concatenate([temporal_qkv, temporal_out], axis=0),
        size,
        (both_tokens, both_gains, clips),
    )
    both_tokens, both_gains, clips = others
    wide = pltpu.VMEM((rows.total, FRAME), F32)
    qkv_wide = pltpu.VMEM((rows.qkv_total, FRAME), F32)
    out_wide = pltpu.VMEM((rows.out_total, FRAME), F32)
    blocks = len(layouts[0])
    sems = pltpu.SemaphoreType.DMA((2, blocks))
    weight_shape = jax.ShapeDtypeStruct((blocks, rows.total // blocks, features), BF16)
    groups = [list(range(first, first + near)) for first in range(0, size, near)]

    direct = 4 if near == 8 and slots % 16 == 0 else 0
    part = jax.ShapeDtypeStruct((FRAME // 2 if direct else FRAME, rows.total), BF16)
    parts = (part,) * (2 if direct else 1)
    stage = pltpu.VMEM((FRAME, rows.total), BF16)

    def exchange(sent):
        if not direct:
            arrived = lax.all_to_all(
                sent[0].reshape(near, slots, rows.total),
                "ctx",
                split_axis=0,
                concat_axis=0,
                axis_index_groups=groups,
                tiled=True,
            )
            return [arrived.reshape(FRAME, rows.total)]
        own, to_twin = sent
        from_twin = lax.ppermute(to_twin, "ctx", [(index, index ^ 1) for index in range(size)])
        joined = jax.ShapeDtypeStruct((2 * slots, rows.total), BF16)
        here, *away = call(
            functools.partial(join, direct), (joined,) * direct, [], None, (own, from_twin)
        )
        return [here] + [
            lax.ppermute(rows_away, "ctx", [(index, index ^ (2 * distance)) for index in range(size)])
            for distance, rows_away in list(enumerate(away, 1))[::-1]
        ][::-1]

    hidden, saved, shares, space_weights, time_weights, *sent = call(
        functools.partial(front, rows, layouts, order_of, direct),
        (
            jax.ShapeDtypeStruct((FRAME, features), BF16),
            jax.ShapeDtypeStruct((rows.qkv_total, FRAME), BF16),
            jax.ShapeDtypeStruct((HEADS, FRAME, FRAME), BF16),
            weight_shape,
            weight_shape,
            *parts,
        ),
        [qkv_wide, out_wide, stage, sems],
        clips,
        (both_tokens, both_gains, *pieces),
    )
    arrived = exchange(sent)
    sent = call(
        functools.partial(time_core, rows, near, slots, direct),
        parts,
        [wide, wide, stage],
        clips,
        arrived,
    )
    arrived = exchange(sent)
    result, grad_tokens, gains = call(
        functools.partial(finish, rows, direct),
        (
            jax.ShapeDtypeStruct((FRAME, features), BF16),
            jax.ShapeDtypeStruct((FRAME, features), BF16),
            jax.ShapeDtypeStruct((everyone, 2, features), BF16),
        ),
        [out_wide, qkv_wide, stage],
        clips,
        (*arrived, both_tokens, both_gains, time_weights, space_weights, hidden, saved, shares),
    )
    gains = lax.all_to_all(gains, ("dp", "ctx"), split_axis=0, concat_axis=0, tiled=True)
    gain_grads = jnp.sum(gains.astype(F32), axis=0) * (1.0 / math.sqrt(everyone * FRAME))
    return result[None], grad_tokens[None], gain_grads


def solution(mesh):
    return jax.shard_map(
        shards,
        mesh=mesh,
        in_specs=(
            P("dp", "ctx", None),
            P("dp", "ctx", None),
            P("dp", None),
            P("dp", None),
            P("dp", None),
            P("dp", None),
            P(),
            P("ctx", None),
            P("ctx", None),
            P(),
            P("ctx", None),
            P("ctx", None),
        ),
        out_specs=(P("dp", "ctx", None), P("dp", "ctx", None), P()),
        check_vma=False,
    )
```

```python
import functools
import math

import jax
import jax.numpy as jnp
from jax import lax
from jax.experimental import pallas as pl
from jax.experimental.pallas import tpu as pltpu
from jax.sharding import PartitionSpec as P

HEADS = 8
FRAME = 128
EPSILON = 1e-06
ROPE_BASE = 10000.0
MASKED = -1e30
F32 = jnp.float32
BF16 = jnp.bfloat16
VMEM_LIMIT = 12 * 1024 * 1024


def nn(a, b):
    return lax.dot_general(a, b, (((1,), (0,)), ((), ())), preferred_element_type=F32)


def nt(a, b):
    return lax.dot_general(a, b, (((1,), (1,)), ((), ())), preferred_element_type=F32)


def tn(a, b):
    return lax.dot_general(a, b, (((0,), (0,)), ((), ())), preferred_element_type=F32)


class Rows:
    def __init__(self, qkv_rows, out_rows, size):
        self.qkv, self.out = qkv_rows, out_rows
        self.shard = qkv_rows + out_rows
        self.total = self.shard * size
        self.inner = out_rows * size
        self.head = self.inner // HEADS
        cut = self.shard % 16 == 0
        self.qkv_cut = -(-qkv_rows // 16) * 16 if cut else self.shard
        self.out_cut = qkv_rows // 16 * 16 if cut else 0
        self.qkv_total = self.qkv_cut * size
        self.out_total = (self.shard - self.out_cut) * size

    def spans(self, first, count, per_shard, stride, shift):
        found = []
        row = first
        while row < first + count:
            block, inside = divmod(row, per_shard)
            length = min(per_shard - inside, first + count - row)
            place = block * stride + shift + inside
            if found and found[-1][0] + found[-1][1] == place:
                found[-1] = (found[-1][0], found[-1][1] + length)
            else:
                found.append((place, length))
            row += length
        return found

    def qkv_spans(self, which, head, stride):
        return self.spans(which * self.inner + head * self.head, self.head, self.qkv, stride, 0)

    def out_spans(self, head, cut):
        stride = self.shard - cut
        return self.spans(head * self.head, self.head, self.out, stride, self.qkv - cut)

    def qkv_weight(self, ref):
        if self.qkv_cut == self.shard:
            return ref[...].reshape(self.total, -1)
        return ref[:, : self.qkv_cut, :].reshape(self.qkv_total, -1)

    def out_weight(self, ref):
        if self.out_cut == 0:
            return ref[...].reshape(self.total, -1)
        return ref[:, self.out_cut :, :].reshape(self.out_total, -1)


def read_rows(ref, spans):
    parts = [ref[place : place + length, :] for place, length in spans]
    return parts[0] if len(parts) == 1 else jnp.concatenate(parts, axis=0)


def write_rows(ref, spans, value):
    done = 0
    for place, length in spans:
        ref[place : place + length, :] = value[done : done + length, :]
        done += length


def inverse_size(values):
    return lax.rsqrt(jnp.mean(values * values, axis=-1, keepdims=True) + EPSILON)


def norm_back(values, inverse, gain, grad):
    scaled = grad * gain
    middle = jnp.mean(scaled * values, axis=-1, keepdims=True)
    grad_values = inverse * scaled - values * (inverse * inverse * inverse * middle)
    grad_gain = jnp.sum(grad * (values * inverse), axis=0, keepdims=True)
    return grad_values, grad_gain


def shares_of(queries, keys, allowed, live, scale):
    scores = [tn(key, query) for key, query in zip(keys, queries)]
    weights = [jnp.exp(jnp.where(allowed, score * scale, MASKED)) for score in scores]
    totals = [jnp.sum(weight, axis=0, keepdims=True) + (1.0 - live) for weight in weights]
    return [weight * (1.0 / total) for weight, total in zip(weights, totals)]


def attend_back(queries, keys, values, shares, shares_low, grads, scale):
    grad_shares = [tn(value, grad) for value, grad in zip(values, grads)]
    middles = [jnp.sum(a * b, axis=0, keepdims=True) for a, b in zip(shares, grad_shares)]
    grad_scores = [
        (share * (grad_share - middle) * scale).astype(BF16)
        for share, grad_share, middle in zip(shares, grad_shares, middles)
    ]
    return (
        [nn(key, grad_score) for key, grad_score in zip(keys, grad_scores)],
        [nt(query, grad_score) for query, grad_score in zip(queries, grad_scores)],
        [nt(grad, share) for grad, share in zip(grads, shares_low)],
    )


def clips_at(clips, frames):
    counts, times, numbers = (jnp.zeros_like(frames) for _ in range(3))
    for clip in range(clips.shape[1]):
        start = clips[1, clip] // FRAME
        member = (frames >= start) & (frames < start + clips[0, clip])
        counts = jnp.where(member, clips[2, clip] * clips[3, clip], counts)
        times = jnp.where(member, frames - start, times)
        numbers = jnp.where(member, clip + 1, numbers)
    return counts, times, numbers


def ids(shape, dim):
    return lax.broadcasted_iota(jnp.int32, shape, dim)


def space_masks(clips):
    count = clips_at(clips, lax.axis_index("ctx").astype(jnp.int32))[0]
    return ids((FRAME, FRAME), 0) < count, (ids((1, FRAME), 1) < count).astype(F32)


def time_masks(clips, near, slots):
    rank = lax.axis_index("ctx")
    token = ids((1, FRAME), 1)
    slot = lax.rem(token, slots)
    counts, times, numbers = clips_at(clips, (rank // near) * near + token // slots)
    alive = lax.rem(rank, near) * slots + slot < counts
    group = (numbers * FRAME + slot).astype(F32)
    keys = jnp.where(alive, group, -1.0)
    allowed = jnp.broadcast_to(keys, (FRAME, FRAME)).T == group
    return allowed, alive.astype(F32), times.astype(F32)


def turn_tables(times, half):
    frequency = jnp.exp(ids((half, FRAME), 0).astype(F32) * (-math.log(ROPE_BASE) / half))
    angles = frequency * times
    cosine, sine = jnp.cos(angles), jnp.sin(angles)
    return jnp.concatenate([cosine, cosine], axis=0), jnp.concatenate([-sine, sine], axis=0)


def out_columns(rows):
    return lax.rem(ids((1, rows.total), 1), rows.shard) >= rows.qkv


def weight_copies(layout, order, pieces, target, sems, which):
    count = target.shape[1]
    return [
        pltpu.make_async_copy(
            pieces[piece].at[pl.ds(first, count)], target.at[order[index]], sems.at[which, index]
        )
        for index, (piece, first) in enumerate(layout)
    ]


def gate(rows, *events, others=()):
    anywhere = pl.BlockSpec(memory_space=pl.ANY)
    arrays = (rows, *others)
    count = len(arrays)
    results = pl.pallas_call(
        lambda *refs: None,
        out_shape=tuple(jax.ShapeDtypeStruct(array.shape, array.dtype) for array in arrays),
        in_specs=[anywhere] * (count + len(events)),
        out_specs=(anywhere,) * count,
        input_output_aliases={index: index for index in range(count)},
        compiler_params=pltpu.CompilerParams(vmem_limit_bytes=1024 * 1024),
    )(*arrays, *events)
    return results if others else results[0]


def start_weights(layouts, order, pieces, space, time, sems):
    def start(first, second):
        for copy in weight_copies(first, order, pieces, space, sems, 0):
            copy.start()
        for copy in weight_copies(second, order, pieces, time, sems, 1):
            copy.start()

    plane = order[len(layouts[0])]

    @pl.when(plane == 0)
    def _():
        start(layouts[0], layouts[1])

    @pl.when(plane != 0)
    def _():
        start(layouts[1], layouts[0])


def wait_weights(layouts, order, pieces, target, sems, which):
    for copy in weight_copies(layouts[0], order, pieces, target, sems, which):
        copy.wait()


def give(direct, stage, outs):
    if not direct:
        outs[0][...] = stage[...]
        return
    core = lax.rem(lax.axis_index("ctx"), 2)
    length = FRAME // (2 * direct)
    for chip in range(direct):
        for out, to in zip(outs, (core, 1 - core)):
            source = pl.ds(pl.multiple_of((2 * chip + to) * length, 16), length)
            out[chip * length : (chip + 1) * length, :] = stage[source, :]


def join(direct, own, from_twin, *outs):
    rank = lax.axis_index("ctx")
    core, chip = lax.rem(rank, 2), lax.rem(rank // 2, direct)
    length = own.shape[0] // direct
    for distance, out in enumerate(outs):
        source = pl.ds(pl.multiple_of((chip ^ distance) * length, 16), length)
        out[pl.ds(pl.multiple_of(core * length, 16), length), :] = own[source, :]
        out[pl.ds(pl.multiple_of((1 - core) * length, 16), length), :] = from_twin[source, :]


def collect(direct, arrived, stage):
    if not direct:
        return arrived[0]
    chip = lax.rem(lax.axis_index("ctx") // 2, direct)
    length = arrived[0].shape[0]
    for distance, part in enumerate(arrived):
        target = pl.ds(pl.multiple_of((chip ^ distance) * length, 16), length)
        stage[target, :] = part[...]
    return stage


def front(rows, layouts, order_of, direct, clips, tokens, gains, *refs):
    sends = 2 if direct else 1
    pieces, refs = refs[: -9 - sends], refs[-9 - sends :]
    hidden, saved, shares_out, space, time = refs[:5]
    project, mixed, stage, sems = refs[-4:]
    order = order_of()
    start_weights(layouts, order, pieces, space, time, sems)
    allowed, live = space_masks(clips)
    values = tokens[0].astype(F32)
    normed = (values * inverse_size(values) * gains[:1]).astype(BF16)
    mixed[...] = jnp.zeros_like(mixed)
    stride = rows.qkv_cut
    length = stride if len(layouts[0]) > 1 else rows.total

    def project_from(layout):
        for index, (piece, first) in enumerate(layout):
            target = pl.ds(pl.multiple_of(order[index] * length, 16), length)
            project[target, :] = nt(pieces[piece][first : first + length, :], normed)

    pl.when(order[-1] == 0)(lambda: project_from(layouts[0]))
    pl.when(order[-1] != 0)(lambda: project_from(layouts[1]))
    saved[...] = project[...].astype(BF16)
    scale = rows.head ** (-0.5)
    queries, keys, values_in = (
        [read_rows(project, rows.qkv_spans(which, head, stride)).astype(BF16) for head in range(HEADS)]
        for which in range(3)
    )
    shares = [share.astype(BF16) for share in shares_of(queries, keys, allowed, live, scale)]
    blended = [nn(value, share) * live for value, share in zip(values_in, shares)]
    for head in range(HEADS):
        shares_out[head] = shares[head]
        write_rows(mixed, rows.out_spans(head, rows.out_cut), blended[head])
    wait_weights(layouts, order, pieces, space, sems, 0)
    update = tn(mixed[...].astype(BF16), rows.out_weight(space))
    low = (values + update).astype(BF16)
    hidden[...] = low
    values = low.astype(F32)
    normed = (values * inverse_size(values) * gains[1:]).astype(BF16)
    wait_weights(layouts, order, pieces, time, sems, 1)
    both = nt(jnp.concatenate([normed, tokens[1]], axis=0), time[...].reshape(rows.total, -1))
    count = values.shape[0]
    stage[...] = jnp.where(out_columns(rows), both[count:], both[:count]).astype(BF16)
    give(direct, stage, refs[5:-4])


def time_core(rows, near, slots, direct, clips, *refs):
    project, result, stage = refs[-3:]
    arrived = collect(direct, refs[: direct or 1], stage)
    allowed, live, times = time_masks(clips, near, slots)
    for first in range(0, rows.total, FRAME):
        project[first : first + FRAME, :] = arrived[:, first : first + FRAME].astype(F32).T
    scale = rows.head ** (-0.5)
    half = rows.head // 2
    cosine, sine = turn_tables(times, half)

    def swapped(vectors):
        return jnp.concatenate([vectors[half:], vectors[:half]], axis=0)

    heads = range(HEADS)
    turned = []
    for which in range(2):
        vectors = [read_rows(project, rows.qkv_spans(which, head, rows.shard)) for head in heads]
        turned.append([(part * cosine + swapped(part) * sine).astype(BF16) for part in vectors])
    queries, keys = turned
    values = [read_rows(project, rows.qkv_spans(2, head, rows.shard)).astype(BF16) for head in heads]
    grads = [(read_rows(project, rows.out_spans(head, 0)) * live).astype(BF16) for head in heads]
    shares = shares_of(queries, keys, allowed, live, scale)
    shares_low = [share.astype(BF16) for share in shares]
    blended = [nn(value, share) * live for value, share in zip(values, shares_low)]
    parts = attend_back(queries, keys, values, shares, shares_low, grads, scale)
    for head in heads:
        write_rows(result, rows.out_spans(head, 0), blended[head])
        for which in range(2):
            turned_grad = parts[which][head].astype(BF16).astype(F32)
            write_rows(
                result,
                rows.qkv_spans(which, head, rows.shard),
                turned_grad * cosine - swapped(turned_grad) * sine,
            )
        write_rows(result, rows.qkv_spans(2, head, rows.shard), parts[2][head])
    for first in range(0, rows.total, FRAME):
        stage[:, first : first + FRAME] = result[first : first + FRAME, :].T.astype(BF16)
    give(direct, stage, refs[direct or 1 : -3])


def time_back(rows, direct, clips, *refs):
    arrived, refs = refs[: direct or 1], refs[direct or 1 :]
    tokens, gains, time, space, hidden, saved, shares_in = refs[:7]
    grad_hidden_out, grad_normed_out, gain_parts, project, grad_project, stage = refs[7:]
    arrived = collect(direct, arrived, stage)
    live = space_masks(clips)[1]
    received = arrived[...]
    mask = jnp.broadcast_to(out_columns(rows), received.shape)
    left = jnp.where(mask, jnp.zeros_like(received), received)
    grad_normed = nn(left, time[...].reshape(rows.total, -1)).astype(BF16).astype(F32)
    values = hidden[...].astype(F32)
    grad_front, grad_time_gain = norm_back(values, inverse_size(values), gains[1:], grad_normed)
    grad_hidden = (tokens[1].astype(F32) + grad_front).astype(BF16)
    grad_hidden_out[...] = grad_hidden

    project[...] = nt(rows.out_weight(space), grad_hidden)
    grad_project[...] = jnp.zeros_like(grad_project)
    scale = rows.head ** (-0.5)
    heads = range(HEADS)
    spans = [[rows.qkv_spans(which, head, rows.qkv_cut) for head in heads] for which in range(3)]
    queries, keys, values_in = (
        [read_rows(saved, where).astype(BF16) for where in places] for places in spans
    )
    grads = [
        (read_rows(project, rows.out_spans(head, rows.out_cut)) * live).astype(BF16) for head in heads
    ]
    shares_low = [shares_in[head] for head in heads]
    shares = [share.astype(F32) for share in shares_low]
    parts = attend_back(queries, keys, values_in, shares, shares_low, grads, scale)
    for places, found in zip(spans, parts):
        for where, part in zip(places, found):
            write_rows(grad_project, where, part)
    grad_normed = tn(grad_project[...].astype(BF16), rows.qkv_weight(space)).astype(BF16)
    grad_normed_out[...] = grad_normed
    values = tokens[0].astype(F32)
    normed = values * inverse_size(values)
    grad_space_gain = jnp.sum(grad_normed.astype(F32) * normed, axis=0, keepdims=True)
    both_gains = jnp.concatenate([grad_space_gain, grad_time_gain], axis=0).astype(gain_parts.dtype)
    gain_parts[...] = jnp.broadcast_to(both_gains[None], gain_parts.shape)


def finish(rows, direct, *refs):
    arrived, refs = refs[: direct or 1], refs[direct or 1 :]
    tokens, gains, time, hidden, grad_hidden, grad_normed, output, grad_tokens, stage = refs
    received = collect(direct, arrived, stage)[...]
    mask = jnp.broadcast_to(out_columns(rows), received.shape)
    left = jnp.where(mask, received, jnp.zeros_like(received))
    update = nn(left, time[...].reshape(rows.total, -1))
    output[...] = (hidden[...].astype(F32) + update).astype(BF16)
    values = tokens[0].astype(F32)
    grad = grad_normed[...].astype(F32)
    grad_values, _ = norm_back(values, inverse_size(values), gains[:1], grad)
    grad_tokens[...] = (grad_hidden[...].astype(F32) + grad_values).astype(BF16)


def call(body, out_shapes, scratch, clips, operands):
    clips = () if clips is None else (clips,)
    whole = pl.BlockSpec(memory_space=pltpu.VMEM)
    scalars = pl.BlockSpec(memory_space=pltpu.SMEM)
    return pl.pallas_call(
        body,
        out_shape=out_shapes,
        in_specs=[scalars] * len(clips) + [whole] * len(operands),
        out_specs=jax.tree.map(lambda _: whole, out_shapes),
        scratch_shapes=scratch,
        compiler_params=pltpu.CompilerParams(vmem_limit_bytes=VMEM_LIMIT),
    )(*clips, *operands)


def gather_ring(space_rows, time_rows, size, others):
    chips = size // 2
    chain = chips // 2
    shard = space_rows.shape[0]

    def chip_at(place):
        place = place % chips
        return 2 * place if place < chain else 2 * (chips - 1 - place) + 1

    ring_pairs = []
    for place in range(chips):
        ring_pairs.append((2 * chip_at(place), 2 * chip_at(place + 1)))
        ring_pairs.append((2 * chip_at(place) + 1, 2 * chip_at(place - 1) + 1))
    planes = lax.axis_size("dp")
    plane = lax.rem(lax.axis_index("dp"), 2)

    def ring(rows):
        return lax.ppermute(rows, "ctx", ring_pairs)

    def across(rows):
        return lax.ppermute(rows, "dp", [(index, index ^ 1) for index in range(planes)])

    def twin(rows):
        return lax.ppermute(rows, "ctx", [(index, index ^ 1) for index in range(size)])

    own = jnp.where(plane == 0, space_rows, time_rows)
    own_other = jnp.where(plane == 0, time_rows, space_rows)
    t0 = twin(own)
    o1 = ring(own)
    t1 = ring(t0)
    t0_other = twin(own_other)
    o2 = ring(o1)
    x_o1 = across(o1)
    o1_twin = twin(o1)
    o2 = gate(o2, t1, o1_twin, t0_other)
    t2 = ring(t1)
    x_o1_twin = twin(x_o1)
    x_t1 = across(t1)
    t1_twin = twin(t1)
    t2 = gate(t2, o2, t1_twin)
    o3 = ring(o2)
    o3 = gate(o3, t2, x_o1)
    o2_twin = twin(o2)
    t3 = ring(t2)
    t2_twin = twin(t2)
    x_t1, *others = gate(x_t1, t3, x_o1_twin, t2_twin, others=others)
    o4 = ring(o3)
    o4 = gate(o4, x_t1, t3)
    x_o3 = across(o3)
    o3_twin = twin(o3)
    x_o2 = ring(x_o1)
    t3_twin = twin(t3)
    x_t1_twin = twin(x_t1)
    x_t2 = ring(x_t1)
    x_o4 = across(o4)
    o4_twin = twin(o4)
    x_t2 = gate(x_t2, o4_twin, t3_twin, x_o3, x_o2)
    x_t3 = ring(x_t2)
    x_o2_twin = twin(x_o2)
    x_t2_twin = twin(x_t2)
    x_o3_twin = twin(x_o3)
    x_o4_twin = twin(x_o4)
    x_t3_twin = twin(x_t3)
    mine = {"o0": (own, 0), "t0": (t0, 0)}
    other = {"o0": (own_other, 0), "t0": (t0_other, 0)}
    mine |= {"o1": (o1, 0), "o1_twin": (o1_twin, 0)}
    other |= {"o1": (x_o1, 0), "o1_twin": (x_o1_twin, 0)}
    mine |= {"t1": (t1, 0), "t1_twin": (t1_twin, 0)}
    other |= {"t1": (x_t1, 0), "t1_twin": (x_t1_twin, 0)}
    mine |= {"o2": (o2, 0), "o2_twin": (o2_twin, 0)}
    other |= {"o2": (x_o2, 0), "o2_twin": (x_o2_twin, 0)}
    mine |= {"t2": (t2, 0), "t2_twin": (t2_twin, 0)}
    other |= {"t2": (x_t2, 0), "t2_twin": (x_t2_twin, 0)}
    mine |= {"o3": (o3, 0), "o3_twin": (o3_twin, 0)}
    other |= {"o3": (x_o3, 0), "o3_twin": (x_o3_twin, 0)}
    mine |= {"t3": (t3, 0), "t3_twin": (t3_twin, 0)}
    other |= {"t3": (x_t3, 0), "t3_twin": (x_t3_twin, 0)}
    mine |= {"o4": (o4, 0), "o4_twin": (o4_twin, 0)}
    other |= {"o4": (x_o4, 0), "o4_twin": (x_o4_twin, 0)}
    names = ["o0", "t0", "o1", "o2", "o3", "o4", "t1", "t2", "t3"]
    twins = names[2:]

    def order_of():
        rank = lax.axis_index("ctx")
        chip, core = rank // 2, lax.rem(rank, 2)
        column, level = lax.rem(chip, 2), chip // 2
        place = jnp.where(column == 0, level, chips - 1 - level)

        def came(carrier, name):
            steps, shard_core = int(name[1]), carrier if name[0] == "o" else 1 - carrier
            at = lax.rem(place + steps * (2 * carrier - 1) + chips, chips)
            return 2 * jnp.where(at < chain, 2 * at, 2 * (chips - 1 - at) + 1) + shard_core

        order = [came(core, name) for name in names] + [came(1 - core, name) for name in twins]
        return order + [lax.rem(lax.axis_index("dp"), 2)]

    pieces, layouts = [], ([], [])
    for half, found in enumerate((mine, other)):
        for name in names + [name + "_twin" for name in twins]:
            array, first = found[name]
            place_in = [index for index, piece in enumerate(pieces) if piece is array]
            if not place_in:
                place_in = [len(pieces)]
                pieces.append(array)
            layouts[half].append((place_in[0], first * shard))
    return pieces, layouts, order_of, others


def gather_weights(space_rows, time_rows, size, others):
    if size == 16 and lax.axis_size("dp") % 2 == 0:
        return gather_ring(space_rows, time_rows, size, others)
    shard, features = space_rows.shape
    gathered = lax.all_gather(jnp.concatenate([space_rows, time_rows], axis=0), "ctx", axis=0)
    gathered = gathered.reshape(size, 2, shard, features)
    halves = [gathered[:, half].reshape(size * shard, features) for half in range(2)]
    return halves, ([(0, 0)], [(1, 0)]), lambda: [0, 0], others


def shards(
    tokens,
    cotangent,
    clip_frames,
    clip_offsets,
    clip_heights,
    clip_widths,
    spatial_gain,
    spatial_qkv,
    spatial_out,
    temporal_gain,
    temporal_qkv,
    temporal_out,
):
    size = lax.axis_size("ctx")
    everyone = lax.axis_size("dp") * size
    count, features = tokens.shape[1], tokens.shape[2]
    assert count == FRAME and FRAME % size == 0
    near = size // 2
    slots = FRAME // near
    rows = Rows(spatial_qkv.shape[0], spatial_out.shape[0], size)
    both_tokens = jnp.concatenate([tokens, cotangent], axis=0)
    both_gains = jnp.stack([spatial_gain, temporal_gain])
    clips = jnp.concatenate([clip_frames, clip_offsets, clip_heights, clip_widths], axis=0)
    pieces, layouts, order_of, others = gather_weights(
        jnp.concatenate([spatial_qkv, spatial_out], axis=0),
        jnp.concatenate([temporal_qkv, temporal_out], axis=0),
        size,
        (both_tokens, both_gains, clips),
    )
    both_tokens, both_gains, clips = others
    wide = pltpu.VMEM((rows.total, FRAME), F32)
    qkv_wide = pltpu.VMEM((rows.qkv_total, FRAME), F32)
    out_wide = pltpu.VMEM((rows.out_total, FRAME), F32)
    blocks = len(layouts[0])
    sems = pltpu.SemaphoreType.DMA((2, blocks))
    weight_shape = jax.ShapeDtypeStruct((blocks, rows.total // blocks, features), BF16)
    groups = [list(range(first, first + near)) for first in range(0, size, near)]

    direct = 4 if near == 8 and slots % 16 == 0 else 0
    part = jax.ShapeDtypeStruct((FRAME // 2 if direct else FRAME, rows.total), BF16)
    parts = (part,) * (2 if direct else 1)
    stage = pltpu.VMEM((FRAME, rows.total), BF16)

    def exchange(sent):
        if not direct:
            arrived = lax.all_to_all(
                sent[0].reshape(near, slots, rows.total),
                "ctx",
                split_axis=0,
                concat_axis=0,
                axis_index_groups=groups,
                tiled=True,
            )
            return [arrived.reshape(FRAME, rows.total)]
        own, to_twin = sent
        from_twin = lax.ppermute(to_twin, "ctx", [(index, index ^ 1) for index in range(size)])
        joined = jax.ShapeDtypeStruct((2 * slots, rows.total), BF16)
        here, *away = call(
            functools.partial(join, direct), (joined,) * direct, [], None, (own, from_twin)
        )
        return [here] + [
            lax.ppermute(rows_away, "ctx", [(index, index ^ (2 * distance)) for index in range(size)])
            for distance, rows_away in list(enumerate(away, 1))[::-1]
        ][::-1]

    hidden, saved, shares, space_weights, time_weights, *sent = call(
        functools.partial(front, rows, layouts, order_of, direct),
        (
            jax.ShapeDtypeStruct((FRAME, features), BF16),
            jax.ShapeDtypeStruct((rows.qkv_total, FRAME), BF16),
            jax.ShapeDtypeStruct((HEADS, FRAME, FRAME), BF16),
            weight_shape,
            weight_shape,
            *parts,
        ),
        [qkv_wide, out_wide, stage, sems],
        clips,
        (both_tokens, both_gains, *pieces),
    )
    arrived = exchange(sent)
    sent = call(
        functools.partial(time_core, rows, near, slots, direct),
        parts,
        [wide, wide, stage],
        clips,
        arrived,
    )
    arrived = exchange(sent)
    whole = jax.ShapeDtypeStruct((FRAME, features), BF16)
    grad_hidden, grad_normed, gains = call(
        functools.partial(time_back, rows, direct),
        (whole, whole, jax.ShapeDtypeStruct((everyone, 2, features), BF16)),
        [out_wide, qkv_wide, stage],
        clips,
        (*arrived, both_tokens, both_gains, time_weights, space_weights, hidden, saved, shares),
    )
    gains = lax.all_to_all(gains, ("dp", "ctx"), split_axis=0, concat_axis=0, tiled=True)
    result, grad_tokens = call(
        functools.partial(finish, rows, direct),
        (whole, whole),
        [stage],
        None,
        (*arrived, both_tokens, both_gains, time_weights, hidden, grad_hidden, grad_normed),
    )
    gain_grads = jnp.sum(gains.astype(F32), axis=0) * (1.0 / math.sqrt(everyone * FRAME))
    return result[None], grad_tokens[None], gain_grads


def solution(mesh):
    return jax.shard_map(
        shards,
        mesh=mesh,
        in_specs=(
            P("dp", "ctx", None),
            P("dp", "ctx", None),
            P("dp", None),
            P("dp", None),
            P("dp", None),
            P("dp", None),
            P(),
            P("ctx", None),
            P("ctx", None),
            P(),
            P("ctx", None),
            P("ctx", None),
        ),
        out_specs=(P("dp", "ctx", None), P("dp", "ctx", None), P()),
        check_vma=False,
    )
```

```python
import functools
import math

import jax
import jax.numpy as jnp
from jax import lax
from jax.experimental import pallas as pl
from jax.experimental.pallas import tpu as pltpu
from jax.sharding import PartitionSpec as P

HEADS = 8
FRAME = 128
EPSILON = 1e-06
ROPE_BASE = 10000.0
MASKED = -1e30
F32 = jnp.float32
BF16 = jnp.bfloat16
VMEM_LIMIT = 12 * 1024 * 1024


def nn(a, b):
    return lax.dot_general(a, b, (((1,), (0,)), ((), ())), preferred_element_type=F32)


def nt(a, b):
    return lax.dot_general(a, b, (((1,), (1,)), ((), ())), preferred_element_type=F32)


def tn(a, b):
    return lax.dot_general(a, b, (((0,), (0,)), ((), ())), preferred_element_type=F32)


class Rows:
    def __init__(self, qkv_rows, out_rows, size):
        self.qkv, self.out = qkv_rows, out_rows
        self.shard = qkv_rows + out_rows
        self.total = self.shard * size
        self.inner = out_rows * size
        self.head = self.inner // HEADS
        cut = self.shard % 16 == 0
        self.qkv_cut = -(-qkv_rows // 16) * 16 if cut else self.shard
        self.out_cut = qkv_rows // 16 * 16 if cut else 0
        self.qkv_total = self.qkv_cut * size
        self.out_total = (self.shard - self.out_cut) * size

    def spans(self, first, count, per_shard, stride, shift):
        found = []
        row = first
        while row < first + count:
            block, inside = divmod(row, per_shard)
            length = min(per_shard - inside, first + count - row)
            place = block * stride + shift + inside
            if found and found[-1][0] + found[-1][1] == place:
                found[-1] = (found[-1][0], found[-1][1] + length)
            else:
                found.append((place, length))
            row += length
        return found

    def qkv_spans(self, which, head, stride):
        return self.spans(which * self.inner + head * self.head, self.head, self.qkv, stride, 0)

    def out_spans(self, head, cut):
        stride = self.shard - cut
        return self.spans(head * self.head, self.head, self.out, stride, self.qkv - cut)

    def qkv_weight(self, ref):
        if self.qkv_cut == self.shard:
            return ref[...].reshape(self.total, -1)
        return ref[:, : self.qkv_cut, :].reshape(self.qkv_total, -1)

    def out_weight(self, ref):
        if self.out_cut == 0:
            return ref[...].reshape(self.total, -1)
        return ref[:, self.out_cut :, :].reshape(self.out_total, -1)


def read_rows(ref, spans):
    parts = [ref[place : place + length, :] for place, length in spans]
    return parts[0] if len(parts) == 1 else jnp.concatenate(parts, axis=0)


def write_rows(ref, spans, value):
    done = 0
    for place, length in spans:
        ref[place : place + length, :] = value[done : done + length, :]
        done += length


def inverse_size(values):
    return lax.rsqrt(jnp.mean(values * values, axis=-1, keepdims=True) + EPSILON)


def norm_back(values, inverse, gain, grad):
    scaled = grad * gain
    middle = jnp.mean(scaled * values, axis=-1, keepdims=True)
    grad_values = inverse * scaled - values * (inverse * inverse * inverse * middle)
    grad_gain = jnp.sum(grad * (values * inverse), axis=0, keepdims=True)
    return grad_values, grad_gain


def shares_of(queries, keys, allowed, live, scale):
    scores = [tn(key, query) for key, query in zip(keys, queries)]
    weights = [jnp.exp(jnp.where(allowed, score * scale, MASKED)) for score in scores]
    totals = [jnp.sum(weight, axis=0, keepdims=True) + (1.0 - live) for weight in weights]
    return [weight * (1.0 / total) for weight, total in zip(weights, totals)]


def attend_back(queries, keys, values, shares, shares_low, grads, scale):
    grad_shares = [tn(value, grad) for value, grad in zip(values, grads)]
    middles = [jnp.sum(a * b, axis=0, keepdims=True) for a, b in zip(shares, grad_shares)]
    grad_scores = [
        (share * (grad_share - middle) * scale).astype(BF16)
        for share, grad_share, middle in zip(shares, grad_shares, middles)
    ]
    return (
        [nn(key, grad_score) for key, grad_score in zip(keys, grad_scores)],
        [nt(query, grad_score) for query, grad_score in zip(queries, grad_scores)],
        [nt(grad, share) for grad, share in zip(grads, shares_low)],
    )


def clips_at(clips, frames):
    counts, times, numbers = (jnp.zeros_like(frames) for _ in range(3))
    for clip in range(clips.shape[1]):
        start = clips[1, clip] // FRAME
        member = (frames >= start) & (frames < start + clips[0, clip])
        counts = jnp.where(member, clips[2, clip] * clips[3, clip], counts)
        times = jnp.where(member, frames - start, times)
        numbers = jnp.where(member, clip + 1, numbers)
    return counts, times, numbers


def ids(shape, dim):
    return lax.broadcasted_iota(jnp.int32, shape, dim)


def space_masks(clips):
    count = clips_at(clips, lax.axis_index("ctx").astype(jnp.int32))[0]
    return ids((FRAME, FRAME), 0) < count, (ids((1, FRAME), 1) < count).astype(F32)


def time_masks(clips, near, slots):
    rank = lax.axis_index("ctx")
    token = ids((1, FRAME), 1)
    slot = lax.rem(token, slots)
    counts, times, numbers = clips_at(clips, (rank // near) * near + token // slots)
    alive = lax.rem(rank, near) * slots + slot < counts
    group = (numbers * FRAME + slot).astype(F32)
    keys = jnp.where(alive, group, -1.0)
    allowed = jnp.broadcast_to(keys, (FRAME, FRAME)).T == group
    return allowed, alive.astype(F32), times.astype(F32)


def turn_tables(times, half):
    frequency = jnp.exp(ids((half, FRAME), 0).astype(F32) * (-math.log(ROPE_BASE) / half))
    angles = frequency * times
    cosine, sine = jnp.cos(angles), jnp.sin(angles)
    return jnp.concatenate([cosine, cosine], axis=0), jnp.concatenate([-sine, sine], axis=0)


def out_columns(rows):
    return lax.rem(ids((1, rows.total), 1), rows.shard) >= rows.qkv


def weight_copies(layout, order, pieces, target, sems, which):
    count = target.shape[1]
    return [
        pltpu.make_async_copy(
            pieces[piece].at[pl.ds(first, count)], target.at[order[index]], sems.at[which, index]
        )
        for index, (piece, first) in enumerate(layout)
    ]


def gate(rows, *events, others=()):
    anywhere = pl.BlockSpec(memory_space=pl.ANY)
    arrays = (rows, *others)
    count = len(arrays)
    results = pl.pallas_call(
        lambda *refs: None,
        out_shape=tuple(jax.ShapeDtypeStruct(array.shape, array.dtype) for array in arrays),
        in_specs=[anywhere] * (count + len(events)),
        out_specs=(anywhere,) * count,
        input_output_aliases={index: index for index in range(count)},
        compiler_params=pltpu.CompilerParams(vmem_limit_bytes=1024 * 1024),
    )(*arrays, *events)
    return results if others else results[0]


def start_weights(layouts, order, pieces, space, time, sems):
    def start(first, second):
        for copy in weight_copies(first, order, pieces, space, sems, 0):
            copy.start()
        for copy in weight_copies(second, order, pieces, time, sems, 1):
            copy.start()

    plane = order[len(layouts[0])]

    @pl.when(plane == 0)
    def _():
        start(layouts[0], layouts[1])

    @pl.when(plane != 0)
    def _():
        start(layouts[1], layouts[0])


def wait_weights(layouts, order, pieces, target, sems, which):
    for copy in weight_copies(layouts[0], order, pieces, target, sems, which):
        copy.wait()


def give(direct, stage, outs):
    if not direct:
        outs[0][...] = stage[...]
        return
    core = lax.rem(lax.axis_index("ctx"), 2)
    length = FRAME // (2 * direct)
    for chip in range(direct):
        for out, to in zip(outs, (core, 1 - core)):
            source = pl.ds(pl.multiple_of((2 * chip + to) * length, 16), length)
            out[chip * length : (chip + 1) * length, :] = stage[source, :]


def join(direct, own, from_twin, *outs):
    rank = lax.axis_index("ctx")
    core, chip = lax.rem(rank, 2), lax.rem(rank // 2, direct)
    length = own.shape[0] // direct
    for distance, out in enumerate(outs):
        source = pl.ds(pl.multiple_of((chip ^ distance) * length, 16), length)
        out[pl.ds(pl.multiple_of(core * length, 16), length), :] = own[source, :]
        out[pl.ds(pl.multiple_of((1 - core) * length, 16), length), :] = from_twin[source, :]


def collect(direct, arrived, stage):
    if not direct:
        return arrived[0]
    chip = lax.rem(lax.axis_index("ctx") // 2, direct)
    length = arrived[0].shape[0]
    for distance, part in enumerate(arrived):
        target = pl.ds(pl.multiple_of((chip ^ distance) * length, 16), length)
        stage[target, :] = part[...]
    return stage


def front(rows, layouts, order_of, direct, clips, tokens, gains, *refs):
    sends = 2 if direct else 1
    pieces, refs = refs[: -9 - sends], refs[-9 - sends :]
    hidden, saved, shares_out, space, time = refs[:5]
    project, mixed, stage, sems = refs[-4:]
    order = order_of()
    start_weights(layouts, order, pieces, space, time, sems)
    allowed, live = space_masks(clips)
    values = tokens[0].astype(F32)
    normed = (values * inverse_size(values) * gains[:1]).astype(BF16)
    mixed[...] = jnp.zeros_like(mixed)
    stride = rows.qkv_cut
    length = stride if len(layouts[0]) > 1 else rows.total

    def project_from(layout):
        for index, (piece, first) in enumerate(layout):
            target = pl.ds(pl.multiple_of(order[index] * length, 16), length)
            project[target, :] = nt(pieces[piece][first : first + length, :], normed)

    pl.when(order[-1] == 0)(lambda: project_from(layouts[0]))
    pl.when(order[-1] != 0)(lambda: project_from(layouts[1]))
    saved[...] = project[...].astype(BF16)
    scale = rows.head ** (-0.5)
    queries, keys, values_in = (
        [read_rows(project, rows.qkv_spans(which, head, stride)).astype(BF16) for head in range(HEADS)]
        for which in range(3)
    )
    shares = [share.astype(BF16) for share in shares_of(queries, keys, allowed, live, scale)]
    blended = [nn(value, share) * live for value, share in zip(values_in, shares)]
    for head in range(HEADS):
        shares_out[head] = shares[head]
        write_rows(mixed, rows.out_spans(head, rows.out_cut), blended[head])
    wait_weights(layouts, order, pieces, space, sems, 0)
    update = tn(mixed[...].astype(BF16), rows.out_weight(space))
    low = (values + update).astype(BF16)
    hidden[...] = low
    values = low.astype(F32)
    normed = (values * inverse_size(values) * gains[1:]).astype(BF16)
    wait_weights(layouts, order, pieces, time, sems, 1)
    both = nt(jnp.concatenate([normed, tokens[1]], axis=0), time[...].reshape(rows.total, -1))
    count = values.shape[0]
    stage[...] = jnp.where(out_columns(rows), both[count:], both[:count]).astype(BF16)
    give(direct, stage, refs[5:-4])


def time_core(rows, near, slots, direct, clips, *refs):
    project, result, stage = refs[-3:]
    arrived = collect(direct, refs[: direct or 1], stage)
    allowed, live, times = time_masks(clips, near, slots)
    for first in range(0, rows.total, FRAME):
        project[first : first + FRAME, :] = arrived[:, first : first + FRAME].astype(F32).T
    scale = rows.head ** (-0.5)
    half = rows.head // 2
    cosine, sine = turn_tables(times, half)

    def swapped(vectors):
        return jnp.concatenate([vectors[half:], vectors[:half]], axis=0)

    heads = range(HEADS)
    turned = []
    for which in range(2):
        vectors = [read_rows(project, rows.qkv_spans(which, head, rows.shard)) for head in heads]
        turned.append([(part * cosine + swapped(part) * sine).astype(BF16) for part in vectors])
    queries, keys = turned
    values = [read_rows(project, rows.qkv_spans(2, head, rows.shard)).astype(BF16) for head in heads]
    grads = [(read_rows(project, rows.out_spans(head, 0)) * live).astype(BF16) for head in heads]
    shares = shares_of(queries, keys, allowed, live, scale)
    shares_low = [share.astype(BF16) for share in shares]
    blended = [nn(value, share) * live for value, share in zip(values, shares_low)]
    parts = attend_back(queries, keys, values, shares, shares_low, grads, scale)
    for head in heads:
        write_rows(result, rows.out_spans(head, 0), blended[head])
        for which in range(2):
            turned_grad = parts[which][head].astype(BF16).astype(F32)
            write_rows(
                result,
                rows.qkv_spans(which, head, rows.shard),
                turned_grad * cosine - swapped(turned_grad) * sine,
            )
        write_rows(result, rows.qkv_spans(2, head, rows.shard), parts[2][head])
    for first in range(0, rows.total, FRAME):
        stage[:, first : first + FRAME] = result[first : first + FRAME, :].T.astype(BF16)
    give(direct, stage, refs[direct or 1 : -3])


def time_back(rows, direct, clips, *refs):
    arrived, refs = refs[: direct or 1], refs[direct or 1 :]
    tokens, gains, time, space, hidden, saved, shares_in = refs[:7]
    grad_hidden_out, grad_normed_out, gain_parts, project, grad_project, stage = refs[7:]
    arrived = collect(direct, arrived, stage)
    live = space_masks(clips)[1]
    received = arrived[...]
    mask = jnp.broadcast_to(out_columns(rows), received.shape)
    left = jnp.where(mask, jnp.zeros_like(received), received)
    grad_normed = nn(left, time[...].reshape(rows.total, -1)).astype(BF16).astype(F32)
    values = hidden[...].astype(F32)
    grad_front, grad_time_gain = norm_back(values, inverse_size(values), gains[1:], grad_normed)
    grad_hidden = (tokens[1].astype(F32) + grad_front).astype(BF16)
    grad_hidden_out[...] = grad_hidden

    project[...] = nt(rows.out_weight(space), grad_hidden)
    grad_project[...] = jnp.zeros_like(grad_project)
    scale = rows.head ** (-0.5)
    heads = range(HEADS)
    spans = [[rows.qkv_spans(which, head, rows.qkv_cut) for head in heads] for which in range(3)]
    queries, keys, values_in = (
        [read_rows(saved, where).astype(BF16) for where in places] for places in spans
    )
    grads = [
        (read_rows(project, rows.out_spans(head, rows.out_cut)) * live).astype(BF16) for head in heads
    ]
    shares_low = [shares_in[head] for head in heads]
    shares = [share.astype(F32) for share in shares_low]
    parts = attend_back(queries, keys, values_in, shares, shares_low, grads, scale)
    for places, found in zip(spans, parts):
        for where, part in zip(places, found):
            write_rows(grad_project, where, part)
    grad_normed = tn(grad_project[...].astype(BF16), rows.qkv_weight(space)).astype(BF16)
    grad_normed_out[...] = grad_normed
    values = tokens[0].astype(F32)
    normed = values * inverse_size(values)
    grad_space_gain = jnp.sum(grad_normed.astype(F32) * normed, axis=0, keepdims=True)
    gain_parts[...] = jnp.concatenate([grad_space_gain, grad_time_gain], axis=0)


def spread(parts, from_twin, outs):
    chip_sum = (parts[...] + from_twin[...]).astype(outs.dtype)
    outs[...] = jnp.broadcast_to(chip_sum[None], outs.shape)


def finish(rows, direct, *refs):
    arrived, refs = refs[: direct or 1], refs[direct or 1 :]
    tokens, gains, time, hidden, grad_hidden, grad_normed, output, grad_tokens, stage = refs
    received = collect(direct, arrived, stage)[...]
    mask = jnp.broadcast_to(out_columns(rows), received.shape)
    left = jnp.where(mask, received, jnp.zeros_like(received))
    update = nn(left, time[...].reshape(rows.total, -1))
    output[...] = (hidden[...].astype(F32) + update).astype(BF16)
    values = tokens[0].astype(F32)
    grad = grad_normed[...].astype(F32)
    grad_values, _ = norm_back(values, inverse_size(values), gains[:1], grad)
    grad_tokens[...] = (grad_hidden[...].astype(F32) + grad_values).astype(BF16)


def call(body, out_shapes, scratch, clips, operands):
    clips = () if clips is None else (clips,)
    whole = pl.BlockSpec(memory_space=pltpu.VMEM)
    scalars = pl.BlockSpec(memory_space=pltpu.SMEM)
    return pl.pallas_call(
        body,
        out_shape=out_shapes,
        in_specs=[scalars] * len(clips) + [whole] * len(operands),
        out_specs=jax.tree.map(lambda _: whole, out_shapes),
        scratch_shapes=scratch,
        compiler_params=pltpu.CompilerParams(vmem_limit_bytes=VMEM_LIMIT),
    )(*clips, *operands)


def gather_ring(space_rows, time_rows, size, others):
    chips = size // 2
    chain = chips // 2
    shard = space_rows.shape[0]

    def chip_at(place):
        place = place % chips
        return 2 * place if place < chain else 2 * (chips - 1 - place) + 1

    ring_pairs = []
    for place in range(chips):
        ring_pairs.append((2 * chip_at(place), 2 * chip_at(place + 1)))
        ring_pairs.append((2 * chip_at(place) + 1, 2 * chip_at(place - 1) + 1))
    planes = lax.axis_size("dp")
    plane = lax.rem(lax.axis_index("dp"), 2)

    def ring(rows):
        return lax.ppermute(rows, "ctx", ring_pairs)

    def across(rows):
        return lax.ppermute(rows, "dp", [(index, index ^ 1) for index in range(planes)])

    def twin(rows):
        return lax.ppermute(rows, "ctx", [(index, index ^ 1) for index in range(size)])

    own = jnp.where(plane == 0, space_rows, time_rows)
    own_other = jnp.where(plane == 0, time_rows, space_rows)
    t0 = twin(own)
    o1 = ring(own)
    t1 = ring(t0)
    t0_other = twin(own_other)
    o2 = ring(o1)
    x_o1 = across(o1)
    o1_twin = twin(o1)
    o2 = gate(o2, t1, o1_twin, t0_other)
    t2 = ring(t1)
    x_o1_twin = twin(x_o1)
    x_t1 = across(t1)
    t1_twin = twin(t1)
    t2 = gate(t2, o2, t1_twin)
    o3 = ring(o2)
    o3 = gate(o3, t2, x_o1)
    o2_twin = twin(o2)
    t3 = ring(t2)
    t2_twin = twin(t2)
    x_t1, *others = gate(x_t1, t3, x_o1_twin, t2_twin, others=others)
    o4 = ring(o3)
    o4 = gate(o4, x_t1, t3)
    x_o3 = across(o3)
    o3_twin = twin(o3)
    x_o2 = ring(x_o1)
    t3_twin = twin(t3)
    x_t1_twin = twin(x_t1)
    x_t2 = ring(x_t1)
    x_o4 = across(o4)
    o4_twin = twin(o4)
    x_t2 = gate(x_t2, o4_twin, t3_twin, x_o3, x_o2)
    x_t3 = ring(x_t2)
    x_o2_twin = twin(x_o2)
    x_t2_twin = twin(x_t2)
    x_o3_twin = twin(x_o3)
    x_t3_twin = twin(x_t3)
    x_o4_twin = twin(x_o4)
    mine = {"o0": (own, 0), "t0": (t0, 0)}
    other = {"o0": (own_other, 0), "t0": (t0_other, 0)}
    mine |= {"o1": (o1, 0), "o1_twin": (o1_twin, 0)}
    other |= {"o1": (x_o1, 0), "o1_twin": (x_o1_twin, 0)}
    mine |= {"t1": (t1, 0), "t1_twin": (t1_twin, 0)}
    other |= {"t1": (x_t1, 0), "t1_twin": (x_t1_twin, 0)}
    mine |= {"o2": (o2, 0), "o2_twin": (o2_twin, 0)}
    other |= {"o2": (x_o2, 0), "o2_twin": (x_o2_twin, 0)}
    mine |= {"t2": (t2, 0), "t2_twin": (t2_twin, 0)}
    other |= {"t2": (x_t2, 0), "t2_twin": (x_t2_twin, 0)}
    mine |= {"o3": (o3, 0), "o3_twin": (o3_twin, 0)}
    other |= {"o3": (x_o3, 0), "o3_twin": (x_o3_twin, 0)}
    mine |= {"t3": (t3, 0), "t3_twin": (t3_twin, 0)}
    other |= {"t3": (x_t3, 0), "t3_twin": (x_t3_twin, 0)}
    mine |= {"o4": (o4, 0), "o4_twin": (o4_twin, 0)}
    other |= {"o4": (x_o4, 0), "o4_twin": (x_o4_twin, 0)}
    names = ["o0", "t0", "o1", "o2", "o3", "o4", "t1", "t2", "t3"]
    twins = names[2:]

    def order_of():
        rank = lax.axis_index("ctx")
        chip, core = rank // 2, lax.rem(rank, 2)
        column, level = lax.rem(chip, 2), chip // 2
        place = jnp.where(column == 0, level, chips - 1 - level)

        def came(carrier, name):
            steps, shard_core = int(name[1]), carrier if name[0] == "o" else 1 - carrier
            at = lax.rem(place + steps * (2 * carrier - 1) + chips, chips)
            return 2 * jnp.where(at < chain, 2 * at, 2 * (chips - 1 - at) + 1) + shard_core

        order = [came(core, name) for name in names] + [came(1 - core, name) for name in twins]
        return order + [lax.rem(lax.axis_index("dp"), 2)]

    pieces, layouts = [], ([], [])
    for half, found in enumerate((mine, other)):
        for name in names + [name + "_twin" for name in twins]:
            array, first = found[name]
            place_in = [index for index, piece in enumerate(pieces) if piece is array]
            if not place_in:
                place_in = [len(pieces)]
                pieces.append(array)
            layouts[half].append((place_in[0], first * shard))
    return pieces, layouts, order_of, others


def gather_weights(space_rows, time_rows, size, others):
    if size == 16 and lax.axis_size("dp") % 2 == 0:
        return gather_ring(space_rows, time_rows, size, others)
    shard, features = space_rows.shape
    gathered = lax.all_gather(jnp.concatenate([space_rows, time_rows], axis=0), "ctx", axis=0)
    gathered = gathered.reshape(size, 2, shard, features)
    halves = [gathered[:, half].reshape(size * shard, features) for half in range(2)]
    return halves, ([(0, 0)], [(1, 0)]), lambda: [0, 0], others


def shards(
    tokens,
    cotangent,
    clip_frames,
    clip_offsets,
    clip_heights,
    clip_widths,
    spatial_gain,
    spatial_qkv,
    spatial_out,
    temporal_gain,
    temporal_qkv,
    temporal_out,
):
    size = lax.axis_size("ctx")
    everyone = lax.axis_size("dp") * size
    count, features = tokens.shape[1], tokens.shape[2]
    assert count == FRAME and FRAME % size == 0
    near = size // 2
    slots = FRAME // near
    rows = Rows(spatial_qkv.shape[0], spatial_out.shape[0], size)
    both_tokens = jnp.concatenate([tokens, cotangent], axis=0)
    both_gains = jnp.stack([spatial_gain, temporal_gain])
    clips = jnp.concatenate([clip_frames, clip_offsets, clip_heights, clip_widths], axis=0)
    pieces, layouts, order_of, others = gather_weights(
        jnp.concatenate([spatial_qkv, spatial_out], axis=0),
        jnp.concatenate([temporal_qkv, temporal_out], axis=0),
        size,
        (both_tokens, both_gains, clips),
    )
    both_tokens, both_gains, clips = others
    wide = pltpu.VMEM((rows.total, FRAME), F32)
    qkv_wide = pltpu.VMEM((rows.qkv_total, FRAME), F32)
    out_wide = pltpu.VMEM((rows.out_total, FRAME), F32)
    blocks = len(layouts[0])
    sems = pltpu.SemaphoreType.DMA((2, blocks))
    weight_shape = jax.ShapeDtypeStruct((blocks, rows.total // blocks, features), BF16)
    groups = [list(range(first, first + near)) for first in range(0, size, near)]

    direct = 4 if near == 8 and slots % 16 == 0 else 0
    part = jax.ShapeDtypeStruct((FRAME // 2 if direct else FRAME, rows.total), BF16)
    parts = (part,) * (2 if direct else 1)
    stage = pltpu.VMEM((FRAME, rows.total), BF16)

    def exchange(sent):
        if not direct:
            arrived = lax.all_to_all(
                sent[0].reshape(near, slots, rows.total),
                "ctx",
                split_axis=0,
                concat_axis=0,
                axis_index_groups=groups,
                tiled=True,
            )
            return [arrived.reshape(FRAME, rows.total)]
        own, to_twin = sent
        from_twin = lax.ppermute(to_twin, "ctx", [(index, index ^ 1) for index in range(size)])
        joined = jax.ShapeDtypeStruct((2 * slots, rows.total), BF16)
        here, *away = call(
            functools.partial(join, direct), (joined,) * direct, [], None, (own, from_twin)
        )
        return [here] + [
            lax.ppermute(rows_away, "ctx", [(index, index ^ (2 * distance)) for index in range(size)])
            for distance, rows_away in list(enumerate(away, 1))[::-1]
        ][::-1]

    hidden, saved, shares, space_weights, time_weights, *sent = call(
        functools.partial(front, rows, layouts, order_of, direct),
        (
            jax.ShapeDtypeStruct((FRAME, features), BF16),
            jax.ShapeDtypeStruct((rows.qkv_total, FRAME), BF16),
            jax.ShapeDtypeStruct((HEADS, FRAME, FRAME), BF16),
            weight_shape,
            weight_shape,
            *parts,
        ),
        [qkv_wide, out_wide, stage, sems],
        clips,
        (both_tokens, both_gains, *pieces),
    )
    arrived = exchange(sent)
    sent = call(
        functools.partial(time_core, rows, near, slots, direct),
        parts,
        [wide, wide, stage],
        clips,
        arrived,
    )
    arrived = exchange(sent)
    whole = jax.ShapeDtypeStruct((FRAME, features), BF16)
    grad_hidden, grad_normed, gains = call(
        functools.partial(time_back, rows, direct),
        (whole, whole, jax.ShapeDtypeStruct((2, features), F32)),
        [out_wide, qkv_wide, stage],
        clips,
        (*arrived, both_tokens, both_gains, time_weights, space_weights, hidden, saved, shares),
    )
    gains = call(
        spread,
        jax.ShapeDtypeStruct((everyone // 2, 2, features), BF16),
        [],
        None,
        (gains, lax.ppermute(gains, "ctx", [(index, index ^ 1) for index in range(size)])),
    )
    gains = lax.all_to_all(
        gains,
        ("dp", "ctx"),
        split_axis=0,
        concat_axis=0,
        axis_index_groups=[list(range(core, everyone, 2)) for core in range(2)],
        tiled=True,
    )
    result, grad_tokens = call(
        functools.partial(finish, rows, direct),
        (whole, whole),
        [stage],
        None,
        (*arrived, both_tokens, both_gains, time_weights, hidden, grad_hidden, grad_normed),
    )
    gain_grads = jnp.sum(gains.astype(F32), axis=0) * (1.0 / math.sqrt(everyone * FRAME))
    return result[None], grad_tokens[None], gain_grads


def solution(mesh):
    return jax.shard_map(
        shards,
        mesh=mesh,
        in_specs=(
            P("dp", "ctx", None),
            P("dp", "ctx", None),
            P("dp", None),
            P("dp", None),
            P("dp", None),
            P("dp", None),
            P(),
            P("ctx", None),
            P("ctx", None),
            P(),
            P("ctx", None),
            P("ctx", None),
        ),
        out_specs=(P("dp", "ctx", None), P("dp", "ctx", None), P()),
        check_vma=False,
    )
```

```python
import functools
import math

import jax
import jax.numpy as jnp
from jax import lax
from jax.experimental import pallas as pl
from jax.experimental.pallas import tpu as pltpu
from jax.sharding import PartitionSpec as P

HEADS = 8
FRAME = 128
EPSILON = 1e-06
ROPE_BASE = 10000.0
MASKED = -1e30
F32 = jnp.float32
BF16 = jnp.bfloat16
VMEM_LIMIT = 12 * 1024 * 1024


def nn(a, b):
    return lax.dot_general(a, b, (((1,), (0,)), ((), ())), preferred_element_type=F32)


def nt(a, b):
    return lax.dot_general(a, b, (((1,), (1,)), ((), ())), preferred_element_type=F32)


def tn(a, b):
    return lax.dot_general(a, b, (((0,), (0,)), ((), ())), preferred_element_type=F32)


class Rows:
    def __init__(self, qkv_rows, out_rows, size):
        self.qkv, self.out = qkv_rows, out_rows
        self.shard = qkv_rows + out_rows
        self.total = self.shard * size
        self.inner = out_rows * size
        self.head = self.inner // HEADS
        cut = self.shard % 16 == 0
        self.qkv_cut = -(-qkv_rows // 16) * 16 if cut else self.shard
        self.out_cut = qkv_rows // 16 * 16 if cut else 0
        self.qkv_total = self.qkv_cut * size
        self.out_total = (self.shard - self.out_cut) * size

    def spans(self, first, count, per_shard, stride, shift):
        found = []
        row = first
        while row < first + count:
            block, inside = divmod(row, per_shard)
            length = min(per_shard - inside, first + count - row)
            place = block * stride + shift + inside
            if found and found[-1][0] + found[-1][1] == place:
                found[-1] = (found[-1][0], found[-1][1] + length)
            else:
                found.append((place, length))
            row += length
        return found

    def qkv_spans(self, which, head, stride):
        return self.spans(which * self.inner + head * self.head, self.head, self.qkv, stride, 0)

    def out_spans(self, head, cut):
        stride = self.shard - cut
        return self.spans(head * self.head, self.head, self.out, stride, self.qkv - cut)

    def qkv_weight(self, ref):
        if self.qkv_cut == self.shard:
            return ref[...].reshape(self.total, -1)
        return ref[:, : self.qkv_cut, :].reshape(self.qkv_total, -1)

    def out_weight(self, ref):
        if self.out_cut == 0:
            return ref[...].reshape(self.total, -1)
        return ref[:, self.out_cut :, :].reshape(self.out_total, -1)


def read_rows(ref, spans):
    parts = [ref[place : place + length, :] for place, length in spans]
    return parts[0] if len(parts) == 1 else jnp.concatenate(parts, axis=0)


def write_rows(ref, spans, value):
    done = 0
    for place, length in spans:
        ref[place : place + length, :] = value[done : done + length, :]
        done += length


def inverse_size(values):
    return lax.rsqrt(jnp.mean(values * values, axis=-1, keepdims=True) + EPSILON)


def norm_back(values, inverse, gain, grad):
    scaled = grad * gain
    middle = jnp.mean(scaled * values, axis=-1, keepdims=True)
    grad_values = inverse * scaled - values * (inverse * inverse * inverse * middle)
    grad_gain = jnp.sum(grad * (values * inverse), axis=0, keepdims=True)
    return grad_values, grad_gain


def shares_of(queries, keys, allowed, live, scale):
    scores = [tn(key, query) for key, query in zip(keys, queries)]
    weights = [jnp.exp(jnp.where(allowed, score * scale, MASKED)) for score in scores]
    totals = [jnp.sum(weight, axis=0, keepdims=True) + (1.0 - live) for weight in weights]
    return [weight * (1.0 / total) for weight, total in zip(weights, totals)]


def attend_back(queries, keys, values, shares, shares_low, grads, scale):
    grad_shares = [tn(value, grad) for value, grad in zip(values, grads)]
    middles = [jnp.sum(a * b, axis=0, keepdims=True) for a, b in zip(shares, grad_shares)]
    grad_scores = [
        (share * (grad_share - middle) * scale).astype(BF16)
        for share, grad_share, middle in zip(shares, grad_shares, middles)
    ]
    return (
        [nn(key, grad_score) for key, grad_score in zip(keys, grad_scores)],
        [nt(query, grad_score) for query, grad_score in zip(queries, grad_scores)],
        [nt(grad, share) for grad, share in zip(grads, shares_low)],
    )


def clips_at(clips, frames):
    counts, times, numbers = (jnp.zeros_like(frames) for _ in range(3))
    for clip in range(clips.shape[1]):
        start = clips[1, clip] // FRAME
        member = (frames >= start) & (frames < start + clips[0, clip])
        counts = jnp.where(member, clips[2, clip] * clips[3, clip], counts)
        times = jnp.where(member, frames - start, times)
        numbers = jnp.where(member, clip + 1, numbers)
    return counts, times, numbers


def ids(shape, dim):
    return lax.broadcasted_iota(jnp.int32, shape, dim)


def space_masks(clips):
    count = clips_at(clips, lax.axis_index("ctx").astype(jnp.int32))[0]
    return ids((FRAME, FRAME), 0) < count, (ids((1, FRAME), 1) < count).astype(F32)


def time_masks(clips, near, slots):
    rank = lax.axis_index("ctx")
    token = ids((1, FRAME), 1)
    slot = lax.rem(token, slots)
    counts, times, numbers = clips_at(clips, (rank // near) * near + token // slots)
    alive = lax.rem(rank, near) * slots + slot < counts
    group = (numbers * FRAME + slot).astype(F32)
    keys = jnp.where(alive, group, -1.0)
    allowed = jnp.broadcast_to(keys, (FRAME, FRAME)).T == group
    return allowed, alive.astype(F32), times.astype(F32)


def turn_tables(times, half):
    frequency = jnp.exp(ids((half, FRAME), 0).astype(F32) * (-math.log(ROPE_BASE) / half))
    angles = frequency * times
    cosine, sine = jnp.cos(angles), jnp.sin(angles)
    return jnp.concatenate([cosine, cosine], axis=0), jnp.concatenate([-sine, sine], axis=0)


def out_columns(rows):
    return lax.rem(ids((1, rows.total), 1), rows.shard) >= rows.qkv


def gate(rows, *events, others=()):
    anywhere = pl.BlockSpec(memory_space=pl.ANY)
    arrays = (rows, *others)
    count = len(arrays)
    results = pl.pallas_call(
        lambda *refs: None,
        out_shape=tuple(jax.ShapeDtypeStruct(array.shape, array.dtype) for array in arrays),
        in_specs=[anywhere] * (count + len(events)),
        out_specs=(anywhere,) * count,
        input_output_aliases={index: index for index in range(count)},
        compiler_params=pltpu.CompilerParams(vmem_limit_bytes=1024 * 1024),
    )(*arrays, *events)
    return results if others else results[0]


def assemble(layouts, order, pieces, space, time):
    count = space.shape[1]

    def put(layout, target):
        for index, (piece, first) in enumerate(layout):
            target[order[index]] = pieces[piece][first : first + count, :]

    @pl.when(order[-1] == 0)
    def _():
        put(layouts[0], space)
        put(layouts[1], time)

    @pl.when(order[-1] != 0)
    def _():
        put(layouts[1], space)
        put(layouts[0], time)


def give(direct, stage, outs):
    if not direct:
        outs[0][...] = stage[...]
        return
    core = lax.rem(lax.axis_index("ctx"), 2)
    length = FRAME // (2 * direct)
    for chip in range(direct):
        for out, to in zip(outs, (core, 1 - core)):
            source = pl.ds(pl.multiple_of((2 * chip + to) * length, 16), length)
            out[chip * length : (chip + 1) * length, :] = stage[source, :]


def join(direct, own, from_twin, *outs):
    rank = lax.axis_index("ctx")
    core, chip = lax.rem(rank, 2), lax.rem(rank // 2, direct)
    length = own.shape[0] // direct
    for distance, out in enumerate(outs):
        source = pl.ds(pl.multiple_of((chip ^ distance) * length, 16), length)
        out[pl.ds(pl.multiple_of(core * length, 16), length), :] = own[source, :]
        out[pl.ds(pl.multiple_of((1 - core) * length, 16), length), :] = from_twin[source, :]


def collect(direct, arrived, stage):
    if not direct:
        return arrived[0]
    chip = lax.rem(lax.axis_index("ctx") // 2, direct)
    length = arrived[0].shape[0]
    for distance, part in enumerate(arrived):
        target = pl.ds(pl.multiple_of((chip ^ distance) * length, 16), length)
        stage[target, :] = part[...]
    return stage


def front(rows, layouts, order_of, direct, clips, tokens, gains, *refs):
    sends = 2 if direct else 1
    pieces, refs = refs[: -8 - sends], refs[-8 - sends :]
    hidden, saved, shares_out, space, time = refs[:5]
    project, mixed, stage = refs[-3:]
    assemble(layouts, order_of(), pieces, space, time)
    allowed, live = space_masks(clips)
    values = tokens[0].astype(F32)
    normed = (values * inverse_size(values) * gains[:1]).astype(BF16)
    mixed[...] = jnp.zeros_like(mixed)
    stride = rows.qkv_cut
    project[...] = nt(rows.qkv_weight(space), normed)
    saved[...] = project[...].astype(BF16)
    scale = rows.head ** (-0.5)
    queries, keys, values_in = (
        [read_rows(project, rows.qkv_spans(which, head, stride)).astype(BF16) for head in range(HEADS)]
        for which in range(3)
    )
    shares = [share.astype(BF16) for share in shares_of(queries, keys, allowed, live, scale)]
    blended = [nn(value, share) * live for value, share in zip(values_in, shares)]
    for head in range(HEADS):
        shares_out[head] = shares[head]
        write_rows(mixed, rows.out_spans(head, rows.out_cut), blended[head])
    update = tn(mixed[...].astype(BF16), rows.out_weight(space))
    low = (values + update).astype(BF16)
    hidden[...] = low
    values = low.astype(F32)
    normed = (values * inverse_size(values) * gains[1:]).astype(BF16)
    both = nt(jnp.concatenate([normed, tokens[1]], axis=0), time[...].reshape(rows.total, -1))
    count = values.shape[0]
    stage[...] = jnp.where(out_columns(rows), both[count:], both[:count]).astype(BF16)
    give(direct, stage, refs[5:-3])


def time_core(rows, near, slots, direct, clips, *refs):
    project, result, stage = refs[-3:]
    arrived = collect(direct, refs[: direct or 1], stage)
    allowed, live, times = time_masks(clips, near, slots)
    for first in range(0, rows.total, FRAME):
        project[first : first + FRAME, :] = arrived[:, first : first + FRAME].astype(F32).T
    scale = rows.head ** (-0.5)
    half = rows.head // 2
    cosine, sine = turn_tables(times, half)

    def swapped(vectors):
        return jnp.concatenate([vectors[half:], vectors[:half]], axis=0)

    heads = range(HEADS)
    turned = []
    for which in range(2):
        vectors = [read_rows(project, rows.qkv_spans(which, head, rows.shard)) for head in heads]
        turned.append([(part * cosine + swapped(part) * sine).astype(BF16) for part in vectors])
    queries, keys = turned
    values = [read_rows(project, rows.qkv_spans(2, head, rows.shard)).astype(BF16) for head in heads]
    grads = [(read_rows(project, rows.out_spans(head, 0)) * live).astype(BF16) for head in heads]
    shares = shares_of(queries, keys, allowed, live, scale)
    shares_low = [share.astype(BF16) for share in shares]
    blended = [nn(value, share) * live for value, share in zip(values, shares_low)]
    parts = attend_back(queries, keys, values, shares, shares_low, grads, scale)
    for head in heads:
        write_rows(result, rows.out_spans(head, 0), blended[head])
        for which in range(2):
            turned_grad = parts[which][head].astype(BF16).astype(F32)
            write_rows(
                result,
                rows.qkv_spans(which, head, rows.shard),
                turned_grad * cosine - swapped(turned_grad) * sine,
            )
        write_rows(result, rows.qkv_spans(2, head, rows.shard), parts[2][head])
    for first in range(0, rows.total, FRAME):
        stage[:, first : first + FRAME] = result[first : first + FRAME, :].T.astype(BF16)
    give(direct, stage, refs[direct or 1 : -3])


def time_back(rows, direct, factor, clips, *refs):
    arrived, refs = refs[: direct or 1], refs[direct or 1 :]
    tokens, gains, time, space, hidden, saved, shares_in = refs[:7]
    grad_hidden_out, grad_normed_out, gain_parts, project, grad_project, stage = refs[7:]
    arrived = collect(direct, arrived, stage)
    live = space_masks(clips)[1]
    received = arrived[...]
    mask = jnp.broadcast_to(out_columns(rows), received.shape)
    left = jnp.where(mask, jnp.zeros_like(received), received)
    grad_normed = nn(left, time[...].reshape(rows.total, -1)).astype(BF16).astype(F32)
    values = hidden[...].astype(F32)
    grad_front, grad_time_gain = norm_back(values, inverse_size(values), gains[1:], grad_normed)
    grad_hidden = (tokens[1].astype(F32) + grad_front).astype(BF16)
    grad_hidden_out[...] = grad_hidden

    project[...] = nt(rows.out_weight(space), grad_hidden)
    grad_project[...] = jnp.zeros_like(grad_project)
    scale = rows.head ** (-0.5)
    heads = range(HEADS)
    spans = [[rows.qkv_spans(which, head, rows.qkv_cut) for head in heads] for which in range(3)]
    queries, keys, values_in = (
        [read_rows(saved, where).astype(BF16) for where in places] for places in spans
    )
    grads = [
        (read_rows(project, rows.out_spans(head, rows.out_cut)) * live).astype(BF16) for head in heads
    ]
    shares_low = [shares_in[head] for head in heads]
    shares = [share.astype(F32) for share in shares_low]
    parts = attend_back(queries, keys, values_in, shares, shares_low, grads, scale)
    for places, found in zip(spans, parts):
        for where, part in zip(places, found):
            write_rows(grad_project, where, part)
    grad_normed = tn(grad_project[...].astype(BF16), rows.qkv_weight(space)).astype(BF16)
    grad_normed_out[...] = grad_normed
    values = tokens[0].astype(F32)
    normed = values * inverse_size(values)
    grad_space_gain = jnp.sum(grad_normed.astype(F32) * normed, axis=0, keepdims=True)
    both_gains = jnp.concatenate([grad_space_gain, grad_time_gain], axis=0) * factor
    both_gains = both_gains.astype(gain_parts.dtype)
    gain_parts[...] = jnp.broadcast_to(both_gains[None], gain_parts.shape)


def finish(rows, direct, *refs):
    arrived, refs = refs[: direct or 1], refs[direct or 1 :]
    tokens, gains, time, hidden, grad_hidden, grad_normed, output, grad_tokens, stage = refs
    received = collect(direct, arrived, stage)[...]
    mask = jnp.broadcast_to(out_columns(rows), received.shape)
    left = jnp.where(mask, received, jnp.zeros_like(received))
    update = nn(left, time[...].reshape(rows.total, -1))
    output[...] = (hidden[...].astype(F32) + update).astype(BF16)
    values = tokens[0].astype(F32)
    grad = grad_normed[...].astype(F32)
    grad_values, _ = norm_back(values, inverse_size(values), gains[:1], grad)
    grad_tokens[...] = (grad_hidden[...].astype(F32) + grad_values).astype(BF16)


def call(body, out_shapes, scratch, clips, operands):
    clips = () if clips is None else (clips,)
    whole = pl.BlockSpec(memory_space=pltpu.VMEM)
    scalars = pl.BlockSpec(memory_space=pltpu.SMEM)
    return pl.pallas_call(
        body,
        out_shape=out_shapes,
        in_specs=[scalars] * len(clips) + [whole] * len(operands),
        out_specs=jax.tree.map(lambda _: whole, out_shapes),
        scratch_shapes=scratch,
        compiler_params=pltpu.CompilerParams(vmem_limit_bytes=VMEM_LIMIT),
    )(*clips, *operands)


def gather_ring(space_rows, time_rows, size, others):
    chips = size // 2
    chain = chips // 2
    shard = space_rows.shape[0]

    def chip_at(place):
        place = place % chips
        return 2 * place if place < chain else 2 * (chips - 1 - place) + 1

    ring_pairs = []
    for place in range(chips):
        ring_pairs.append((2 * chip_at(place), 2 * chip_at(place + 1)))
        ring_pairs.append((2 * chip_at(place) + 1, 2 * chip_at(place - 1) + 1))
    planes = lax.axis_size("dp")
    plane = lax.rem(lax.axis_index("dp"), 2)

    def ring(rows):
        return lax.ppermute(rows, "ctx", ring_pairs)

    def across(rows):
        return lax.ppermute(rows, "dp", [(index, index ^ 1) for index in range(planes)])

    def twin(rows):
        return lax.ppermute(rows, "ctx", [(index, index ^ 1) for index in range(size)])

    own = jnp.where(plane == 0, space_rows, time_rows)
    own_other = jnp.where(plane == 0, time_rows, space_rows)
    t0 = twin(own)
    o1 = ring(own)
    t1 = ring(t0)
    t1 = gate(t1, o1)
    t0_other = twin(own_other)
    o2 = ring(o1)
    x_o1 = across(o1)
    o1_twin = twin(o1)
    o2 = gate(o2, t1, o1_twin, t0_other)
    t2 = ring(t1)
    x_o1_twin = twin(x_o1)
    x_t1 = across(t1)
    t1_twin = twin(t1)
    t2 = gate(t2, o2, t1_twin)
    o3 = ring(o2)
    o3 = gate(o3, t2, x_o1)
    o2_twin = twin(o2)
    t3 = ring(t2)
    t2_twin = twin(t2)
    x_t1, *others = gate(x_t1, t3, x_o1_twin, t2_twin, others=others)
    o4 = ring(o3)
    o4 = gate(o4, x_t1, t3)
    x_o3 = across(o3)
    o3_twin = twin(o3)
    t3_twin = twin(t3)
    x_t1_twin = twin(x_t1)
    x_t2 = ring(x_t1)
    x_o4 = ring(x_o3)
    x_o4_twin = twin(x_o4)
    o4_twin = twin(o4)
    x_o3_twin = twin(x_o3)
    x_o2 = ring(x_o1)
    x_t2 = gate(x_t2, o4_twin, t3_twin, x_o3, x_o2)
    x_t3 = ring(x_t2)
    x_o2_twin = twin(x_o2)
    x_t2_twin = twin(x_t2)
    x_t3_twin = twin(x_t3)
    mine = {"o0": (own, 0), "t0": (t0, 0)}
    other = {"o0": (own_other, 0), "t0": (t0_other, 0)}
    mine |= {"o1": (o1, 0), "o1_twin": (o1_twin, 0)}
    other |= {"o1": (x_o1, 0), "o1_twin": (x_o1_twin, 0)}
    mine |= {"t1": (t1, 0), "t1_twin": (t1_twin, 0)}
    other |= {"t1": (x_t1, 0), "t1_twin": (x_t1_twin, 0)}
    mine |= {"o2": (o2, 0), "o2_twin": (o2_twin, 0)}
    other |= {"o2": (x_o2, 0), "o2_twin": (x_o2_twin, 0)}
    mine |= {"t2": (t2, 0), "t2_twin": (t2_twin, 0)}
    other |= {"t2": (x_t2, 0), "t2_twin": (x_t2_twin, 0)}
    mine |= {"o3": (o3, 0), "o3_twin": (o3_twin, 0)}
    other |= {"o3": (x_o3, 0), "o3_twin": (x_o3_twin, 0)}
    mine |= {"t3": (t3, 0), "t3_twin": (t3_twin, 0)}
    other |= {"t3": (x_t3, 0), "t3_twin": (x_t3_twin, 0)}
    mine |= {"o4": (o4, 0), "o4_twin": (o4_twin, 0)}
    other |= {"o4": (x_o4, 0), "o4_twin": (x_o4_twin, 0)}
    names = ["o0", "t0", "o1", "o2", "o3", "o4", "t1", "t2", "t3"]
    twins = names[2:]

    def order_of():
        rank = lax.axis_index("ctx")
        chip, core = rank // 2, lax.rem(rank, 2)
        column, level = lax.rem(chip, 2), chip // 2
        place = jnp.where(column == 0, level, chips - 1 - level)

        def came(carrier, name):
            steps, shard_core = int(name[1]), carrier if name[0] == "o" else 1 - carrier
            at = lax.rem(place + steps * (2 * carrier - 1) + chips, chips)
            return 2 * jnp.where(at < chain, 2 * at, 2 * (chips - 1 - at) + 1) + shard_core

        order = [came(core, name) for name in names] + [came(1 - core, name) for name in twins]
        return order + [lax.rem(lax.axis_index("dp"), 2)]

    pieces, layouts = [], ([], [])
    for half, found in enumerate((mine, other)):
        for name in names + [name + "_twin" for name in twins]:
            array, first = found[name]
            place_in = [index for index, piece in enumerate(pieces) if piece is array]
            if not place_in:
                place_in = [len(pieces)]
                pieces.append(array)
            layouts[half].append((place_in[0], first * shard))
    return pieces, layouts, order_of, others


def gather_weights(space_rows, time_rows, size, others):
    if size == 16 and lax.axis_size("dp") % 2 == 0:
        return gather_ring(space_rows, time_rows, size, others)
    shard, features = space_rows.shape
    gathered = lax.all_gather(jnp.concatenate([space_rows, time_rows], axis=0), "ctx", axis=0)
    gathered = gathered.reshape(size, 2, shard, features)
    halves = [gathered[:, half].reshape(size * shard, features) for half in range(2)]
    return halves, ([(0, 0)], [(1, 0)]), lambda: [0, 0], others


def shards(
    tokens,
    cotangent,
    clip_frames,
    clip_offsets,
    clip_heights,
    clip_widths,
    spatial_gain,
    spatial_qkv,
    spatial_out,
    temporal_gain,
    temporal_qkv,
    temporal_out,
):
    size = lax.axis_size("ctx")
    everyone = lax.axis_size("dp") * size
    count, features = tokens.shape[1], tokens.shape[2]
    assert count == FRAME and FRAME % size == 0
    near = size // 2
    slots = FRAME // near
    rows = Rows(spatial_qkv.shape[0], spatial_out.shape[0], size)
    both_tokens = jnp.concatenate([tokens, cotangent], axis=0)
    both_gains = jnp.stack([spatial_gain, temporal_gain])
    clips = jnp.concatenate([clip_frames, clip_offsets, clip_heights, clip_widths], axis=0)
    pieces, layouts, order_of, others = gather_weights(
        jnp.concatenate([spatial_qkv, spatial_out], axis=0),
        jnp.concatenate([temporal_qkv, temporal_out], axis=0),
        size,
        (both_tokens, both_gains, clips),
    )
    both_tokens, both_gains, clips = others
    wide = pltpu.VMEM((rows.total, FRAME), F32)
    qkv_wide = pltpu.VMEM((rows.qkv_total, FRAME), F32)
    out_wide = pltpu.VMEM((rows.out_total, FRAME), F32)
    blocks = len(layouts[0])
    weight_shape = jax.ShapeDtypeStruct((blocks, rows.total // blocks, features), BF16)
    groups = [list(range(first, first + near)) for first in range(0, size, near)]

    direct = 4 if near == 8 and slots % 16 == 0 else 0
    part = jax.ShapeDtypeStruct((FRAME // 2 if direct else FRAME, rows.total), BF16)
    parts = (part,) * (2 if direct else 1)
    stage = pltpu.VMEM((FRAME, rows.total), BF16)

    def exchange(sent):
        if not direct:
            arrived = lax.all_to_all(
                sent[0].reshape(near, slots, rows.total),
                "ctx",
                split_axis=0,
                concat_axis=0,
                axis_index_groups=groups,
                tiled=True,
            )
            return [arrived.reshape(FRAME, rows.total)]
        own, to_twin = sent
        from_twin = lax.ppermute(to_twin, "ctx", [(index, index ^ 1) for index in range(size)])
        joined = jax.ShapeDtypeStruct((2 * slots, rows.total), BF16)
        here, *away = call(
            functools.partial(join, direct), (joined,) * direct, [], None, (own, from_twin)
        )
        return [here] + [
            lax.ppermute(rows_away, "ctx", [(index, index ^ (2 * distance)) for index in range(size)])
            for distance, rows_away in list(enumerate(away, 1))[::-1]
        ][::-1]

    hidden, saved, shares, space_weights, time_weights, *sent = call(
        functools.partial(front, rows, layouts, order_of, direct),
        (
            jax.ShapeDtypeStruct((FRAME, features), BF16),
            jax.ShapeDtypeStruct((rows.qkv_total, FRAME), BF16),
            jax.ShapeDtypeStruct((HEADS, FRAME, FRAME), BF16),
            weight_shape,
            weight_shape,
            *parts,
        ),
        [qkv_wide, out_wide, stage],
        clips,
        (both_tokens, both_gains, *pieces),
    )
    arrived = exchange(sent)
    sent = call(
        functools.partial(time_core, rows, near, slots, direct),
        parts,
        [wide, wide, stage],
        clips,
        arrived,
    )
    arrived = exchange(sent)
    whole = jax.ShapeDtypeStruct((FRAME, features), BF16)
    grad_hidden, grad_normed, gains = call(
        functools.partial(time_back, rows, direct, 1.0 / math.sqrt(everyone * FRAME)),
        (whole, whole, jax.ShapeDtypeStruct((everyone, 2, features), BF16)),
        [out_wide, qkv_wide, stage],
        clips,
        (*arrived, both_tokens, both_gains, time_weights, space_weights, hidden, saved, shares),
    )
    gains = lax.all_to_all(gains, ("dp", "ctx"), split_axis=0, concat_axis=0, tiled=True)
    result, grad_tokens = call(
        functools.partial(finish, rows, direct),
        (whole, whole),
        [stage],
        None,
        (*arrived, both_tokens, both_gains, time_weights, hidden, grad_hidden, grad_normed),
    )
    gain_grads = jnp.sum(gains.astype(F32), axis=0)
    return result[None], grad_tokens[None], gain_grads


def solution(mesh):
    return jax.shard_map(
        shards,
        mesh=mesh,
        in_specs=(
            P("dp", "ctx", None),
            P("dp", "ctx", None),
            P("dp", None),
            P("dp", None),
            P("dp", None),
            P("dp", None),
            P(),
            P("ctx", None),
            P("ctx", None),
            P(),
            P("ctx", None),
            P("ctx", None),
        ),
        out_specs=(P("dp", "ctx", None), P("dp", "ctx", None), P()),
        check_vma=False,
    )
```

```python
import functools
import math

import jax
import jax.numpy as jnp
from jax import lax
from jax.experimental import pallas as pl
from jax.experimental.pallas import tpu as pltpu
from jax.sharding import PartitionSpec as P

HEADS = 8
FRAME = 128
EPSILON = 1e-06
ROPE_BASE = 10000.0
MASKED = -1e30
F32 = jnp.float32
BF16 = jnp.bfloat16
VMEM_LIMIT = 12 * 1024 * 1024


def nn(a, b):
    return lax.dot_general(a, b, (((1,), (0,)), ((), ())), preferred_element_type=F32)


def nt(a, b):
    return lax.dot_general(a, b, (((1,), (1,)), ((), ())), preferred_element_type=F32)


def tn(a, b):
    return lax.dot_general(a, b, (((0,), (0,)), ((), ())), preferred_element_type=F32)


class Rows:
    def __init__(self, qkv_rows, out_rows, size):
        self.qkv, self.out = qkv_rows, out_rows
        self.shard = qkv_rows + out_rows
        self.total = self.shard * size
        self.inner = out_rows * size
        self.head = self.inner // HEADS
        cut = self.shard % 16 == 0
        self.qkv_cut = -(-qkv_rows // 16) * 16 if cut else self.shard
        self.out_cut = qkv_rows // 16 * 16 if cut else 0
        self.qkv_total = self.qkv_cut * size
        self.out_total = (self.shard - self.out_cut) * size

    def spans(self, first, count, per_shard, stride, shift):
        found = []
        row = first
        while row < first + count:
            block, inside = divmod(row, per_shard)
            length = min(per_shard - inside, first + count - row)
            place = block * stride + shift + inside
            if found and found[-1][0] + found[-1][1] == place:
                found[-1] = (found[-1][0], found[-1][1] + length)
            else:
                found.append((place, length))
            row += length
        return found

    def qkv_spans(self, which, head, stride):
        return self.spans(which * self.inner + head * self.head, self.head, self.qkv, stride, 0)

    def out_spans(self, head, cut):
        stride = self.shard - cut
        return self.spans(head * self.head, self.head, self.out, stride, self.qkv - cut)

    def qkv_weight(self, ref):
        if self.qkv_cut == self.shard:
            return ref[...].reshape(self.total, -1)
        return ref[:, : self.qkv_cut, :].reshape(self.qkv_total, -1)

    def out_weight(self, ref):
        if self.out_cut == 0:
            return ref[...].reshape(self.total, -1)
        return ref[:, self.out_cut :, :].reshape(self.out_total, -1)


def read_rows(ref, spans):
    parts = [ref[place : place + length, :] for place, length in spans]
    return parts[0] if len(parts) == 1 else jnp.concatenate(parts, axis=0)


def write_rows(ref, spans, value):
    done = 0
    for place, length in spans:
        ref[place : place + length, :] = value[done : done + length, :]
        done += length


def inverse_size(values):
    return lax.rsqrt(jnp.mean(values * values, axis=-1, keepdims=True) + EPSILON)


def norm_back(values, inverse, gain, grad):
    scaled = grad * gain
    middle = jnp.mean(scaled * values, axis=-1, keepdims=True)
    grad_values = inverse * scaled - values * (inverse * inverse * inverse * middle)
    grad_gain = jnp.sum(grad * (values * inverse), axis=0, keepdims=True)
    return grad_values, grad_gain


def shares_of(queries, keys, allowed, live, scale):
    scores = [tn(key, query) for key, query in zip(keys, queries)]
    weights = [jnp.exp(jnp.where(allowed, score * scale, MASKED)) for score in scores]
    totals = [jnp.sum(weight, axis=0, keepdims=True) + (1.0 - live) for weight in weights]
    return [weight * (1.0 / total) for weight, total in zip(weights, totals)]


def attend_back(queries, keys, values, shares, shares_low, grads, scale):
    grad_shares = [tn(value, grad) for value, grad in zip(values, grads)]
    middles = [jnp.sum(a * b, axis=0, keepdims=True) for a, b in zip(shares, grad_shares)]
    grad_scores = [
        (share * (grad_share - middle) * scale).astype(BF16)
        for share, grad_share, middle in zip(shares, grad_shares, middles)
    ]
    return (
        [nn(key, grad_score) for key, grad_score in zip(keys, grad_scores)],
        [nt(query, grad_score) for query, grad_score in zip(queries, grad_scores)],
        [nt(grad, share) for grad, share in zip(grads, shares_low)],
    )


def clips_at(clips, frames):
    counts, times, numbers = (jnp.zeros_like(frames) for _ in range(3))
    for clip in range(clips.shape[1]):
        start = clips[1, clip] // FRAME
        member = (frames >= start) & (frames < start + clips[0, clip])
        counts = jnp.where(member, clips[2, clip] * clips[3, clip], counts)
        times = jnp.where(member, frames - start, times)
        numbers = jnp.where(member, clip + 1, numbers)
    return counts, times, numbers


def ids(shape, dim):
    return lax.broadcasted_iota(jnp.int32, shape, dim)


def space_masks(clips):
    count = clips_at(clips, lax.axis_index("ctx").astype(jnp.int32))[0]
    return ids((FRAME, FRAME), 0) < count, (ids((1, FRAME), 1) < count).astype(F32)


def time_masks(clips, near, slots):
    rank = lax.axis_index("ctx")
    token = ids((1, FRAME), 1)
    slot = lax.rem(token, slots)
    counts, times, numbers = clips_at(clips, (rank // near) * near + token // slots)
    alive = lax.rem(rank, near) * slots + slot < counts
    group = (numbers * FRAME + slot).astype(F32)
    keys = jnp.where(alive, group, -1.0)
    allowed = jnp.broadcast_to(keys, (FRAME, FRAME)).T == group
    return allowed, alive.astype(F32), times.astype(F32)


def turn_tables(times, half):
    frequency = jnp.exp(ids((half, FRAME), 0).astype(F32) * (-math.log(ROPE_BASE) / half))
    angles = frequency * times
    cosine, sine = jnp.cos(angles), jnp.sin(angles)
    return jnp.concatenate([cosine, cosine], axis=0), jnp.concatenate([-sine, sine], axis=0)


def out_columns(rows):
    return lax.rem(ids((1, rows.total), 1), rows.shard) >= rows.qkv


def gate(rows, *events, others=()):
    anywhere = pl.BlockSpec(memory_space=pl.ANY)
    arrays = (rows, *others)
    count = len(arrays)
    results = pl.pallas_call(
        lambda *refs: None,
        out_shape=tuple(jax.ShapeDtypeStruct(array.shape, array.dtype) for array in arrays),
        in_specs=[anywhere] * (count + len(events)),
        out_specs=(anywhere,) * count,
        input_output_aliases={index: index for index in range(count)},
        compiler_params=pltpu.CompilerParams(vmem_limit_bytes=1024 * 1024),
    )(*arrays, *events)
    return results if others else results[0]


def assemble(layouts, order, pieces, space, time):
    count = space.shape[1]

    def put(layout, target):
        for index, (piece, first) in enumerate(layout):
            target[order[index]] = pieces[piece][first : first + count, :]

    @pl.when(order[-1] == 0)
    def _():
        put(layouts[0], space)
        put(layouts[1], time)

    @pl.when(order[-1] != 0)
    def _():
        put(layouts[1], space)
        put(layouts[0], time)


def give(direct, stage, outs):
    if not direct:
        outs[0][...] = stage[...]
        return
    core = lax.rem(lax.axis_index("ctx"), 2)
    length = FRAME // (2 * direct)
    for chip in range(direct):
        for out, to in zip(outs, (core, 1 - core)):
            source = pl.ds(pl.multiple_of((2 * chip + to) * length, 16), length)
            out[chip * length : (chip + 1) * length, :] = stage[source, :]


def join(direct, own, from_twin, *outs):
    rank = lax.axis_index("ctx")
    core, chip = lax.rem(rank, 2), lax.rem(rank // 2, direct)
    length = own.shape[0] // direct
    for distance, out in enumerate(outs):
        source = pl.ds(pl.multiple_of((chip ^ distance) * length, 16), length)
        out[pl.ds(pl.multiple_of(core * length, 16), length), :] = own[source, :]
        out[pl.ds(pl.multiple_of((1 - core) * length, 16), length), :] = from_twin[source, :]


def collect(direct, arrived, stage):
    if not direct:
        return arrived[0]
    chip = lax.rem(lax.axis_index("ctx") // 2, direct)
    length = arrived[0].shape[0]
    for distance, part in enumerate(arrived):
        target = pl.ds(pl.multiple_of((chip ^ distance) * length, 16), length)
        stage[target, :] = part[...]
    return stage


def front(rows, layouts, order_of, direct, clips, tokens, gains, *refs):
    sends = 2 if direct else 1
    pieces, refs = refs[: -8 - sends], refs[-8 - sends :]
    hidden, saved, shares_out, space, time = refs[:5]
    project, mixed, stage = refs[-3:]
    assemble(layouts, order_of(), pieces, space, time)
    allowed, live = space_masks(clips)
    values = tokens[0].astype(F32)
    normed = (values * inverse_size(values) * gains[:1]).astype(BF16)
    mixed[...] = jnp.zeros_like(mixed)
    stride = rows.qkv_cut
    project[...] = nt(rows.qkv_weight(space), normed)
    saved[...] = project[...].astype(BF16)
    scale = rows.head ** (-0.5)
    queries, keys, values_in = (
        [read_rows(project, rows.qkv_spans(which, head, stride)).astype(BF16) for head in range(HEADS)]
        for which in range(3)
    )
    shares = [share.astype(BF16) for share in shares_of(queries, keys, allowed, live, scale)]
    blended = [nn(value, share) * live for value, share in zip(values_in, shares)]
    for head in range(HEADS):
        shares_out[head] = shares[head]
        write_rows(mixed, rows.out_spans(head, rows.out_cut), blended[head])
    update = tn(mixed[...].astype(BF16), rows.out_weight(space))
    low = (values + update).astype(BF16)
    hidden[...] = low
    values = low.astype(F32)
    normed = (values * inverse_size(values) * gains[1:]).astype(BF16)
    both = nt(jnp.concatenate([normed, tokens[1]], axis=0), time[...].reshape(rows.total, -1))
    count = values.shape[0]
    stage[...] = jnp.where(out_columns(rows), both[count:], both[:count]).astype(BF16)
    give(direct, stage, refs[5:-3])


def time_core(rows, near, slots, direct, clips, *refs):
    project, result, stage = refs[-3:]
    arrived = collect(direct, refs[: direct or 1], stage)
    allowed, live, times = time_masks(clips, near, slots)
    for first in range(0, rows.total, FRAME):
        project[first : first + FRAME, :] = arrived[:, first : first + FRAME].astype(F32).T
    scale = rows.head ** (-0.5)
    half = rows.head // 2
    cosine, sine = turn_tables(times, half)

    def swapped(vectors):
        return jnp.concatenate([vectors[half:], vectors[:half]], axis=0)

    heads = range(HEADS)
    turned = []
    for which in range(2):
        vectors = [read_rows(project, rows.qkv_spans(which, head, rows.shard)) for head in heads]
        turned.append([(part * cosine + swapped(part) * sine).astype(BF16) for part in vectors])
    queries, keys = turned
    values = [read_rows(project, rows.qkv_spans(2, head, rows.shard)).astype(BF16) for head in heads]
    grads = [(read_rows(project, rows.out_spans(head, 0)) * live).astype(BF16) for head in heads]
    shares = shares_of(queries, keys, allowed, live, scale)
    shares_low = [share.astype(BF16) for share in shares]
    blended = [nn(value, share) * live for value, share in zip(values, shares_low)]
    parts = attend_back(queries, keys, values, shares, shares_low, grads, scale)
    for head in heads:
        write_rows(result, rows.out_spans(head, 0), blended[head])
        for which in range(2):
            turned_grad = parts[which][head].astype(BF16).astype(F32)
            write_rows(
                result,
                rows.qkv_spans(which, head, rows.shard),
                turned_grad * cosine - swapped(turned_grad) * sine,
            )
        write_rows(result, rows.qkv_spans(2, head, rows.shard), parts[2][head])
    for first in range(0, rows.total, FRAME):
        stage[:, first : first + FRAME] = result[first : first + FRAME, :].T.astype(BF16)
    give(direct, stage, refs[direct or 1 : -3])


def time_back(rows, direct, factor, clips, *refs):
    arrived, refs = refs[: direct or 1], refs[direct or 1 :]
    tokens, gains, time, space, hidden, saved, shares_in = refs[:7]
    grad_hidden_out, grad_normed_out, gain_parts, project, grad_project, stage = refs[7:]
    arrived = collect(direct, arrived, stage)
    live = space_masks(clips)[1]
    received = arrived[...]
    mask = jnp.broadcast_to(out_columns(rows), received.shape)
    left = jnp.where(mask, jnp.zeros_like(received), received)
    grad_normed = nn(left, time[...].reshape(rows.total, -1)).astype(BF16).astype(F32)
    values = hidden[...].astype(F32)
    grad_front, grad_time_gain = norm_back(values, inverse_size(values), gains[1:], grad_normed)
    grad_hidden = (tokens[1].astype(F32) + grad_front).astype(BF16)
    grad_hidden_out[...] = grad_hidden

    project[...] = nt(rows.out_weight(space), grad_hidden)
    grad_project[...] = jnp.zeros_like(grad_project)
    scale = rows.head ** (-0.5)
    heads = range(HEADS)
    spans = [[rows.qkv_spans(which, head, rows.qkv_cut) for head in heads] for which in range(3)]
    queries, keys, values_in = (
        [read_rows(saved, where).astype(BF16) for where in places] for places in spans
    )
    grads = [
        (read_rows(project, rows.out_spans(head, rows.out_cut)) * live).astype(BF16) for head in heads
    ]
    shares_low = [shares_in[head] for head in heads]
    shares = [share.astype(F32) for share in shares_low]
    parts = attend_back(queries, keys, values_in, shares, shares_low, grads, scale)
    for places, found in zip(spans, parts):
        for where, part in zip(places, found):
            write_rows(grad_project, where, part)
    grad_normed = tn(grad_project[...].astype(BF16), rows.qkv_weight(space)).astype(BF16)
    grad_normed_out[...] = grad_normed
    values = tokens[0].astype(F32)
    normed = values * inverse_size(values)
    grad_space_gain = jnp.sum(grad_normed.astype(F32) * normed, axis=0, keepdims=True)
    both_gains = jnp.concatenate([grad_space_gain, grad_time_gain], axis=0) * factor
    both_gains = both_gains.astype(gain_parts.dtype)
    gain_parts[...] = jnp.broadcast_to(both_gains[None], gain_parts.shape)


def finish(rows, direct, *refs):
    arrived, refs = refs[: direct or 1], refs[direct or 1 :]
    tokens, gains, time, hidden, grad_hidden, grad_normed, output, grad_tokens, stage = refs
    received = collect(direct, arrived, stage)[...]
    mask = jnp.broadcast_to(out_columns(rows), received.shape)
    left = jnp.where(mask, received, jnp.zeros_like(received))
    update = nn(left, time[...].reshape(rows.total, -1))
    output[...] = (hidden[...].astype(F32) + update).astype(BF16)
    values = tokens[0].astype(F32)
    grad = grad_normed[...].astype(F32)
    grad_values, _ = norm_back(values, inverse_size(values), gains[:1], grad)
    grad_tokens[...] = (grad_hidden[...].astype(F32) + grad_values).astype(BF16)


def call(body, out_shapes, scratch, clips, operands):
    clips = () if clips is None else (clips,)
    whole = pl.BlockSpec(memory_space=pltpu.VMEM)
    scalars = pl.BlockSpec(memory_space=pltpu.SMEM)
    return pl.pallas_call(
        body,
        out_shape=out_shapes,
        in_specs=[scalars] * len(clips) + [whole] * len(operands),
        out_specs=jax.tree.map(lambda _: whole, out_shapes),
        scratch_shapes=scratch,
        compiler_params=pltpu.CompilerParams(vmem_limit_bytes=VMEM_LIMIT),
    )(*clips, *operands)


def gather_ring(space_rows, time_rows, size, others):
    chips = size // 2
    chain = chips // 2
    shard = space_rows.shape[0]

    def chip_at(place):
        place = place % chips
        return 2 * place if place < chain else 2 * (chips - 1 - place) + 1

    ring_pairs = []
    for place in range(chips):
        ring_pairs.append((2 * chip_at(place), 2 * chip_at(place + 1)))
        ring_pairs.append((2 * chip_at(place) + 1, 2 * chip_at(place - 1) + 1))
    planes = lax.axis_size("dp")
    plane = lax.rem(lax.axis_index("dp"), 2)

    def ring(rows):
        return lax.ppermute(rows, "ctx", ring_pairs)

    def across(rows):
        return lax.ppermute(rows, "dp", [(index, index ^ 1) for index in range(planes)])

    def twin(rows):
        return lax.ppermute(rows, "ctx", [(index, index ^ 1) for index in range(size)])

    own = jnp.where(plane == 0, space_rows, time_rows)
    own_other = jnp.where(plane == 0, time_rows, space_rows)
    t0 = twin(own)
    o1 = ring(own)
    t1 = ring(t0)
    t0_other = twin(own_other)
    o2 = ring(o1)
    x_o1 = across(o1)
    o1_twin = twin(o1)
    o2 = gate(o2, t1, o1_twin, t0_other)
    t2 = ring(t1)
    x_o1_twin = twin(x_o1)
    x_t1 = across(t1)
    t1_twin = twin(t1)
    t2 = gate(t2, o2, t1_twin)
    o3 = ring(o2)
    o3 = gate(o3, t2, x_o1)
    o2_twin = twin(o2)
    t3 = ring(t2)
    t2_twin = twin(t2)
    x_t1, *others = gate(x_t1, t3, x_o1_twin, t2_twin, others=others)
    o4 = ring(o3)
    o4 = gate(o4, x_t1, t3)
    x_o3 = across(o3)
    o3_twin = twin(o3)
    x_o2 = ring(x_o1)
    t3_twin = twin(t3)
    x_t1_twin = twin(x_t1)
    x_t2 = ring(x_t1)
    x_o4 = across(o4)
    o4_twin = twin(o4)
    x_t2 = gate(x_t2, o4_twin, t3_twin, x_o3, x_o2)
    x_t3 = ring(x_t2)
    x_o2_twin = twin(x_o2)
    x_t2_twin = twin(x_t2)
    x_o3_twin = twin(x_o3)
    x_t3_twin = twin(x_t3)
    x_o4_twin = twin(x_o4)
    mine = {"o0": (own, 0), "t0": (t0, 0)}
    other = {"o0": (own_other, 0), "t0": (t0_other, 0)}
    mine |= {"o1": (o1, 0), "o1_twin": (o1_twin, 0)}
    other |= {"o1": (x_o1, 0), "o1_twin": (x_o1_twin, 0)}
    mine |= {"t1": (t1, 0), "t1_twin": (t1_twin, 0)}
    other |= {"t1": (x_t1, 0), "t1_twin": (x_t1_twin, 0)}
    mine |= {"o2": (o2, 0), "o2_twin": (o2_twin, 0)}
    other |= {"o2": (x_o2, 0), "o2_twin": (x_o2_twin, 0)}
    mine |= {"t2": (t2, 0), "t2_twin": (t2_twin, 0)}
    other |= {"t2": (x_t2, 0), "t2_twin": (x_t2_twin, 0)}
    mine |= {"o3": (o3, 0), "o3_twin": (o3_twin, 0)}
    other |= {"o3": (x_o3, 0), "o3_twin": (x_o3_twin, 0)}
    mine |= {"t3": (t3, 0), "t3_twin": (t3_twin, 0)}
    other |= {"t3": (x_t3, 0), "t3_twin": (x_t3_twin, 0)}
    mine |= {"o4": (o4, 0), "o4_twin": (o4_twin, 0)}
    other |= {"o4": (x_o4, 0), "o4_twin": (x_o4_twin, 0)}
    names = ["o0", "t0", "o1", "o2", "o3", "o4", "t1", "t2", "t3"]
    twins = names[2:]

    def order_of():
        rank = lax.axis_index("ctx")
        chip, core = rank // 2, lax.rem(rank, 2)
        column, level = lax.rem(chip, 2), chip // 2
        place = jnp.where(column == 0, level, chips - 1 - level)

        def came(carrier, name):
            steps, shard_core = int(name[1]), carrier if name[0] == "o" else 1 - carrier
            at = lax.rem(place + steps * (2 * carrier - 1) + chips, chips)
            return 2 * jnp.where(at < chain, 2 * at, 2 * (chips - 1 - at) + 1) + shard_core

        order = [came(core, name) for name in names] + [came(1 - core, name) for name in twins]
        return order + [lax.rem(lax.axis_index("dp"), 2)]

    pieces, layouts = [], ([], [])
    for half, found in enumerate((mine, other)):
        for name in names + [name + "_twin" for name in twins]:
            array, first = found[name]
            place_in = [index for index, piece in enumerate(pieces) if piece is array]
            if not place_in:
                place_in = [len(pieces)]
                pieces.append(array)
            layouts[half].append((place_in[0], first * shard))
    return pieces, layouts, order_of, others


def gather_weights(space_rows, time_rows, size, others):
    if size == 16 and lax.axis_size("dp") % 2 == 0:
        return gather_ring(space_rows, time_rows, size, others)
    shard, features = space_rows.shape
    gathered = lax.all_gather(jnp.concatenate([space_rows, time_rows], axis=0), "ctx", axis=0)
    gathered = gathered.reshape(size, 2, shard, features)
    halves = [gathered[:, half].reshape(size * shard, features) for half in range(2)]
    return halves, ([(0, 0)], [(1, 0)]), lambda: [0, 0], others


def shards(
    tokens,
    cotangent,
    clip_frames,
    clip_offsets,
    clip_heights,
    clip_widths,
    spatial_gain,
    spatial_qkv,
    spatial_out,
    temporal_gain,
    temporal_qkv,
    temporal_out,
):
    size = lax.axis_size("ctx")
    everyone = lax.axis_size("dp") * size
    count, features = tokens.shape[1], tokens.shape[2]
    assert count == FRAME and FRAME % size == 0
    near = size // 2
    slots = FRAME // near
    rows = Rows(spatial_qkv.shape[0], spatial_out.shape[0], size)
    both_tokens = jnp.concatenate([tokens, cotangent], axis=0)
    both_gains = jnp.stack([spatial_gain, temporal_gain])
    clips = jnp.concatenate([clip_frames, clip_offsets, clip_heights, clip_widths], axis=0)
    pieces, layouts, order_of, others = gather_weights(
        jnp.concatenate([spatial_qkv, spatial_out], axis=0),
        jnp.concatenate([temporal_qkv, temporal_out], axis=0),
        size,
        (both_tokens, both_gains, clips),
    )
    both_tokens, both_gains, clips = others
    wide = pltpu.VMEM((rows.total, FRAME), F32)
    qkv_wide = pltpu.VMEM((rows.qkv_total, FRAME), F32)
    out_wide = pltpu.VMEM((rows.out_total, FRAME), F32)
    blocks = len(layouts[0])
    weight_shape = jax.ShapeDtypeStruct((blocks, rows.total // blocks, features), BF16)
    groups = [list(range(first, first + near)) for first in range(0, size, near)]

    direct = 4 if near == 8 and slots % 16 == 0 else 0
    part = jax.ShapeDtypeStruct((FRAME // 2 if direct else FRAME, rows.total), BF16)
    parts = (part,) * (2 if direct else 1)
    stage = pltpu.VMEM((FRAME, rows.total), BF16)

    def exchange(sent):
        if not direct:
            arrived = lax.all_to_all(
                sent[0].reshape(near, slots, rows.total),
                "ctx",
                split_axis=0,
                concat_axis=0,
                axis_index_groups=groups,
                tiled=True,
            )
            return [arrived.reshape(FRAME, rows.total)]
        own, to_twin = sent
        from_twin = lax.ppermute(to_twin, "ctx", [(index, index ^ 1) for index in range(size)])
        joined = jax.ShapeDtypeStruct((2 * slots, rows.total), BF16)
        here, *away = call(
            functools.partial(join, direct), (joined,) * direct, [], None, (own, from_twin)
        )
        return [here] + [
            lax.ppermute(rows_away, "ctx", [(index, index ^ (2 * distance)) for index in range(size)])
            for distance, rows_away in list(enumerate(away, 1))[::-1]
        ][::-1]

    hidden, saved, shares, space_weights, time_weights, *sent = call(
        functools.partial(front, rows, layouts, order_of, direct),
        (
            jax.ShapeDtypeStruct((FRAME, features), BF16),
            jax.ShapeDtypeStruct((rows.qkv_total, FRAME), BF16),
            jax.ShapeDtypeStruct((HEADS, FRAME, FRAME), BF16),
            weight_shape,
            weight_shape,
            *parts,
        ),
        [qkv_wide, out_wide, stage],
        clips,
        (both_tokens, both_gains, *pieces),
    )
    arrived = exchange(sent)
    sent = call(
        functools.partial(time_core, rows, near, slots, direct),
        parts,
        [wide, wide, stage],
        clips,
        arrived,
    )
    arrived = exchange(sent)
    whole = jax.ShapeDtypeStruct((FRAME, features), BF16)
    grad_hidden, grad_normed, gains = call(
        functools.partial(time_back, rows, direct, 1.0 / math.sqrt(everyone * FRAME)),
        (whole, whole, jax.ShapeDtypeStruct((everyone, 2, features), BF16)),
        [out_wide, qkv_wide, stage],
        clips,
        (*arrived, both_tokens, both_gains, time_weights, space_weights, hidden, saved, shares),
    )
    gains = lax.all_to_all(gains, ("dp", "ctx"), split_axis=0, concat_axis=0, tiled=True)
    result, grad_tokens = call(
        functools.partial(finish, rows, direct),
        (whole, whole),
        [stage],
        None,
        (*arrived, both_tokens, both_gains, time_weights, hidden, grad_hidden, grad_normed),
    )
    gain_grads = jnp.sum(gains.astype(F32), axis=0)
    return result[None], grad_tokens[None], gain_grads


def solution(mesh):
    return jax.shard_map(
        shards,
        mesh=mesh,
        in_specs=(
            P("dp", "ctx", None),
            P("dp", "ctx", None),
            P("dp", None),
            P("dp", None),
            P("dp", None),
            P("dp", None),
            P(),
            P("ctx", None),
            P("ctx", None),
            P(),
            P("ctx", None),
            P("ctx", None),
        ),
        out_specs=(P("dp", "ctx", None), P("dp", "ctx", None), P()),
        check_vma=False,
    )
```

```python
import functools
import math

import jax
import jax.numpy as jnp
from jax import lax
from jax.experimental import pallas as pl
from jax.experimental.pallas import tpu as pltpu
from jax.sharding import PartitionSpec as P

HEADS = 8
FRAME = 128
EPSILON = 1e-06
ROPE_BASE = 10000.0
MASKED = -1e30
F32 = jnp.float32
BF16 = jnp.bfloat16
VMEM_LIMIT = 12 * 1024 * 1024


def nn(a, b):
    return lax.dot_general(a, b, (((1,), (0,)), ((), ())), preferred_element_type=F32)


def nt(a, b):
    return lax.dot_general(a, b, (((1,), (1,)), ((), ())), preferred_element_type=F32)


def tn(a, b):
    return lax.dot_general(a, b, (((0,), (0,)), ((), ())), preferred_element_type=F32)


class Rows:
    def __init__(self, qkv_rows, out_rows, size):
        self.qkv, self.out = qkv_rows, out_rows
        self.shard = qkv_rows + out_rows
        self.total = self.shard * size
        self.inner = out_rows * size
        self.head = self.inner // HEADS
        cut = self.shard % 16 == 0
        self.qkv_cut = -(-qkv_rows // 16) * 16 if cut else self.shard
        self.out_cut = qkv_rows // 16 * 16 if cut else 0
        self.qkv_total = self.qkv_cut * size
        self.out_total = (self.shard - self.out_cut) * size

    def spans(self, first, count, per_shard, stride, shift):
        found = []
        row = first
        while row < first + count:
            block, inside = divmod(row, per_shard)
            length = min(per_shard - inside, first + count - row)
            place = block * stride + shift + inside
            if found and found[-1][0] + found[-1][1] == place:
                found[-1] = (found[-1][0], found[-1][1] + length)
            else:
                found.append((place, length))
            row += length
        return found

    def qkv_spans(self, which, head, stride):
        return self.spans(which * self.inner + head * self.head, self.head, self.qkv, stride, 0)

    def out_spans(self, head, cut):
        stride = self.shard - cut
        return self.spans(head * self.head, self.head, self.out, stride, self.qkv - cut)

    def qkv_weight(self, ref):
        if self.qkv_cut == self.shard:
            return ref[...].reshape(self.total, -1)
        return ref[:, : self.qkv_cut, :].reshape(self.qkv_total, -1)

    def out_weight(self, ref):
        if self.out_cut == 0:
            return ref[...].reshape(self.total, -1)
        return ref[:, self.out_cut :, :].reshape(self.out_total, -1)


def read_rows(ref, spans):
    parts = [ref[place : place + length, :] for place, length in spans]
    return parts[0] if len(parts) == 1 else jnp.concatenate(parts, axis=0)


def write_rows(ref, spans, value):
    done = 0
    for place, length in spans:
        ref[place : place + length, :] = value[done : done + length, :]
        done += length


def inverse_size(values):
    return lax.rsqrt(jnp.mean(values * values, axis=-1, keepdims=True) + EPSILON)


def norm_back(values, inverse, gain, grad):
    scaled = grad * gain
    middle = jnp.mean(scaled * values, axis=-1, keepdims=True)
    grad_values = inverse * scaled - values * (inverse * inverse * inverse * middle)
    grad_gain = jnp.sum(grad * (values * inverse), axis=0, keepdims=True)
    return grad_values, grad_gain


def shares_of(queries, keys, allowed, live, scale):
    scores = [tn(key, query) for key, query in zip(keys, queries)]
    weights = [jnp.exp(jnp.where(allowed, score * scale, MASKED)) for score in scores]
    totals = [jnp.sum(weight, axis=0, keepdims=True) + (1.0 - live) for weight in weights]
    return [weight * (1.0 / total) for weight, total in zip(weights, totals)]


def attend_back(queries, keys, values, shares, shares_low, grads, scale):
    grad_shares = [tn(value, grad) for value, grad in zip(values, grads)]
    middles = [jnp.sum(a * b, axis=0, keepdims=True) for a, b in zip(shares, grad_shares)]
    grad_scores = [
        (share * (grad_share - middle) * scale).astype(BF16)
        for share, grad_share, middle in zip(shares, grad_shares, middles)
    ]
    return (
        [nn(key, grad_score) for key, grad_score in zip(keys, grad_scores)],
        [nt(query, grad_score) for query, grad_score in zip(queries, grad_scores)],
        [nt(grad, share) for grad, share in zip(grads, shares_low)],
    )


def clips_at(clips, frames):
    counts, times, numbers = (jnp.zeros_like(frames) for _ in range(3))
    for clip in range(clips.shape[1]):
        start = clips[1, clip] // FRAME
        member = (frames >= start) & (frames < start + clips[0, clip])
        counts = jnp.where(member, clips[2, clip] * clips[3, clip], counts)
        times = jnp.where(member, frames - start, times)
        numbers = jnp.where(member, clip + 1, numbers)
    return counts, times, numbers


def ids(shape, dim):
    return lax.broadcasted_iota(jnp.int32, shape, dim)


def space_masks(clips):
    count = clips_at(clips, lax.axis_index("ctx").astype(jnp.int32))[0]
    return ids((FRAME, FRAME), 0) < count, (ids((1, FRAME), 1) < count).astype(F32)


def time_masks(clips, near, slots):
    rank = lax.axis_index("ctx")
    token = ids((1, FRAME), 1)
    slot = lax.rem(token, slots)
    counts, times, numbers = clips_at(clips, (rank // near) * near + token // slots)
    alive = lax.rem(rank, near) * slots + slot < counts
    group = (numbers * FRAME + slot).astype(F32)
    keys = jnp.where(alive, group, -1.0)
    allowed = jnp.broadcast_to(keys, (FRAME, FRAME)).T == group
    return allowed, alive.astype(F32), times.astype(F32)


def turn_tables(times, half):
    frequency = jnp.exp(ids((half, FRAME), 0).astype(F32) * (-math.log(ROPE_BASE) / half))
    angles = frequency * times
    cosine, sine = jnp.cos(angles), jnp.sin(angles)
    return jnp.concatenate([cosine, cosine], axis=0), jnp.concatenate([-sine, sine], axis=0)


def out_columns(rows):
    return lax.rem(ids((1, rows.total), 1), rows.shard) >= rows.qkv


def gate(rows, *events, others=()):
    anywhere = pl.BlockSpec(memory_space=pl.ANY)
    arrays = (rows, *others)
    count = len(arrays)
    results = pl.pallas_call(
        lambda *refs: None,
        out_shape=tuple(jax.ShapeDtypeStruct(array.shape, array.dtype) for array in arrays),
        in_specs=[anywhere] * (count + len(events)),
        out_specs=(anywhere,) * count,
        input_output_aliases={index: index for index in range(count)},
        compiler_params=pltpu.CompilerParams(vmem_limit_bytes=1024 * 1024),
    )(*arrays, *events)
    return results if others else results[0]


def assemble(layouts, order, pieces, space, time):
    count = space.shape[1]

    def put(layout, target):
        for index, (piece, first) in enumerate(layout):
            target[order[index]] = pieces[piece][first : first + count, :]

    @pl.when(order[-1] == 0)
    def _():
        put(layouts[0], space)
        put(layouts[1], time)

    @pl.when(order[-1] != 0)
    def _():
        put(layouts[1], space)
        put(layouts[0], time)


def give(direct, stage, outs):
    if not direct:
        outs[0][...] = stage[...]
        return
    core = lax.rem(lax.axis_index("ctx"), 2)
    length = FRAME // (2 * direct)
    for chip in range(direct):
        for out, to in zip(outs, (core, 1 - core)):
            source = pl.ds(pl.multiple_of((2 * chip + to) * length, 16), length)
            out[chip * length : (chip + 1) * length, :] = stage[source, :]


def join(direct, own, from_twin, *outs):
    rank = lax.axis_index("ctx")
    core, chip = lax.rem(rank, 2), lax.rem(rank // 2, direct)
    length = own.shape[0] // direct
    for distance, out in enumerate(outs):
        source = pl.ds(pl.multiple_of((chip ^ distance) * length, 16), length)
        out[pl.ds(pl.multiple_of(core * length, 16), length), :] = own[source, :]
        out[pl.ds(pl.multiple_of((1 - core) * length, 16), length), :] = from_twin[source, :]


def collect(direct, arrived, stage):
    if not direct:
        return arrived[0]
    chip = lax.rem(lax.axis_index("ctx") // 2, direct)
    length = arrived[0].shape[0]
    for distance, part in enumerate(arrived):
        target = pl.ds(pl.multiple_of((chip ^ distance) * length, 16), length)
        stage[target, :] = part[...]
    return stage


def front(rows, layouts, order_of, direct, clips, tokens, gains, *refs):
    sends = 2 if direct else 1
    pieces, refs = refs[: -7 - sends], refs[-7 - sends :]
    hidden, saved, shares_out, space, time = refs[:5]
    mixed, stage = refs[-2:]
    assemble(layouts, order_of(), pieces, space, time)
    allowed, live = space_masks(clips)
    values = tokens[0].astype(F32)
    normed = (values * inverse_size(values) * gains[:1]).astype(BF16)
    mixed[...] = jnp.zeros_like(mixed)
    stride = rows.qkv_cut
    saved[...] = nt(rows.qkv_weight(space), normed)
    scale = rows.head ** (-0.5)
    queries, keys, values_in = (
        [read_rows(saved, rows.qkv_spans(which, head, stride)).astype(BF16) for head in range(HEADS)]
        for which in range(3)
    )
    shares = [share.astype(BF16) for share in shares_of(queries, keys, allowed, live, scale)]
    blended = [nn(value, share) * live for value, share in zip(values_in, shares)]
    for head in range(HEADS):
        shares_out[head] = shares[head]
        write_rows(mixed, rows.out_spans(head, rows.out_cut), blended[head])
    update = tn(mixed[...].astype(BF16), rows.out_weight(space))
    low = (values + update).astype(BF16)
    hidden[...] = low
    values = low.astype(F32)
    normed = (values * inverse_size(values) * gains[1:]).astype(BF16)
    both = nt(jnp.concatenate([normed, tokens[1]], axis=0), time[...].reshape(rows.total, -1))
    count = values.shape[0]
    stage[...] = jnp.where(out_columns(rows), both[count:], both[:count]).astype(BF16)
    give(direct, stage, refs[5:-2])


def time_core(rows, near, slots, direct, clips, *refs):
    project, result, stage = refs[-3:]
    arrived = collect(direct, refs[: direct or 1], stage)
    allowed, live, times = time_masks(clips, near, slots)
    for first in range(0, rows.total, FRAME):
        project[first : first + FRAME, :] = arrived[:, first : first + FRAME].astype(F32).T
    scale = rows.head ** (-0.5)
    half = rows.head // 2
    cosine, sine = turn_tables(times, half)

    def swapped(vectors):
        return jnp.concatenate([vectors[half:], vectors[:half]], axis=0)

    heads = range(HEADS)
    turned = []
    for which in range(2):
        vectors = [read_rows(project, rows.qkv_spans(which, head, rows.shard)) for head in heads]
        turned.append([(part * cosine + swapped(part) * sine).astype(BF16) for part in vectors])
    queries, keys = turned
    values = [read_rows(project, rows.qkv_spans(2, head, rows.shard)).astype(BF16) for head in heads]
    grads = [(read_rows(project, rows.out_spans(head, 0)) * live).astype(BF16) for head in heads]
    shares = shares_of(queries, keys, allowed, live, scale)
    shares_low = [share.astype(BF16) for share in shares]
    blended = [nn(value, share) * live for value, share in zip(values, shares_low)]
    parts = attend_back(queries, keys, values, shares, shares_low, grads, scale)
    for head in heads:
        write_rows(result, rows.out_spans(head, 0), blended[head])
        for which in range(2):
            turned_grad = parts[which][head].astype(BF16).astype(F32)
            write_rows(
                result,
                rows.qkv_spans(which, head, rows.shard),
                turned_grad * cosine - swapped(turned_grad) * sine,
            )
        write_rows(result, rows.qkv_spans(2, head, rows.shard), parts[2][head])
    for first in range(0, rows.total, FRAME):
        stage[:, first : first + FRAME] = result[first : first + FRAME, :].T.astype(BF16)
    give(direct, stage, refs[direct or 1 : -3])


def time_back(rows, direct, factor, clips, *refs):
    arrived, refs = refs[: direct or 1], refs[direct or 1 :]
    tokens, gains, time, space, hidden, saved, shares_in = refs[:7]
    grad_hidden_out, grad_normed_out, gain_parts, project, grad_project, stage = refs[7:]
    arrived = collect(direct, arrived, stage)
    live = space_masks(clips)[1]
    received = arrived[...]
    mask = jnp.broadcast_to(out_columns(rows), received.shape)
    left = jnp.where(mask, jnp.zeros_like(received), received)
    grad_normed = nn(left, time[...].reshape(rows.total, -1)).astype(BF16).astype(F32)
    values = hidden[...].astype(F32)
    grad_front, grad_time_gain = norm_back(values, inverse_size(values), gains[1:], grad_normed)
    grad_hidden = (tokens[1].astype(F32) + grad_front).astype(BF16)
    grad_hidden_out[...] = grad_hidden

    project[...] = nt(rows.out_weight(space), grad_hidden)
    grad_project[...] = jnp.zeros_like(grad_project)
    scale = rows.head ** (-0.5)
    heads = range(HEADS)
    spans = [[rows.qkv_spans(which, head, rows.qkv_cut) for head in heads] for which in range(3)]
    queries, keys, values_in = (
        [read_rows(saved, where).astype(BF16) for where in places] for places in spans
    )
    grads = [
        (read_rows(project, rows.out_spans(head, rows.out_cut)) * live).astype(BF16) for head in heads
    ]
    shares_low = [shares_in[head] for head in heads]
    shares = [share.astype(F32) for share in shares_low]
    parts = attend_back(queries, keys, values_in, shares, shares_low, grads, scale)
    for places, found in zip(spans, parts):
        for where, part in zip(places, found):
            write_rows(grad_project, where, part)
    grad_normed = tn(grad_project[...].astype(BF16), rows.qkv_weight(space)).astype(BF16)
    grad_normed_out[...] = grad_normed
    values = tokens[0].astype(F32)
    normed = values * inverse_size(values)
    grad_space_gain = jnp.sum(grad_normed.astype(F32) * normed, axis=0, keepdims=True)
    both_gains = jnp.concatenate([grad_space_gain, grad_time_gain], axis=0) * factor
    both_gains = both_gains.astype(gain_parts.dtype)
    gain_parts[...] = jnp.broadcast_to(both_gains[None], gain_parts.shape)


def finish(rows, direct, *refs):
    arrived, refs = refs[: direct or 1], refs[direct or 1 :]
    tokens, gains, time, hidden, grad_hidden, grad_normed, output, grad_tokens, stage = refs
    received = collect(direct, arrived, stage)[...]
    mask = jnp.broadcast_to(out_columns(rows), received.shape)
    left = jnp.where(mask, received, jnp.zeros_like(received))
    update = nn(left, time[...].reshape(rows.total, -1))
    output[...] = (hidden[...].astype(F32) + update).astype(BF16)
    values = tokens[0].astype(F32)
    grad = grad_normed[...].astype(F32)
    grad_values, _ = norm_back(values, inverse_size(values), gains[:1], grad)
    grad_tokens[...] = (grad_hidden[...].astype(F32) + grad_values).astype(BF16)


def call(body, out_shapes, scratch, clips, operands):
    clips = () if clips is None else (clips,)
    whole = pl.BlockSpec(memory_space=pltpu.VMEM)
    scalars = pl.BlockSpec(memory_space=pltpu.SMEM)
    return pl.pallas_call(
        body,
        out_shape=out_shapes,
        in_specs=[scalars] * len(clips) + [whole] * len(operands),
        out_specs=jax.tree.map(lambda _: whole, out_shapes),
        scratch_shapes=scratch,
        compiler_params=pltpu.CompilerParams(vmem_limit_bytes=VMEM_LIMIT),
    )(*clips, *operands)


def gather_ring(space_rows, time_rows, size, others):
    chips = size // 2
    chain = chips // 2
    shard = space_rows.shape[0]

    def chip_at(place):
        place = place % chips
        return 2 * place if place < chain else 2 * (chips - 1 - place) + 1

    ring_pairs = []
    for place in range(chips):
        ring_pairs.append((2 * chip_at(place), 2 * chip_at(place + 1)))
        ring_pairs.append((2 * chip_at(place) + 1, 2 * chip_at(place - 1) + 1))
    planes = lax.axis_size("dp")
    plane = lax.rem(lax.axis_index("dp"), 2)

    def ring(rows):
        return lax.ppermute(rows, "ctx", ring_pairs)

    def across(rows):
        return lax.ppermute(rows, "dp", [(index, index ^ 1) for index in range(planes)])

    def twin(rows):
        return lax.ppermute(rows, "ctx", [(index, index ^ 1) for index in range(size)])

    own = jnp.where(plane == 0, space_rows, time_rows)
    own_other = jnp.where(plane == 0, time_rows, space_rows)
    t0 = twin(own)
    o1 = ring(own)
    t1 = ring(t0)
    t0_other = twin(own_other)
    o2 = ring(o1)
    x_o1 = across(o1)
    o1_twin = twin(o1)
    o2 = gate(o2, t1, o1_twin, t0_other)
    t2 = ring(t1)
    x_o1_twin = twin(x_o1)
    x_t1 = across(t1)
    t1_twin = twin(t1)
    t2 = gate(t2, o2, t1_twin)
    o3 = ring(o2)
    o3 = gate(o3, t2, x_o1)
    o2_twin = twin(o2)
    t3 = ring(t2)
    t2_twin = twin(t2)
    x_t1, *others = gate(x_t1, t3, x_o1_twin, t2_twin, others=others)
    o4 = ring(o3)
    o4 = gate(o4, x_t1, t3)
    x_o3 = across(o3)
    o3_twin = twin(o3)
    x_o2 = ring(x_o1)
    t3_twin = twin(t3)
    x_t1_twin = twin(x_t1)
    x_t2 = ring(x_t1)
    x_o4 = across(o4)
    o4_twin = twin(o4)
    x_t2 = gate(x_t2, o4_twin, t3_twin, x_o3, x_o2)
    x_t3 = ring(x_t2)
    x_o2_twin = twin(x_o2)
    x_t2_twin = twin(x_t2)
    x_o3_twin = twin(x_o3)
    x_o4_twin = twin(x_o4)
    x_t3_twin = twin(x_t3)
    mine = {"o0": (own, 0), "t0": (t0, 0)}
    other = {"o0": (own_other, 0), "t0": (t0_other, 0)}
    mine |= {"o1": (o1, 0), "o1_twin": (o1_twin, 0)}
    other |= {"o1": (x_o1, 0), "o1_twin": (x_o1_twin, 0)}
    mine |= {"t1": (t1, 0), "t1_twin": (t1_twin, 0)}
    other |= {"t1": (x_t1, 0), "t1_twin": (x_t1_twin, 0)}
    mine |= {"o2": (o2, 0), "o2_twin": (o2_twin, 0)}
    other |= {"o2": (x_o2, 0), "o2_twin": (x_o2_twin, 0)}
    mine |= {"t2": (t2, 0), "t2_twin": (t2_twin, 0)}
    other |= {"t2": (x_t2, 0), "t2_twin": (x_t2_twin, 0)}
    mine |= {"o3": (o3, 0), "o3_twin": (o3_twin, 0)}
    other |= {"o3": (x_o3, 0), "o3_twin": (x_o3_twin, 0)}
    mine |= {"t3": (t3, 0), "t3_twin": (t3_twin, 0)}
    other |= {"t3": (x_t3, 0), "t3_twin": (x_t3_twin, 0)}
    mine |= {"o4": (o4, 0), "o4_twin": (o4_twin, 0)}
    other |= {"o4": (x_o4, 0), "o4_twin": (x_o4_twin, 0)}
    names = ["o0", "t0", "o1", "o2", "o3", "o4", "t1", "t2", "t3"]
    twins = names[2:]

    def order_of():
        rank = lax.axis_index("ctx")
        chip, core = rank // 2, lax.rem(rank, 2)
        column, level = lax.rem(chip, 2), chip // 2
        place = jnp.where(column == 0, level, chips - 1 - level)

        def came(carrier, name):
            steps, shard_core = int(name[1]), carrier if name[0] == "o" else 1 - carrier
            at = lax.rem(place + steps * (2 * carrier - 1) + chips, chips)
            return 2 * jnp.where(at < chain, 2 * at, 2 * (chips - 1 - at) + 1) + shard_core

        order = [came(core, name) for name in names] + [came(1 - core, name) for name in twins]
        return order + [lax.rem(lax.axis_index("dp"), 2)]

    pieces, layouts = [], ([], [])
    for half, found in enumerate((mine, other)):
        for name in names + [name + "_twin" for name in twins]:
            array, first = found[name]
            place_in = [index for index, piece in enumerate(pieces) if piece is array]
            if not place_in:
                place_in = [len(pieces)]
                pieces.append(array)
            layouts[half].append((place_in[0], first * shard))
    return pieces, layouts, order_of, others


def gather_weights(space_rows, time_rows, size, others):
    if size == 16 and lax.axis_size("dp") % 2 == 0:
        return gather_ring(space_rows, time_rows, size, others)
    shard, features = space_rows.shape
    gathered = lax.all_gather(jnp.concatenate([space_rows, time_rows], axis=0), "ctx", axis=0)
    gathered = gathered.reshape(size, 2, shard, features)
    halves = [gathered[:, half].reshape(size * shard, features) for half in range(2)]
    return halves, ([(0, 0)], [(1, 0)]), lambda: [0, 0], others


def shards(
    tokens,
    cotangent,
    clip_frames,
    clip_offsets,
    clip_heights,
    clip_widths,
    spatial_gain,
    spatial_qkv,
    spatial_out,
    temporal_gain,
    temporal_qkv,
    temporal_out,
):
    size = lax.axis_size("ctx")
    everyone = lax.axis_size("dp") * size
    count, features = tokens.shape[1], tokens.shape[2]
    assert count == FRAME and FRAME % size == 0
    near = size // 2
    slots = FRAME // near
    rows = Rows(spatial_qkv.shape[0], spatial_out.shape[0], size)
    both_tokens = jnp.concatenate([tokens, cotangent], axis=0)
    both_gains = jnp.stack([spatial_gain, temporal_gain])
    clips = jnp.concatenate([clip_frames, clip_offsets, clip_heights, clip_widths], axis=0)
    pieces, layouts, order_of, others = gather_weights(
        jnp.concatenate([spatial_qkv, spatial_out], axis=0),
        jnp.concatenate([temporal_qkv, temporal_out], axis=0),
        size,
        (both_tokens, both_gains, clips),
    )
    both_tokens, both_gains, clips = others
    wide = pltpu.VMEM((rows.total, FRAME), F32)
    qkv_wide = pltpu.VMEM((rows.qkv_total, FRAME), F32)
    out_wide = pltpu.VMEM((rows.out_total, FRAME), F32)
    blocks = len(layouts[0])
    weight_shape = jax.ShapeDtypeStruct((blocks, rows.total // blocks, features), BF16)
    groups = [list(range(first, first + near)) for first in range(0, size, near)]

    direct = 4 if near == 8 and slots % 16 == 0 else 0
    part = jax.ShapeDtypeStruct((FRAME // 2 if direct else FRAME, rows.total), BF16)
    parts = (part,) * (2 if direct else 1)
    stage = pltpu.VMEM((FRAME, rows.total), BF16)

    def exchange(sent):
        if not direct:
            arrived = lax.all_to_all(
                sent[0].reshape(near, slots, rows.total),
                "ctx",
                split_axis=0,
                concat_axis=0,
                axis_index_groups=groups,
                tiled=True,
            )
            return [arrived.reshape(FRAME, rows.total)]
        own, to_twin = sent
        from_twin = lax.ppermute(to_twin, "ctx", [(index, index ^ 1) for index in range(size)])
        joined = jax.ShapeDtypeStruct((2 * slots, rows.total), BF16)
        here, *away = call(
            functools.partial(join, direct), (joined,) * direct, [], None, (own, from_twin)
        )
        return [here] + [
            lax.ppermute(rows_away, "ctx", [(index, index ^ (2 * distance)) for index in range(size)])
            for distance, rows_away in list(enumerate(away, 1))[::-1]
        ][::-1]

    hidden, saved, shares, space_weights, time_weights, *sent = call(
        functools.partial(front, rows, layouts, order_of, direct),
        (
            jax.ShapeDtypeStruct((FRAME, features), BF16),
            jax.ShapeDtypeStruct((rows.qkv_total, FRAME), F32),
            jax.ShapeDtypeStruct((HEADS, FRAME, FRAME), BF16),
            weight_shape,
            weight_shape,
            *parts,
        ),
        [out_wide, stage],
        clips,
        (both_tokens, both_gains, *pieces),
    )
    arrived = exchange(sent)
    sent = call(
        functools.partial(time_core, rows, near, slots, direct),
        parts,
        [wide, wide, stage],
        clips,
        arrived,
    )
    arrived = exchange(sent)
    whole = jax.ShapeDtypeStruct((FRAME, features), BF16)
    grad_hidden, grad_normed, gains = call(
        functools.partial(time_back, rows, direct, 1.0 / math.sqrt(everyone * FRAME)),
        (whole, whole, jax.ShapeDtypeStruct((everyone, 2, features), BF16)),
        [out_wide, qkv_wide, stage],
        clips,
        (*arrived, both_tokens, both_gains, time_weights, space_weights, hidden, saved, shares),
    )
    gains = lax.all_to_all(gains, ("dp", "ctx"), split_axis=0, concat_axis=0, tiled=True)
    result, grad_tokens = call(
        functools.partial(finish, rows, direct),
        (whole, whole),
        [stage],
        None,
        (*arrived, both_tokens, both_gains, time_weights, hidden, grad_hidden, grad_normed),
    )
    gain_grads = jnp.sum(gains.astype(F32), axis=0)
    return result[None], grad_tokens[None], gain_grads


def solution(mesh):
    return jax.shard_map(
        shards,
        mesh=mesh,
        in_specs=(
            P("dp", "ctx", None),
            P("dp", "ctx", None),
            P("dp", None),
            P("dp", None),
            P("dp", None),
            P("dp", None),
            P(),
            P("ctx", None),
            P("ctx", None),
            P(),
            P("ctx", None),
            P("ctx", None),
        ),
        out_specs=(P("dp", "ctx", None), P("dp", "ctx", None), P()),
        check_vma=False,
    )
```

```python
import functools
import math

import jax
import jax.numpy as jnp
from jax import lax
from jax.experimental import pallas as pl
from jax.experimental.pallas import tpu as pltpu
from jax.sharding import PartitionSpec as P

HEADS = 8
FRAME = 128
EPSILON = 1e-06
ROPE_BASE = 10000.0
MASKED = -1e30
F32 = jnp.float32
BF16 = jnp.bfloat16
VMEM_LIMIT = 12 * 1024 * 1024


def nn(a, b):
    return lax.dot_general(a, b, (((1,), (0,)), ((), ())), preferred_element_type=F32)


def nt(a, b):
    return lax.dot_general(a, b, (((1,), (1,)), ((), ())), preferred_element_type=F32)


def tn(a, b):
    return lax.dot_general(a, b, (((0,), (0,)), ((), ())), preferred_element_type=F32)


class Rows:
    def __init__(self, qkv_rows, out_rows, size):
        self.qkv, self.out = qkv_rows, out_rows
        self.shard = qkv_rows + out_rows
        self.total = self.shard * size
        self.inner = out_rows * size
        self.head = self.inner // HEADS
        cut = self.shard % 16 == 0
        self.qkv_cut = -(-qkv_rows // 16) * 16 if cut else self.shard
        self.out_cut = qkv_rows // 16 * 16 if cut else 0
        self.qkv_total = self.qkv_cut * size
        self.out_total = (self.shard - self.out_cut) * size

    def spans(self, first, count, per_shard, stride, shift):
        found = []
        row = first
        while row < first + count:
            block, inside = divmod(row, per_shard)
            length = min(per_shard - inside, first + count - row)
            place = block * stride + shift + inside
            if found and found[-1][0] + found[-1][1] == place:
                found[-1] = (found[-1][0], found[-1][1] + length)
            else:
                found.append((place, length))
            row += length
        return found

    def qkv_spans(self, which, head, stride):
        return self.spans(which * self.inner + head * self.head, self.head, self.qkv, stride, 0)

    def out_spans(self, head, cut):
        stride = self.shard - cut
        return self.spans(head * self.head, self.head, self.out, stride, self.qkv - cut)

    def qkv_weight(self, ref):
        if self.qkv_cut == self.shard:
            return ref[...].reshape(self.total, -1)
        return ref[:, : self.qkv_cut, :].reshape(self.qkv_total, -1)

    def out_weight(self, ref):
        if self.out_cut == 0:
            return ref[...].reshape(self.total, -1)
        return ref[:, self.out_cut :, :].reshape(self.out_total, -1)


def read_rows(ref, spans):
    parts = [ref[place : place + length, :] for place, length in spans]
    return parts[0] if len(parts) == 1 else jnp.concatenate(parts, axis=0)


def write_rows(ref, spans, value):
    done = 0
    for place, length in spans:
        ref[place : place + length, :] = value[done : done + length, :]
        done += length


def inverse_size(values):
    return lax.rsqrt(jnp.mean(values * values, axis=-1, keepdims=True) + EPSILON)


def norm_back(values, inverse, gain, grad):
    scaled = grad * gain
    middle = jnp.mean(scaled * values, axis=-1, keepdims=True)
    grad_values = inverse * scaled - values * (inverse * inverse * inverse * middle)
    grad_gain = jnp.sum(grad * (values * inverse), axis=0, keepdims=True)
    return grad_values, grad_gain


def shares_of(queries, keys, allowed, live, scale):
    scores = [tn(key, query) for key, query in zip(keys, queries)]
    weights = [jnp.exp(jnp.where(allowed, score * scale, MASKED)) for score in scores]
    totals = [jnp.sum(weight, axis=0, keepdims=True) + (1.0 - live) for weight in weights]
    return [weight * (1.0 / total) for weight, total in zip(weights, totals)]


def attend_back(queries, keys, values, shares, shares_low, grads, scale):
    grad_shares = [tn(value, grad) for value, grad in zip(values, grads)]
    middles = [jnp.sum(a * b, axis=0, keepdims=True) for a, b in zip(shares, grad_shares)]
    grad_scores = [
        (share * (grad_share - middle) * scale).astype(BF16)
        for share, grad_share, middle in zip(shares, grad_shares, middles)
    ]
    return (
        [nn(key, grad_score) for key, grad_score in zip(keys, grad_scores)],
        [nt(query, grad_score) for query, grad_score in zip(queries, grad_scores)],
        [nt(grad, share) for grad, share in zip(grads, shares_low)],
    )


def clips_at(clips, frames):
    counts, times, numbers = (jnp.zeros_like(frames) for _ in range(3))
    for clip in range(clips.shape[1]):
        start = clips[1, clip] // FRAME
        member = (frames >= start) & (frames < start + clips[0, clip])
        counts = jnp.where(member, clips[2, clip] * clips[3, clip], counts)
        times = jnp.where(member, frames - start, times)
        numbers = jnp.where(member, clip + 1, numbers)
    return counts, times, numbers


def ids(shape, dim):
    return lax.broadcasted_iota(jnp.int32, shape, dim)


def space_masks(clips):
    count = clips_at(clips, lax.axis_index("ctx").astype(jnp.int32))[0]
    return ids((FRAME, FRAME), 0) < count, (ids((1, FRAME), 1) < count).astype(F32)


def time_masks(clips, near, slots):
    rank = lax.axis_index("ctx")
    token = ids((1, FRAME), 1)
    slot = lax.rem(token, slots)
    counts, times, numbers = clips_at(clips, (rank // near) * near + token // slots)
    alive = lax.rem(rank, near) * slots + slot < counts
    group = (numbers * FRAME + slot).astype(F32)
    keys = jnp.where(alive, group, -1.0)
    allowed = jnp.broadcast_to(keys, (FRAME, FRAME)).T == group
    return allowed, alive.astype(F32), times.astype(F32)


def turn_tables(times, half):
    frequency = jnp.exp(ids((half, FRAME), 0).astype(F32) * (-math.log(ROPE_BASE) / half))
    angles = frequency * times
    cosine, sine = jnp.cos(angles), jnp.sin(angles)
    return jnp.concatenate([cosine, cosine], axis=0), jnp.concatenate([-sine, sine], axis=0)


def out_columns(rows):
    return lax.rem(ids((1, rows.total), 1), rows.shard) >= rows.qkv


def gate(rows, *events, others=()):
    anywhere = pl.BlockSpec(memory_space=pl.ANY)
    arrays = (rows, *others)
    count = len(arrays)
    results = pl.pallas_call(
        lambda *refs: None,
        out_shape=tuple(jax.ShapeDtypeStruct(array.shape, array.dtype) for array in arrays),
        in_specs=[anywhere] * (count + len(events)),
        out_specs=(anywhere,) * count,
        input_output_aliases={index: index for index in range(count)},
        compiler_params=pltpu.CompilerParams(vmem_limit_bytes=1024 * 1024),
    )(*arrays, *events)
    return results if others else results[0]


def assemble(layouts, order, pieces, space, time):
    count = space.shape[1]

    def put(layout, target):
        for index, (piece, first) in enumerate(layout):
            target[order[index]] = pieces[piece][first : first + count, :]

    @pl.when(order[-1] == 0)
    def _():
        put(layouts[0], space)
        put(layouts[1], time)

    @pl.when(order[-1] != 0)
    def _():
        put(layouts[1], space)
        put(layouts[0], time)


def give(direct, stage, outs):
    if not direct:
        outs[0][...] = stage[...]
        return
    core = lax.rem(lax.axis_index("ctx"), 2)
    length = FRAME // (2 * direct)
    for chip in range(direct):
        for out, to in zip(outs, (core, 1 - core)):
            source = pl.ds(pl.multiple_of((2 * chip + to) * length, 16), length)
            out[chip * length : (chip + 1) * length, :] = stage[source, :]


def join(direct, own, from_twin, *outs):
    rank = lax.axis_index("ctx")
    core, chip = lax.rem(rank, 2), lax.rem(rank // 2, direct)
    length = own.shape[0] // direct
    for distance, out in enumerate(outs):
        source = pl.ds(pl.multiple_of((chip ^ distance) * length, 16), length)
        out[pl.ds(pl.multiple_of(core * length, 16), length), :] = own[source, :]
        out[pl.ds(pl.multiple_of((1 - core) * length, 16), length), :] = from_twin[source, :]


def collect(direct, arrived, stage):
    if not direct:
        return arrived[0]
    chip = lax.rem(lax.axis_index("ctx") // 2, direct)
    length = arrived[0].shape[0]
    for distance, part in enumerate(arrived):
        target = pl.ds(pl.multiple_of((chip ^ distance) * length, 16), length)
        stage[target, :] = part[...]
    return stage


def front(rows, layouts, order_of, direct, clips, tokens, gains, *refs):
    sends = 2 if direct else 1
    pieces, refs = refs[: -7 - sends], refs[-7 - sends :]
    hidden, saved, shares_out, space, time = refs[:5]
    mixed, stage = refs[-2:]
    assemble(layouts, order_of(), pieces, space, time)
    allowed, live = space_masks(clips)
    values = tokens[0].astype(F32)
    normed = (values * inverse_size(values) * gains[:1]).astype(BF16)
    mixed[...] = jnp.zeros_like(mixed)
    stride = rows.qkv_cut
    saved[...] = nt(rows.qkv_weight(space), normed)
    scale = rows.head ** (-0.5)
    queries, keys, values_in = (
        [read_rows(saved, rows.qkv_spans(which, head, stride)).astype(BF16) for head in range(HEADS)]
        for which in range(3)
    )
    shares = [share.astype(BF16) for share in shares_of(queries, keys, allowed, live, scale)]
    blended = [nn(value, share) * live for value, share in zip(values_in, shares)]
    for head in range(HEADS):
        shares_out[head] = shares[head]
        write_rows(mixed, rows.out_spans(head, rows.out_cut), blended[head])
    update = tn(mixed[...].astype(BF16), rows.out_weight(space))
    low = (values + update).astype(BF16)
    hidden[...] = low
    values = low.astype(F32)
    normed = (values * inverse_size(values) * gains[1:]).astype(BF16)
    both = nt(jnp.concatenate([normed, tokens[1]], axis=0), time[...].reshape(rows.total, -1))
    count = values.shape[0]
    stage[...] = jnp.where(out_columns(rows), both[count:], both[:count]).astype(BF16)
    give(direct, stage, refs[5:-2])


def time_core(rows, near, slots, direct, clips, *refs):
    project, result, stage = refs[-3:]
    arrived = collect(direct, refs[: direct or 1], stage)
    allowed, live, times = time_masks(clips, near, slots)
    for first in range(0, rows.total, FRAME):
        project[first : first + FRAME, :] = arrived[:, first : first + FRAME].astype(F32).T
    scale = rows.head ** (-0.5)
    half = rows.head // 2
    cosine, sine = turn_tables(times, half)

    def swapped(vectors):
        return jnp.concatenate([vectors[half:], vectors[:half]], axis=0)

    heads = range(HEADS)
    turned = []
    for which in range(2):
        vectors = [read_rows(project, rows.qkv_spans(which, head, rows.shard)) for head in heads]
        turned.append([(part * cosine + swapped(part) * sine).astype(BF16) for part in vectors])
    queries, keys = turned
    values = [read_rows(project, rows.qkv_spans(2, head, rows.shard)).astype(BF16) for head in heads]
    grads = [(read_rows(project, rows.out_spans(head, 0)) * live).astype(BF16) for head in heads]
    shares = shares_of(queries, keys, allowed, live, scale)
    shares_low = [share.astype(BF16) for share in shares]
    blended = [nn(value, share) * live for value, share in zip(values, shares_low)]
    parts = attend_back(queries, keys, values, shares, shares_low, grads, scale)
    for head in heads:
        write_rows(result, rows.out_spans(head, 0), blended[head])
        for which in range(2):
            turned_grad = parts[which][head].astype(BF16).astype(F32)
            write_rows(
                result,
                rows.qkv_spans(which, head, rows.shard),
                turned_grad * cosine - swapped(turned_grad) * sine,
            )
        write_rows(result, rows.qkv_spans(2, head, rows.shard), parts[2][head])
    for first in range(0, rows.total, FRAME):
        stage[:, first : first + FRAME] = result[first : first + FRAME, :].T.astype(BF16)
    give(direct, stage, refs[direct or 1 : -3])


def time_back(rows, direct, factor, clips, *refs):
    arrived, refs = refs[: direct or 1], refs[direct or 1 :]
    tokens, gains, time, space, hidden, saved, shares_in = refs[:7]
    grad_hidden_out, grad_normed_out, gain_parts, project, grad_project, stage = refs[7:]
    arrived = collect(direct, arrived, stage)
    live = space_masks(clips)[1]
    received = arrived[...]
    mask = jnp.broadcast_to(out_columns(rows), received.shape)
    left = jnp.where(mask, jnp.zeros_like(received), received)
    grad_normed = nn(left, time[...].reshape(rows.total, -1)).astype(BF16).astype(F32)
    values = hidden[...].astype(F32)
    grad_front, grad_time_gain = norm_back(values, inverse_size(values), gains[1:], grad_normed)
    grad_hidden = (tokens[1].astype(F32) + grad_front).astype(BF16)
    grad_hidden_out[...] = grad_hidden

    project[...] = nt(rows.out_weight(space), grad_hidden)
    grad_project[...] = jnp.zeros_like(grad_project)
    scale = rows.head ** (-0.5)
    heads = range(HEADS)
    spans = [[rows.qkv_spans(which, head, rows.qkv_cut) for head in heads] for which in range(3)]
    queries, keys, values_in = (
        [read_rows(saved, where).astype(BF16) for where in places] for places in spans
    )
    grads = [
        (read_rows(project, rows.out_spans(head, rows.out_cut)) * live).astype(BF16) for head in heads
    ]
    shares_low = [shares_in[head] for head in heads]
    shares = [share.astype(F32) for share in shares_low]
    parts = attend_back(queries, keys, values_in, shares, shares_low, grads, scale)
    for places, found in zip(spans, parts):
        for where, part in zip(places, found):
            write_rows(grad_project, where, part)
    grad_normed = tn(grad_project[...].astype(BF16), rows.qkv_weight(space)).astype(BF16)
    grad_normed_out[...] = grad_normed
    values = tokens[0].astype(F32)
    normed = values * inverse_size(values)
    grad_space_gain = jnp.sum(grad_normed.astype(F32) * normed, axis=0, keepdims=True)
    both_gains = jnp.concatenate([grad_space_gain, grad_time_gain], axis=0) * factor
    both_gains = both_gains.astype(gain_parts.dtype)
    gain_parts[...] = jnp.broadcast_to(both_gains[None], gain_parts.shape)


def finish(rows, direct, *refs):
    arrived, refs = refs[: direct or 1], refs[direct or 1 :]
    tokens, gains, time, hidden, grad_hidden, grad_normed, output, grad_tokens, stage = refs
    received = collect(direct, arrived, stage)[...]
    mask = jnp.broadcast_to(out_columns(rows), received.shape)
    left = jnp.where(mask, received, jnp.zeros_like(received))
    update = nn(left, time[...].reshape(rows.total, -1))
    output[...] = (hidden[...].astype(F32) + update).astype(BF16)
    values = tokens[0].astype(F32)
    grad = grad_normed[...].astype(F32)
    grad_values, _ = norm_back(values, inverse_size(values), gains[:1], grad)
    grad_tokens[...] = (grad_hidden[...].astype(F32) + grad_values).astype(BF16)


def call(body, out_shapes, scratch, clips, operands):
    clips = () if clips is None else (clips,)
    whole = pl.BlockSpec(memory_space=pltpu.VMEM)
    scalars = pl.BlockSpec(memory_space=pltpu.SMEM)
    return pl.pallas_call(
        body,
        out_shape=out_shapes,
        in_specs=[scalars] * len(clips) + [whole] * len(operands),
        out_specs=jax.tree.map(lambda _: whole, out_shapes),
        scratch_shapes=scratch,
        compiler_params=pltpu.CompilerParams(vmem_limit_bytes=VMEM_LIMIT),
    )(*clips, *operands)


def gather_ring(space_rows, time_rows, size, others):
    chips = size // 2
    chain = chips // 2
    shard = space_rows.shape[0]

    def chip_at(place):
        place = place % chips
        return 2 * place if place < chain else 2 * (chips - 1 - place) + 1

    ring_pairs = []
    for place in range(chips):
        ring_pairs.append((2 * chip_at(place), 2 * chip_at(place + 1)))
        ring_pairs.append((2 * chip_at(place) + 1, 2 * chip_at(place - 1) + 1))
    planes = lax.axis_size("dp")
    plane = lax.rem(lax.axis_index("dp"), 2)

    def ring(rows):
        return lax.ppermute(rows, "ctx", ring_pairs)

    def across(rows):
        return lax.ppermute(rows, "dp", [(index, index ^ 1) for index in range(planes)])

    def twin(rows):
        return lax.ppermute(rows, "ctx", [(index, index ^ 1) for index in range(size)])

    own = jnp.where(plane == 0, space_rows, time_rows)
    own_other = jnp.where(plane == 0, time_rows, space_rows)
    t0 = twin(own)
    o1 = ring(own)
    t1 = ring(t0)
    t0_other = twin(own_other)
    o2 = ring(o1)
    x_o1 = across(o1)
    o1_twin = twin(o1)
    o2 = gate(o2, t1, o1_twin, t0_other)
    t2 = ring(t1)
    x_o1_twin = twin(x_o1)
    x_t1 = across(t1)
    t1_twin = twin(t1)
    t2 = gate(t2, o2, t1_twin)
    o3 = ring(o2)
    o3 = gate(o3, t2, x_o1)
    o2_twin = twin(o2)
    t3 = ring(t2)
    t2_twin = twin(t2)
    x_t1, *others = gate(x_t1, t3, x_o1_twin, t2_twin, others=others)
    o4 = ring(o3)
    o4 = gate(o4, x_t1, t3)
    x_o3 = across(o3)
    o3_twin = twin(o3)
    x_o2 = ring(x_o1)
    t3_twin = twin(t3)
    x_t1_twin = twin(x_t1)
    x_t2 = ring(x_t1)
    x_o4 = across(o4)
    o4_twin = twin(o4)
    x_t2 = gate(x_t2, o4_twin, t3_twin, x_o3, x_o2)
    x_t3 = ring(x_t2)
    x_o2_twin = twin(x_o2)
    x_t2_twin = twin(x_t2)
    x_o3_twin = twin(x_o3)
    x_t3_twin = twin(x_t3)
    x_o4_twin = twin(x_o4)
    mine = {"o0": (own, 0), "t0": (t0, 0)}
    other = {"o0": (own_other, 0), "t0": (t0_other, 0)}
    mine |= {"o1": (o1, 0), "o1_twin": (o1_twin, 0)}
    other |= {"o1": (x_o1, 0), "o1_twin": (x_o1_twin, 0)}
    mine |= {"t1": (t1, 0), "t1_twin": (t1_twin, 0)}
    other |= {"t1": (x_t1, 0), "t1_twin": (x_t1_twin, 0)}
    mine |= {"o2": (o2, 0), "o2_twin": (o2_twin, 0)}
    other |= {"o2": (x_o2, 0), "o2_twin": (x_o2_twin, 0)}
    mine |= {"t2": (t2, 0), "t2_twin": (t2_twin, 0)}
    other |= {"t2": (x_t2, 0), "t2_twin": (x_t2_twin, 0)}
    mine |= {"o3": (o3, 0), "o3_twin": (o3_twin, 0)}
    other |= {"o3": (x_o3, 0), "o3_twin": (x_o3_twin, 0)}
    mine |= {"t3": (t3, 0), "t3_twin": (t3_twin, 0)}
    other |= {"t3": (x_t3, 0), "t3_twin": (x_t3_twin, 0)}
    mine |= {"o4": (o4, 0), "o4_twin": (o4_twin, 0)}
    other |= {"o4": (x_o4, 0), "o4_twin": (x_o4_twin, 0)}
    names = ["o0", "t0", "o1", "o2", "o3", "o4", "t1", "t2", "t3"]
    twins = names[2:]

    def order_of():
        rank = lax.axis_index("ctx")
        chip, core = rank // 2, lax.rem(rank, 2)
        column, level = lax.rem(chip, 2), chip // 2
        place = jnp.where(column == 0, level, chips - 1 - level)

        def came(carrier, name):
            steps, shard_core = int(name[1]), carrier if name[0] == "o" else 1 - carrier
            at = lax.rem(place + steps * (2 * carrier - 1) + chips, chips)
            return 2 * jnp.where(at < chain, 2 * at, 2 * (chips - 1 - at) + 1) + shard_core

        order = [came(core, name) for name in names] + [came(1 - core, name) for name in twins]
        return order + [lax.rem(lax.axis_index("dp"), 2)]

    pieces, layouts = [], ([], [])
    for half, found in enumerate((mine, other)):
        for name in names + [name + "_twin" for name in twins]:
            array, first = found[name]
            place_in = [index for index, piece in enumerate(pieces) if piece is array]
            if not place_in:
                place_in = [len(pieces)]
                pieces.append(array)
            layouts[half].append((place_in[0], first * shard))
    return pieces, layouts, order_of, others


def gather_weights(space_rows, time_rows, size, others):
    if size == 16 and lax.axis_size("dp") % 2 == 0:
        return gather_ring(space_rows, time_rows, size, others)
    shard, features = space_rows.shape
    gathered = lax.all_gather(jnp.concatenate([space_rows, time_rows], axis=0), "ctx", axis=0)
    gathered = gathered.reshape(size, 2, shard, features)
    halves = [gathered[:, half].reshape(size * shard, features) for half in range(2)]
    return halves, ([(0, 0)], [(1, 0)]), lambda: [0, 0], others


def shards(
    tokens,
    cotangent,
    clip_frames,
    clip_offsets,
    clip_heights,
    clip_widths,
    spatial_gain,
    spatial_qkv,
    spatial_out,
    temporal_gain,
    temporal_qkv,
    temporal_out,
):
    size = lax.axis_size("ctx")
    everyone = lax.axis_size("dp") * size
    count, features = tokens.shape[1], tokens.shape[2]
    assert count == FRAME and FRAME % size == 0
    near = size // 2
    slots = FRAME // near
    rows = Rows(spatial_qkv.shape[0], spatial_out.shape[0], size)
    both_tokens = jnp.concatenate([tokens, cotangent], axis=0)
    both_gains = jnp.stack([spatial_gain, temporal_gain])
    clips = jnp.concatenate([clip_frames, clip_offsets, clip_heights, clip_widths], axis=0)
    pieces, layouts, order_of, others = gather_weights(
        jnp.concatenate([spatial_qkv, spatial_out], axis=0),
        jnp.concatenate([temporal_qkv, temporal_out], axis=0),
        size,
        (both_tokens, both_gains, clips),
    )
    both_tokens, both_gains, clips = others
    wide = pltpu.VMEM((rows.total, FRAME), F32)
    qkv_wide = pltpu.VMEM((rows.qkv_total, FRAME), F32)
    out_wide = pltpu.VMEM((rows.out_total, FRAME), F32)
    blocks = len(layouts[0])
    weight_shape = jax.ShapeDtypeStruct((blocks, rows.total // blocks, features), BF16)
    groups = [list(range(first, first + near)) for first in range(0, size, near)]

    direct = 4 if near == 8 and slots % 16 == 0 else 0
    part = jax.ShapeDtypeStruct((FRAME // 2 if direct else FRAME, rows.total), BF16)
    parts = (part,) * (2 if direct else 1)
    stage = pltpu.VMEM((FRAME, rows.total), BF16)

    def exchange(sent):
        if not direct:
            arrived = lax.all_to_all(
                sent[0].reshape(near, slots, rows.total),
                "ctx",
                split_axis=0,
                concat_axis=0,
                axis_index_groups=groups,
                tiled=True,
            )
            return [arrived.reshape(FRAME, rows.total)]
        own, to_twin = sent
        from_twin = lax.ppermute(to_twin, "ctx", [(index, index ^ 1) for index in range(size)])
        joined = jax.ShapeDtypeStruct((2 * slots, rows.total), BF16)
        here, *away = call(
            functools.partial(join, direct), (joined,) * direct, [], None, (own, from_twin)
        )
        return [here] + [
            lax.ppermute(rows_away, "ctx", [(index, index ^ (2 * distance)) for index in range(size)])
            for distance, rows_away in list(enumerate(away, 1))[::-1]
        ][::-1]

    hidden, saved, shares, space_weights, time_weights, *sent = call(
        functools.partial(front, rows, layouts, order_of, direct),
        (
            jax.ShapeDtypeStruct((FRAME, features), BF16),
            jax.ShapeDtypeStruct((rows.qkv_total, FRAME), F32),
            jax.ShapeDtypeStruct((HEADS, FRAME, FRAME), BF16),
            weight_shape,
            weight_shape,
            *parts,
        ),
        [out_wide, stage],
        clips,
        (both_tokens, both_gains, *pieces),
    )
    arrived = exchange(sent)
    sent = call(
        functools.partial(time_core, rows, near, slots, direct),
        parts,
        [wide, wide, stage],
        clips,
        arrived,
    )
    arrived = exchange(sent)
    whole = jax.ShapeDtypeStruct((FRAME, features), BF16)
    grad_hidden, grad_normed, gains = call(
        functools.partial(time_back, rows, direct, 1.0 / math.sqrt(everyone * FRAME)),
        (whole, whole, jax.ShapeDtypeStruct((everyone, 2, features), BF16)),
        [out_wide, qkv_wide, stage],
        clips,
        (*arrived, both_tokens, both_gains, time_weights, space_weights, hidden, saved, shares),
    )
    gains = lax.all_to_all(gains, ("dp", "ctx"), split_axis=0, concat_axis=0, tiled=True)
    result, grad_tokens = call(
        functools.partial(finish, rows, direct),
        (whole, whole),
        [stage],
        None,
        (*arrived, both_tokens, both_gains, time_weights, hidden, grad_hidden, grad_normed),
    )
    gain_grads = jnp.sum(gains.astype(F32), axis=0)
    return result[None], grad_tokens[None], gain_grads


def solution(mesh):
    return jax.shard_map(
        shards,
        mesh=mesh,
        in_specs=(
            P("dp", "ctx", None),
            P("dp", "ctx", None),
            P("dp", None),
            P("dp", None),
            P("dp", None),
            P("dp", None),
            P(),
            P("ctx", None),
            P("ctx", None),
            P(),
            P("ctx", None),
            P("ctx", None),
        ),
        out_specs=(P("dp", "ctx", None), P("dp", "ctx", None), P()),
        check_vma=False,
    )
```
